32 devices in a mesh: shard: 4 (over y, core), ctx: 2 (over x), tp: 4 (over z).
Axes of the slice: x: 2, y: 2, z: 4, core: 2. Of those that a mesh axis runs over, the one named last changes fastest.
Arguments:
- hidden_in: bfloat16 [6144, 1536], P(('shard', 'ctx')), may hold values from -6 to 6
- seq_lengths: int32 [4], P('shard'), may hold values from 384 to 1536, as said below
- attn_gain: bfloat16 [1536], P(('shard', 'ctx')), may hold values from 0.5 to 1.5
- ffn_gain: bfloat16 [1536], P(('shard', 'ctx')), may hold values from 0.5 to 1.5
- query_gain: bfloat16 [64], replicated, may hold values from 0.5 to 1.5
- key_gain: bfloat16 [64], replicated, may hold values from 0.5 to 1.5
- w_query: bfloat16 [1536, 1536], P(('shard', 'ctx'), 'tp'), may hold values from -0.15625 to 0.15625
- w_key: bfloat16 [1536, 512], P(('shard', 'ctx'), 'tp'), may hold values from -0.15625 to 0.15625
- w_value: bfloat16 [1536, 512], P(('shard', 'ctx'), 'tp'), may hold values from -0.15625 to 0.15625
- w_out: bfloat16 [1536, 1536], P('tp', ('shard', 'ctx')), may hold values from -1.25 to 1.25
- w_gate: bfloat16 [1536, 6912], P(('shard', 'ctx'), 'tp'), may hold values from -0.15625 to 0.15625
- w_up: bfloat16 [1536, 6912], P(('shard', 'ctx'), 'tp'), may hold values from -0.15625 to 0.15625
- w_down: bfloat16 [6912, 1536], P('tp', ('shard', 'ctx')), may hold values from -0.078125 to 0.078125
- out_grad: bfloat16 [6144, 1536], P(('shard', 'ctx')), may hold values from -6 to 6
Outputs:
- block_out: bfloat16 [6144, 1536], P(('shard', 'ctx'))
- input_grad: float32 [6144, 1536], P(('shard', 'ctx'))
- attn_gain_grad: float32 [1536], P(('shard', 'ctx'))
- ffn_gain_grad: float32 [1536], P(('shard', 'ctx'))
- query_gain_grad: float32 [64], replicated
- key_gain_grad: float32 [64], replicated
- w_query_grad: float32 [1536, 1536], P(('shard', 'ctx'), 'tp')
- w_key_grad: float32 [1536, 512], P(('shard', 'ctx'), 'tp')
- w_value_grad: float32 [1536, 512], P(('shard', 'ctx'), 'tp')
- w_out_grad: float32 [1536, 1536], P('tp', ('shard', 'ctx'))
- w_gate_grad: float32 [1536, 6912], P(('shard', 'ctx'), 'tp')
- w_up_grad: float32 [1536, 6912], P(('shard', 'ctx'), 'tp')
- w_down_grad: float32 [6912, 1536], P('tp', ('shard', 'ctx'))
The draws below stay inside these ranges and needn't reach their ends.
Inputs may be any that keep to these rules, and one draw needn't show every extreme that they name: `seq_lengths`: one sequence, drawn from the seed, has all 1536 positions valid; every sequence has at least a quarter of them.
All inputs are finite; a program needn't handle non-finite values.
Results may differ from the reference program's by a relative error of at most 0.013.
Values may be sent and summed in bfloat16 or wider, within the bound.
A program may use at most 192 MiB of HBM per device.

```python
import jax
import jax.numpy as jnp
from jax import lax

D = 1536
QH = 24
KVH = 8
HD = 64
FF = 6912
TOK_DEV = 768
TOKENS = 6144
N_SHARD = 4
N_CTX = 2


def draw_seq_lengths(key, part):
    key = jax.random.fold_in(key, 7)
    first, second = jax.random.split(key)
    full = TOK_DEV * N_CTX
    picked = jax.random.randint(first, (), 0, N_SHARD)
    drawn = jax.random.randint(second, (N_SHARD,), full // 4, full + 1)
    return jnp.where(jnp.arange(N_SHARD) == picked, full, drawn).astype(jnp.int32)


def levels(stream_key, extent, shards, low, high):
    def one(axis_at, shards_of):
        heights = jax.random.uniform(jax.random.fold_in(jax.random.fold_in(stream_key, 6), axis_at), (shards_of,), jnp.float32, low / len(shards), high / len(shards))
        return jnp.repeat(jnp.exp(heights), extent[axis_at] // shards_of).reshape((-1,) + (1,) * (len(extent) - axis_at - 1))

    level = one(*shards[0])
    for cut in shards[1:]:
        level = level * one(*cut)
    return level


def scatter_about(own_key, shape, spread, most, cuts=(), held_as=jnp.bfloat16):
    values = jax.random.normal(own_key, shape, jnp.float32) * spread
    if len(cuts) > 0:
        values = levels(own_key, shape, cuts, -0.22, 0.18) * values
    return jnp.clip(values, min=-most, max=most).astype(held_as)


def setup_inputs(seed: int = 0) -> dict:
    key_list = jax.random.split(jax.random.key(seed), 15)
    return {
        "hidden_in": scatter_about(key_list[0], (TOKENS, D), 1.0, 6.0, ((0, 8),)),
        "seq_lengths": draw_seq_lengths(jax.random.fold_in(key_list[14], 71), 0),
        "attn_gain": jnp.clip(1.0 + 0.1 * jax.random.normal(key_list[2], (D,), jnp.float32), 0.5, 1.5).astype(jnp.bfloat16),
        "ffn_gain": jnp.clip(1.0 + 0.1 * jax.random.normal(key_list[3], (D,), jnp.float32), 0.5, 1.5).astype(jnp.bfloat16),
        "query_gain": jnp.clip(1.0 + 0.1 * jax.random.normal(key_list[4], (HD,), jnp.float32), 0.5, 1.5).astype(jnp.bfloat16),
        "key_gain": jnp.clip(1.0 + 0.1 * jax.random.normal(key_list[5], (HD,), jnp.float32), 0.5, 1.5).astype(jnp.bfloat16),
        "w_query": scatter_about(key_list[6], (D, QH * HD), D ** -0.5, 0.15625, ((0, 8), (1, 4))),
        "w_key": scatter_about(key_list[7], (D, KVH * HD), D ** -0.5, 0.15625, ((0, 8), (1, 4))),
        "w_value": scatter_about(key_list[8], (D, KVH * HD), D ** -0.5, 0.15625, ((0, 8), (1, 4))),
        "w_out": scatter_about(key_list[9], (QH * HD, D), (QH * HD // 64) ** -0.5, 1.25, ((0, 4), (1, 8))),
        "w_gate": scatter_about(key_list[10], (D, FF), D ** -0.5, 0.15625, ((0, 8), (1, 4))),
        "w_up": scatter_about(key_list[11], (D, FF), D ** -0.5, 0.15625, ((0, 8), (1, 4))),
        "w_down": scatter_about(key_list[12], (FF, D), FF ** -0.5, 0.078125, ((0, 4), (1, 8))),
        "out_grad": scatter_about(key_list[13], (TOKENS, D), 1.0, 6.0, ((0, 8),)),
    }


EPSILON = 1e-05
ROPE_BASE = 1000000.0

@jax.custom_vjp
def low(v):
    return lax.optimization_barrier(v.astype(jnp.bfloat16)).astype(jnp.float32)

@jax.custom_vjp
def low_back(v):
    return v

def low_keep(v):
    return (low(v), None)

def low_pass(kept, grad):
    return (grad,)

def back_keep(v):
    return (v, None)

def back_low(kept, grad):
    return (low(grad),)
low.defvjp(low_keep, low_pass)
low_back.defvjp(back_keep, back_low)

def norm_rows(value, gain):
    scale = lax.rsqrt(lax.optimization_barrier(jnp.mean(value * value, axis=-1, keepdims=True)) + EPSILON)
    return value * scale * gain

def rotate(values, positions):
    half = values.shape[-1] // 2
    freq = ROPE_BASE ** (-jnp.arange(half, dtype=jnp.float32) / half)
    angle = positions.astype(jnp.float32)[:, None] * freq[None, :]
    cosine = jnp.cos(angle)[:, None, :]
    sine = jnp.sin(angle)[:, None, :]
    first = values[..., :half]
    second = values[..., half:]
    return jnp.concatenate([first * cosine - second * sine, second * cosine + first * sine], axis=-1)

def head_prep(proj, gain, positions):
    heads = proj.reshape(proj.shape[0], -1, gain.shape[0])
    return rotate(norm_rows(heads, gain), positions)

def matmul(left, right):
    return jnp.dot(left, right, precision=lax.Precision.HIGHEST)

def attend(queries, keys, values, length):
    seq = queries.shape[0]
    block = min(512, seq)
    scale = 1.0 / HD ** 0.5
    key_pos = jnp.arange(seq, dtype=jnp.int32)

    def one_block(start):
        query_rows = lax.dynamic_slice_in_dim(queries, start, block, 0)
        query_pos = start + jnp.arange(block, dtype=jnp.int32)
        score = jnp.einsum('tkgd,skd->kgts', query_rows, keys, precision=lax.Precision.HIGHEST) * scale
        score = low_back(score)
        mask = (key_pos[None, :] <= query_pos[:, None]) & (key_pos[None, :] < length)
        masked = jnp.where(mask, score, -1e+30)
        log_total = jax.nn.logsumexp(masked, axis=-1, keepdims=True)
        probs = low(jnp.where(mask, jnp.exp(masked - log_total), 0.0))
        return jnp.einsum('kgts,skd->tkgd', probs, values, precision=lax.Precision.HIGHEST)
    starts = jnp.arange(seq // block, dtype=jnp.int32) * block
    mixed = lax.map(jax.checkpoint(one_block), starts)
    return mixed.reshape(seq, -1)

def sequence(hidden, length, params):
    gain_one, gain_two, q_gain, k_gain, wq_full, wk_full, wv_full, wo_full, wg_full, wu_full, wd_full = params
    seq = hidden.shape[0]
    positions = jnp.arange(seq, dtype=jnp.int32)
    valid = (positions < length).astype(jnp.float32)[:, None]
    normed_one = low(norm_rows(hidden, gain_one))
    query_proj = low_back(matmul(normed_one, wq_full))
    key_proj = low_back(matmul(normed_one, wk_full))
    value_proj = low_back(matmul(normed_one, wv_full))
    queries = low(head_prep(query_proj, q_gain, positions)).reshape(seq, KVH, QH // KVH, HD)
    keys = low(head_prep(key_proj, k_gain, positions))
    values = low(value_proj.reshape(seq, KVH, HD))
    heads_out = low_back(low(attend(queries, keys, values, length)))
    resid = hidden + low_back(matmul(heads_out, wo_full))
    normed_two = low(norm_rows(resid, gain_two))
    gate = low_back(matmul(normed_two, wg_full))
    up = low_back(matmul(normed_two, wu_full))
    middle = low(jax.nn.silu(gate) * up)
    return valid * (resid + low_back(matmul(middle, wd_full)))

def reference(hidden_in, seq_lengths, attn_gain, ffn_gain, query_gain, key_gain, w_query, w_key, w_value, w_out, w_gate, w_up, w_down, out_grad):
    params = tuple((weight.astype(jnp.float32) for weight in (attn_gain, ffn_gain, query_gain, key_gain, w_query, w_key, w_value, w_out, w_gate, w_up, w_down)))
    stacked = hidden_in.astype(jnp.float32).reshape(N_SHARD, -1, D)

    def forward(inputs, weights):

        def one_sequence(pair):
            return sequence(pair[0], pair[1], weights)
        return lax.map(one_sequence, (inputs, seq_lengths))
    result, pull = jax.vjp(forward, stacked, params)
    input_grads, grads = pull(out_grad.astype(jnp.float32).reshape(result.shape))
    return (result.reshape(-1, D).astype(jnp.bfloat16), input_grads.reshape(-1, D), grads[0], grads[1], grads[2], grads[3], grads[4], grads[5], grads[6], grads[7], grads[8], grads[9], grads[10])
```

```python
import functools
import math

import jax
import jax.numpy as jnp
import numpy as np
from jax import lax
from jax.experimental import pallas as pl
from jax.experimental.pallas import tpu as pltpu
from jax.sharding import PartitionSpec as P

EPSILON = 1e-05
ROPE_BASE = 1000000.0
MESH = pl.DeviceIdType.MESH
F32 = jnp.float32
BF16 = jnp.bfloat16
VMEM_LIMIT = 60 << 20


def norm_rows(value, gain):
    scale = lax.rsqrt(jnp.mean(value * value, axis=-1, keepdims=True) + EPSILON)
    return value * scale * gain


def rotate(values, positions):
    half = values.shape[-1] // 2
    freq = ROPE_BASE ** (-jnp.arange(half, dtype=jnp.float32) / half)
    angle = positions.astype(jnp.float32)[:, None] * freq[None, :]
    cosine = jnp.cos(angle)[:, None, :]
    sine = jnp.sin(angle)[:, None, :]
    first = values[..., :half]
    second = values[..., half:]
    return jnp.concatenate(
        [first * cosine - second * sine, second * cosine + first * sine], axis=-1
    )


def head_prep(proj, gain, positions):
    heads = proj.reshape(proj.shape[0], -1, gain.shape[0])
    return rotate(norm_rows(heads, gain), positions)


def activation(gate_in, up_in):
    return jax.nn.silu(gate_in) * up_in


def forward_product(left, right):
    return jnp.dot(left, right, preferred_element_type=jnp.float32)


def outer_product(left, right):
    return lax.dot_general(
        left, right, (((0,), (0,)), ((), ())), preferred_element_type=jnp.float32
    )


def back_product(grad, weight):
    return lax.dot_general(
        grad, weight, (((1,), (1,)), ((), ())), preferred_element_type=jnp.float32
    )


def body(
    hidden_in,
    seq_lengths,
    attn_gain,
    ffn_gain,
    query_gain,
    key_gain,
    w_query,
    w_key,
    w_value,
    w_out,
    w_gate,
    w_up,
    w_down,
    out_grad,
):
    rows = hidden_in.shape[0]
    head_dim = query_gain.shape[0]
    kv_heads = w_key.shape[1] // head_dim
    q_heads = w_query.shape[1] // head_dim
    group = q_heads // kv_heads
    pieces = lax.axis_size("ctx")
    scale = 1.0 / math.sqrt(head_dim)
    positions = lax.axis_index("ctx") * rows + jnp.arange(rows, dtype=jnp.int32)
    length = seq_lengths[0]
    valid = (positions < length).astype(jnp.float32)[:, None]
    live_blocks = jnp.minimum(lax.axis_index("ctx"), (length - 1) // rows) + 1
    gathered = (
        lax.all_gather(attn_gain, ("shard", "ctx"), axis=0, tiled=True),
        lax.all_gather(ffn_gain, ("shard", "ctx"), axis=0, tiled=True),
        lax.all_gather(w_query, ("shard", "ctx"), axis=0, tiled=True),
        lax.all_gather(w_key, ("shard", "ctx"), axis=0, tiled=True),
        lax.all_gather(w_value, ("shard", "ctx"), axis=0, tiled=True),
        lax.all_gather(w_gate, ("shard", "ctx"), axis=0, tiled=True),
        lax.all_gather(w_up, ("shard", "ctx"), axis=0, tiled=True),
        lax.all_gather(w_out, ("shard", "ctx"), axis=1, tiled=True),
        lax.all_gather(w_down, ("shard", "ctx"), axis=1, tiled=True),
    )
    gain_one = gathered[0].astype(jnp.float32)
    gain_two = gathered[1].astype(jnp.float32)
    full_query, full_key, full_value, full_gate, full_up, full_out, full_down = gathered[2:]
    q_gain = query_gain.astype(jnp.float32)
    k_gain = key_gain.astype(jnp.float32)
    hidden = hidden_in.astype(jnp.float32)
    normed_one = norm_rows(hidden, gain_one).astype(jnp.bfloat16)
    query_proj = forward_product(normed_one, full_query)
    key_proj = forward_product(normed_one, full_key)
    value_proj = forward_product(normed_one, full_value)
    queries = (
        head_prep(query_proj, q_gain, positions)
        .astype(jnp.bfloat16)
        .reshape(rows, kv_heads, group, head_dim)
    )
    keys_own = head_prep(key_proj, k_gain, positions).astype(jnp.bfloat16)
    values_own = value_proj.reshape(rows, kv_heads, head_dim).astype(jnp.bfloat16)
    keys_all, values_all = (
        lax.all_gather(keys_own, "ctx", axis=0, tiled=True),
        lax.all_gather(values_own, "ctx", axis=0, tiled=True),
    )
    key_blocks = keys_all.reshape(pieces, rows, kv_heads, head_dim)
    value_blocks = values_all.reshape(pieces, rows, kv_heads, head_dim)

    def key_at(index):
        return lax.dynamic_index_in_dim(key_blocks, index, 0, keepdims=False)

    def value_at(index):
        return lax.dynamic_index_in_dim(value_blocks, index, 0, keepdims=False)

    def block_scores(key_block, index):
        key_pos = index * rows + jnp.arange(rows, dtype=jnp.int32)
        mask = ((key_pos[None, :] <= positions[:, None]) & (key_pos[None, :] < length))[None, None]
        raw = (
            jnp.einsum("tkgd,skd->kgts", queries, key_block, preferred_element_type=jnp.float32)
            * scale
        )
        return (jnp.where(mask, raw, -1e30), mask)

    def stats_step(index, carry):
        top, total = carry
        masked, mask = block_scores(key_at(index), index)
        new_top = jnp.maximum(top, jnp.max(masked, axis=-1))
        weight = jnp.where(mask, jnp.exp(masked - new_top[..., None]), 0.0)
        total = total * jnp.exp(top - new_top) + jnp.sum(weight, axis=-1)
        return (new_top, total)

    start = (
        jnp.full((kv_heads, group, rows), -1e30, jnp.float32),
        jnp.zeros((kv_heads, group, rows), jnp.float32),
    )
    top, total = lax.fori_loop(0, live_blocks, stats_step, start)
    log_total = top + jnp.log(total)

    def probs_of(key_block, index):
        masked, mask = block_scores(key_block, index)
        return jnp.where(mask, jnp.exp(masked - log_total[..., None]), 0.0)

    def mix_step(index, accum):
        probs = probs_of(key_at(index), index).astype(jnp.bfloat16)
        return accum + jnp.einsum(
            "kgts,skd->tkgd", probs, value_at(index), preferred_element_type=jnp.float32
        )

    head_zeros = jnp.zeros((rows, kv_heads, group, head_dim), jnp.float32)
    mixed = lax.fori_loop(0, live_blocks, mix_step, head_zeros)
    heads_out = mixed.reshape(rows, -1).astype(jnp.bfloat16)
    attn_term = forward_product(heads_out, full_out)
    resid = hidden + lax.psum(attn_term, "tp")
    normed_two = norm_rows(resid, gain_two).astype(jnp.bfloat16)
    gate = forward_product(normed_two, full_gate)
    up = forward_product(normed_two, full_up)
    middle = activation(gate, up).astype(jnp.bfloat16)
    ffn_term = forward_product(middle, full_down)
    ffn = lax.psum(ffn_term.astype(jnp.bfloat16), "tp").astype(jnp.float32)
    block_out = (valid * (resid + ffn)).astype(jnp.bfloat16)
    grad_top = valid * out_grad.astype(jnp.float32)
    grad_low = grad_top.astype(jnp.bfloat16)
    down_wgrad = outer_product(middle, grad_low)
    mid_grad = back_product(grad_low, full_down)
    _, pull_act = jax.vjp(activation, gate, up)
    gate_float, up_float = pull_act(mid_grad)
    gate_low = gate_float.astype(jnp.bfloat16)
    up_low = up_float.astype(jnp.bfloat16)
    gate_wgrad = outer_product(normed_two, gate_low)
    up_wgrad = outer_product(normed_two, up_low)
    normed_two_part = back_product(gate_low, full_gate) + back_product(up_low, full_up)
    normed_two_grad = lax.psum(normed_two_part, "tp")
    _, pull_two = jax.vjp(norm_rows, resid, gain_two)
    resid_part, gain_two_grad = pull_two(normed_two_grad)
    resid_grad = grad_top + resid_part
    attn_low = resid_grad.astype(jnp.bfloat16)
    out_wgrad = outer_product(heads_out, attn_low)
    heads_grad = (
        back_product(attn_low, full_out)
        .astype(jnp.bfloat16)
        .reshape(rows, kv_heads, group, head_dim)
    )

    def delta_step(index, accum):
        probs = probs_of(key_at(index), index)
        prob_grad = jnp.einsum(
            "tkgd,skd->kgts", heads_grad, value_at(index), preferred_element_type=jnp.float32
        )
        return accum + jnp.sum(probs * prob_grad, axis=-1)

    delta = lax.fori_loop(
        0, live_blocks, delta_step, jnp.zeros((kv_heads, group, rows), jnp.float32)
    )

    def grad_step(index, carry):
        accum, key_store, value_store = carry
        key_block = key_at(index)
        probs = probs_of(key_block, index)
        prob_grad = jnp.einsum(
            "tkgd,skd->kgts", heads_grad, value_at(index), preferred_element_type=jnp.float32
        )
        score_grad = (probs * (prob_grad - delta[..., None])).astype(jnp.bfloat16)
        accum = (
            accum
            + jnp.einsum(
                "kgts,skd->tkgd", score_grad, key_block, preferred_element_type=jnp.float32
            )
            * scale
        )
        key_grad = (
            jnp.einsum("kgts,tkgd->skd", score_grad, queries, preferred_element_type=jnp.float32)
            * scale
        )
        value_grad = jnp.einsum(
            "kgts,tkgd->skd",
            probs.astype(jnp.bfloat16),
            heads_grad,
            preferred_element_type=jnp.float32,
        )
        key_store = lax.dynamic_update_index_in_dim(key_store, key_grad, index, 0)
        value_store = lax.dynamic_update_index_in_dim(value_store, value_grad, index, 0)
        return (accum, key_store, value_store)

    store_zeros = jnp.zeros((pieces, rows, kv_heads, head_dim), jnp.float32)
    query_grad, key_grads, value_grads = lax.fori_loop(
        0, live_blocks, grad_step, (head_zeros, store_zeros, store_zeros)
    )
    key_grad_own, value_grad_own = (
        lax.psum_scatter(
            key_grads.reshape(pieces * rows, kv_heads, head_dim),
            "ctx",
            scatter_dimension=0,
            tiled=True,
        ),
        lax.psum_scatter(
            value_grads.reshape(pieces * rows, kv_heads, head_dim),
            "ctx",
            scatter_dimension=0,
            tiled=True,
        ),
    )

    def query_prep(proj, gain):
        return head_prep(proj, gain, positions)

    _, pull_query = jax.vjp(query_prep, query_proj, q_gain)
    query_proj_grad, q_gain_grad = pull_query(query_grad.reshape(rows, q_heads, head_dim))
    _, pull_key = jax.vjp(query_prep, key_proj, k_gain)
    key_proj_grad, k_gain_grad = pull_key(key_grad_own)
    query_low = query_proj_grad.astype(jnp.bfloat16)
    key_low = key_proj_grad.astype(jnp.bfloat16)
    value_low = value_grad_own.reshape(rows, -1).astype(jnp.bfloat16)
    query_wgrad = outer_product(normed_one, query_low)
    key_wgrad = outer_product(normed_one, key_low)
    value_wgrad = outer_product(normed_one, value_low)
    normed_one_part = (
        back_product(query_low, full_query)
        + back_product(key_low, full_key)
        + back_product(value_low, full_value)
    )
    normed_one_grad = lax.psum(normed_one_part, "tp")
    _, pull_one = jax.vjp(norm_rows, hidden, gain_one)
    hidden_part, gain_one_grad = pull_one(normed_one_grad)
    input_grad = resid_grad + hidden_part
    head_sums = lax.psum((q_gain_grad, k_gain_grad), ("shard", "ctx", "tp"))
    summed = (
        lax.psum_scatter(gain_one_grad, ("shard", "ctx"), scatter_dimension=0, tiled=True),
        lax.psum_scatter(gain_two_grad, ("shard", "ctx"), scatter_dimension=0, tiled=True),
        lax.psum_scatter(query_wgrad, ("shard", "ctx"), scatter_dimension=0, tiled=True),
        lax.psum_scatter(key_wgrad, ("shard", "ctx"), scatter_dimension=0, tiled=True),
        lax.psum_scatter(value_wgrad, ("shard", "ctx"), scatter_dimension=0, tiled=True),
        lax.psum_scatter(gate_wgrad, ("shard", "ctx"), scatter_dimension=0, tiled=True),
        lax.psum_scatter(up_wgrad, ("shard", "ctx"), scatter_dimension=0, tiled=True),
        lax.psum_scatter(out_wgrad, ("shard", "ctx"), scatter_dimension=1, tiled=True),
        lax.psum_scatter(down_wgrad, ("shard", "ctx"), scatter_dimension=1, tiled=True),
    )
    (
        gain_one_out,
        gain_two_out,
        query_out,
        key_out,
        value_out,
        gate_out,
        up_out,
        out_out,
        down_out,
    ) = summed
    return (
        block_out,
        input_grad,
        gain_one_out,
        gain_two_out,
        head_sums[0],
        head_sums[1],
        query_out,
        key_out,
        value_out,
        out_out,
        gate_out,
        up_out,
        down_out,
    )


def remote(src, dst, send, recv, dev):
    return pltpu.make_async_remote_copy(
        src_ref=src,
        dst_ref=dst,
        send_sem=send,
        recv_sem=recv,
        device_id=dev,
        device_id_type=MESH,
    )


def mm(a, b):
    return jnp.dot(a, b, preferred_element_type=F32)


def mm_nt(a, b):
    return lax.dot_general(a, b, (((1,), (1,)), ((), ())), preferred_element_type=F32)


class Place:
    def __init__(self, n_shard, n_tp):
        s = lax.axis_index("shard")
        c = lax.axis_index("ctx")
        t = lax.axis_index("tp")
        self.s, self.c, self.t = s, c, t
        self.core = lax.rem(s, 2)
        sib = s + 1 - 2 * self.core
        far = lax.rem(s + 2, n_shard)
        far_sib = far + 1 - 2 * self.core
        self.sib = (sib, c, t)
        self.x = (s, 1 - c, t)
        self.y = (far, c, t)
        first = 1 - self.core
        self.relay = (
            first * s + self.core * far,
            first * (1 - c) + self.core * c,
            t,
        )
        slot = lambda a, b: a * 2 + b
        self.own = slot(s, c)
        self.slots = {
            "S": slot(sib, c),
            "X": slot(s, 1 - c),
            "Y": slot(far, c),
            "D": slot(far, 1 - c),
            "SX": slot(sib, 1 - c),
            "SY": slot(far_sib, c),
            "SD": slot(far_sib, 1 - c),
        }
        self.relayed = first * self.slots["Y"] + self.core * self.slots["X"]
        self.n_tp = n_tp

    def z(self, t):
        return (self.s, self.c, t)

    def greet(self):
        peers = [self.sib, self.x, self.y]
        peers += [
            self.z(lax.rem(self.t + d, self.n_tp)) for d in range(1, self.n_tp)
        ]
        barrier = pltpu.get_barrier_semaphore()
        for peer in peers:
            pl.semaphore_signal(barrier, inc=1, device_id=peer, device_id_type=MESH)
        pl.semaphore_wait(barrier, len(peers))


ROLES = ("S", "X", "Y", "D", "SX", "SY", "SD")


class Gather:
    def __init__(self, at, own, full, send, recv, index):
        self.at, self.own, self.full = at, own, full
        self.send, self.recv, self.index = send, recv, index
        self.rows = own.shape[0]

    def block(self, slot):
        return self.full.at[pl.ds(pl.multiple_of(slot * self.rows, self.rows), self.rows)]

    def copy(self, role, src, slot, dev):
        k = ROLES.index(role)
        return remote(
            src,
            self.block(slot),
            self.send.at[self.index, k],
            self.recv.at[self.index, k],
            dev,
        )

    def arrived(self, role):
        slot = self.at.slots[role]
        self.copy(role, self.block(slot), slot, self.at.sib).wait_recv()

    def start_x(self):
        self.copy("X", self.own, self.at.own, self.at.x).start()

    def start_y(self):
        self.copy("Y", self.own, self.at.own, self.at.y).start()

    def start_s(self):
        self.copy("S", self.own, self.at.own, self.at.sib).start()

    def start(self):
        self.start_x()
        self.start_y()
        self.start_s()

    def relay(self):
        at = self.at
        self.arrived("X")
        self.arrived("Y")
        self.copy("D", self.block(at.relayed), at.relayed, at.relay).start()
        for role in ("X", "Y"):
            slot = at.slots[role]
            self.copy("S" + role, self.block(slot), slot, at.sib).start()

    def relay_last(self):
        self.arrived("D")
        slot = self.at.slots["D"]
        self.copy("SD", self.block(slot), slot, self.at.sib).start()

    def finish(self):
        for role in ("S", "SX", "SY", "SD"):
            self.arrived(role)
        for role in ROLES:
            self.copy(role, self.own, self.at.own, self.at.sib).wait_send()


def column(row_ref, n):
    wide = jnp.broadcast_to(row_ref[...].astype(F32), (8, n))
    return wide.T[:, 0:1]


def kernel_a(
    shape,
    length_ref,
    hid_ref,
    gain_one_ref,
    gain_two_ref,
    q_gain_ref,
    k_gain_ref,
    wq_ref,
    wk_ref,
    wv_ref,
    wo_ref,
    wg_ref,
    wu_ref,
    wd_ref,
    cos_ref,
    sin_ref,
    wqkv_full,
    wo_full,
    wg_full,
    wu_full,
    wd_full,
    heads_all,
    q_t,
    kv_all,
    inv_den,
    proj_t,
    s_qkv,
    s_woz,
    s_wg,
    s_wu,
    h1,
    k_own,
    k_off,
    v_own,
    v_off,
    acc,
    g_send,
    g_recv,
    z_send,
    z_recv,
    h_send,
    h_recv,
    kv_sem,
    loc_sem,
):
    n_shard, n_tp, hd = shape
    at = Place(n_shard, n_tp)
    c, t = at.c, at.t
    rows, width = hid_ref.shape
    q_cols, kv_cols = wq_ref.shape[1], wk_ref.shape[1]
    q_heads, kv_heads = q_cols // hd, kv_cols // hd
    group = q_heads // kv_heads
    half = hd // 2
    at.greet()

    col_one = column(gain_one_ref, gain_one_ref.shape[1])
    s_qkv[:, 0:q_cols] = (wq_ref[...].astype(F32) * col_one).astype(BF16)
    s_qkv[:, q_cols : q_cols + kv_cols] = (wk_ref[...].astype(F32) * col_one).astype(BF16)
    s_qkv[:, q_cols + kv_cols :] = (wv_ref[...].astype(F32) * col_one).astype(BF16)
    qkv = Gather(at, s_qkv, wqkv_full, g_send, g_recv, 0)
    out = Gather(at, s_woz, wo_full, g_send, g_recv, 1)
    gate = Gather(at, s_wg, wg_full, g_send, g_recv, 2)
    up = Gather(at, s_wu, wu_full, g_send, g_recv, 3)
    down = Gather(at, wd_ref, wd_full, g_send, g_recv, 4)
    gathers = (qkv, out, gate, up, down)
    local = [
        pltpu.make_async_copy(g.own, g.block(at.own), loc_sem.at[i])
        for i, g in enumerate(gathers)
    ]
    qkv.start()
    local[0].start()

    wo_cols = pl.ds(pl.multiple_of(t * q_cols, q_cols), q_cols)
    s_woz[:, wo_cols] = wo_ref[...]

    def wo_part(d, owner):
        cols = pl.ds(pl.multiple_of(owner * q_cols, q_cols), q_cols)
        return remote(
            s_woz.at[:, cols],
            s_woz.at[:, cols],
            z_send.at[d],
            z_recv.at[d],
            at.z(lax.rem(t + d + 1, n_tp)),
        )

    for d in range(n_tp - 1):
        wo_part(d, t).start()

    def norm_one(i, _):
        r = pl.ds(pl.multiple_of(i * 64, 64), 64)
        x = hid_ref[r, :].astype(F32)
        scale = lax.rsqrt(jnp.mean(x * x, axis=-1, keepdims=True) + EPSILON)
        h1[r, :] = (x * scale).astype(BF16)
        return 0

    lax.fori_loop(0, rows // 64, norm_one, 0)
    qkv.relay()
    col_two = column(gain_two_ref, gain_two_ref.shape[1])
    s_wg[...] = (wg_ref[...].astype(F32) * col_two).astype(BF16)
    s_wu[...] = (wu_ref[...].astype(F32) * col_two).astype(BF16)
    qkv.relay_last()
    for d in range(n_tp - 1):
        wo_part(d, lax.rem(t + n_tp - d - 1, n_tp)).wait_recv()
    out.start_y()
    out.start_s()
    gate.start_y()
    local[0].wait()
    for cp in local[1:]:
        cp.start()
    qkv.finish()

    def project(i, _):
        r = pl.ds(pl.multiple_of(i * 256, 256), 256)
        proj_t[:, r] = mm(h1[r, :], wqkv_full[...]).T
        return 0

    lax.fori_loop(0, rows // 256, project, 0)
    here = pl.ds(pl.multiple_of(c * rows, rows), rows)
    k_gain = column(k_gain_ref, hd)
    q_gain = column(q_gain_ref, hd)

    def prepared(row, gain, factor):
        x = proj_t[pl.ds(pl.multiple_of(row, hd), hd), :]
        scale = lax.rsqrt(jnp.mean(x * x, axis=0, keepdims=True) + EPSILON)
        y = x * (scale * factor) * gain
        a, b = y[:half], y[half:]
        cosine, sine = cos_ref[:, here], sin_ref[:, here]
        return jnp.concatenate([a * cosine - b * sine, b * cosine + a * sine], axis=0)

    for g in range(kv_heads):
        key = prepared(q_cols + g * hd, k_gain, 1.0).astype(BF16)
        kv_all[c, g * hd : (g + 1) * hd, :] = key
    kv_all[c, kv_cols:, :] = proj_t[q_cols + kv_cols :, :].astype(BF16)
    kv_copy = remote(kv_all.at[c], kv_all.at[c], kv_sem.at[0], kv_sem.at[1], at.x)
    kv_back = remote(
        kv_all.at[1 - c], kv_all.at[1 - c], kv_sem.at[0], kv_sem.at[1], at.x
    )

    @pl.when(c == 0)
    def _():
        kv_copy.start()

    out.start_x()
    gate.start_x()
    gate.start_s()

    def prep_q(h, _):
        r = pl.multiple_of(h * hd, hd)
        q_t[pl.ds(r, hd), :] = prepared(r, q_gain, 1.0 / math.sqrt(hd)).astype(BF16)
        return 0

    lax.fori_loop(0, q_heads, prep_q, 0)
    length = length_ref[0]

    def load_block(index, k_nat, v_ext):
        pos = index * rows + lax.broadcasted_iota(jnp.int32, (1, rows), 1)
        live = (pos < length).astype(F32)
        first = (lax.broadcasted_iota(jnp.int32, (16, rows), 0) == 0).astype(F32)
        for g in range(kv_heads):
            k_nat[g] = kv_all[index, g * hd : (g + 1) * hd, :].astype(F32).T.astype(BF16)
            v = kv_all[index, kv_cols + g * hd : kv_cols + (g + 1) * hd, :].astype(F32)
            v_ext[g, 0:hd, :] = (v * live).astype(BF16)
            v_ext[g, hd:, :] = (first * live).astype(BF16)

    load_block(c, k_own, v_own)
    below = lax.broadcasted_iota(jnp.int32, (256, 256), 0) <= lax.broadcasted_iota(
        jnp.int32, (256, 256), 1
    )

    def own_block(h, _):
        g = h // group
        qh = q_t[pl.ds(pl.multiple_of(h * hd, hd), hd), :]
        for i in range(rows // 256):
            qi = qh[:, i * 256 : (i + 1) * 256]
            top = i * 256
            e = jnp.exp(mm(k_own[g, top : top + 256, :], qi))
            e = jnp.where(below, e, 0.0).astype(BF16)
            total = mm(v_own[g, :, top : top + 256], e)
            if i:
                e = jnp.exp(mm(k_own[g, 0:top, :], qi)).astype(BF16)
                total += mm(v_own[g, :, 0:top], e)
            acc[h, :, top : top + 256] = total
        return 0

    lax.fori_loop(0, q_heads, own_block, 0)

    @pl.when(c == 1)
    def _():
        kv_back.wait_recv()
        load_block(1 - c, k_off, v_off)

        def other_block(h, _):
            g = h // group
            qh = q_t[pl.ds(pl.multiple_of(h * hd, hd), hd), :]
            for i in range(rows // 256):
                cols = slice(i * 256, (i + 1) * 256)
                e = jnp.exp(mm(k_off[g], qh[:, cols])).astype(BF16)
                acc[h, :, cols] += mm(v_off[g], e)
            return 0

        lax.fori_loop(0, q_heads, other_block, 0)

    out.relay()
    up.start()

    def chunk_cols(owner, j):
        return pl.ds(pl.multiple_of(owner * q_cols + j * 128, 128), 128)

    def along(owner, j, way):
        ref = heads_all.at[:, chunk_cols(owner, j)]
        dev = at.z(jnp.minimum(t + 1, n_tp - 1) if way == 0 else jnp.maximum(t - 1, 0))
        return remote(ref, ref, h_send.at[way, owner, j], h_recv.at[way, owner, j], dev)

    chunks = q_cols // 128

    def pass_on(owner, j, way):
        @pl.when(t < n_tp - 1 if way == 0 else t > 0)
        def _():
            along(owner, j, way).start()

    for j in range(chunks):
        parts = []
        for h in range(2 * j, 2 * j + 2):
            inverse = 1.0 / acc[h, hd : hd + 1, :]
            inv_den[h : h + 1, :] = inverse
            parts.append(acc[h, 0:hd, :] * inverse)
        pair = jnp.concatenate(parts, axis=0)
        heads_all[:, chunk_cols(t, j)] = pair.T.astype(BF16)
        for way in (0, 1):
            pass_on(t, j, way)
    inv_den[q_heads:, :] = jnp.zeros((8 - q_heads, rows), F32)

    for d in range(1, n_tp):
        for j in range(chunks):

            @pl.when(t >= d)
            def _():
                along(t - d, j, 0).wait_recv()
                pass_on(t - d, j, 0)

            @pl.when(t + d < n_tp)
            def _():
                along(t + d, j, 1).wait_recv()
                pass_on(t + d, j, 1)

            step = (d - 1) * chunks + j
            if step == 2:
                gate.relay()
                down.start()
            if step == 4:
                out.relay_last()
            if step == 7:
                up.relay()

    gate.relay_last()
    down.relay()
    up.relay_last()
    down.relay_last()
    for g in gathers[1:]:
        g.finish()
    for cp in local[1:]:
        cp.wait()
    for owner in range(n_tp):
        for j in range(chunks):

            @pl.when(jnp.logical_and(t < n_tp - 1, owner <= t))
            def _():
                along(owner, j, 0).wait_send()

            @pl.when(jnp.logical_and(t > 0, owner >= t))
            def _():
                along(owner, j, 1).wait_send()

    for d in range(n_tp - 1):
        wo_part(d, t).wait_send()

    @pl.when(c == 0)
    def _():
        kv_copy.wait_send()
        kv_all[1 - c] = jnp.zeros(kv_all.shape[1:], BF16)


def rope_tables(positions, hd):
    freq = ROPE_BASE ** (-np.arange(hd // 2, dtype=np.float64) / (hd // 2))
    angle = freq[:, None] * np.arange(positions, dtype=np.float64)[None, :]
    return np.cos(angle).astype(np.float32), np.sin(angle).astype(np.float32)


def call_a(mesh, args):
    (hidden_in, seq_lengths, attn_gain, ffn_gain, query_gain, key_gain,
     w_query, w_key, w_value, w_out, w_gate, w_up, w_down) = args
    n_shard, n_ctx, n_tp = mesh.shape["shard"], mesh.shape["ctx"], mesh.shape["tp"]
    rows, width = hidden_in.shape
    hd = query_gain.shape[0]
    q_cols, kv_cols = w_query.shape[1], w_key.shape[1]
    q_heads, kv_heads = q_cols // hd, kv_cols // hd
    block = w_query.shape[0]
    hidden_units = w_gate.shape[1]
    cosine, sine = rope_tables(n_ctx * rows, hd)
    vm = pl.BlockSpec(memory_space=pltpu.VMEM)
    hbm = pl.BlockSpec(memory_space=pltpu.HBM)
    sm = pl.BlockSpec(memory_space=pltpu.SMEM)
    qkv_cols = q_cols + 2 * kv_cols
    S = jax.ShapeDtypeStruct
    dma = pltpu.SemaphoreType.DMA
    chunks = q_cols // 128
    return pl.pallas_call(
        functools.partial(kernel_a, (n_shard, n_tp, hd)),
        out_shape=(
            S((width, qkv_cols), BF16),
            S((width, n_tp * q_cols), BF16),
            S((width, hidden_units), BF16),
            S((width, hidden_units), BF16),
            S((width, hidden_units), BF16),
            S((rows, n_tp * q_cols), BF16),
            S((q_cols, rows), BF16),
            S((n_ctx, 2 * kv_cols, rows), BF16),
            S((8, rows), F32),
            S((qkv_cols, rows), F32),
        ),
        in_specs=[sm] + [vm] * 14,
        out_specs=(vm, hbm, hbm, hbm, hbm, vm, vm, vm, vm, vm),
        scratch_shapes=[
            pltpu.VMEM((block, qkv_cols), BF16),
            pltpu.VMEM((block, n_tp * q_cols), BF16),
            pltpu.VMEM((block, hidden_units), BF16),
            pltpu.VMEM((block, hidden_units), BF16),
            pltpu.VMEM((rows, width), BF16),
            pltpu.VMEM((kv_heads, rows, hd), BF16),
            pltpu.VMEM((kv_heads, rows, hd), BF16),
            pltpu.VMEM((kv_heads, hd + 16, rows), BF16),
            pltpu.VMEM((kv_heads, hd + 16, rows), BF16),
            pltpu.VMEM((q_heads, hd + 16, rows), F32),
            dma((5, 7)),
            dma((5, 7)),
            dma((n_tp - 1,)),
            dma((n_tp - 1,)),
            dma((2, n_tp, chunks)),
            dma((2, n_tp, chunks)),
            dma((2,)),
            dma((5,)),
        ],
        compiler_params=pltpu.CompilerParams(
            collective_id=0, has_side_effects=True, vmem_limit_bytes=VMEM_LIMIT
        ),
    )(
        seq_lengths, hidden_in, attn_gain.reshape(1, -1), ffn_gain.reshape(1, -1),
        query_gain.reshape(1, -1), key_gain.reshape(1, -1), w_query, w_key, w_value,
        w_out.T, w_gate, w_up, w_down.T, jnp.asarray(cosine), jnp.asarray(sine),
    )


def fast_body(mesh, *args):
    (hidden_in, seq_lengths, attn_gain, ffn_gain, query_gain, key_gain,
     w_query, w_key, w_value, w_out, w_gate, w_up, w_down, out_grad) = args
    (wqkv_full, wo_full, wg_full, wu_full, wd_full, heads_all, q_t, kv_all, inv_den,
     proj_t) = call_a(mesh, args[:13])
    rows = hidden_in.shape[0]
    hd = query_gain.shape[0]
    q_cols, kv_cols = w_query.shape[1], w_key.shape[1]
    kv_heads, q_heads = kv_cols // hd, q_cols // hd
    group = q_heads // kv_heads
    scale = 1.0 / math.sqrt(hd)
    t = lax.axis_index("tp")
    positions = lax.axis_index("ctx") * rows + jnp.arange(rows, dtype=jnp.int32)
    length = seq_lengths[0]
    valid = (positions < length).astype(F32)[:, None]
    hidden = hidden_in.astype(F32)

    def rms(v):
        return v * lax.rsqrt(jnp.mean(v * v, axis=-1, keepdims=True) + EPSILON)

    def psum16(v):
        return lax.psum(v.astype(BF16), "tp").astype(F32)

    resid = hidden + back_product(heads_all, wo_full)
    h2 = rms(resid).astype(BF16)
    gate = forward_product(h2, wg_full)
    up = forward_product(h2, wu_full)
    middle = activation(gate, up).astype(BF16)
    ffn = psum16(back_product(middle, wd_full))
    block_out = (valid * (resid + ffn)).astype(BF16)
    grad_top = valid * out_grad.astype(F32)
    grad_low = grad_top.astype(BF16)
    down_wgrad = outer_product(grad_low, middle)
    mid_grad = forward_product(grad_low, wd_full)
    _, pull_act = jax.vjp(activation, gate, up)
    gate_low, up_low = (v.astype(BF16) for v in pull_act(mid_grad))
    gate_wgrad = outer_product(h2, gate_low)
    up_wgrad = outer_product(h2, up_low)
    d2 = psum16(back_product(gate_low, wg_full) + back_product(up_low, wu_full))
    _, pull_two = jax.vjp(rms, resid)
    resid_grad = grad_top + pull_two(d2)[0]
    attn_low = resid_grad.astype(BF16)
    heads_own = lax.dynamic_slice_in_dim(heads_all, t * q_cols, q_cols, 1)
    wo_own = lax.dynamic_slice_in_dim(wo_full, t * q_cols, q_cols, 1)
    out_wgrad = outer_product(attn_low, heads_own)
    heads_grad = forward_product(attn_low, wo_own).astype(BF16)
    delta = jnp.sum(
        (heads_grad.astype(F32) * heads_own.astype(F32)).reshape(rows, q_heads, hd), -1
    ).T.reshape(kv_heads, group, 1, rows)
    keys = kv_all[:, :kv_cols].reshape(-1, kv_heads, hd, rows)
    values = kv_all[:, kv_cols:].reshape(-1, kv_heads, hd, rows)
    q4 = q_t.reshape(kv_heads, group, hd, rows)
    g4 = heads_grad.T.reshape(kv_heads, group, hd, rows)
    score = jnp.einsum("ckds,kgdt->kgcst", keys, q4, preferred_element_type=F32)
    pos_k = jnp.arange(keys.shape[0] * rows, dtype=jnp.int32).reshape(-1, rows, 1)
    mask = (pos_k <= positions) & (pos_k < length)
    probs = jnp.where(mask, jnp.exp(score), 0.0) * inv_den[:q_heads].reshape(
        kv_heads, group, 1, 1, rows
    )
    prob_grad = jnp.einsum("ckds,kgdt->kgcst", values, g4, preferred_element_type=F32)
    score_grad = (probs * (prob_grad - delta[:, :, None])).astype(BF16)
    query_grad = (
        jnp.einsum("kgcst,ckds->tkgd", score_grad, keys, preferred_element_type=F32) * scale
    )
    key_grads = jnp.einsum("kgcst,kgdt->cskd", score_grad, q4, preferred_element_type=F32)
    value_grads = jnp.einsum(
        "kgcst,kgdt->cskd", probs.astype(BF16), g4, preferred_element_type=F32
    )
    both = jnp.concatenate(
        [key_grads.reshape(-1, kv_cols), value_grads.reshape(-1, kv_cols)], axis=1
    )
    both = lax.psum_scatter(both, "ctx", scatter_dimension=0, tiled=True)

    def query_prep(proj, gain):
        return head_prep(proj, gain, positions)

    q_gain, k_gain = query_gain.astype(F32), key_gain.astype(F32)
    proj = proj_t.T
    _, pull_query = jax.vjp(query_prep, proj[:, :q_cols], q_gain)
    dq, q_gain_grad = pull_query(query_grad.reshape(rows, q_heads, hd))
    _, pull_key = jax.vjp(query_prep, proj[:, q_cols : q_cols + kv_cols], k_gain)
    dk, k_gain_grad = pull_key(both[:, :kv_cols].reshape(rows, kv_heads, hd))
    dqkv = jnp.concatenate([dq, dk, both[:, kv_cols:]], axis=1).astype(BF16)
    h1 = rms(hidden).astype(BF16)
    qkv_wgrad = outer_product(h1, dqkv)
    d1 = psum16(back_product(dqkv, wqkv_full))
    _, pull_one = jax.vjp(rms, hidden)
    input_grad = resid_grad + pull_one(d1)[0]
    q_sum, k_sum = lax.psum((q_gain_grad, k_gain_grad), ("shard", "ctx", "tp"))

    def scatter(v):
        v = lax.psum_scatter(
            v.astype(BF16), ("shard", "ctx"), scatter_dimension=0, tiled=True
        )
        return v.astype(F32)

    qkv_g, gate_g, up_g, down_g, out_g = (
        scatter(v) for v in (qkv_wgrad, gate_wgrad, up_wgrad, down_wgrad, out_wgrad)
    )
    g_one, g_two = attn_gain.astype(F32)[:, None], ffn_gain.astype(F32)[:, None]
    w_one = jnp.concatenate([w_query, w_key, w_value], axis=1).astype(F32)
    gains = jnp.stack(
        [
            jnp.sum(w_one * qkv_g, axis=1),
            jnp.sum(w_gate.astype(F32) * gate_g + w_up.astype(F32) * up_g, axis=1),
        ]
    )
    gains = lax.psum(gains, "tp")
    qkv_g = qkv_g * g_one
    return (
        block_out, input_grad, gains[0], gains[1], q_sum, k_sum,
        qkv_g[:, :q_cols], qkv_g[:, q_cols : q_cols + kv_cols], qkv_g[:, q_cols + kv_cols :],
        out_g.T, gate_g * g_two, up_g * g_two, down_g.T,
    )


def solution(mesh):
    sizes = mesh.shape
    plane_of_eight = sizes["shard"] == 4 and sizes["ctx"] == 2 and sizes["tp"] > 1
    run = functools.partial(fast_body, mesh) if plane_of_eight else body
    placed = (
        P(("shard", "ctx"), None),
        P("shard"),
        P(("shard", "ctx")),
        P(("shard", "ctx")),
        P(),
        P(),
        P(("shard", "ctx"), "tp"),
        P(("shard", "ctx"), "tp"),
        P(("shard", "ctx"), "tp"),
        P("tp", ("shard", "ctx")),
        P(("shard", "ctx"), "tp"),
        P(("shard", "ctx"), "tp"),
        P("tp", ("shard", "ctx")),
        P(("shard", "ctx"), None),
    )
    return jax.shard_map(
        run,
        mesh=mesh,
        in_specs=placed,
        out_specs=(
            P(("shard", "ctx"), None),
            P(("shard", "ctx"), None),
            P(("shard", "ctx")),
            P(("shard", "ctx")),
            P(),
            P(),
            P(("shard", "ctx"), "tp"),
            P(("shard", "ctx"), "tp"),
            P(("shard", "ctx"), "tp"),
            P("tp", ("shard", "ctx")),
            P(("shard", "ctx"), "tp"),
            P(("shard", "ctx"), "tp"),
            P("tp", ("shard", "ctx")),
        ),
        check_vma=False,
    )
```

```python
import functools
import math

import jax
import jax.numpy as jnp
import numpy as np
from jax import lax
from jax.experimental import pallas as pl
from jax.experimental.pallas import tpu as pltpu
from jax.sharding import PartitionSpec as P

EPSILON = 1e-05
ROPE_BASE = 1000000.0
MESH = pl.DeviceIdType.MESH
F32 = jnp.float32
BF16 = jnp.bfloat16
VMEM_LIMIT = 60 << 20


def norm_rows(value, gain):
    scale = lax.rsqrt(jnp.mean(value * value, axis=-1, keepdims=True) + EPSILON)
    return value * scale * gain


def rotate(values, positions):
    half = values.shape[-1] // 2
    freq = ROPE_BASE ** (-jnp.arange(half, dtype=jnp.float32) / half)
    angle = positions.astype(jnp.float32)[:, None] * freq[None, :]
    cosine = jnp.cos(angle)[:, None, :]
    sine = jnp.sin(angle)[:, None, :]
    first = values[..., :half]
    second = values[..., half:]
    return jnp.concatenate(
        [first * cosine - second * sine, second * cosine + first * sine], axis=-1
    )


def head_prep(proj, gain, positions):
    heads = proj.reshape(proj.shape[0], -1, gain.shape[0])
    return rotate(norm_rows(heads, gain), positions)


def activation(gate_in, up_in):
    return jax.nn.silu(gate_in) * up_in


def forward_product(left, right):
    return jnp.dot(left, right, preferred_element_type=jnp.float32)


def outer_product(left, right):
    return lax.dot_general(
        left, right, (((0,), (0,)), ((), ())), preferred_element_type=jnp.float32
    )


def back_product(grad, weight):
    return lax.dot_general(
        grad, weight, (((1,), (1,)), ((), ())), preferred_element_type=jnp.float32
    )


def body(
    hidden_in,
    seq_lengths,
    attn_gain,
    ffn_gain,
    query_gain,
    key_gain,
    w_query,
    w_key,
    w_value,
    w_out,
    w_gate,
    w_up,
    w_down,
    out_grad,
):
    rows = hidden_in.shape[0]
    head_dim = query_gain.shape[0]
    kv_heads = w_key.shape[1] // head_dim
    q_heads = w_query.shape[1] // head_dim
    group = q_heads // kv_heads
    pieces = lax.axis_size("ctx")
    scale = 1.0 / math.sqrt(head_dim)
    positions = lax.axis_index("ctx") * rows + jnp.arange(rows, dtype=jnp.int32)
    length = seq_lengths[0]
    valid = (positions < length).astype(jnp.float32)[:, None]
    live_blocks = jnp.minimum(lax.axis_index("ctx"), (length - 1) // rows) + 1
    gathered = (
        lax.all_gather(attn_gain, ("shard", "ctx"), axis=0, tiled=True),
        lax.all_gather(ffn_gain, ("shard", "ctx"), axis=0, tiled=True),
        lax.all_gather(w_query, ("shard", "ctx"), axis=0, tiled=True),
        lax.all_gather(w_key, ("shard", "ctx"), axis=0, tiled=True),
        lax.all_gather(w_value, ("shard", "ctx"), axis=0, tiled=True),
        lax.all_gather(w_gate, ("shard", "ctx"), axis=0, tiled=True),
        lax.all_gather(w_up, ("shard", "ctx"), axis=0, tiled=True),
        lax.all_gather(w_out, ("shard", "ctx"), axis=1, tiled=True),
        lax.all_gather(w_down, ("shard", "ctx"), axis=1, tiled=True),
    )
    gain_one = gathered[0].astype(jnp.float32)
    gain_two = gathered[1].astype(jnp.float32)
    full_query, full_key, full_value, full_gate, full_up, full_out, full_down = gathered[2:]
    q_gain = query_gain.astype(jnp.float32)
    k_gain = key_gain.astype(jnp.float32)
    hidden = hidden_in.astype(jnp.float32)
    normed_one = norm_rows(hidden, gain_one).astype(jnp.bfloat16)
    query_proj = forward_product(normed_one, full_query)
    key_proj = forward_product(normed_one, full_key)
    value_proj = forward_product(normed_one, full_value)
    queries = (
        head_prep(query_proj, q_gain, positions)
        .astype(jnp.bfloat16)
        .reshape(rows, kv_heads, group, head_dim)
    )
    keys_own = head_prep(key_proj, k_gain, positions).astype(jnp.bfloat16)
    values_own = value_proj.reshape(rows, kv_heads, head_dim).astype(jnp.bfloat16)
    keys_all, values_all = (
        lax.all_gather(keys_own, "ctx", axis=0, tiled=True),
        lax.all_gather(values_own, "ctx", axis=0, tiled=True),
    )
    key_blocks = keys_all.reshape(pieces, rows, kv_heads, head_dim)
    value_blocks = values_all.reshape(pieces, rows, kv_heads, head_dim)

    def key_at(index):
        return lax.dynamic_index_in_dim(key_blocks, index, 0, keepdims=False)

    def value_at(index):
        return lax.dynamic_index_in_dim(value_blocks, index, 0, keepdims=False)

    def block_scores(key_block, index):
        key_pos = index * rows + jnp.arange(rows, dtype=jnp.int32)
        mask = ((key_pos[None, :] <= positions[:, None]) & (key_pos[None, :] < length))[None, None]
        raw = (
            jnp.einsum("tkgd,skd->kgts", queries, key_block, preferred_element_type=jnp.float32)
            * scale
        )
        return (jnp.where(mask, raw, -1e30), mask)

    def stats_step(index, carry):
        top, total = carry
        masked, mask = block_scores(key_at(index), index)
        new_top = jnp.maximum(top, jnp.max(masked, axis=-1))
        weight = jnp.where(mask, jnp.exp(masked - new_top[..., None]), 0.0)
        total = total * jnp.exp(top - new_top) + jnp.sum(weight, axis=-1)
        return (new_top, total)

    start = (
        jnp.full((kv_heads, group, rows), -1e30, jnp.float32),
        jnp.zeros((kv_heads, group, rows), jnp.float32),
    )
    top, total = lax.fori_loop(0, live_blocks, stats_step, start)
    log_total = top + jnp.log(total)

    def probs_of(key_block, index):
        masked, mask = block_scores(key_block, index)
        return jnp.where(mask, jnp.exp(masked - log_total[..., None]), 0.0)

    def mix_step(index, accum):
        probs = probs_of(key_at(index), index).astype(jnp.bfloat16)
        return accum + jnp.einsum(
            "kgts,skd->tkgd", probs, value_at(index), preferred_element_type=jnp.float32
        )

    head_zeros = jnp.zeros((rows, kv_heads, group, head_dim), jnp.float32)
    mixed = lax.fori_loop(0, live_blocks, mix_step, head_zeros)
    heads_out = mixed.reshape(rows, -1).astype(jnp.bfloat16)
    attn_term = forward_product(heads_out, full_out)
    resid = hidden + lax.psum(attn_term, "tp")
    normed_two = norm_rows(resid, gain_two).astype(jnp.bfloat16)
    gate = forward_product(normed_two, full_gate)
    up = forward_product(normed_two, full_up)
    middle = activation(gate, up).astype(jnp.bfloat16)
    ffn_term = forward_product(middle, full_down)
    ffn = lax.psum(ffn_term.astype(jnp.bfloat16), "tp").astype(jnp.float32)
    block_out = (valid * (resid + ffn)).astype(jnp.bfloat16)
    grad_top = valid * out_grad.astype(jnp.float32)
    grad_low = grad_top.astype(jnp.bfloat16)
    down_wgrad = outer_product(middle, grad_low)
    mid_grad = back_product(grad_low, full_down)
    _, pull_act = jax.vjp(activation, gate, up)
    gate_float, up_float = pull_act(mid_grad)
    gate_low = gate_float.astype(jnp.bfloat16)
    up_low = up_float.astype(jnp.bfloat16)
    gate_wgrad = outer_product(normed_two, gate_low)
    up_wgrad = outer_product(normed_two, up_low)
    normed_two_part = back_product(gate_low, full_gate) + back_product(up_low, full_up)
    normed_two_grad = lax.psum(normed_two_part, "tp")
    _, pull_two = jax.vjp(norm_rows, resid, gain_two)
    resid_part, gain_two_grad = pull_two(normed_two_grad)
    resid_grad = grad_top + resid_part
    attn_low = resid_grad.astype(jnp.bfloat16)
    out_wgrad = outer_product(heads_out, attn_low)
    heads_grad = (
        back_product(attn_low, full_out)
        .astype(jnp.bfloat16)
        .reshape(rows, kv_heads, group, head_dim)
    )

    def delta_step(index, accum):
        probs = probs_of(key_at(index), index)
        prob_grad = jnp.einsum(
            "tkgd,skd->kgts", heads_grad, value_at(index), preferred_element_type=jnp.float32
        )
        return accum + jnp.sum(probs * prob_grad, axis=-1)

    delta = lax.fori_loop(
        0, live_blocks, delta_step, jnp.zeros((kv_heads, group, rows), jnp.float32)
    )

    def grad_step(index, carry):
        accum, key_store, value_store = carry
        key_block = key_at(index)
        probs = probs_of(key_block, index)
        prob_grad = jnp.einsum(
            "tkgd,skd->kgts", heads_grad, value_at(index), preferred_element_type=jnp.float32
        )
        score_grad = (probs * (prob_grad - delta[..., None])).astype(jnp.bfloat16)
        accum = (
            accum
            + jnp.einsum(
                "kgts,skd->tkgd", score_grad, key_block, preferred_element_type=jnp.float32
            )
            * scale
        )
        key_grad = (
            jnp.einsum("kgts,tkgd->skd", score_grad, queries, preferred_element_type=jnp.float32)
            * scale
        )
        value_grad = jnp.einsum(
            "kgts,tkgd->skd",
            probs.astype(jnp.bfloat16),
            heads_grad,
            preferred_element_type=jnp.float32,
        )
        key_store = lax.dynamic_update_index_in_dim(key_store, key_grad, index, 0)
        value_store = lax.dynamic_update_index_in_dim(value_store, value_grad, index, 0)
        return (accum, key_store, value_store)

    store_zeros = jnp.zeros((pieces, rows, kv_heads, head_dim), jnp.float32)
    query_grad, key_grads, value_grads = lax.fori_loop(
        0, live_blocks, grad_step, (head_zeros, store_zeros, store_zeros)
    )
    key_grad_own, value_grad_own = (
        lax.psum_scatter(
            key_grads.reshape(pieces * rows, kv_heads, head_dim),
            "ctx",
            scatter_dimension=0,
            tiled=True,
        ),
        lax.psum_scatter(
            value_grads.reshape(pieces * rows, kv_heads, head_dim),
            "ctx",
            scatter_dimension=0,
            tiled=True,
        ),
    )

    def query_prep(proj, gain):
        return head_prep(proj, gain, positions)

    _, pull_query = jax.vjp(query_prep, query_proj, q_gain)
    query_proj_grad, q_gain_grad = pull_query(query_grad.reshape(rows, q_heads, head_dim))
    _, pull_key = jax.vjp(query_prep, key_proj, k_gain)
    key_proj_grad, k_gain_grad = pull_key(key_grad_own)
    query_low = query_proj_grad.astype(jnp.bfloat16)
    key_low = key_proj_grad.astype(jnp.bfloat16)
    value_low = value_grad_own.reshape(rows, -1).astype(jnp.bfloat16)
    query_wgrad = outer_product(normed_one, query_low)
    key_wgrad = outer_product(normed_one, key_low)
    value_wgrad = outer_product(normed_one, value_low)
    normed_one_part = (
        back_product(query_low, full_query)
        + back_product(key_low, full_key)
        + back_product(value_low, full_value)
    )
    normed_one_grad = lax.psum(normed_one_part, "tp")
    _, pull_one = jax.vjp(norm_rows, hidden, gain_one)
    hidden_part, gain_one_grad = pull_one(normed_one_grad)
    input_grad = resid_grad + hidden_part
    head_sums = lax.psum((q_gain_grad, k_gain_grad), ("shard", "ctx", "tp"))
    summed = (
        lax.psum_scatter(gain_one_grad, ("shard", "ctx"), scatter_dimension=0, tiled=True),
        lax.psum_scatter(gain_two_grad, ("shard", "ctx"), scatter_dimension=0, tiled=True),
        lax.psum_scatter(query_wgrad, ("shard", "ctx"), scatter_dimension=0, tiled=True),
        lax.psum_scatter(key_wgrad, ("shard", "ctx"), scatter_dimension=0, tiled=True),
        lax.psum_scatter(value_wgrad, ("shard", "ctx"), scatter_dimension=0, tiled=True),
        lax.psum_scatter(gate_wgrad, ("shard", "ctx"), scatter_dimension=0, tiled=True),
        lax.psum_scatter(up_wgrad, ("shard", "ctx"), scatter_dimension=0, tiled=True),
        lax.psum_scatter(out_wgrad, ("shard", "ctx"), scatter_dimension=1, tiled=True),
        lax.psum_scatter(down_wgrad, ("shard", "ctx"), scatter_dimension=1, tiled=True),
    )
    (
        gain_one_out,
        gain_two_out,
        query_out,
        key_out,
        value_out,
        gate_out,
        up_out,
        out_out,
        down_out,
    ) = summed
    return (
        block_out,
        input_grad,
        gain_one_out,
        gain_two_out,
        head_sums[0],
        head_sums[1],
        query_out,
        key_out,
        value_out,
        out_out,
        gate_out,
        up_out,
        down_out,
    )


def remote(src, dst, send, recv, dev):
    return pltpu.make_async_remote_copy(
        src_ref=src,
        dst_ref=dst,
        send_sem=send,
        recv_sem=recv,
        device_id=dev,
        device_id_type=MESH,
    )


def mm(a, b):
    return jnp.dot(a, b, preferred_element_type=F32)


def mm_nt(a, b):
    return lax.dot_general(a, b, (((1,), (1,)), ((), ())), preferred_element_type=F32)


def round_up(units):
    return -(-units // 256) * 256


class Place:
    def __init__(self, n_shard, n_tp):
        s = lax.axis_index("shard")
        c = lax.axis_index("ctx")
        t = lax.axis_index("tp")
        self.s, self.c, self.t = s, c, t
        self.core = lax.rem(s, 2)
        sib = s + 1 - 2 * self.core
        far = lax.rem(s + 2, n_shard)
        far_sib = far + 1 - 2 * self.core
        self.sib = (sib, c, t)
        self.x = (s, 1 - c, t)
        self.y = (far, c, t)
        first = 1 - self.core
        self.relay = (
            first * s + self.core * far,
            first * (1 - c) + self.core * c,
            t,
        )
        slot = lambda a, b: a * 2 + b
        self.own = slot(s, c)
        self.slots = {
            "S": slot(sib, c),
            "X": slot(s, 1 - c),
            "Y": slot(far, c),
            "D": slot(far, 1 - c),
            "SX": slot(sib, 1 - c),
            "SY": slot(far_sib, c),
            "SD": slot(far_sib, 1 - c),
        }
        self.relayed = first * self.slots["Y"] + self.core * self.slots["X"]
        self.n_tp = n_tp

    def z(self, t):
        return (self.s, self.c, t)

    def greet(self):
        peers = [self.sib, self.x, self.y]
        peers += [
            self.z(lax.rem(self.t + d, self.n_tp)) for d in range(1, self.n_tp)
        ]
        barrier = pltpu.get_barrier_semaphore()
        for peer in peers:
            pl.semaphore_signal(barrier, inc=1, device_id=peer, device_id_type=MESH)
        pl.semaphore_wait(barrier, len(peers))


ROLES = ("S", "X", "Y", "D", "SX", "SY", "SD")


class Gather:
    def __init__(self, at, own, full, send, recv, index):
        self.at, self.own, self.full = at, own, full
        self.send, self.recv, self.index = send, recv, index
        self.rows = own.shape[0]

    def block(self, slot):
        return self.full.at[pl.ds(pl.multiple_of(slot * self.rows, self.rows), self.rows)]

    def copy(self, role, src, slot, dev):
        k = ROLES.index(role)
        return remote(
            src,
            self.block(slot),
            self.send.at[self.index, k],
            self.recv.at[self.index, k],
            dev,
        )

    def arrived(self, role):
        slot = self.at.slots[role]
        self.copy(role, self.block(slot), slot, self.at.sib).wait_recv()

    def start_x(self):
        self.copy("X", self.own, self.at.own, self.at.x).start()

    def start_y(self):
        self.copy("Y", self.own, self.at.own, self.at.y).start()

    def start_s(self):
        self.copy("S", self.own, self.at.own, self.at.sib).start()

    def start(self):
        self.start_x()
        self.start_y()
        self.start_s()

    def relay(self):
        at = self.at
        self.arrived("X")
        self.arrived("Y")
        self.copy("D", self.block(at.relayed), at.relayed, at.relay).start()
        for role in ("X", "Y"):
            slot = at.slots[role]
            self.copy("S" + role, self.block(slot), slot, at.sib).start()

    def relay_last(self):
        self.arrived("D")
        slot = self.at.slots["D"]
        self.copy("SD", self.block(slot), slot, self.at.sib).start()

    def finish(self):
        for role in ("S", "SX", "SY", "SD"):
            self.arrived(role)
        for role in ROLES:
            self.copy(role, self.own, self.at.own, self.at.sib).wait_send()


def column(row_ref, n):
    wide = jnp.broadcast_to(row_ref[...].astype(F32), (8, n))
    return wide.T[:, 0:1]


def kernel_a(
    shape,
    length_ref,
    hid_ref,
    gain_one_ref,
    gain_two_ref,
    q_gain_ref,
    k_gain_ref,
    wq_ref,
    wk_ref,
    wv_ref,
    wo_ref,
    wg_ref,
    wu_ref,
    cos_ref,
    sin_ref,
    wqkv_full,
    wo_full,
    wg_full,
    wu_full,
    heads_all,
    q_t,
    kv_all,
    inv_den,
    proj_t,
    s_qkv,
    s_woz,
    s_wg,
    s_wu,
    h1,
    k_own,
    k_off,
    v_own,
    v_off,
    acc,
    g_send,
    g_recv,
    z_send,
    z_recv,
    h_send,
    h_recv,
    kv_sem,
    loc_sem,
):
    n_shard, n_tp, hd = shape
    at = Place(n_shard, n_tp)
    c, t = at.c, at.t
    rows, width = hid_ref.shape
    q_cols, kv_cols = wq_ref.shape[1], wk_ref.shape[1]
    q_heads, kv_heads = q_cols // hd, kv_cols // hd
    group = q_heads // kv_heads
    half = hd // 2
    at.greet()

    col_one = column(gain_one_ref, gain_one_ref.shape[1])
    s_qkv[:, 0:q_cols] = (wq_ref[...].astype(F32) * col_one).astype(BF16)
    s_qkv[:, q_cols : q_cols + kv_cols] = (wk_ref[...].astype(F32) * col_one).astype(BF16)
    s_qkv[:, q_cols + kv_cols :] = (wv_ref[...].astype(F32) * col_one).astype(BF16)
    qkv = Gather(at, s_qkv, wqkv_full, g_send, g_recv, 0)
    out = Gather(at, s_woz, wo_full, g_send, g_recv, 1)
    gate = Gather(at, s_wg, wg_full, g_send, g_recv, 2)
    up = Gather(at, s_wu, wu_full, g_send, g_recv, 3)
    gathers = (qkv, out, gate, up)
    local = [
        pltpu.make_async_copy(g.own, g.block(at.own), loc_sem.at[i])
        for i, g in enumerate(gathers)
    ]
    qkv.start()
    local[0].start()

    wo_cols = pl.ds(pl.multiple_of(t * q_cols, q_cols), q_cols)
    s_woz[:, wo_cols] = wo_ref[...]

    def wo_part(d, owner):
        cols = pl.ds(pl.multiple_of(owner * q_cols, q_cols), q_cols)
        return remote(
            s_woz.at[:, cols],
            s_woz.at[:, cols],
            z_send.at[d],
            z_recv.at[d],
            at.z(lax.rem(t + d + 1, n_tp)),
        )

    for d in range(n_tp - 1):
        wo_part(d, t).start()

    def norm_one(i, _):
        r = pl.ds(pl.multiple_of(i * 64, 64), 64)
        x = hid_ref[r, :].astype(F32)
        scale = lax.rsqrt(jnp.mean(x * x, axis=-1, keepdims=True) + EPSILON)
        h1[r, :] = (x * scale).astype(BF16)
        return 0

    lax.fori_loop(0, rows // 64, norm_one, 0)
    qkv.relay()
    col_two = column(gain_two_ref, gain_two_ref.shape[1])
    units = wg_ref.shape[1]
    for src, dst in ((wg_ref, s_wg), (wu_ref, s_wu)):
        dst[:, 0:units] = (src[...].astype(F32) * col_two).astype(BF16)
        dst[:, units:] = jnp.zeros((dst.shape[0], dst.shape[1] - units), BF16)
    qkv.relay_last()
    for d in range(n_tp - 1):
        wo_part(d, lax.rem(t + n_tp - d - 1, n_tp)).wait_recv()
    out.start_y()
    out.start_s()
    gate.start_y()
    local[0].wait()
    for cp in local[1:]:
        cp.start()
    qkv.finish()

    def project(i, _):
        r = pl.ds(pl.multiple_of(i * 256, 256), 256)
        proj_t[:, r] = mm(h1[r, :], wqkv_full[...]).T
        return 0

    lax.fori_loop(0, rows // 256, project, 0)
    here = pl.ds(pl.multiple_of(c * rows, rows), rows)
    k_gain = column(k_gain_ref, hd)
    q_gain = column(q_gain_ref, hd)

    def prepared(row, gain, factor):
        x = proj_t[pl.ds(pl.multiple_of(row, hd), hd), :]
        scale = lax.rsqrt(jnp.mean(x * x, axis=0, keepdims=True) + EPSILON)
        y = x * (scale * factor) * gain
        a, b = y[:half], y[half:]
        cosine, sine = cos_ref[:, here], sin_ref[:, here]
        return jnp.concatenate([a * cosine - b * sine, b * cosine + a * sine], axis=0)

    for g in range(kv_heads):
        key = prepared(q_cols + g * hd, k_gain, 1.0).astype(BF16)
        kv_all[c, g * hd : (g + 1) * hd, :] = key
    kv_all[c, kv_cols:, :] = proj_t[q_cols + kv_cols :, :].astype(BF16)
    kv_copy = remote(kv_all.at[c], kv_all.at[c], kv_sem.at[0], kv_sem.at[1], at.x)
    kv_back = remote(
        kv_all.at[1 - c], kv_all.at[1 - c], kv_sem.at[0], kv_sem.at[1], at.x
    )

    @pl.when(c == 0)
    def _():
        kv_copy.start()

    out.start_x()
    gate.start_x()
    gate.start_s()

    def prep_q(h, _):
        r = pl.multiple_of(h * hd, hd)
        q_t[pl.ds(r, hd), :] = prepared(r, q_gain, 1.0 / math.sqrt(hd)).astype(BF16)
        return 0

    lax.fori_loop(0, q_heads, prep_q, 0)
    length = length_ref[0]

    def load_block(index, k_nat, v_ext):
        pos = index * rows + lax.broadcasted_iota(jnp.int32, (1, rows), 1)
        live = (pos < length).astype(F32)
        first = (lax.broadcasted_iota(jnp.int32, (16, rows), 0) == 0).astype(F32)
        for g in range(kv_heads):
            k_nat[g] = kv_all[index, g * hd : (g + 1) * hd, :].astype(F32).T.astype(BF16)
            v = kv_all[index, kv_cols + g * hd : kv_cols + (g + 1) * hd, :].astype(F32)
            v_ext[g, 0:hd, :] = (v * live).astype(BF16)
            v_ext[g, hd:, :] = (first * live).astype(BF16)

    load_block(c, k_own, v_own)
    below = lax.broadcasted_iota(jnp.int32, (256, 256), 0) <= lax.broadcasted_iota(
        jnp.int32, (256, 256), 1
    )

    def own_block(h, _):
        g = h // group
        qh = q_t[pl.ds(pl.multiple_of(h * hd, hd), hd), :]
        for i in range(rows // 256):
            qi = qh[:, i * 256 : (i + 1) * 256]
            top = i * 256
            e = jnp.exp(mm(k_own[g, top : top + 256, :], qi))
            e = jnp.where(below, e, 0.0).astype(BF16)
            total = mm(v_own[g, :, top : top + 256], e)
            if i:
                e = jnp.exp(mm(k_own[g, 0:top, :], qi)).astype(BF16)
                total += mm(v_own[g, :, 0:top], e)
            acc[h, :, top : top + 256] = total
        return 0

    lax.fori_loop(0, q_heads, own_block, 0)

    @pl.when(c == 1)
    def _():
        kv_back.wait_recv()
        load_block(1 - c, k_off, v_off)

        def other_block(h, _):
            g = h // group
            qh = q_t[pl.ds(pl.multiple_of(h * hd, hd), hd), :]
            for i in range(rows // 256):
                cols = slice(i * 256, (i + 1) * 256)
                e = jnp.exp(mm(k_off[g], qh[:, cols])).astype(BF16)
                acc[h, :, cols] += mm(v_off[g], e)
            return 0

        lax.fori_loop(0, q_heads, other_block, 0)

    out.relay()
    up.start()

    def chunk_cols(owner, j):
        return pl.ds(pl.multiple_of(owner * q_cols + j * 128, 128), 128)

    def along(owner, j, way):
        ref = heads_all.at[:, chunk_cols(owner, j)]
        dev = at.z(jnp.minimum(t + 1, n_tp - 1) if way == 0 else jnp.maximum(t - 1, 0))
        return remote(ref, ref, h_send.at[way, owner, j], h_recv.at[way, owner, j], dev)

    chunks = q_cols // 128

    def pass_on(owner, j, way):
        @pl.when(t < n_tp - 1 if way == 0 else t > 0)
        def _():
            along(owner, j, way).start()

    for j in range(chunks):
        parts = []
        for h in range(2 * j, 2 * j + 2):
            inverse = 1.0 / acc[h, hd : hd + 1, :]
            inv_den[h : h + 1, :] = inverse
            parts.append(acc[h, 0:hd, :] * inverse)
        pair = jnp.concatenate(parts, axis=0)
        heads_all[:, chunk_cols(t, j)] = pair.T.astype(BF16)
        for way in (0, 1):
            pass_on(t, j, way)
    inv_den[q_heads:, :] = jnp.zeros((8 - q_heads, rows), F32)

    for d in range(1, n_tp):
        for j in range(chunks):

            @pl.when(t >= d)
            def _():
                along(t - d, j, 0).wait_recv()
                pass_on(t - d, j, 0)

            @pl.when(t + d < n_tp)
            def _():
                along(t + d, j, 1).wait_recv()
                pass_on(t + d, j, 1)

            step = (d - 1) * chunks + j
            if step == 2:
                gate.relay()
            if step == 4:
                out.relay_last()
            if step == 7:
                up.relay()

    gate.relay_last()
    up.relay_last()
    for g in gathers[1:]:
        g.finish()
    for cp in local[1:]:
        cp.wait()
    for owner in range(n_tp):
        for j in range(chunks):

            @pl.when(jnp.logical_and(t < n_tp - 1, owner <= t))
            def _():
                along(owner, j, 0).wait_send()

            @pl.when(jnp.logical_and(t > 0, owner >= t))
            def _():
                along(owner, j, 1).wait_send()

    for d in range(n_tp - 1):
        wo_part(d, t).wait_send()

    @pl.when(c == 0)
    def _():
        kv_copy.wait_send()
        kv_all[1 - c] = jnp.zeros(kv_all.shape[1:], BF16)


def rope_tables(positions, hd):
    freq = ROPE_BASE ** (-np.arange(hd // 2, dtype=np.float64) / (hd // 2))
    angle = freq[:, None] * np.arange(positions, dtype=np.float64)[None, :]
    return np.cos(angle).astype(np.float32), np.sin(angle).astype(np.float32)


def call_a(mesh, args):
    (hidden_in, seq_lengths, attn_gain, ffn_gain, query_gain, key_gain,
     w_query, w_key, w_value, w_out, w_gate, w_up) = args
    n_shard, n_ctx, n_tp = mesh.shape["shard"], mesh.shape["ctx"], mesh.shape["tp"]
    rows, width = hidden_in.shape
    hd = query_gain.shape[0]
    q_cols, kv_cols = w_query.shape[1], w_key.shape[1]
    q_heads, kv_heads = q_cols // hd, kv_cols // hd
    block = w_query.shape[0]
    padded = round_up(w_gate.shape[1])
    cosine, sine = rope_tables(n_ctx * rows, hd)
    vm = pl.BlockSpec(memory_space=pltpu.VMEM)
    hbm = pl.BlockSpec(memory_space=pltpu.HBM)
    sm = pl.BlockSpec(memory_space=pltpu.SMEM)
    qkv_cols = q_cols + 2 * kv_cols
    S = jax.ShapeDtypeStruct
    dma = pltpu.SemaphoreType.DMA
    chunks = q_cols // 128
    return pl.pallas_call(
        functools.partial(kernel_a, (n_shard, n_tp, hd)),
        out_shape=(
            S((width, qkv_cols), BF16),
            S((width, n_tp * q_cols), BF16),
            S((width, padded), BF16),
            S((width, padded), BF16),
            S((rows, n_tp * q_cols), BF16),
            S((q_cols, rows), BF16),
            S((n_ctx, 2 * kv_cols, rows), BF16),
            S((8, rows), F32),
            S((qkv_cols, rows), F32),
        ),
        in_specs=[sm] + [vm] * 13,
        out_specs=(vm, hbm, hbm, hbm, vm, vm, vm, vm, vm),
        scratch_shapes=[
            pltpu.VMEM((block, qkv_cols), BF16),
            pltpu.VMEM((block, n_tp * q_cols), BF16),
            pltpu.VMEM((block, padded), BF16),
            pltpu.VMEM((block, padded), BF16),
            pltpu.VMEM((rows, width), BF16),
            pltpu.VMEM((kv_heads, rows, hd), BF16),
            pltpu.VMEM((kv_heads, rows, hd), BF16),
            pltpu.VMEM((kv_heads, hd + 16, rows), BF16),
            pltpu.VMEM((kv_heads, hd + 16, rows), BF16),
            pltpu.VMEM((q_heads, hd + 16, rows), F32),
            dma((4, 7)),
            dma((4, 7)),
            dma((n_tp - 1,)),
            dma((n_tp - 1,)),
            dma((2, n_tp, chunks)),
            dma((2, n_tp, chunks)),
            dma((2,)),
            dma((4,)),
        ],
        compiler_params=pltpu.CompilerParams(
            collective_id=0, has_side_effects=True, vmem_limit_bytes=VMEM_LIMIT
        ),
    )(
        seq_lengths, hidden_in, attn_gain.reshape(1, -1), ffn_gain.reshape(1, -1),
        query_gain.reshape(1, -1), key_gain.reshape(1, -1), w_query, w_key, w_value,
        w_out.T, w_gate, w_up, jnp.asarray(cosine), jnp.asarray(sine),
    )


class Line:
    def __init__(self, at, part, landing, send, recv, chunks):
        self.at, self.part, self.landing = at, part, landing
        self.send, self.recv, self.chunks = send, recv, chunks
        self.half = landing.shape[1]
        self.size = self.half // chunks
        self.last = at.n_tp - 1

    def pos(self, way):
        return self.at.t if way == 0 else self.last - self.at.t

    def dev(self, way, step):
        to = self.at.t + (step if way == 0 else -step)
        return self.at.z(jnp.clip(to, 0, self.last))

    def local(self, k):
        return pl.ds(pl.multiple_of(k * self.size, self.size), self.size)

    def rows(self, way, k):
        start = (1 - way) * self.half + k * self.size
        return pl.ds(pl.multiple_of(start, self.size), self.size)

    def copy(self, way, k):
        return remote(
            self.part.at[self.rows(way, k)],
            self.landing.at[way, self.local(k)],
            self.send.at[way, k],
            self.recv.at[way, k],
            self.dev(way, 1),
        )

    def reduce(self, step, final):
        for way in (0, 1):
            pos = self.pos(way)
            k = step - pos
            live = jnp.logical_and(k >= 0, k < self.chunks)

            @pl.when(jnp.logical_and(live, pos > 0))
            def _():
                self.copy(way, k).wait_recv()
                value = self.part[self.rows(way, k), :].astype(F32)
                value += self.landing[way, self.local(k), :].astype(F32)

                @pl.when(pos < self.last)
                def _():
                    self.part[self.rows(way, k), :] = value.astype(BF16)

                @pl.when(pos == self.last)
                def _():
                    final(way, k, value)

            @pl.when(jnp.logical_and(live, pos < self.last))
            def _():
                self.copy(way, k).start()

    def drain(self):
        for way in (0, 1):

            @pl.when(self.pos(way) < self.last)
            def _():
                def one(k, _):
                    self.copy(way, k).wait_send()
                    return 0

                lax.fori_loop(0, self.chunks, one, 0)


class Back:
    def __init__(self, line, whole, send, recv, source=None):
        self.line, self.whole, self.send, self.recv = line, whole, send, recv
        self.source = source

    def copy(self, way, k, first=False):
        line = self.line
        dst = self.whole.at[line.rows(way, k)]
        src = self.source.at[line.local(k)] if first and self.source is not None else dst
        return remote(src, dst, self.send.at[way, k], self.recv.at[way, k], line.dev(way, -1))

    def step(self, step):
        line = self.line
        for way in (0, 1):
            pos = line.pos(way)
            k = step - (line.last - pos)
            live = jnp.logical_and(k >= 0, k < line.chunks)

            @pl.when(jnp.logical_and(live, pos < line.last))
            def _():
                self.copy(way, k).wait_recv()

                @pl.when(pos > 0)
                def _():
                    self.copy(way, k).start()

            @pl.when(jnp.logical_and(live, pos == line.last))
            def _():
                self.copy(way, k, True).start()

    def drain(self):
        line = self.line
        for way in (0, 1):

            @pl.when(line.pos(way) > 0)
            def _():
                def one(k, _):
                    self.copy(way, k).wait_send()
                    return 0

                lax.fori_loop(0, line.chunks, one, 0)


def kernel_b(
    shape,
    length_ref,
    hid_ref,
    heads_ref,
    og_ref,
    wd_ref,
    wo_hbm,
    wg_hbm,
    wu_hbm,
    attn_low,
    rg_own,
    blk_own,
    wgrads,
    wo,
    wg,
    wu,
    wd,
    resid,
    h2,
    gl,
    act,
    land_f,
    land_d,
    stage,
    g_send,
    g_recv,
    f_send,
    f_recv,
    d_send,
    d_recv,
    b_send,
    b_recv,
    loc_sem,
    st_sem,
):
    n_shard, n_tp, chunks = shape
    at = Place(n_shard, n_tp)
    rows, width = hid_ref.shape
    units, padded = wd_ref.shape[1], wd.shape[1]
    block = wd_ref.shape[0]
    half = rows // 2
    tiles = padded // 256
    loads = [
        pltpu.make_async_copy(src, dst, loc_sem.at[i])
        for i, (src, dst) in enumerate(((wo_hbm, wo), (wg_hbm, wg), (wu_hbm, wu)))
    ]
    for cp in loads:
        cp.start()
    own = pl.ds(pl.multiple_of(at.own * block, block), block)
    wd[own, 0:units] = wd_ref[...]
    wd[own, units:] = jnp.zeros((block, padded - units), BF16)
    at.greet()
    down = Gather(at, wd.at[own], wd, g_send, g_recv, 0)
    down.start()
    length = length_ref[0]

    def live_rows(start, n):
        pos = at.c * rows + start + lax.broadcasted_iota(jnp.int32, (n, 1), 0)
        return (pos < length).astype(F32)

    def mask_grad(i, _):
        start = pl.multiple_of(i * 64, 64)
        r = pl.ds(start, 64)
        gl[r, :] = (og_ref[r, :].astype(F32) * live_rows(start, 64)).astype(BF16)
        return 0

    lax.fori_loop(0, rows // 64, mask_grad, 0)
    loads[0].wait()

    def residual(i, _):
        r = pl.ds(pl.multiple_of(i * 128, 128), 128)
        x = hid_ref[r, :].astype(F32) + mm_nt(heads_ref[r, :], wo[...])
        resid[r, :] = x
        scale = lax.rsqrt(jnp.mean(x * x, axis=-1, keepdims=True) + EPSILON)
        h2[r, :] = (x * scale).astype(BF16)
        return 0

    lax.fori_loop(0, rows // 128, residual, 0)
    loads[1].wait()
    loads[2].wait()

    def gate_up(f, _):
        cols = pl.ds(pl.multiple_of(f * 256, 256), 256)
        for i in (0, 1):
            r = slice(i * half, (i + 1) * half)
            g = mm(h2[r, :], wg[:, cols])
            u = mm(h2[r, :], wu[:, cols])
            s = 1.0 / (1.0 + jnp.exp(-g))
            silu = g * s
            act[0, r, cols] = (silu * u).astype(BF16)
            act[1, r, cols] = (u * (s * (1.0 + g * (1.0 - s)))).astype(BF16)
            act[2, r, cols] = silu.astype(BF16)

        @pl.when(f == 2)
        def _():
            down.relay()

        @pl.when(f == tiles - 1)
        def _():
            down.relay_last()

        return 0

    lax.fori_loop(0, tiles, gate_up, 0)
    down.finish()

    f_part, d_part = wo.at[0:rows], wo.at[rows:]
    quarter = half // 2
    ffn = Line(at, f_part, land_f, f_send, f_recv, chunks)
    d2 = Line(at, d_part, land_d, d_send, d_recv, chunks)
    back = Back(d2, attn_low, b_send, b_recv)

    def final_ffn(way, k, value):
        r = ffn.rows(way, k)
        x = resid[r, :] + value
        live = live_rows((1 - way) * half + k * ffn.size, ffn.size)
        blk_own[ffn.local(k), :] = (x * live).astype(BF16)

    def final_d2(way, k, value):
        r = d2.rows(way, k)
        x = resid[r, :]
        scale = lax.rsqrt(jnp.mean(x * x, axis=-1, keepdims=True) + EPSILON)
        h = x * scale
        inner = jnp.mean(value * h, axis=-1, keepdims=True)
        grad = gl[r, :].astype(F32) + scale * (value - h * inner)
        rg_own[d2.local(k), :] = grad
        attn_low[r, :] = grad.astype(BF16)

    order = (0, 2, 1, 3)
    for q in order:
        r = slice(q * quarter, (q + 1) * quarter)
        f_part[r, :] = mm_nt(act[0, r, :], wd[...]).astype(BF16)

    def mid(f, _):
        cols = pl.ds(pl.multiple_of(f * 256, 256), 256)
        for i in (0, 1):
            r = slice(i * half, (i + 1) * half)
            g = mm(gl[r, :], wd[:, cols])
            act[1, r, cols] = (g * act[1, r, cols].astype(F32)).astype(BF16)
            act[2, r, cols] = (g * act[2, r, cols].astype(F32)).astype(BF16)

        @pl.when(lax.rem(f, 3) == 0)
        def _():
            ffn.reduce(lax.div(f, 3), final_ffn)

        return 0

    lax.fori_loop(0, tiles, mid, 0)
    done = -(-tiles // 3)
    for n, q in enumerate(order):
        r = slice(q * quarter, (q + 1) * quarter)
        total = mm_nt(act[1, r, :], wg[...]) + mm_nt(act[2, r, :], wu[...])
        d_part[r, :] = total.astype(BF16)
        ffn.reduce(done + n, final_ffn)
    done += len(order)

    def turn(i, _):
        r = pl.ds(pl.multiple_of(i * 128, 128), 128)
        r2 = pl.ds(pl.multiple_of(rows + i * 128, 128), 128)
        wu[:, r] = h2[r, :].T
        wu[:, r2] = gl[r, :].T
        return 0

    last = n_tp - 1
    per_step = 2
    count = 3 * (width // block)

    def stage_copy(n):
        a, w = lax.div(n, width // block), lax.rem(n, width // block)
        slot = lax.rem(n, 2)
        return pltpu.make_async_copy(
            stage.at[slot],
            wgrads.at[a, pl.ds(pl.multiple_of(w * block, block), block)],
            st_sem.at[slot],
        )

    def weight_grad(n):
        a, w = lax.div(n, width // block), lax.rem(n, width // block)
        slot = lax.rem(n, 2)

        @pl.when(n >= 2)
        def _():
            stage_copy(n - 2).wait()

        first = pl.multiple_of(jnp.where(a == 0, rows, 0), 128)
        left = wu[pl.ds(pl.multiple_of(w * block, block), block), pl.ds(first, rows)]
        for f in range(tiles):
            cols = slice(f * 256, (f + 1) * 256)
            stage[slot, :, cols] = mm(left, act[a, :, cols]).astype(BF16)
        stage_copy(n).start()

    def tail(step, _):
        @pl.when(step + done < chunks + last)
        def _():
            ffn.reduce(step + done, final_ffn)

        d2.reduce(step, final_d2)
        back.step(step - last)

        @pl.when(step == 0)
        def _():
            lax.fori_loop(0, rows // 128, turn, 0)

        for n in range(per_step):

            @pl.when(step * per_step + n < count)
            def _():
                weight_grad(step * per_step + n)

        return 0

    steps = max(chunks + 2 * last, -(-count // per_step), chunks + last - done)
    lax.fori_loop(0, steps, tail, 0)
    stage_copy(count - 2).wait()
    stage_copy(count - 1).wait()
    ffn.drain()
    d2.drain()
    back.drain()


def call_b(mesh, chunks, seq_lengths, hidden_in, heads_all, out_grad, w_down, wo_full, wg_full, wu_full):
    n_shard, n_tp = mesh.shape["shard"], mesh.shape["tp"]
    rows, width = hidden_in.shape
    block = w_down.shape[1]
    padded = wg_full.shape[1]
    half = rows // 2
    vm = pl.BlockSpec(memory_space=pltpu.VMEM)
    hbm = pl.BlockSpec(memory_space=pltpu.HBM)
    sm = pl.BlockSpec(memory_space=pltpu.SMEM)
    S = jax.ShapeDtypeStruct
    dma = pltpu.SemaphoreType.DMA
    return pl.pallas_call(
        functools.partial(kernel_b, (n_shard, n_tp, chunks)),
        out_shape=(
            S((rows, width), BF16),
            S((half, width), F32),
            S((half, width), BF16),
            S((3, width, padded), BF16),
        ),
        in_specs=[sm] + [vm] * 4 + [hbm] * 3,
        out_specs=(vm, vm, vm, hbm),
        scratch_shapes=[
            pltpu.VMEM((width, width), BF16),
            pltpu.VMEM((width, padded), BF16),
            pltpu.VMEM((width, padded), BF16),
            pltpu.VMEM((width, padded), BF16),
            pltpu.VMEM((rows, width), F32),
            pltpu.VMEM((rows, width), BF16),
            pltpu.VMEM((rows, width), BF16),
            pltpu.VMEM((3, rows, padded), BF16),
            pltpu.VMEM((2, half, width), BF16),
            pltpu.VMEM((2, half, width), BF16),
            pltpu.VMEM((2, block, padded), BF16),
            dma((1, 7)),
            dma((1, 7)),
            dma((2, chunks)),
            dma((2, chunks)),
            dma((2, chunks)),
            dma((2, chunks)),
            dma((2, chunks)),
            dma((2, chunks)),
            dma((3,)),
            dma((2,)),
        ],
        compiler_params=pltpu.CompilerParams(
            collective_id=1, has_side_effects=True, vmem_limit_bytes=VMEM_LIMIT
        ),
    )(seq_lengths, hidden_in, heads_all, out_grad, w_down.T, wo_full, wg_full, wu_full)


class Scatter:
    def __init__(self, at, source, land, relayed, final, tmp, tmp_sem, send, recv, index):
        self.at, self.source, self.land = at, source, land
        self.relayed, self.final = relayed, final
        self.tmp, self.tmp_sem = tmp, tmp_sem
        self.send, self.recv, self.index = send, recv, index
        self.rows = land.shape[1]
        self.direct, self.indirect = 1 + at.core, 2 - at.core
        self.other = (
            at.core * at.x[0] + (1 - at.core) * at.y[0],
            at.core * at.x[1] + (1 - at.core) * at.y[1],
            at.t,
        )
        names = (("own", "X", "Y", "D"), ("S", "SX", "SY", "SD"))
        find = lambda n: at.own if n == "own" else at.slots[n]
        self.mine = [find(n) for n in names[0]]
        self.theirs = [find(n) for n in names[1]]

    def block(self, slot):
        return self.source.at[pl.ds(pl.multiple_of(slot * self.rows, self.rows), self.rows)]

    def copy(self, k, src, dst, dev):
        return remote(src, dst, self.send.at[self.index, k], self.recv.at[self.index, k], dev)

    def share(self, j):
        return self.copy(j, self.block(self.theirs[j]), self.land.at[j], self.at.sib)

    def start(self):
        for j in (3, 1, 2, 0):
            self.share(j).start()

    def slot(self, j):
        if isinstance(j, int):
            return self.mine[j]
        return jnp.where(j == 1, self.mine[1], self.mine[2])

    def arrived(self, j):
        ref = self.land.at[j]
        self.copy(j, ref, ref, self.at.sib).wait_recv()

    def fetch(self, j):
        return pltpu.make_async_copy(self.block(self.slot(j)), self.tmp, self.tmp_sem)

    def add(self, j, extra=()):
        self.fetch(j).start()
        self.arrived(j)
        self.fetch(j).wait()

        def piece(i, _):
            r = pl.ds(pl.multiple_of(i * 64, 64), 64)
            value = self.land[j, r, :].astype(F32) + self.tmp[r, :].astype(F32)
            for ref in extra:
                value += ref[r, :].astype(F32)
            self.land[j, r, :] = value.astype(BF16)
            return 0

        lax.fori_loop(0, self.rows // 64, piece, 0)

    def hop(self, k):
        at = self.at
        if k == 4:
            return self.copy(4, self.land.at[3], self.relayed, at.relay)
        if k == 5:
            return self.copy(5, self.land.at[self.direct], self.final.at[0], at.relay)
        return self.copy(6, self.land.at[self.indirect], self.final.at[1], self.other)

    def first(self):
        self.add(3)
        self.hop(4).start()
        self.add(self.direct)
        self.hop(5).start()

    def second(self):
        self.hop(4).wait_recv()
        self.add(self.indirect, (self.relayed,))
        self.hop(6).start()

    def finish(self, use):
        self.fetch(0).start()
        self.arrived(0)
        self.hop(5).wait_recv()
        self.hop(6).wait_recv()
        self.fetch(0).wait()

        def piece(i, _):
            r = pl.ds(pl.multiple_of(i * 64, 64), 64)
            value = self.land[0, r, :].astype(F32) + self.tmp[r, :].astype(F32)
            value += self.final[0, r, :].astype(F32) + self.final[1, r, :].astype(F32)
            use(r, value)
            return 0

        lax.fori_loop(0, self.rows // 64, piece, 0)

    def drain(self):
        for j in range(4):
            self.share(j).wait_send()
        for k in (4, 5, 6):
            self.hop(k).wait_send()


def kernel_c(
    shape,
    length_ref,
    attn_low,
    rg_own,
    hid_ref,
    wqkv,
    q_t,
    kv_all,
    inv_den,
    proj_t,
    gain_one_ref,
    gain_two_ref,
    q_gain_ref,
    k_gain_ref,
    wq_ref,
    wk_ref,
    wv_ref,
    wg_ref,
    wu_ref,
    cos_ref,
    sin_ref,
    blk_own,
    wgrads,
    heads_hbm,
    wo_hbm,
    block_out,
    inp,
    g_query,
    g_key,
    g_value,
    g_out,
    g_gate,
    g_up,
    g_down,
    small,
    heads_own,
    wo_own,
    hg_t,
    delta,
    k_own,
    v_own,
    kt_own,
    dq_t,
    dkv,
    dkv_send,
    dkv_land,
    gain_acc,
    dqkv,
    d_part,
    land_d,
    left_t,
    part,
    land_w,
    rel_w,
    fin_w,
    land_p,
    rel_p,
    fin_p,
    tmp_w,
    tmp_p,
    cols_acc,
    qk,
    qk_land,
    tile,
    s_send,
    s_recv,
    d_send,
    d_recv,
    b_send,
    b_recv,
    o_send,
    o_recv,
    e_send,
    e_recv,
    t_send,
    t_recv,
    loc_sem,
):
    n_shard, n_tp, chunks, hd = shape
    at = Place(n_shard, n_tp)
    c, t = at.c, at.t
    rows, width = hid_ref.shape
    q_cols, kv_cols = wq_ref.shape[1], wk_ref.shape[1]
    q_heads, kv_heads = q_cols // hd, kv_cols // hd
    group = q_heads // kv_heads
    halfd = hd // 2
    half = rows // 2
    block = wq_ref.shape[0]
    units = wg_ref.shape[1]
    last = n_tp - 1
    own_cols = pl.ds(pl.multiple_of(t * q_cols, q_cols), q_cols)
    loads = [
        pltpu.make_async_copy(heads_hbm.at[:, own_cols], heads_own, loc_sem.at[0]),
        pltpu.make_async_copy(wo_hbm.at[:, own_cols], wo_own, loc_sem.at[1]),
    ]
    for cp in loads:
        cp.start()
    at.greet()
    weights = [
        Scatter(
            at, wgrads.at[i], land_w.at[i], rel_w.at[i], fin_w.at[i], tmp_w,
            loc_sem.at[2], s_send, s_recv, i,
        )
        for i in range(3)
    ]
    rest = Scatter(
        at, part, land_p, rel_p, fin_p, tmp_p, loc_sem.at[3], s_send, s_recv, 3
    )
    for w in weights:
        w.start()
    d1 = Line(at, d_part, land_d, d_send, d_recv, chunks)
    back = Back(d1, inp, b_send, b_recv)
    back_block = Back(d1, block_out, o_send, o_recv, blk_own)

    def keep(start):
        return pltpu.make_async_copy(
            blk_own, block_out.at[pl.ds(start, half)], loc_sem.at[4]
        )

    @pl.when(t == 0)
    def _():
        keep(0).start()

    @pl.when(t == last)
    def _():
        keep(half).start()

    back_block.step(0)
    length = length_ref[0]
    for cp in loads:
        cp.wait()

    def heads_grad(i, _):
        r = pl.ds(pl.multiple_of(i * 256, 256), 256)
        hg_t[:, r] = mm(attn_low[r, :], wo_own[...]).T.astype(BF16)
        return 0

    lax.fori_loop(0, rows // 256, heads_grad, 0)
    for j in range(q_cols // 128):
        cols = slice(j * 128, (j + 1) * 128)
        both = heads_own[:, cols].astype(F32).T * hg_t[cols, :].astype(F32)
        for n in range(128 // hd):
            h = j * (128 // hd) + n
            delta[h : h + 1, :] = jnp.sum(both[n * hd : (n + 1) * hd], axis=0, keepdims=True)
    back_block.step(1)
    weights[0].first()

    def live_keys(index):
        pos = index * rows + lax.broadcasted_iota(jnp.int32, (1, rows), 1)
        return (pos < length).astype(F32)

    def load_block(index, k_nat, v_nat, kt):
        live = live_keys(index)
        for g in range(kv_heads):
            key = kv_all[index, g * hd : (g + 1) * hd, :].astype(F32)
            k_nat[g] = key.T.astype(BF16)
            kt[g] = (key * live).astype(BF16)
            value = kv_all[index, kv_cols + g * hd : kv_cols + (g + 1) * hd, :]
            v_nat[g] = value.astype(F32).T.astype(BF16)

    below = lax.broadcasted_iota(jnp.int32, (256, 256), 0) <= lax.broadcasted_iota(
        jnp.int32, (256, 256), 1
    )

    def segment(h, g, i, lo, hi, masked, k_nat, v_nat, kt):
        cols = slice(i * 256, (i + 1) * 256)
        hr = pl.ds(pl.multiple_of(h * hd, hd), hd)
        qi, oi = q_t[hr, cols], hg_t[hr, cols]
        p = jnp.exp(mm(k_nat[g, lo:hi, :], qi)) * inv_den[pl.ds(h, 1), cols]
        if masked:
            p = jnp.where(below, p, 0.0)
        dp = mm(v_nat[g, lo:hi, :], oi)
        ds = (p * (dp - delta[pl.ds(h, 1), cols])).astype(BF16)
        dq_t[hr, cols] += mm(kt[g, :, lo:hi], ds)
        dkv[g, :, lo:hi] += mm_nt(qi, ds)
        dkv[kv_heads + g, :, lo:hi] += mm_nt(oi, p.astype(BF16))

    dq_t[...] = jnp.zeros_like(dq_t)
    dkv[...] = jnp.zeros_like(dkv)
    give = remote(dkv_send, dkv_land, e_send.at[3], e_recv.at[3], at.x)

    @pl.when(c == 1)
    def _():
        load_block(0, k_own, v_own, kt_own)

        def one(h, _):
            for i in range(rows // 256):
                segment(h, h // group, i, 0, rows, False, k_own, v_own, kt_own)
            return 0

        lax.fori_loop(0, q_heads, one, 0)
        live = live_keys(0)
        for n in range(2 * kv_heads):
            dkv_send[n] = (dkv[n] * live).astype(BF16)
        give.start()
        dkv[...] = jnp.zeros_like(dkv)

    back_block.step(2)
    weights[1].first()
    weights[0].second()
    load_block(c, k_own, v_own, kt_own)

    def own_block(h, _):
        for i in range(rows // 256):
            segment(h, h // group, i, i * 256, (i + 1) * 256, True, k_own, v_own, kt_own)
            if i:
                segment(h, h // group, i, 0, i * 256, False, k_own, v_own, kt_own)

        back_block.step(3 + h)
        return 0

    lax.fori_loop(0, q_heads, own_block, 0)
    live = live_keys(c)
    for n in range(2 * kv_heads):
        dkv[n] = dkv[n] * live

    @pl.when(c == 0)
    def _():
        give.wait_recv()
        for n in range(2 * kv_heads):
            dkv[n] += dkv_land[n].astype(F32)

    here = pl.ds(pl.multiple_of(c * rows, rows), rows)
    gain_acc[...] = jnp.zeros_like(gain_acc)

    def through(which, row, grad, gain):
        x = proj_t[pl.ds(pl.multiple_of(row, hd), hd), :]
        scale = lax.rsqrt(jnp.mean(x * x, axis=0, keepdims=True) + EPSILON)
        xh = x * scale
        cosine, sine = cos_ref[:, here], sin_ref[:, here]
        a, b = grad[:halfd], grad[halfd:]
        grad = jnp.concatenate([a * cosine + b * sine, b * cosine - a * sine], axis=0)
        gain_acc[which] += grad * xh
        grad = grad * gain
        inner = jnp.mean(grad * xh, axis=0, keepdims=True)
        return scale * (grad - xh * inner)

    q_gain, k_gain = column(q_gain_ref, hd), column(k_gain_ref, hd)
    factor = 1.0 / math.sqrt(hd)

    def query_back(h, _):
        row = pl.multiple_of(h * hd, hd)
        r = pl.ds(row, hd)
        dq_t[r, :] = through(0, row, dq_t[r, :] * factor, q_gain)
        return 0

    lax.fori_loop(0, q_heads, query_back, 0)
    dqkv[:, 0:q_cols] = dq_t[...].T.astype(BF16)
    pair = jnp.concatenate(
        [through(1, q_cols + g * hd, dkv[g], k_gain) for g in range(kv_heads)], axis=0
    )
    dqkv[:, q_cols : q_cols + kv_cols] = pair.T.astype(BF16)
    pair = jnp.concatenate([dkv[kv_heads + g] for g in range(kv_heads)], axis=0)
    dqkv[:, q_cols + kv_cols :] = pair.T.astype(BF16)
    quarter = half // 2
    for q in (0, 2, 1, 3):
        r = slice(q * quarter, (q + 1) * quarter)
        d_part[r, :] = mm_nt(dqkv[r, :], wqkv[...]).astype(BF16)

    def as_row(v):
        return jnp.broadcast_to(v, (v.shape[0], 128)).T[0:1, :]

    qk[...] = jnp.zeros_like(qk)
    for n in (0, 1):
        qk[0, n : n + 1, 0:hd] = as_row(jnp.sum(gain_acc[n], axis=1, keepdims=True))

    def trade(n):
        dev = (at.sib, at.x, at.y)[n]
        return remote(qk.at[n], qk_land.at[n], e_send.at[n], e_recv.at[n], dev)

    def traded(n):
        trade(n).wait_recv()
        qk[n + 1] = qk[n] + qk_land[n]

    weights[2].first()
    weights[1].second()

    def final(way, k, value):
        r = d1.rows(way, k)
        x = hid_ref[r, :].astype(F32)
        scale = lax.rsqrt(jnp.mean(x * x, axis=-1, keepdims=True) + EPSILON)
        h = x * scale
        inner = jnp.mean(value * h, axis=-1, keepdims=True)
        grad = rg_own[d1.local(k), :] + scale * (value - h * inner)
        inp[r, :] = grad.astype(BF16)

    def turn_hidden(i, _):
        r = pl.ds(pl.multiple_of(i * 128, 128), 128)
        x = hid_ref[r, :].astype(F32)
        scale = lax.rsqrt(jnp.mean(x * x, axis=-1, keepdims=True) + EPSILON)
        left_t[0, :, r] = (x * scale).astype(BF16).T
        left_t[1, :, r] = attn_low[r, :].T
        return 0

    def weight_part(w, _):
        r = pl.ds(pl.multiple_of(w * block, block), block)
        part[r, 0 : dqkv.shape[1]] = mm(left_t[0, r, :], dqkv[...]).astype(BF16)
        part[r, dqkv.shape[1] :] = mm(left_t[1, r, :], heads_own[...]).astype(BF16)
        return 0

    g_one = column(gain_one_ref, block)
    g_two = column(gain_two_ref, block)
    cols_acc[0] = jnp.broadcast_to(g_one, (block, 128))
    cols_acc[1] = jnp.broadcast_to(g_two, (block, 128))

    def use_down(r, value):
        g_down[r, :] = value[:, 0:units]

    def use_gate(r, value):
        value = value[:, 0:units]
        total = jnp.sum(wg_ref[r, :].astype(F32) * value, axis=1, keepdims=True)
        cols_acc[3, r, :] = jnp.broadcast_to(total, (64, 128))
        g_gate[r, :] = value * cols_acc[1, r, 0:1]

    def use_up(r, value):
        value = value[:, 0:units]
        total = jnp.sum(wu_ref[r, :].astype(F32) * value, axis=1, keepdims=True)
        cols_acc[3, r, :] += jnp.broadcast_to(total, (64, 128))
        g_up[r, :] = value * cols_acc[1, r, 0:1]

    def use_rest(r, value):
        gain = cols_acc[0, r, 0:1]
        vq = value[:, 0:q_cols]
        vk = value[:, q_cols : q_cols + kv_cols]
        vv = value[:, q_cols + kv_cols : q_cols + 2 * kv_cols]
        total = jnp.sum(wq_ref[r, :].astype(F32) * vq, axis=1, keepdims=True)
        total += jnp.sum(wk_ref[r, :].astype(F32) * vk, axis=1, keepdims=True)
        total += jnp.sum(wv_ref[r, :].astype(F32) * vv, axis=1, keepdims=True)
        cols_acc[2, r, :] = jnp.broadcast_to(total, (64, 128))
        g_query[r, :] = vq * gain
        g_key[r, :] = vk * gain
        g_value[r, :] = vv * gain
        g_out[r, :] = value[:, q_cols + 2 * kv_cols :]

    def turn_all():
        lax.fori_loop(0, rows // 128, turn_hidden, 0)

    def parts():
        lax.fori_loop(0, width // block, weight_part, 0)
        rest.start()

    events = {
        0: (lambda: trade(0).start(), turn_all),
        1: (parts, lambda: traded(0), lambda: trade(1).start()),
        2: (rest.first, lambda: traded(1), lambda: trade(2).start()),
        3: (weights[2].second, lambda: traded(2)),
        4: (rest.second, lambda: weights[0].finish(use_down)),
        7: (lambda: weights[1].finish(use_gate),),
        10: (lambda: weights[2].finish(use_up),),
        12: (lambda: rest.finish(use_rest),),
    }

    def tail(step, _):
        d1.reduce(step, final)
        back.step(step - last)
        back_block.step(step + 3 + q_heads)
        for when, todo in events.items():

            @pl.when(step == when)
            def _():
                for thing in todo:
                    thing()

        return 0

    lax.fori_loop(0, max(chunks + 2 * last, 13), tail, 0)

    def give_tile(d, owner):
        return remote(
            tile.at[owner], tile.at[owner], t_send.at[d], t_recv.at[d],
            at.z(lax.rem(t + d + 1, n_tp)),
        )

    tile[t] = jnp.zeros(tile.shape[1:], F32)
    tile[t, 0:1, 0:block] = cols_acc[2].T[0:1, :]
    tile[t, 1:2, 0:block] = cols_acc[3].T[0:1, :]
    tile[t, 2:4, 0:128] = qk[3, 0:2, :]
    for d in range(n_tp - 1):
        give_tile(d, t).start()
    for w in weights + [rest]:
        w.drain()
    d1.drain()
    back.drain()
    back_block.drain()

    @pl.when(t == 0)
    def _():
        keep(0).wait()

    @pl.when(t == last)
    def _():
        keep(half).wait()

    @pl.when(c == 1)
    def _():
        give.wait_send()

    for n in range(3):
        trade(n).wait_send()
    for d in range(n_tp - 1):
        give_tile(d, lax.rem(t + n_tp - d - 1, n_tp)).wait_recv()
    total = tile[0]
    for n in range(1, n_tp):
        total = total + tile[n]
    small[...] = total
    for d in range(n_tp - 1):
        give_tile(d, t).wait_send()


def call_c(mesh, chunks, args, kept):
    (hidden_in, seq_lengths, attn_gain, ffn_gain, query_gain, key_gain,
     w_query, w_key, w_value, w_gate, w_up) = args
    (attn_low, rg_own, blk_own, wgrads, wqkv_full, wo_full, heads_all, q_t, kv_all, inv_den,
     proj_t) = kept
    n_shard, n_ctx, n_tp = mesh.shape["shard"], mesh.shape["ctx"], mesh.shape["tp"]
    rows, width = hidden_in.shape
    half = rows // 2
    hd = query_gain.shape[0]
    q_cols, kv_cols = w_query.shape[1], w_key.shape[1]
    qkv_cols = q_cols + 2 * kv_cols
    kv_heads = kv_cols // hd
    block, units = w_gate.shape
    padded = wgrads.shape[2]
    cosine, sine = rope_tables(n_ctx * rows, hd)
    vm = pl.BlockSpec(memory_space=pltpu.VMEM)
    hbm = pl.BlockSpec(memory_space=pltpu.HBM)
    sm = pl.BlockSpec(memory_space=pltpu.SMEM)
    S = jax.ShapeDtypeStruct
    V = pltpu.VMEM
    dma = pltpu.SemaphoreType.DMA
    return pl.pallas_call(
        functools.partial(kernel_c, (n_shard, n_tp, chunks, hd)),
        out_shape=(
            S((rows, width), BF16),
            S((rows, width), BF16),
            S((block, q_cols), F32),
            S((block, kv_cols), F32),
            S((block, kv_cols), F32),
            S((block, q_cols), F32),
            S((block, units), F32),
            S((block, units), F32),
            S((block, units), F32),
            S((8, 256), F32),
        ),
        in_specs=[sm] + [vm] * 19 + [hbm] * 4,
        out_specs=(hbm,) + (vm,) * 9,
        scratch_shapes=[
            V((rows, q_cols), BF16),
            V((width, q_cols), BF16),
            V((q_cols, rows), BF16),
            V((8, rows), F32),
            V((kv_heads, rows, hd), BF16),
            V((kv_heads, rows, hd), BF16),
            V((kv_heads, hd, rows), BF16),
            V((q_cols, rows), F32),
            V((2 * kv_heads, hd, rows), F32),
            V((2 * kv_heads, hd, rows), BF16),
            V((2 * kv_heads, hd, rows), BF16),
            V((2, hd, rows), F32),
            V((rows, qkv_cols), BF16),
            V((rows, width), BF16),
            V((2, half, width), BF16),
            V((2, width, rows), BF16),
            V((width, qkv_cols + q_cols), BF16),
            V((3, 4, block, padded), BF16),
            V((3, block, padded), BF16),
            V((3, 2, block, padded), BF16),
            V((4, block, qkv_cols + q_cols), BF16),
            V((block, qkv_cols + q_cols), BF16),
            V((2, block, qkv_cols + q_cols), BF16),
            V((block, padded), BF16),
            V((block, qkv_cols + q_cols), BF16),
            V((4, block, 128), F32),
            V((4, 8, 128), F32),
            V((3, 8, 128), F32),
            V((n_tp, 8, 256), F32),
            dma((4, 7)),
            dma((4, 7)),
            dma((2, chunks)),
            dma((2, chunks)),
            dma((2, chunks)),
            dma((2, chunks)),
            dma((2, chunks)),
            dma((2, chunks)),
            dma((4,)),
            dma((4,)),
            dma((n_tp - 1,)),
            dma((n_tp - 1,)),
            dma((5,)),
        ],
        compiler_params=pltpu.CompilerParams(
            collective_id=2, has_side_effects=True, vmem_limit_bytes=VMEM_LIMIT
        ),
    )(
        seq_lengths, attn_low, rg_own, hidden_in, wqkv_full, q_t, kv_all, inv_den, proj_t,
        attn_gain.reshape(1, -1), ffn_gain.reshape(1, -1), query_gain.reshape(1, -1),
        key_gain.reshape(1, -1), w_query, w_key, w_value, w_gate, w_up,
        jnp.asarray(cosine), jnp.asarray(sine), blk_own, wgrads, heads_all, wo_full,
    )


CHUNKS = 8


def fast_body(mesh, *args):
    (hidden_in, seq_lengths, attn_gain, ffn_gain, query_gain, key_gain,
     w_query, w_key, w_value, w_out, w_gate, w_up, w_down, out_grad) = args
    (wqkv_full, wo_full, wg_full, wu_full, heads_all, q_t, kv_all, inv_den,
     proj_t) = call_a(mesh, args[:12])
    attn_low, rg_own, blk_own, wgrads = call_b(
        mesh, CHUNKS, seq_lengths, hidden_in, heads_all, out_grad, w_down, wo_full, wg_full, wu_full
    )
    (block_out, inp, g_query, g_key, g_value, g_out, g_gate, g_up, g_down, small) = call_c(
        mesh, CHUNKS,
        (hidden_in, seq_lengths, attn_gain, ffn_gain, query_gain, key_gain, w_query, w_key,
         w_value, w_gate, w_up),
        (attn_low, rg_own, blk_own, wgrads, wqkv_full, wo_full, heads_all, q_t, kv_all, inv_den,
         proj_t),
    )
    block, hd = w_query.shape[0], query_gain.shape[0]
    return (
        block_out, inp.astype(F32), small[0, :block], small[1, :block], small[2, :hd],
        small[3, :hd], g_query, g_key, g_value, g_out.T, g_gate, g_up, g_down.T,
    )


def solution(mesh):
    sizes = mesh.shape
    plane_of_eight = sizes["shard"] == 4 and sizes["ctx"] == 2 and sizes["tp"] > 1
    run = functools.partial(fast_body, mesh) if plane_of_eight else body
    placed = (
        P(("shard", "ctx"), None),
        P("shard"),
        P(("shard", "ctx")),
        P(("shard", "ctx")),
        P(),
        P(),
        P(("shard", "ctx"), "tp"),
        P(("shard", "ctx"), "tp"),
        P(("shard", "ctx"), "tp"),
        P("tp", ("shard", "ctx")),
        P(("shard", "ctx"), "tp"),
        P(("shard", "ctx"), "tp"),
        P("tp", ("shard", "ctx")),
        P(("shard", "ctx"), None),
    )
    return jax.shard_map(
        run,
        mesh=mesh,
        in_specs=placed,
        out_specs=(
            P(("shard", "ctx"), None),
            P(("shard", "ctx"), None),
            P(("shard", "ctx")),
            P(("shard", "ctx")),
            P(),
            P(),
            P(("shard", "ctx"), "tp"),
            P(("shard", "ctx"), "tp"),
            P(("shard", "ctx"), "tp"),
            P("tp", ("shard", "ctx")),
            P(("shard", "ctx"), "tp"),
            P(("shard", "ctx"), "tp"),
            P("tp", ("shard", "ctx")),
        ),
        check_vma=False,
    )
```

```python
import functools
import math

import jax
import jax.numpy as jnp
import numpy as np
from jax import lax
from jax.experimental import pallas as pl
from jax.experimental.pallas import tpu as pltpu
from jax.sharding import PartitionSpec as P

EPSILON = 1e-05
ROPE_BASE = 1000000.0
MESH = pl.DeviceIdType.MESH
F32 = jnp.float32
BF16 = jnp.bfloat16
VMEM_LIMIT = 60 << 20


def norm_rows(value, gain):
    scale = lax.rsqrt(jnp.mean(value * value, axis=-1, keepdims=True) + EPSILON)
    return value * scale * gain


def rotate(values, positions):
    half = values.shape[-1] // 2
    freq = ROPE_BASE ** (-jnp.arange(half, dtype=jnp.float32) / half)
    angle = positions.astype(jnp.float32)[:, None] * freq[None, :]
    cosine = jnp.cos(angle)[:, None, :]
    sine = jnp.sin(angle)[:, None, :]
    first = values[..., :half]
    second = values[..., half:]
    return jnp.concatenate(
        [first * cosine - second * sine, second * cosine + first * sine], axis=-1
    )


def head_prep(proj, gain, positions):
    heads = proj.reshape(proj.shape[0], -1, gain.shape[0])
    return rotate(norm_rows(heads, gain), positions)


def activation(gate_in, up_in):
    return jax.nn.silu(gate_in) * up_in


def forward_product(left, right):
    return jnp.dot(left, right, preferred_element_type=jnp.float32)


def outer_product(left, right):
    return lax.dot_general(
        left, right, (((0,), (0,)), ((), ())), preferred_element_type=jnp.float32
    )


def back_product(grad, weight):
    return lax.dot_general(
        grad, weight, (((1,), (1,)), ((), ())), preferred_element_type=jnp.float32
    )


def body(
    hidden_in,
    seq_lengths,
    attn_gain,
    ffn_gain,
    query_gain,
    key_gain,
    w_query,
    w_key,
    w_value,
    w_out,
    w_gate,
    w_up,
    w_down,
    out_grad,
):
    rows = hidden_in.shape[0]
    head_dim = query_gain.shape[0]
    kv_heads = w_key.shape[1] // head_dim
    q_heads = w_query.shape[1] // head_dim
    group = q_heads // kv_heads
    pieces = lax.axis_size("ctx")
    scale = 1.0 / math.sqrt(head_dim)
    positions = lax.axis_index("ctx") * rows + jnp.arange(rows, dtype=jnp.int32)
    length = seq_lengths[0]
    valid = (positions < length).astype(jnp.float32)[:, None]
    live_blocks = jnp.minimum(lax.axis_index("ctx"), (length - 1) // rows) + 1
    gathered = (
        lax.all_gather(attn_gain, ("shard", "ctx"), axis=0, tiled=True),
        lax.all_gather(ffn_gain, ("shard", "ctx"), axis=0, tiled=True),
        lax.all_gather(w_query, ("shard", "ctx"), axis=0, tiled=True),
        lax.all_gather(w_key, ("shard", "ctx"), axis=0, tiled=True),
        lax.all_gather(w_value, ("shard", "ctx"), axis=0, tiled=True),
        lax.all_gather(w_gate, ("shard", "ctx"), axis=0, tiled=True),
        lax.all_gather(w_up, ("shard", "ctx"), axis=0, tiled=True),
        lax.all_gather(w_out, ("shard", "ctx"), axis=1, tiled=True),
        lax.all_gather(w_down, ("shard", "ctx"), axis=1, tiled=True),
    )
    gain_one = gathered[0].astype(jnp.float32)
    gain_two = gathered[1].astype(jnp.float32)
    full_query, full_key, full_value, full_gate, full_up, full_out, full_down = gathered[2:]
    q_gain = query_gain.astype(jnp.float32)
    k_gain = key_gain.astype(jnp.float32)
    hidden = hidden_in.astype(jnp.float32)
    normed_one = norm_rows(hidden, gain_one).astype(jnp.bfloat16)
    query_proj = forward_product(normed_one, full_query)
    key_proj = forward_product(normed_one, full_key)
    value_proj = forward_product(normed_one, full_value)
    queries = (
        head_prep(query_proj, q_gain, positions)
        .astype(jnp.bfloat16)
        .reshape(rows, kv_heads, group, head_dim)
    )
    keys_own = head_prep(key_proj, k_gain, positions).astype(jnp.bfloat16)
    values_own = value_proj.reshape(rows, kv_heads, head_dim).astype(jnp.bfloat16)
    keys_all, values_all = (
        lax.all_gather(keys_own, "ctx", axis=0, tiled=True),
        lax.all_gather(values_own, "ctx", axis=0, tiled=True),
    )
    key_blocks = keys_all.reshape(pieces, rows, kv_heads, head_dim)
    value_blocks = values_all.reshape(pieces, rows, kv_heads, head_dim)

    def key_at(index):
        return lax.dynamic_index_in_dim(key_blocks, index, 0, keepdims=False)

    def value_at(index):
        return lax.dynamic_index_in_dim(value_blocks, index, 0, keepdims=False)

    def block_scores(key_block, index):
        key_pos = index * rows + jnp.arange(rows, dtype=jnp.int32)
        mask = ((key_pos[None, :] <= positions[:, None]) & (key_pos[None, :] < length))[None, None]
        raw = (
            jnp.einsum("tkgd,skd->kgts", queries, key_block, preferred_element_type=jnp.float32)
            * scale
        )
        return (jnp.where(mask, raw, -1e30), mask)

    def stats_step(index, carry):
        top, total = carry
        masked, mask = block_scores(key_at(index), index)
        new_top = jnp.maximum(top, jnp.max(masked, axis=-1))
        weight = jnp.where(mask, jnp.exp(masked - new_top[..., None]), 0.0)
        total = total * jnp.exp(top - new_top) + jnp.sum(weight, axis=-1)
        return (new_top, total)

    start = (
        jnp.full((kv_heads, group, rows), -1e30, jnp.float32),
        jnp.zeros((kv_heads, group, rows), jnp.float32),
    )
    top, total = lax.fori_loop(0, live_blocks, stats_step, start)
    log_total = top + jnp.log(total)

    def probs_of(key_block, index):
        masked, mask = block_scores(key_block, index)
        return jnp.where(mask, jnp.exp(masked - log_total[..., None]), 0.0)

    def mix_step(index, accum):
        probs = probs_of(key_at(index), index).astype(jnp.bfloat16)
        return accum + jnp.einsum(
            "kgts,skd->tkgd", probs, value_at(index), preferred_element_type=jnp.float32
        )

    head_zeros = jnp.zeros((rows, kv_heads, group, head_dim), jnp.float32)
    mixed = lax.fori_loop(0, live_blocks, mix_step, head_zeros)
    heads_out = mixed.reshape(rows, -1).astype(jnp.bfloat16)
    attn_term = forward_product(heads_out, full_out)
    resid = hidden + lax.psum(attn_term, "tp")
    normed_two = norm_rows(resid, gain_two).astype(jnp.bfloat16)
    gate = forward_product(normed_two, full_gate)
    up = forward_product(normed_two, full_up)
    middle = activation(gate, up).astype(jnp.bfloat16)
    ffn_term = forward_product(middle, full_down)
    ffn = lax.psum(ffn_term.astype(jnp.bfloat16), "tp").astype(jnp.float32)
    block_out = (valid * (resid + ffn)).astype(jnp.bfloat16)
    grad_top = valid * out_grad.astype(jnp.float32)
    grad_low = grad_top.astype(jnp.bfloat16)
    down_wgrad = outer_product(middle, grad_low)
    mid_grad = back_product(grad_low, full_down)
    _, pull_act = jax.vjp(activation, gate, up)
    gate_float, up_float = pull_act(mid_grad)
    gate_low = gate_float.astype(jnp.bfloat16)
    up_low = up_float.astype(jnp.bfloat16)
    gate_wgrad = outer_product(normed_two, gate_low)
    up_wgrad = outer_product(normed_two, up_low)
    normed_two_part = back_product(gate_low, full_gate) + back_product(up_low, full_up)
    normed_two_grad = lax.psum(normed_two_part, "tp")
    _, pull_two = jax.vjp(norm_rows, resid, gain_two)
    resid_part, gain_two_grad = pull_two(normed_two_grad)
    resid_grad = grad_top + resid_part
    attn_low = resid_grad.astype(jnp.bfloat16)
    out_wgrad = outer_product(heads_out, attn_low)
    heads_grad = (
        back_product(attn_low, full_out)
        .astype(jnp.bfloat16)
        .reshape(rows, kv_heads, group, head_dim)
    )

    def delta_step(index, accum):
        probs = probs_of(key_at(index), index)
        prob_grad = jnp.einsum(
            "tkgd,skd->kgts", heads_grad, value_at(index), preferred_element_type=jnp.float32
        )
        return accum + jnp.sum(probs * prob_grad, axis=-1)

    delta = lax.fori_loop(
        0, live_blocks, delta_step, jnp.zeros((kv_heads, group, rows), jnp.float32)
    )

    def grad_step(index, carry):
        accum, key_store, value_store = carry
        key_block = key_at(index)
        probs = probs_of(key_block, index)
        prob_grad = jnp.einsum(
            "tkgd,skd->kgts", heads_grad, value_at(index), preferred_element_type=jnp.float32
        )
        score_grad = (probs * (prob_grad - delta[..., None])).astype(jnp.bfloat16)
        accum = (
            accum
            + jnp.einsum(
                "kgts,skd->tkgd", score_grad, key_block, preferred_element_type=jnp.float32
            )
            * scale
        )
        key_grad = (
            jnp.einsum("kgts,tkgd->skd", score_grad, queries, preferred_element_type=jnp.float32)
            * scale
        )
        value_grad = jnp.einsum(
            "kgts,tkgd->skd",
            probs.astype(jnp.bfloat16),
            heads_grad,
            preferred_element_type=jnp.float32,
        )
        key_store = lax.dynamic_update_index_in_dim(key_store, key_grad, index, 0)
        value_store = lax.dynamic_update_index_in_dim(value_store, value_grad, index, 0)
        return (accum, key_store, value_store)

    store_zeros = jnp.zeros((pieces, rows, kv_heads, head_dim), jnp.float32)
    query_grad, key_grads, value_grads = lax.fori_loop(
        0, live_blocks, grad_step, (head_zeros, store_zeros, store_zeros)
    )
    key_grad_own, value_grad_own = (
        lax.psum_scatter(
            key_grads.reshape(pieces * rows, kv_heads, head_dim),
            "ctx",
            scatter_dimension=0,
            tiled=True,
        ),
        lax.psum_scatter(
            value_grads.reshape(pieces * rows, kv_heads, head_dim),
            "ctx",
            scatter_dimension=0,
            tiled=True,
        ),
    )

    def query_prep(proj, gain):
        return head_prep(proj, gain, positions)

    _, pull_query = jax.vjp(query_prep, query_proj, q_gain)
    query_proj_grad, q_gain_grad = pull_query(query_grad.reshape(rows, q_heads, head_dim))
    _, pull_key = jax.vjp(query_prep, key_proj, k_gain)
    key_proj_grad, k_gain_grad = pull_key(key_grad_own)
    query_low = query_proj_grad.astype(jnp.bfloat16)
    key_low = key_proj_grad.astype(jnp.bfloat16)
    value_low = value_grad_own.reshape(rows, -1).astype(jnp.bfloat16)
    query_wgrad = outer_product(normed_one, query_low)
    key_wgrad = outer_product(normed_one, key_low)
    value_wgrad = outer_product(normed_one, value_low)
    normed_one_part = (
        back_product(query_low, full_query)
        + back_product(key_low, full_key)
        + back_product(value_low, full_value)
    )
    normed_one_grad = lax.psum(normed_one_part, "tp")
    _, pull_one = jax.vjp(norm_rows, hidden, gain_one)
    hidden_part, gain_one_grad = pull_one(normed_one_grad)
    input_grad = resid_grad + hidden_part
    head_sums = lax.psum((q_gain_grad, k_gain_grad), ("shard", "ctx", "tp"))
    summed = (
        lax.psum_scatter(gain_one_grad, ("shard", "ctx"), scatter_dimension=0, tiled=True),
        lax.psum_scatter(gain_two_grad, ("shard", "ctx"), scatter_dimension=0, tiled=True),
        lax.psum_scatter(query_wgrad, ("shard", "ctx"), scatter_dimension=0, tiled=True),
        lax.psum_scatter(key_wgrad, ("shard", "ctx"), scatter_dimension=0, tiled=True),
        lax.psum_scatter(value_wgrad, ("shard", "ctx"), scatter_dimension=0, tiled=True),
        lax.psum_scatter(gate_wgrad, ("shard", "ctx"), scatter_dimension=0, tiled=True),
        lax.psum_scatter(up_wgrad, ("shard", "ctx"), scatter_dimension=0, tiled=True),
        lax.psum_scatter(out_wgrad, ("shard", "ctx"), scatter_dimension=1, tiled=True),
        lax.psum_scatter(down_wgrad, ("shard", "ctx"), scatter_dimension=1, tiled=True),
    )
    (
        gain_one_out,
        gain_two_out,
        query_out,
        key_out,
        value_out,
        gate_out,
        up_out,
        out_out,
        down_out,
    ) = summed
    return (
        block_out,
        input_grad,
        gain_one_out,
        gain_two_out,
        head_sums[0],
        head_sums[1],
        query_out,
        key_out,
        value_out,
        out_out,
        gate_out,
        up_out,
        down_out,
    )


def remote(src, dst, send, recv, dev):
    return pltpu.make_async_remote_copy(
        src_ref=src,
        dst_ref=dst,
        send_sem=send,
        recv_sem=recv,
        device_id=dev,
        device_id_type=MESH,
    )


def mm(a, b):
    return jnp.dot(a, b, preferred_element_type=F32)


def mm_nt(a, b):
    return lax.dot_general(a, b, (((1,), (1,)), ((), ())), preferred_element_type=F32)


def round_up(units):
    return -(-units // 256) * 256


class Place:
    def __init__(self, n_shard, n_tp):
        s = lax.axis_index("shard")
        c = lax.axis_index("ctx")
        t = lax.axis_index("tp")
        self.s, self.c, self.t = s, c, t
        self.core = lax.rem(s, 2)
        sib = s + 1 - 2 * self.core
        far = lax.rem(s + 2, n_shard)
        far_sib = far + 1 - 2 * self.core
        self.sib = (sib, c, t)
        self.x = (s, 1 - c, t)
        self.y = (far, c, t)
        first = 1 - self.core
        self.relay = (
            first * s + self.core * far,
            first * (1 - c) + self.core * c,
            t,
        )
        slot = lambda a, b: a * 2 + b
        self.own = slot(s, c)
        self.slots = {
            "S": slot(sib, c),
            "X": slot(s, 1 - c),
            "Y": slot(far, c),
            "D": slot(far, 1 - c),
            "SX": slot(sib, 1 - c),
            "SY": slot(far_sib, c),
            "SD": slot(far_sib, 1 - c),
        }
        self.relayed = first * self.slots["Y"] + self.core * self.slots["X"]
        self.n_tp = n_tp

    def z(self, t):
        return (self.s, self.c, t)

    def greet(self):
        peers = [self.sib, self.x, self.y]
        peers += [
            self.z(lax.rem(self.t + d, self.n_tp)) for d in range(1, self.n_tp)
        ]
        barrier = pltpu.get_barrier_semaphore()
        for peer in peers:
            pl.semaphore_signal(barrier, inc=1, device_id=peer, device_id_type=MESH)
        pl.semaphore_wait(barrier, len(peers))


ROLES = ("S", "X", "Y", "D", "SX", "SY", "SD")


class Gather:
    def __init__(self, at, own, full, send, recv, index, stride=0, first=0):
        self.at, self.own, self.full = at, own, full
        self.send, self.recv, self.index = send, recv, index
        self.rows, self.first = own.shape[0], first
        self.stride = stride or self.rows

    def block(self, slot):
        start = slot * self.stride + self.first
        return self.full.at[pl.ds(pl.multiple_of(start, self.rows), self.rows)]

    def copy(self, role, src, slot, dev):
        k = ROLES.index(role)
        return remote(
            src,
            self.block(slot),
            self.send.at[self.index, k],
            self.recv.at[self.index, k],
            dev,
        )

    def arrived(self, role):
        slot = self.at.slots[role]
        self.copy(role, self.block(slot), slot, self.at.sib).wait_recv()

    def start_x(self):
        self.copy("X", self.own, self.at.own, self.at.x).start()

    def start_y(self):
        self.copy("Y", self.own, self.at.own, self.at.y).start()

    def start_s(self):
        self.copy("S", self.own, self.at.own, self.at.sib).start()

    def start(self):
        self.start_x()
        self.start_y()
        self.start_s()

    def relay(self):
        at = self.at
        self.arrived("X")
        self.arrived("Y")
        self.copy("D", self.block(at.relayed), at.relayed, at.relay).start()
        for role in ("X", "Y"):
            slot = at.slots[role]
            self.copy("S" + role, self.block(slot), slot, at.sib).start()

    def relay_last(self):
        self.arrived("D")
        slot = self.at.slots["D"]
        self.copy("SD", self.block(slot), slot, self.at.sib).start()

    def finish(self):
        for role in ("S", "SX", "SY", "SD"):
            self.arrived(role)
        for role in ROLES:
            self.copy(role, self.own, self.at.own, self.at.sib).wait_send()


def column(row_ref, n):
    wide = jnp.broadcast_to(row_ref[...].astype(F32), (8, n))
    return wide.T[:, 0:1]


def kernel_a(
    shape,
    length_ref,
    hid_ref,
    gain_one_ref,
    gain_two_ref,
    q_gain_ref,
    k_gain_ref,
    wq_ref,
    wk_ref,
    wv_ref,
    wo_ref,
    wg_ref,
    wu_ref,
    wd_ref,
    cos_ref,
    sin_ref,
    wqkv_full,
    wo_full,
    wg_full,
    wu_full,
    wd_full,
    heads_all,
    q_t,
    kv_all,
    inv_den,
    proj_t,
    resid,
    h2,
    act_out,
    s_qkv,
    s_woz,
    s_wg,
    s_wu,
    s_wd,
    wg,
    wu,
    act,
    h1,
    k_own,
    k_off,
    v_own,
    v_off,
    acc,
    g_send,
    g_recv,
    z_send,
    z_recv,
    h_send,
    h_recv,
    kv_sem,
    loc_sem,
    act_sem,
):
    n_shard, n_tp, hd = shape
    at = Place(n_shard, n_tp)
    c, t = at.c, at.t
    rows, width = hid_ref.shape
    q_cols, kv_cols = wq_ref.shape[1], wk_ref.shape[1]
    q_heads, kv_heads = q_cols // hd, kv_cols // hd
    group = q_heads // kv_heads
    half = hd // 2
    at.greet()

    col_one = column(gain_one_ref, gain_one_ref.shape[1])
    s_qkv[:, 0:q_cols] = (wq_ref[...].astype(F32) * col_one).astype(BF16)
    s_qkv[:, q_cols : q_cols + kv_cols] = (wk_ref[...].astype(F32) * col_one).astype(BF16)
    s_qkv[:, q_cols + kv_cols :] = (wv_ref[...].astype(F32) * col_one).astype(BF16)
    qkv = Gather(at, s_qkv, wqkv_full, g_send, g_recv, 0)
    out = Gather(at, s_woz, wo_full, g_send, g_recv, 1)
    gate = Gather(at, s_wg, wg_full, g_send, g_recv, 2)
    up = Gather(at, s_wu, wu_full, g_send, g_recv, 3)
    down = Gather(at, s_wd, wd_full, g_send, g_recv, 4)
    gathers = (qkv, out, gate, up, down)
    local = [
        pltpu.make_async_copy(g.own, g.block(at.own), loc_sem.at[i])
        for i, g in enumerate(gathers)
    ]
    loads = [
        pltpu.make_async_copy(wg_full, wg, loc_sem.at[5]),
        pltpu.make_async_copy(wu_full, wu, loc_sem.at[6]),
    ]
    qkv.start()
    local[0].start()

    wo_cols = pl.ds(pl.multiple_of(t * q_cols, q_cols), q_cols)
    s_woz[:, wo_cols] = wo_ref[...]

    def wo_part(d, owner):
        cols = pl.ds(pl.multiple_of(owner * q_cols, q_cols), q_cols)
        return remote(
            s_woz.at[:, cols],
            s_woz.at[:, cols],
            z_send.at[d],
            z_recv.at[d],
            at.z(lax.rem(t + d + 1, n_tp)),
        )

    for d in range(n_tp - 1):
        wo_part(d, t).start()

    def norm_one(i, _):
        r = pl.ds(pl.multiple_of(i * 64, 64), 64)
        x = hid_ref[r, :].astype(F32)
        scale = lax.rsqrt(jnp.mean(x * x, axis=-1, keepdims=True) + EPSILON)
        h1[r, :] = (x * scale).astype(BF16)
        return 0

    lax.fori_loop(0, rows // 64, norm_one, 0)
    qkv.relay()
    col_two = column(gain_two_ref, gain_two_ref.shape[1])
    units = wg_ref.shape[1]
    for src, dst in ((wg_ref, s_wg), (wu_ref, s_wu)):
        dst[:, 0:units] = (src[...].astype(F32) * col_two).astype(BF16)
        dst[:, units:] = jnp.zeros((dst.shape[0], dst.shape[1] - units), BF16)
    s_wd[:, 0:units] = wd_ref[...]
    s_wd[:, units:] = jnp.zeros((s_wd.shape[0], s_wd.shape[1] - units), BF16)
    qkv.relay_last()
    for d in range(n_tp - 1):
        wo_part(d, lax.rem(t + n_tp - d - 1, n_tp)).wait_recv()
    out.start()
    gate.start_y()
    local[0].wait()
    for cp in local[1:]:
        cp.start()
    qkv.finish()

    def project(i, _):
        r = pl.ds(pl.multiple_of(i * 256, 256), 256)
        proj_t[:, r] = mm(h1[r, :], wqkv_full[...]).T
        return 0

    lax.fori_loop(0, rows // 256, project, 0)
    here = pl.ds(pl.multiple_of(c * rows, rows), rows)
    k_gain = column(k_gain_ref, hd)
    q_gain = column(q_gain_ref, hd)

    def prepared(row, gain, factor):
        x = proj_t[pl.ds(pl.multiple_of(row, hd), hd), :]
        scale = lax.rsqrt(jnp.mean(x * x, axis=0, keepdims=True) + EPSILON)
        y = x * (scale * factor) * gain
        a, b = y[:half], y[half:]
        cosine, sine = cos_ref[:, here], sin_ref[:, here]
        return jnp.concatenate([a * cosine - b * sine, b * cosine + a * sine], axis=0)

    for g in range(kv_heads):
        key = prepared(q_cols + g * hd, k_gain, 1.0).astype(BF16)
        kv_all[c, g * hd : (g + 1) * hd, :] = key
    kv_all[c, kv_cols:, :] = proj_t[q_cols + kv_cols :, :].astype(BF16)
    kv_copy = remote(kv_all.at[c], kv_all.at[c], kv_sem.at[0], kv_sem.at[1], at.x)
    kv_back = remote(
        kv_all.at[1 - c], kv_all.at[1 - c], kv_sem.at[0], kv_sem.at[1], at.x
    )

    @pl.when(c == 0)
    def _():
        kv_copy.start()

    gate.start_x()
    gate.start_s()

    def prep_q(h, _):
        r = pl.multiple_of(h * hd, hd)
        q_t[pl.ds(r, hd), :] = prepared(r, q_gain, 1.0 / math.sqrt(hd)).astype(BF16)
        return 0

    lax.fori_loop(0, q_heads, prep_q, 0)
    length = length_ref[0]

    def load_block(index, k_nat, v_ext):
        pos = index * rows + lax.broadcasted_iota(jnp.int32, (1, rows), 1)
        live = (pos < length).astype(F32)
        first = (lax.broadcasted_iota(jnp.int32, (16, rows), 0) == 0).astype(F32)
        for g in range(kv_heads):
            k_nat[g] = kv_all[index, g * hd : (g + 1) * hd, :].astype(F32).T.astype(BF16)
            v = kv_all[index, kv_cols + g * hd : kv_cols + (g + 1) * hd, :].astype(F32)
            v_ext[g, 0:hd, :] = (v * live).astype(BF16)
            v_ext[g, hd:, :] = (first * live).astype(BF16)

    load_block(c, k_own, v_own)
    below = lax.broadcasted_iota(jnp.int32, (256, 256), 0) <= lax.broadcasted_iota(
        jnp.int32, (256, 256), 1
    )

    def own_block(h, _):
        g = h // group
        qh = q_t[pl.ds(pl.multiple_of(h * hd, hd), hd), :]
        for i in range(rows // 256):
            qi = qh[:, i * 256 : (i + 1) * 256]
            top = i * 256
            e = jnp.exp(mm(k_own[g, top : top + 256, :], qi))
            e = jnp.where(below, e, 0.0).astype(BF16)
            total = mm(v_own[g, :, top : top + 256], e)
            if i:
                e = jnp.exp(mm(k_own[g, 0:top, :], qi)).astype(BF16)
                total += mm(v_own[g, :, 0:top], e)
            acc[h, :, top : top + 256] = total
        return 0

    lax.fori_loop(0, q_heads, own_block, 0)
    out.relay()
    up.start()

    @pl.when(c == 1)
    def _():
        kv_back.wait_recv()
        load_block(1 - c, k_off, v_off)

        def other_block(h, _):
            g = h // group
            qh = q_t[pl.ds(pl.multiple_of(h * hd, hd), hd), :]
            for i in range(rows // 256):
                cols = slice(i * 256, (i + 1) * 256)
                e = jnp.exp(mm(k_off[g], qh[:, cols])).astype(BF16)
                acc[h, :, cols] += mm(v_off[g], e)
            return 0

        lax.fori_loop(0, q_heads, other_block, 0)

    def chunk_cols(owner, j):
        return pl.ds(pl.multiple_of(owner * q_cols + j * 128, 128), 128)

    def along(owner, j, way):
        ref = heads_all.at[:, chunk_cols(owner, j)]
        dev = at.z(jnp.minimum(t + 1, n_tp - 1) if way == 0 else jnp.maximum(t - 1, 0))
        return remote(ref, ref, h_send.at[way, owner, j], h_recv.at[way, owner, j], dev)

    chunks = q_cols // 128

    def pass_on(owner, j, way):
        @pl.when(t < n_tp - 1 if way == 0 else t > 0)
        def _():
            along(owner, j, way).start()

    for j in range(chunks):
        parts = []
        for h in range(2 * j, 2 * j + 2):
            inverse = 1.0 / acc[h, hd : hd + 1, :]
            inv_den[h : h + 1, :] = inverse
            parts.append(acc[h, 0:hd, :] * inverse)
        pair = jnp.concatenate(parts, axis=0)
        heads_all[:, chunk_cols(t, j)] = pair.T.astype(BF16)
        for way in (0, 1):
            pass_on(t, j, way)
    inv_den[q_heads:, :] = jnp.zeros((8 - q_heads, rows), F32)

    for d in range(1, n_tp):
        for j in range(chunks):

            @pl.when(t >= d)
            def _():
                along(t - d, j, 0).wait_recv()
                pass_on(t - d, j, 0)

            @pl.when(t + d < n_tp)
            def _():
                along(t + d, j, 1).wait_recv()
                pass_on(t + d, j, 1)

            step = (d - 1) * chunks + j
            if step == 2:
                gate.relay()
            if step == 4:
                out.relay_last()
            if step == 7:
                up.relay()
                down.start()

    out.finish()
    local[1].wait()

    def residual(i, _):
        r = pl.ds(pl.multiple_of(i * 128, 128), 128)
        x = hid_ref[r, :].astype(F32) + mm_nt(heads_all[r, :], wo_full[...])
        resid[r, :] = x
        scale = lax.rsqrt(jnp.mean(x * x, axis=-1, keepdims=True) + EPSILON)
        h2[r, :] = (x * scale).astype(BF16)

        @pl.when(i == 1)
        def _():
            gate.relay_last()

        @pl.when(i == 3)
        def _():
            gate.finish()
            local[2].wait()
            loads[0].start()

        return 0

    lax.fori_loop(0, rows // 128, residual, 0)
    up.relay_last()
    up.finish()
    local[3].wait()
    loads[1].start()
    loads[0].wait()
    loads[1].wait()
    tiles = act.shape[2] // 256
    half = rows // 2

    def act_copy(f):
        cols = pl.ds(pl.multiple_of(f * 256, 256), 256)
        return pltpu.make_async_copy(
            act.at[:, :, cols], act_out.at[:, :, cols], act_sem.at[f]
        )

    def gate_up(f, _):
        cols = pl.ds(pl.multiple_of(f * 256, 256), 256)
        for i in (0, 1):
            r = slice(i * half, (i + 1) * half)
            g = mm(h2[r, :], wg[:, cols])
            u = mm(h2[r, :], wu[:, cols])
            s = 1.0 / (1.0 + jnp.exp(-g))
            silu = g * s
            act[0, r, cols] = (silu * u).astype(BF16)
            act[1, r, cols] = (u * (s * (1.0 + g * (1.0 - s)))).astype(BF16)
            act[2, r, cols] = silu.astype(BF16)

        act_copy(f).start()

        @pl.when(f == tiles - 2)
        def _():
            down.relay()

        return 0

    lax.fori_loop(0, tiles, gate_up, 0)
    down.relay_last()
    down.finish()
    local[4].wait()

    def act_done(f, _):
        act_copy(f).wait()
        return 0

    lax.fori_loop(0, tiles, act_done, 0)
    for owner in range(n_tp):
        for j in range(chunks):

            @pl.when(jnp.logical_and(t < n_tp - 1, owner <= t))
            def _():
                along(owner, j, 0).wait_send()

            @pl.when(jnp.logical_and(t > 0, owner >= t))
            def _():
                along(owner, j, 1).wait_send()

    for d in range(n_tp - 1):
        wo_part(d, t).wait_send()

    @pl.when(c == 0)
    def _():
        kv_copy.wait_send()
        kv_all[1 - c] = jnp.zeros(kv_all.shape[1:], BF16)


def rope_tables(positions, hd):
    freq = ROPE_BASE ** (-np.arange(hd // 2, dtype=np.float64) / (hd // 2))
    angle = freq[:, None] * np.arange(positions, dtype=np.float64)[None, :]
    return np.cos(angle).astype(np.float32), np.sin(angle).astype(np.float32)


def call_a(mesh, args):
    (hidden_in, seq_lengths, attn_gain, ffn_gain, query_gain, key_gain,
     w_query, w_key, w_value, w_out, w_gate, w_up, w_down) = args
    n_shard, n_ctx, n_tp = mesh.shape["shard"], mesh.shape["ctx"], mesh.shape["tp"]
    rows, width = hidden_in.shape
    hd = query_gain.shape[0]
    q_cols, kv_cols = w_query.shape[1], w_key.shape[1]
    q_heads, kv_heads = q_cols // hd, kv_cols // hd
    block = w_query.shape[0]
    padded = round_up(w_gate.shape[1])
    cosine, sine = rope_tables(n_ctx * rows, hd)
    vm = pl.BlockSpec(memory_space=pltpu.VMEM)
    hbm = pl.BlockSpec(memory_space=pltpu.HBM)
    sm = pl.BlockSpec(memory_space=pltpu.SMEM)
    qkv_cols = q_cols + 2 * kv_cols
    S = jax.ShapeDtypeStruct
    dma = pltpu.SemaphoreType.DMA
    chunks = q_cols // 128
    return pl.pallas_call(
        functools.partial(kernel_a, (n_shard, n_tp, hd)),
        out_shape=(
            S((width, qkv_cols), BF16),
            S((width, n_tp * q_cols), BF16),
            S((width, padded), BF16),
            S((width, padded), BF16),
            S((width, padded), BF16),
            S((rows, n_tp * q_cols), BF16),
            S((q_cols, rows), BF16),
            S((n_ctx, 2 * kv_cols, rows), BF16),
            S((8, rows), F32),
            S((qkv_cols, rows), F32),
            S((rows, width), F32),
            S((rows, width), BF16),
            S((3, rows, padded), BF16),
        ),
        in_specs=[sm] + [vm] * 14,
        out_specs=(vm, vm, hbm, hbm, hbm, vm, vm, vm, vm, vm, vm, vm, hbm),
        scratch_shapes=[
            pltpu.VMEM((block, qkv_cols), BF16),
            pltpu.VMEM((block, n_tp * q_cols), BF16),
            pltpu.VMEM((block, padded), BF16),
            pltpu.VMEM((block, padded), BF16),
            pltpu.VMEM((block, padded), BF16),
            pltpu.VMEM((width, padded), BF16),
            pltpu.VMEM((width, padded), BF16),
            pltpu.VMEM((3, rows, padded), BF16),
            pltpu.VMEM((rows, width), BF16),
            pltpu.VMEM((kv_heads, rows, hd), BF16),
            pltpu.VMEM((kv_heads, rows, hd), BF16),
            pltpu.VMEM((kv_heads, hd + 16, rows), BF16),
            pltpu.VMEM((kv_heads, hd + 16, rows), BF16),
            pltpu.VMEM((q_heads, hd + 16, rows), F32),
            dma((5, 7)),
            dma((5, 7)),
            dma((n_tp - 1,)),
            dma((n_tp - 1,)),
            dma((2, n_tp, chunks)),
            dma((2, n_tp, chunks)),
            dma((2,)),
            dma((7,)),
            dma((padded // 256,)),
        ],
        compiler_params=pltpu.CompilerParams(
            collective_id=0, has_side_effects=True, vmem_limit_bytes=VMEM_LIMIT
        ),
    )(
        seq_lengths, hidden_in, attn_gain.reshape(1, -1), ffn_gain.reshape(1, -1),
        query_gain.reshape(1, -1), key_gain.reshape(1, -1), w_query, w_key, w_value,
        w_out.T, w_gate, w_up, w_down.T, jnp.asarray(cosine), jnp.asarray(sine),
    )


LAG = 2


class Line:
    def __init__(self, at, part, landing, send, recv, chunks):
        self.at, self.part, self.landing = at, part, landing
        self.send, self.recv, self.chunks = send, recv, chunks
        self.half = landing.shape[1]
        self.size = self.half // chunks
        self.last = at.n_tp - 1

    def pos(self, way):
        return self.at.t if way == 0 else self.last - self.at.t

    def dev(self, way, step):
        to = self.at.t + (step if way == 0 else -step)
        return self.at.z(jnp.clip(to, 0, self.last))

    def local(self, k):
        return pl.ds(pl.multiple_of(k * self.size, self.size), self.size)

    def rows(self, way, k):
        start = (1 - way) * self.half + k * self.size
        return pl.ds(pl.multiple_of(start, self.size), self.size)

    def copy(self, way, k):
        return remote(
            self.part.at[self.rows(way, k)],
            self.landing.at[way, self.local(k)],
            self.send.at[way, k],
            self.recv.at[way, k],
            self.dev(way, 1),
        )

    def reduce(self, step, final):
        for way in (0, 1):
            pos = self.pos(way)
            k = step - pos * LAG
            live = jnp.logical_and(k >= 0, k < self.chunks)

            @pl.when(jnp.logical_and(live, pos > 0))
            def _():
                self.copy(way, k).wait_recv()
                value = self.part[self.rows(way, k), :].astype(F32)
                value += self.landing[way, self.local(k), :].astype(F32)

                @pl.when(pos < self.last)
                def _():
                    self.part[self.rows(way, k), :] = value.astype(BF16)

                @pl.when(pos == self.last)
                def _():
                    final(way, k, value)

            @pl.when(jnp.logical_and(live, pos < self.last))
            def _():
                self.copy(way, k).start()

    def drain(self):
        for way in (0, 1):

            @pl.when(self.pos(way) < self.last)
            def _():
                def one(k, _):
                    self.copy(way, k).wait_send()
                    return 0

                lax.fori_loop(0, self.chunks, one, 0)


class Back:
    def __init__(self, line, whole, send, recv, source=None):
        self.line, self.whole, self.send, self.recv = line, whole, send, recv
        self.source = source

    def copy(self, way, k, first=False):
        line = self.line
        dst = self.whole.at[line.rows(way, k)]
        src = self.source.at[way, line.local(k)] if first and self.source is not None else dst
        return remote(src, dst, self.send.at[way, k], self.recv.at[way, k], line.dev(way, -1))

    def step(self, step):
        line = self.line
        for way in (0, 1):
            pos = line.pos(way)
            k = step - (line.last - pos) * LAG
            live = jnp.logical_and(k >= 0, k < line.chunks)

            @pl.when(jnp.logical_and(live, pos < line.last))
            def _():
                self.copy(way, k).wait_recv()

                @pl.when(pos > 0)
                def _():
                    self.copy(way, k).start()

            @pl.when(jnp.logical_and(live, pos == line.last))
            def _():
                self.copy(way, k, True).start()

    def drain(self):
        line = self.line
        for way in (0, 1):

            @pl.when(line.pos(way) > 0)
            def _():
                def one(k, _):
                    self.copy(way, k).wait_send()
                    return 0

                lax.fori_loop(0, line.chunks, one, 0)


class Scatter:
    def __init__(self, at, source, room, tmp_sem, send, recv, index):
        self.at, self.source, self.room = at, source, room
        self.tmp_sem, self.send, self.recv, self.index = tmp_sem, send, recv, index
        self.rows = room.shape[0] // 8
        self.tmp, self.relayed = self.land(7), self.land(4)
        self.final = (self.land(5), self.land(6))
        self.direct, self.indirect = 1 + at.core, 2 - at.core
        self.other = (
            at.core * at.x[0] + (1 - at.core) * at.y[0],
            at.core * at.x[1] + (1 - at.core) * at.y[1],
            at.t,
        )
        self.mine = [at.own] + [at.slots[n] for n in ("X", "Y", "D")]
        self.theirs = [at.slots[n] for n in ("S", "SX", "SY", "SD")]

    def land(self, j):
        return self.room.at[pl.ds(pl.multiple_of(j * self.rows, self.rows), self.rows)]

    def block(self, slot):
        return self.source.at[pl.ds(pl.multiple_of(slot * self.rows, self.rows), self.rows)]

    def copy(self, k, src, dst, dev):
        return remote(src, dst, self.send.at[self.index, k], self.recv.at[self.index, k], dev)

    def share(self, j):
        return self.copy(j, self.block(self.theirs[j]), self.land(j), self.at.sib)

    def start(self):
        for j in (3, 1, 2, 0):
            self.share(j).start()

    def slot(self, j):
        if isinstance(j, int):
            return self.mine[j]
        return jnp.where(j == 1, self.mine[1], self.mine[2])

    def arrived(self, j):
        ref = self.land(j)
        self.copy(j, ref, ref, self.at.sib).wait_recv()

    def fetch(self, j):
        return pltpu.make_async_copy(self.block(self.slot(j)), self.tmp, self.tmp_sem)

    def add(self, j, extra=()):
        self.fetch(j).start()
        self.arrived(j)
        self.fetch(j).wait()
        land = self.land(j)

        def piece(i, _):
            r = pl.ds(pl.multiple_of(i * 64, 64), 64)
            value = land[r, :].astype(F32) + self.tmp[r, :].astype(F32)
            for ref in extra:
                value += ref[r, :].astype(F32)
            land[r, :] = value.astype(BF16)
            return 0

        lax.fori_loop(0, self.rows // 64, piece, 0)

    def hop(self, k):
        at = self.at
        if k == 4:
            return self.copy(4, self.land(3), self.relayed, at.relay)
        if k == 5:
            return self.copy(5, self.land(self.direct), self.final[0], at.relay)
        return self.copy(6, self.land(self.indirect), self.final[1], self.other)

    def first(self):
        self.add(3)
        self.hop(4).start()
        self.add(self.direct)
        self.hop(5).start()

    def second(self):
        self.hop(4).wait_recv()
        self.add(self.indirect, (self.relayed,))
        self.hop(6).start()

    def finish(self, use):
        self.fetch(0).start()
        self.arrived(0)
        self.hop(5).wait_recv()
        self.hop(6).wait_recv()
        self.fetch(0).wait()
        land = self.land(0)

        def piece(i, _):
            r = pl.ds(pl.multiple_of(i * 64, 64), 64)
            value = land[r, :].astype(F32) + self.tmp[r, :].astype(F32)
            value += self.final[0][r, :].astype(F32) + self.final[1][r, :].astype(F32)
            use(r, value)
            return 0

        lax.fori_loop(0, self.rows // 64, piece, 0)

    def drain(self):
        for j in range(4):
            self.share(j).wait_send()
        for k in (4, 5, 6):
            self.hop(k).wait_send()


def kernel_b(
    shape,
    length_ref,
    og_ref,
    wd_hbm,
    act_hbm,
    wg_hbm,
    wu_hbm,
    h2_hbm,
    resid_hbm,
    attn_low,
    rg_own,
    gate_sum,
    ffn_part,
    wgrads,
    f_part,
    d_part,
    wg,
    wu,
    wd,
    resid,
    h2,
    gl,
    act,
    land_d,
    stage,
    d_send,
    d_recv,
    b_send,
    b_recv,
    s_send,
    s_recv,
    loc_sem,
    st_sem,
    free_sem,
):
    n_shard, n_tp, chunks = shape
    at = Place(n_shard, n_tp)
    rows, width = og_ref.shape
    padded = wd.shape[1]
    block = stage.shape[1]
    half = rows // 2
    tiles = padded // 256
    last = n_tp - 1
    pairs = ((wd_hbm, wd), (act_hbm, act), (wg_hbm, wg), (wu_hbm, wu), (h2_hbm, h2), (resid_hbm, resid))
    loads = [
        pltpu.make_async_copy(src, dst, loc_sem.at[i]) for i, (src, dst) in enumerate(pairs)
    ]
    for cp in loads:
        cp.start()
    at.greet()
    length = length_ref[0]

    def live_rows(start, n):
        pos = at.c * rows + start + lax.broadcasted_iota(jnp.int32, (n, 1), 0)
        return (pos < length).astype(F32)

    def mask_grad(i, _):
        start = pl.multiple_of(i * 64, 64)
        r = pl.ds(start, 64)
        gl[r, :] = (og_ref[r, :].astype(F32) * live_rows(start, 64)).astype(BF16)
        return 0

    lax.fori_loop(0, rows // 64, mask_grad, 0)
    loads[0].wait()
    loads[1].wait()

    quarter = half // 2
    lines, backs = [], []
    for n in (0, 1):
        r = pl.ds(n * half, half)
        line = Line(at, d_part.at[r], land_d.at[n], d_send.at[n], d_recv.at[n], chunks)
        lines.append(line)
        backs.append(Back(line, attn_low.at[r], b_send.at[n], b_recv.at[n]))

    def final_d2(n):
        def final(way, k, value):
            line = lines[n]
            start = n * half + (1 - way) * quarter + k * line.size
            r = pl.ds(pl.multiple_of(start, line.size), line.size)
            x = resid[r, :]
            scale = lax.rsqrt(jnp.mean(x * x, axis=-1, keepdims=True) + EPSILON)
            h = x * scale
            inner = jnp.mean(value * h, axis=-1, keepdims=True)
            grad = gl[r, :].astype(F32) + scale * (value - h * inner)
            rg_own[pl.ds(pl.multiple_of(n * quarter + k * line.size, line.size), line.size), :] = grad
            attn_low[r, :] = grad.astype(BF16)

        return final

    def move(n, step):
        lines[n].reduce(step, final_d2(n))
        backs[n].step(step - last * LAG)

    def moves(n, slot):
        for i in range(LAG):
            move(n, slot * LAG + i)

    def mid(n):
        r = slice(n * half, (n + 1) * half)

        def one(f, _):
            cols = pl.ds(pl.multiple_of(f * 256, 256), 256)
            g = mm(gl[r, :], wd[:, cols])
            act[1, r, cols] = (g * act[1, r, cols].astype(F32)).astype(BF16)
            act[2, r, cols] = (g * act[2, r, cols].astype(F32)).astype(BF16)
            if n == 1:

                @pl.when(lax.rem(f, 4) == 2)
                def _():
                    moves(0, 1 + lax.div(f, 4))

            return 0

        lax.fori_loop(0, tiles, one, 0)

    def back_part(q):
        r = slice(q * quarter, (q + 1) * quarter)
        total = mm_nt(act[1, r, :], wg[...]) + mm_nt(act[2, r, :], wu[...])
        d_part[r, :] = total.astype(BF16)

    mid(0)
    for cp in loads[2:]:
        cp.wait()
    back_part(0)
    back_part(1)
    moves(0, 0)
    mid(1)
    done = 1 + (tiles + 1) // 4
    back_part(2)
    moves(0, done)
    back_part(3)
    done = (done + 1) * LAG

    peers = (at.sib, at.x, at.y)
    for n, peer in enumerate(peers):
        pl.semaphore_signal(free_sem.at[n], inc=1, device_id=peer, device_id_type=MESH)
    gate = Scatter(at, wgrads.at[1], wg, loc_sem.at[0], s_send, s_recv, 0)

    def free(n):
        pl.semaphore_wait(free_sem.at[n], 1)

    def turn(i, _):
        r = pl.ds(pl.multiple_of(i * 128, 128), 128)
        r2 = pl.ds(pl.multiple_of(rows + i * 128, 128), 128)
        wu[:, r] = h2[r, :].T
        wu[:, r2] = gl[r, :].T
        return 0

    blocks = width // block
    per_step = -(-3 // LAG)
    count = 3 * blocks
    def weight_of(n):
        return lax.rem(lax.div(n, blocks) + 1, 3)

    def stage_copy(n):
        w, slot = lax.rem(n, blocks), lax.rem(n, 2)
        return pltpu.make_async_copy(
            stage.at[slot],
            wgrads.at[weight_of(n), pl.ds(pl.multiple_of(w * block, block), block)],
            st_sem.at[slot],
        )

    def weight_grad(n):
        a, w, slot = weight_of(n), lax.rem(n, blocks), lax.rem(n, 2)

        @pl.when(n >= 2)
        def _():
            stage_copy(n - 2).wait()

        first = pl.multiple_of(jnp.where(a == 0, rows, 0), 128)
        left = wu[pl.ds(pl.multiple_of(w * block, block), block), pl.ds(first, rows)]
        for f in range(tiles):
            cols = slice(f * 256, (f + 1) * 256)
            stage[slot, :, cols] = mm(left, act[a, :, cols]).astype(BF16)
        stage_copy(n).start()

    keeps = pltpu.make_async_copy(f_part, ffn_part, loc_sem.at[1])

    def forward_part(q):
        r = pl.ds(pl.multiple_of(q * quarter, quarter), quarter)
        total = mm_nt(act[0, r, :], wd[...])
        mine = (at.t == lax.rem(q, 2) * last).astype(F32)
        f_part[r, :] = (total + resid[r, :] * mine).astype(BF16)

    def use_gate(r, value):
        gate_sum[r, :] = value.astype(BF16)

    def start_gate():
        free(0)
        gate.start()

    def first_gate():
        free(1)
        free(2)
        gate.first()

    events = {
        3: start_gate,
        4: first_gate,
        7: gate.second,
        9: lambda: gate.finish(use_gate),
    }

    def tail(step, _):
        move(0, step + done)
        move(1, step)

        @pl.when(step == 0)
        def _():
            lax.fori_loop(0, rows // 128, turn, 0)

        for n in range(per_step):

            @pl.when(step * per_step + n < count)
            def _():
                weight_grad(step * per_step + n)

        for when, todo in events.items():

            @pl.when(step == when * LAG)
            def _():
                todo()

        @pl.when(jnp.logical_and(step >= 6 * LAG, step < 6 * LAG + 4))
        def _():
            forward_part(step - 6 * LAG)

        return 0

    steps = max(chunks + 2 * last * LAG, 9 * LAG + 1, 6 * LAG + 4, -(-count // per_step))
    lax.fori_loop(0, steps, tail, 0)
    keeps.start()
    stage_copy(count - 2).wait()
    stage_copy(count - 1).wait()
    gate.drain()
    for n in (0, 1):
        lines[n].drain()
        backs[n].drain()
    keeps.wait()


def call_b(mesh, chunks, seq_lengths, out_grad, wd_full, act, wg_full, wu_full, h2, resid):
    n_shard, n_tp = mesh.shape["shard"], mesh.shape["tp"]
    rows, width = out_grad.shape
    block = width // (n_shard * mesh.shape["ctx"])
    padded = wg_full.shape[1]
    half = rows // 2
    vm = pl.BlockSpec(memory_space=pltpu.VMEM)
    hbm = pl.BlockSpec(memory_space=pltpu.HBM)
    sm = pl.BlockSpec(memory_space=pltpu.SMEM)
    S = jax.ShapeDtypeStruct
    dma = pltpu.SemaphoreType.DMA
    return pl.pallas_call(
        functools.partial(kernel_b, (n_shard, n_tp, chunks)),
        out_shape=(
            S((rows, width), BF16),
            S((half, width), F32),
            S((block, padded), BF16),
            S((rows, width), BF16),
            S((3, width, padded), BF16),
        ),
        in_specs=[sm, vm] + [hbm] * 6,
        out_specs=(vm, vm, vm, hbm, hbm),
        scratch_shapes=[
            pltpu.VMEM((rows, width), BF16),
            pltpu.VMEM((rows, width), BF16),
            pltpu.VMEM((width, padded), BF16),
            pltpu.VMEM((width, padded), BF16),
            pltpu.VMEM((width, padded), BF16),
            pltpu.VMEM((rows, width), F32),
            pltpu.VMEM((rows, width), BF16),
            pltpu.VMEM((rows, width), BF16),
            pltpu.VMEM((3, rows, padded), BF16),
            pltpu.VMEM((2, 2, half // 2, width), BF16),
            pltpu.VMEM((2, block, padded), BF16),
            dma((2, 2, chunks)),
            dma((2, 2, chunks)),
            dma((2, 2, chunks)),
            dma((2, 2, chunks)),
            dma((1, 7)),
            dma((1, 7)),
            dma((6,)),
            dma((2,)),
            pltpu.SemaphoreType.REGULAR((3,)),
        ],
        compiler_params=pltpu.CompilerParams(
            collective_id=1, has_side_effects=True, vmem_limit_bytes=VMEM_LIMIT
        ),
    )(seq_lengths, out_grad, wd_full, act, wg_full, wu_full, h2, resid)


def kernel_c(
    shape,
    length_ref,
    attn_low,
    rg_own,
    hid_ref,
    wqkv,
    q_t,
    kv_all,
    inv_den,
    proj_t,
    gain_one_ref,
    gain_two_ref,
    q_gain_ref,
    k_gain_ref,
    wq_ref,
    wk_ref,
    wv_ref,
    wg_ref,
    wu_ref,
    cos_ref,
    sin_ref,
    gate_sum,
    ffn_hbm,
    wgrads,
    heads_hbm,
    wo_hbm,
    block_out,
    inp,
    g_query,
    g_key,
    g_value,
    g_out,
    g_up,
    g_down,
    small,
    heads_own,
    wo_own,
    hg_t,
    delta,
    k_own,
    v_own,
    kt_own,
    dq_t,
    dkv,
    dkv_send,
    dkv_land,
    gain_acc,
    dqkv,
    f_part,
    d_part,
    land_f,
    land_d,
    left_t,
    part,
    room_w,
    room_p,
    cols_acc,
    qk,
    qk_land,
    tile,
    s_send,
    s_recv,
    f_send,
    f_recv,
    d_send,
    d_recv,
    b_send,
    b_recv,
    o_send,
    o_recv,
    e_send,
    e_recv,
    t_send,
    t_recv,
    loc_sem,
):
    n_shard, n_tp, chunks, hd = shape
    at = Place(n_shard, n_tp)
    c, t = at.c, at.t
    rows, width = hid_ref.shape
    q_cols, kv_cols = wq_ref.shape[1], wk_ref.shape[1]
    q_heads, kv_heads = q_cols // hd, kv_cols // hd
    group = q_heads // kv_heads
    halfd = hd // 2
    half = rows // 2
    block = wq_ref.shape[0]
    units = wg_ref.shape[1]
    last = n_tp - 1
    own_cols = pl.ds(pl.multiple_of(t * q_cols, q_cols), q_cols)
    quarter = half // 2
    loads = [
        pltpu.make_async_copy(heads_hbm.at[:, own_cols], heads_own, loc_sem.at[0]),
        pltpu.make_async_copy(wo_hbm.at[:, own_cols], wo_own, loc_sem.at[1]),
        pltpu.make_async_copy(ffn_hbm, f_part, loc_sem.at[2]),
    ]
    for cp in loads:
        cp.start()
    at.greet()
    down, up = (
        Scatter(at, wgrads.at[k], room_w.at[i], loc_sem.at[3 + i], s_send, s_recv, i)
        for i, k in enumerate((0, 2))
    )
    rest = Scatter(at, part, room_p, loc_sem.at[5], s_send, s_recv, 2)
    down.start()
    up.start()
    f_lines, f_backs, lines, backs = [], [], [], []
    for n in (0, 1):
        r = pl.ds(n * half, half)
        line = Line(at, f_part.at[r], land_f.at[n], f_send.at[n], f_recv.at[n], chunks)
        f_lines.append(line)
        f_backs.append(Back(line, block_out.at[r], o_send.at[n], o_recv.at[n], land_f.at[n]))
        line = Line(at, d_part.at[r], land_d.at[n], d_send.at[n], d_recv.at[n], chunks)
        lines.append(line)
        backs.append(Back(line, inp.at[r], b_send.at[n], b_recv.at[n]))
    length = length_ref[0]

    def start_of(n, way, k):
        size = lines[n].size
        return pl.multiple_of(n * half + (1 - way) * quarter + k * size, size)

    def final_ffn(n):
        def final(way, k, value):
            line = f_lines[n]
            start = start_of(n, way, k)
            pos = c * rows + start + lax.broadcasted_iota(jnp.int32, (line.size, 1), 0)
            value = value * (pos < length).astype(F32)
            land_f[n, way, line.local(k), :] = value.astype(BF16)

        return final

    def move_ffn(step):
        for n in (0, 1):
            f_lines[n].reduce(step - n * chunks, final_ffn(n))
            f_backs[n].step(step - n * chunks - last * LAG)

    def moves_ffn(slot):
        for i in range(LAG):
            move_ffn(slot * LAG + i)

    def keep(n, way):
        return pltpu.make_async_copy(
            land_f.at[n, way],
            block_out.at[pl.ds(start_of(n, way, 0), quarter)],
            loc_sem.at[6 + n],
        )

    def keep_all(act):
        for way in (0, 1):

            @pl.when(t == (last if way == 0 else 0))
            def _():
                for n in (0, 1):
                    act(keep(n, way))

    for cp in loads:
        cp.wait()
    moves_ffn(0)

    def heads_grad(i, _):
        r = pl.ds(pl.multiple_of(i * 256, 256), 256)
        hg_t[:, r] = mm(attn_low[r, :], wo_own[...]).T.astype(BF16)
        return 0

    lax.fori_loop(0, rows // 256, heads_grad, 0)
    for j in range(q_cols // 128):
        cols = slice(j * 128, (j + 1) * 128)
        both = heads_own[:, cols].astype(F32).T * hg_t[cols, :].astype(F32)
        for n in range(128 // hd):
            h = j * (128 // hd) + n
            delta[h : h + 1, :] = jnp.sum(both[n * hd : (n + 1) * hd], axis=0, keepdims=True)
    moves_ffn(1)
    down.first()

    def live_keys(index):
        pos = index * rows + lax.broadcasted_iota(jnp.int32, (1, rows), 1)
        return (pos < length).astype(F32)

    def load_block(index, k_nat, v_nat, kt):
        live = live_keys(index)
        for g in range(kv_heads):
            key = kv_all[index, g * hd : (g + 1) * hd, :].astype(F32)
            k_nat[g] = key.T.astype(BF16)
            kt[g] = (key * live).astype(BF16)
            value = kv_all[index, kv_cols + g * hd : kv_cols + (g + 1) * hd, :]
            v_nat[g] = value.astype(F32).T.astype(BF16)

    below = lax.broadcasted_iota(jnp.int32, (256, 256), 0) <= lax.broadcasted_iota(
        jnp.int32, (256, 256), 1
    )

    def segment(h, g, i, lo, hi, masked, k_nat, v_nat, kt):
        cols = slice(i * 256, (i + 1) * 256)
        hr = pl.ds(pl.multiple_of(h * hd, hd), hd)
        qi, oi = q_t[hr, cols], hg_t[hr, cols]
        p = jnp.exp(mm(k_nat[g, lo:hi, :], qi)) * inv_den[pl.ds(h, 1), cols]
        if masked:
            p = jnp.where(below, p, 0.0)
        dp = mm(v_nat[g, lo:hi, :], oi)
        ds = (p * (dp - delta[pl.ds(h, 1), cols])).astype(BF16)
        dq_t[hr, cols] += mm(kt[g, :, lo:hi], ds)
        dkv[g, :, lo:hi] += mm_nt(qi, ds)
        dkv[kv_heads + g, :, lo:hi] += mm_nt(oi, p.astype(BF16))

    dq_t[...] = jnp.zeros_like(dq_t)
    dkv[...] = jnp.zeros_like(dkv)
    give = remote(dkv_send, dkv_land, e_send.at[3], e_recv.at[3], at.x)

    @pl.when(c == 1)
    def _():
        load_block(0, k_own, v_own, kt_own)

        def one(h, _):
            for i in range(rows // 256):
                segment(h, h // group, i, 0, rows, False, k_own, v_own, kt_own)

            @pl.when(lax.rem(h, 2) == 1)
            def _():
                moves_ffn(2 + lax.div(h, 2))

            return 0

        lax.fori_loop(0, q_heads, one, 0)
        live = live_keys(0)
        for n in range(2 * kv_heads):
            dkv_send[n] = (dkv[n] * live).astype(BF16)
        give.start()
        dkv[...] = jnp.zeros_like(dkv)

    @pl.when(c == 0)
    def _():
        def one(h, _):
            moves_ffn(2 + h)
            return 0

        lax.fori_loop(0, q_heads // 2, one, 0)

    up.first()
    down.second()
    load_block(c, k_own, v_own, kt_own)

    def own_block(h, _):
        for i in range(rows // 256):
            segment(h, h // group, i, i * 256, (i + 1) * 256, True, k_own, v_own, kt_own)
            if i:
                segment(h, h // group, i, 0, i * 256, False, k_own, v_own, kt_own)


        @pl.when(lax.rem(h, 2) == 1)
        def _():
            moves_ffn(2 + lax.div(q_heads, 2) + lax.div(h, 2))

        return 0

    lax.fori_loop(0, q_heads, own_block, 0)
    moved = (2 + 2 * (q_heads // 2)) * LAG
    live = live_keys(c)
    for n in range(2 * kv_heads):
        dkv[n] = dkv[n] * live

    @pl.when(c == 0)
    def _():
        give.wait_recv()
        for n in range(2 * kv_heads):
            dkv[n] += dkv_land[n].astype(F32)

    here = pl.ds(pl.multiple_of(c * rows, rows), rows)
    gain_acc[...] = jnp.zeros_like(gain_acc)

    def through(which, row, grad, gain):
        x = proj_t[pl.ds(pl.multiple_of(row, hd), hd), :]
        scale = lax.rsqrt(jnp.mean(x * x, axis=0, keepdims=True) + EPSILON)
        xh = x * scale
        cosine, sine = cos_ref[:, here], sin_ref[:, here]
        a, b = grad[:halfd], grad[halfd:]
        grad = jnp.concatenate([a * cosine + b * sine, b * cosine - a * sine], axis=0)
        gain_acc[which] += grad * xh
        grad = grad * gain
        inner = jnp.mean(grad * xh, axis=0, keepdims=True)
        return scale * (grad - xh * inner)

    q_gain, k_gain = column(q_gain_ref, hd), column(k_gain_ref, hd)
    factor = 1.0 / math.sqrt(hd)

    def query_back(h, _):
        row = pl.multiple_of(h * hd, hd)
        r = pl.ds(row, hd)
        dq_t[r, :] = through(0, row, dq_t[r, :] * factor, q_gain)
        return 0

    lax.fori_loop(0, q_heads, query_back, 0)
    dqkv[:, 0:q_cols] = dq_t[...].T.astype(BF16)
    pair = jnp.concatenate(
        [through(1, q_cols + g * hd, dkv[g], k_gain) for g in range(kv_heads)], axis=0
    )
    dqkv[:, q_cols : q_cols + kv_cols] = pair.T.astype(BF16)
    pair = jnp.concatenate([dkv[kv_heads + g] for g in range(kv_heads)], axis=0)
    dqkv[:, q_cols + kv_cols :] = pair.T.astype(BF16)
    for q in range(4):
        r = slice(q * quarter, (q + 1) * quarter)
        d_part[r, :] = mm_nt(dqkv[r, :], wqkv[...]).astype(BF16)

    def as_row(v):
        return jnp.broadcast_to(v, (v.shape[0], 128)).T[0:1, :]

    qk[...] = jnp.zeros_like(qk)
    for n in (0, 1):
        qk[0, n : n + 1, 0:hd] = as_row(jnp.sum(gain_acc[n], axis=1, keepdims=True))

    def trade(n):
        dev = (at.sib, at.x, at.y)[n]
        return remote(qk.at[n], qk_land.at[n], e_send.at[n], e_recv.at[n], dev)

    def traded(n):
        trade(n).wait_recv()
        qk[n + 1] = qk[n] + qk_land[n]

    up.second()

    def final_d1(n):
        def final(way, k, value):
            finish_rows(n, way, k, value)

        return final

    def finish_rows(n, way, k, value):
        size = lines[n].size
        r = pl.ds(start_of(n, way, k), size)
        x = hid_ref[r, :].astype(F32)
        scale = lax.rsqrt(jnp.mean(x * x, axis=-1, keepdims=True) + EPSILON)
        h = x * scale
        inner = jnp.mean(value * h, axis=-1, keepdims=True)
        grad = rg_own[pl.ds(pl.multiple_of(n * quarter + k * size, size), size), :] + scale * (value - h * inner)
        inp[r, :] = grad.astype(BF16)

    def turn_hidden(i, _):
        r = pl.ds(pl.multiple_of(i * 128, 128), 128)
        x = hid_ref[r, :].astype(F32)
        scale = lax.rsqrt(jnp.mean(x * x, axis=-1, keepdims=True) + EPSILON)
        left_t[0, :, r] = (x * scale).astype(BF16).T
        left_t[1, :, r] = attn_low[r, :].T
        return 0

    def weight_part(w, _):
        r = pl.ds(pl.multiple_of(w * block, block), block)
        part[r, 0 : dqkv.shape[1]] = mm(left_t[0, r, :], dqkv[...]).astype(BF16)
        part[r, dqkv.shape[1] :] = mm(left_t[1, r, :], heads_own[...]).astype(BF16)
        return 0

    g_one = column(gain_one_ref, block)
    g_two = column(gain_two_ref, block)
    cols_acc[0] = jnp.broadcast_to(g_one, (block, 128))
    cols_acc[1] = jnp.broadcast_to(g_two, (block, 128))

    def use_down(r, value):
        g_down[r, :] = value[:, 0:units]

    def gate_gain():
        def piece(i, _):
            r = pl.ds(pl.multiple_of(i * 64, 64), 64)
            value = gate_sum[r, 0:units].astype(F32)
            total = jnp.sum(wg_ref[r, :].astype(F32) * value, axis=1, keepdims=True)
            cols_acc[3, r, :] = jnp.broadcast_to(total, (64, 128))
            return 0

        lax.fori_loop(0, block // 64, piece, 0)

    def use_up(r, value):
        value = value[:, 0:units]
        total = jnp.sum(wu_ref[r, :].astype(F32) * value, axis=1, keepdims=True)
        cols_acc[3, r, :] += jnp.broadcast_to(total, (64, 128))
        g_up[r, :] = value * cols_acc[1, r, 0:1]

    def use_rest(r, value):
        gain = cols_acc[0, r, 0:1]
        vq = value[:, 0:q_cols]
        vk = value[:, q_cols : q_cols + kv_cols]
        vv = value[:, q_cols + kv_cols : q_cols + 2 * kv_cols]
        total = jnp.sum(wq_ref[r, :].astype(F32) * vq, axis=1, keepdims=True)
        total += jnp.sum(wk_ref[r, :].astype(F32) * vk, axis=1, keepdims=True)
        total += jnp.sum(wv_ref[r, :].astype(F32) * vv, axis=1, keepdims=True)
        cols_acc[2, r, :] = jnp.broadcast_to(total, (64, 128))
        g_query[r, :] = vq * gain
        g_key[r, :] = vk * gain
        g_value[r, :] = vv * gain
        g_out[r, :] = value[:, q_cols + 2 * kv_cols :]

    def turn_all():
        lax.fori_loop(0, rows // 128, turn_hidden, 0)

    def parts():
        lax.fori_loop(0, width // block, weight_part, 0)
        rest.start()

    events = {
        0: (lambda: trade(0).start(), turn_all),
        1: (parts, lambda: traded(0), lambda: trade(1).start()),
        2: (lambda: traded(1), lambda: trade(2).start(), gate_gain),
        3: (rest.first, lambda: traded(2)),
        5: (lambda: down.finish(use_down),),
        6: (rest.second,),
        8: (lambda: up.finish(use_up),),
        10: (lambda: rest.finish(use_rest),),
    }

    def tail(step, _):
        for n in (0, 1):
            lines[n].reduce(step - n * chunks, final_d1(n))
            backs[n].step(step - n * chunks - last * LAG)
        move_ffn(step + moved)
        for when, todo in events.items():

            @pl.when(step == when * LAG)
            def _():
                for thing in todo:
                    thing()

        return 0

    lax.fori_loop(0, max(2 * chunks + 2 * last * LAG, 10 * LAG + 1), tail, 0)
    keep_all(lambda cp: cp.start())

    def give_tile(d, owner):
        return remote(
            tile.at[owner], tile.at[owner], t_send.at[d], t_recv.at[d],
            at.z(lax.rem(t + d + 1, n_tp)),
        )

    tile[t] = jnp.zeros(tile.shape[1:], F32)
    tile[t, 0:1, 0:block] = cols_acc[2].T[0:1, :]
    tile[t, 1:2, 0:block] = cols_acc[3].T[0:1, :]
    tile[t, 2:4, 0:128] = qk[3, 0:2, :]
    for d in range(n_tp - 1):
        give_tile(d, t).start()
    for w in (down, up, rest):
        w.drain()
    for n in (0, 1):
        lines[n].drain()
        backs[n].drain()
        f_lines[n].drain()
        f_backs[n].drain()
    keep_all(lambda cp: cp.wait())

    @pl.when(c == 1)
    def _():
        give.wait_send()

    for n in range(3):
        trade(n).wait_send()
    for d in range(n_tp - 1):
        give_tile(d, lax.rem(t + n_tp - d - 1, n_tp)).wait_recv()
    total = tile[0]
    for n in range(1, n_tp):
        total = total + tile[n]
    small[...] = total
    for d in range(n_tp - 1):
        give_tile(d, t).wait_send()


def call_c(mesh, chunks, args, kept):
    (hidden_in, seq_lengths, attn_gain, ffn_gain, query_gain, key_gain,
     w_query, w_key, w_value, w_gate, w_up) = args
    (attn_low, rg_own, gate_sum, ffn_part, wgrads, wqkv_full, wo_full, heads_all, q_t, kv_all, inv_den,
     proj_t) = kept
    n_shard, n_ctx, n_tp = mesh.shape["shard"], mesh.shape["ctx"], mesh.shape["tp"]
    rows, width = hidden_in.shape
    quarter = rows // 4
    hd = query_gain.shape[0]
    q_cols, kv_cols = w_query.shape[1], w_key.shape[1]
    qkv_cols = q_cols + 2 * kv_cols
    kv_heads = kv_cols // hd
    block, units = w_gate.shape
    padded = wgrads.shape[2]
    cosine, sine = rope_tables(n_ctx * rows, hd)
    vm = pl.BlockSpec(memory_space=pltpu.VMEM)
    hbm = pl.BlockSpec(memory_space=pltpu.HBM)
    sm = pl.BlockSpec(memory_space=pltpu.SMEM)
    S = jax.ShapeDtypeStruct
    V = pltpu.VMEM
    dma = pltpu.SemaphoreType.DMA
    return pl.pallas_call(
        functools.partial(kernel_c, (n_shard, n_tp, chunks, hd)),
        out_shape=(
            S((rows, width), BF16),
            S((rows, width), BF16),
            S((block, q_cols), F32),
            S((block, kv_cols), F32),
            S((block, kv_cols), F32),
            S((block, q_cols), F32),
            S((block, units), F32),
            S((block, units), F32),
            S((8, 256), F32),
        ),
        in_specs=[sm] + [vm] * 20 + [hbm] * 4,
        out_specs=(hbm,) + (vm,) * 8,
        scratch_shapes=[
            V((rows, q_cols), BF16),
            V((width, q_cols), BF16),
            V((q_cols, rows), BF16),
            V((8, rows), F32),
            V((kv_heads, rows, hd), BF16),
            V((kv_heads, rows, hd), BF16),
            V((kv_heads, hd, rows), BF16),
            V((q_cols, rows), F32),
            V((2 * kv_heads, hd, rows), F32),
            V((2 * kv_heads, hd, rows), BF16),
            V((2 * kv_heads, hd, rows), BF16),
            V((2, hd, rows), F32),
            V((rows, qkv_cols), BF16),
            V((rows, width), BF16),
            V((rows, width), BF16),
            V((2, 2, quarter, width), BF16),
            V((2, 2, quarter, width), BF16),
            V((2, width, rows), BF16),
            V((width, qkv_cols + q_cols), BF16),
            V((2, 8 * block, padded), BF16),
            V((8 * block, qkv_cols + q_cols), BF16),
            V((4, block, 128), F32),
            V((4, 8, 128), F32),
            V((3, 8, 128), F32),
            V((n_tp, 8, 256), F32),
            dma((3, 7)),
            dma((3, 7)),
            dma((2, 2, chunks)),
            dma((2, 2, chunks)),
            dma((2, 2, chunks)),
            dma((2, 2, chunks)),
            dma((2, 2, chunks)),
            dma((2, 2, chunks)),
            dma((2, 2, chunks)),
            dma((2, 2, chunks)),
            dma((4,)),
            dma((4,)),
            dma((n_tp - 1,)),
            dma((n_tp - 1,)),
            dma((8,)),
        ],
        compiler_params=pltpu.CompilerParams(
            collective_id=2, has_side_effects=True, vmem_limit_bytes=VMEM_LIMIT
        ),
    )(
        seq_lengths, attn_low, rg_own, hidden_in, wqkv_full, q_t, kv_all, inv_den, proj_t,
        attn_gain.reshape(1, -1), ffn_gain.reshape(1, -1), query_gain.reshape(1, -1),
        key_gain.reshape(1, -1), w_query, w_key, w_value, w_gate, w_up,
        jnp.asarray(cosine), jnp.asarray(sine), gate_sum, ffn_part, wgrads, heads_all, wo_full,
    )


CHUNKS = 6


def fast_body(mesh, *args):
    (hidden_in, seq_lengths, attn_gain, ffn_gain, query_gain, key_gain,
     w_query, w_key, w_value, w_out, w_gate, w_up, w_down, out_grad) = args
    (wqkv_full, wo_full, wg_full, wu_full, wd_full, heads_all, q_t, kv_all, inv_den, proj_t,
     resid, h2, act) = call_a(mesh, args[:13])
    attn_low, rg_own, gate_sum, ffn_part, wgrads = call_b(
        mesh, CHUNKS, seq_lengths, out_grad, wd_full, act, wg_full, wu_full, h2, resid
    )
    (block_out, inp, g_query, g_key, g_value, g_out, g_up, g_down, small) = call_c(
        mesh, CHUNKS,
        (hidden_in, seq_lengths, attn_gain, ffn_gain, query_gain, key_gain, w_query, w_key,
         w_value, w_gate, w_up),
        (attn_low, rg_own, gate_sum, ffn_part, wgrads, wqkv_full, wo_full, heads_all, q_t, kv_all, inv_den,
         proj_t),
    )
    block, hd = w_query.shape[0], query_gain.shape[0]
    g_gate = gate_sum[:, : w_gate.shape[1]].astype(F32) * ffn_gain.astype(F32)[:, None]
    return (
        block_out, inp.astype(F32), small[0, :block], small[1, :block], small[2, :hd],
        small[3, :hd], g_query, g_key, g_value, g_out.T, g_gate, g_up, g_down.T,
    )


def solution(mesh):
    sizes = mesh.shape
    plane_of_eight = sizes["shard"] == 4 and sizes["ctx"] == 2 and sizes["tp"] > 1
    run = functools.partial(fast_body, mesh) if plane_of_eight else body
    placed = (
        P(("shard", "ctx"), None),
        P("shard"),
        P(("shard", "ctx")),
        P(("shard", "ctx")),
        P(),
        P(),
        P(("shard", "ctx"), "tp"),
        P(("shard", "ctx"), "tp"),
        P(("shard", "ctx"), "tp"),
        P("tp", ("shard", "ctx")),
        P(("shard", "ctx"), "tp"),
        P(("shard", "ctx"), "tp"),
        P("tp", ("shard", "ctx")),
        P(("shard", "ctx"), None),
    )
    return jax.shard_map(
        run,
        mesh=mesh,
        in_specs=placed,
        out_specs=(
            P(("shard", "ctx"), None),
            P(("shard", "ctx"), None),
            P(("shard", "ctx")),
            P(("shard", "ctx")),
            P(),
            P(),
            P(("shard", "ctx"), "tp"),
            P(("shard", "ctx"), "tp"),
            P(("shard", "ctx"), "tp"),
            P("tp", ("shard", "ctx")),
            P(("shard", "ctx"), "tp"),
            P(("shard", "ctx"), "tp"),
            P("tp", ("shard", "ctx")),
        ),
        check_vma=False,
    )
```

```python
import functools
import math

import jax
import jax.numpy as jnp
import numpy as np
from jax import lax
from jax.experimental import pallas as pl
from jax.experimental.pallas import tpu as pltpu
from jax.sharding import PartitionSpec as P

EPSILON = 1e-05
ROPE_BASE = 1000000.0
MESH = pl.DeviceIdType.MESH
F32 = jnp.float32
BF16 = jnp.bfloat16
VMEM_LIMIT = 60 << 20


def norm_rows(value, gain):
    scale = lax.rsqrt(jnp.mean(value * value, axis=-1, keepdims=True) + EPSILON)
    return value * scale * gain


def rotate(values, positions):
    half = values.shape[-1] // 2
    freq = ROPE_BASE ** (-jnp.arange(half, dtype=jnp.float32) / half)
    angle = positions.astype(jnp.float32)[:, None] * freq[None, :]
    cosine = jnp.cos(angle)[:, None, :]
    sine = jnp.sin(angle)[:, None, :]
    first = values[..., :half]
    second = values[..., half:]
    return jnp.concatenate(
        [first * cosine - second * sine, second * cosine + first * sine], axis=-1
    )


def head_prep(proj, gain, positions):
    heads = proj.reshape(proj.shape[0], -1, gain.shape[0])
    return rotate(norm_rows(heads, gain), positions)


def activation(gate_in, up_in):
    return jax.nn.silu(gate_in) * up_in


def forward_product(left, right):
    return jnp.dot(left, right, preferred_element_type=jnp.float32)


def outer_product(left, right):
    return lax.dot_general(
        left, right, (((0,), (0,)), ((), ())), preferred_element_type=jnp.float32
    )


def back_product(grad, weight):
    return lax.dot_general(
        grad, weight, (((1,), (1,)), ((), ())), preferred_element_type=jnp.float32
    )


def body(
    hidden_in,
    seq_lengths,
    attn_gain,
    ffn_gain,
    query_gain,
    key_gain,
    w_query,
    w_key,
    w_value,
    w_out,
    w_gate,
    w_up,
    w_down,
    out_grad,
):
    rows = hidden_in.shape[0]
    head_dim = query_gain.shape[0]
    kv_heads = w_key.shape[1] // head_dim
    q_heads = w_query.shape[1] // head_dim
    group = q_heads // kv_heads
    pieces = lax.axis_size("ctx")
    scale = 1.0 / math.sqrt(head_dim)
    positions = lax.axis_index("ctx") * rows + jnp.arange(rows, dtype=jnp.int32)
    length = seq_lengths[0]
    valid = (positions < length).astype(jnp.float32)[:, None]
    live_blocks = jnp.minimum(lax.axis_index("ctx"), (length - 1) // rows) + 1
    gathered = (
        lax.all_gather(attn_gain, ("shard", "ctx"), axis=0, tiled=True),
        lax.all_gather(ffn_gain, ("shard", "ctx"), axis=0, tiled=True),
        lax.all_gather(w_query, ("shard", "ctx"), axis=0, tiled=True),
        lax.all_gather(w_key, ("shard", "ctx"), axis=0, tiled=True),
        lax.all_gather(w_value, ("shard", "ctx"), axis=0, tiled=True),
        lax.all_gather(w_gate, ("shard", "ctx"), axis=0, tiled=True),
        lax.all_gather(w_up, ("shard", "ctx"), axis=0, tiled=True),
        lax.all_gather(w_out, ("shard", "ctx"), axis=1, tiled=True),
        lax.all_gather(w_down, ("shard", "ctx"), axis=1, tiled=True),
    )
    gain_one = gathered[0].astype(jnp.float32)
    gain_two = gathered[1].astype(jnp.float32)
    full_query, full_key, full_value, full_gate, full_up, full_out, full_down = gathered[2:]
    q_gain = query_gain.astype(jnp.float32)
    k_gain = key_gain.astype(jnp.float32)
    hidden = hidden_in.astype(jnp.float32)
    normed_one = norm_rows(hidden, gain_one).astype(jnp.bfloat16)
    query_proj = forward_product(normed_one, full_query)
    key_proj = forward_product(normed_one, full_key)
    value_proj = forward_product(normed_one, full_value)
    queries = (
        head_prep(query_proj, q_gain, positions)
        .astype(jnp.bfloat16)
        .reshape(rows, kv_heads, group, head_dim)
    )
    keys_own = head_prep(key_proj, k_gain, positions).astype(jnp.bfloat16)
    values_own = value_proj.reshape(rows, kv_heads, head_dim).astype(jnp.bfloat16)
    keys_all, values_all = (
        lax.all_gather(keys_own, "ctx", axis=0, tiled=True),
        lax.all_gather(values_own, "ctx", axis=0, tiled=True),
    )
    key_blocks = keys_all.reshape(pieces, rows, kv_heads, head_dim)
    value_blocks = values_all.reshape(pieces, rows, kv_heads, head_dim)

    def key_at(index):
        return lax.dynamic_index_in_dim(key_blocks, index, 0, keepdims=False)

    def value_at(index):
        return lax.dynamic_index_in_dim(value_blocks, index, 0, keepdims=False)

    def block_scores(key_block, index):
        key_pos = index * rows + jnp.arange(rows, dtype=jnp.int32)
        mask = ((key_pos[None, :] <= positions[:, None]) & (key_pos[None, :] < length))[None, None]
        raw = (
            jnp.einsum("tkgd,skd->kgts", queries, key_block, preferred_element_type=jnp.float32)
            * scale
        )
        return (jnp.where(mask, raw, -1e30), mask)

    def stats_step(index, carry):
        top, total = carry
        masked, mask = block_scores(key_at(index), index)
        new_top = jnp.maximum(top, jnp.max(masked, axis=-1))
        weight = jnp.where(mask, jnp.exp(masked - new_top[..., None]), 0.0)
        total = total * jnp.exp(top - new_top) + jnp.sum(weight, axis=-1)
        return (new_top, total)

    start = (
        jnp.full((kv_heads, group, rows), -1e30, jnp.float32),
        jnp.zeros((kv_heads, group, rows), jnp.float32),
    )
    top, total = lax.fori_loop(0, live_blocks, stats_step, start)
    log_total = top + jnp.log(total)

    def probs_of(key_block, index):
        masked, mask = block_scores(key_block, index)
        return jnp.where(mask, jnp.exp(masked - log_total[..., None]), 0.0)

    def mix_step(index, accum):
        probs = probs_of(key_at(index), index).astype(jnp.bfloat16)
        return accum + jnp.einsum(
            "kgts,skd->tkgd", probs, value_at(index), preferred_element_type=jnp.float32
        )

    head_zeros = jnp.zeros((rows, kv_heads, group, head_dim), jnp.float32)
    mixed = lax.fori_loop(0, live_blocks, mix_step, head_zeros)
    heads_out = mixed.reshape(rows, -1).astype(jnp.bfloat16)
    attn_term = forward_product(heads_out, full_out)
    resid = hidden + lax.psum(attn_term, "tp")
    normed_two = norm_rows(resid, gain_two).astype(jnp.bfloat16)
    gate = forward_product(normed_two, full_gate)
    up = forward_product(normed_two, full_up)
    middle = activation(gate, up).astype(jnp.bfloat16)
    ffn_term = forward_product(middle, full_down)
    ffn = lax.psum(ffn_term.astype(jnp.bfloat16), "tp").astype(jnp.float32)
    block_out = (valid * (resid + ffn)).astype(jnp.bfloat16)
    grad_top = valid * out_grad.astype(jnp.float32)
    grad_low = grad_top.astype(jnp.bfloat16)
    down_wgrad = outer_product(middle, grad_low)
    mid_grad = back_product(grad_low, full_down)
    _, pull_act = jax.vjp(activation, gate, up)
    gate_float, up_float = pull_act(mid_grad)
    gate_low = gate_float.astype(jnp.bfloat16)
    up_low = up_float.astype(jnp.bfloat16)
    gate_wgrad = outer_product(normed_two, gate_low)
    up_wgrad = outer_product(normed_two, up_low)
    normed_two_part = back_product(gate_low, full_gate) + back_product(up_low, full_up)
    normed_two_grad = lax.psum(normed_two_part, "tp")
    _, pull_two = jax.vjp(norm_rows, resid, gain_two)
    resid_part, gain_two_grad = pull_two(normed_two_grad)
    resid_grad = grad_top + resid_part
    attn_low = resid_grad.astype(jnp.bfloat16)
    out_wgrad = outer_product(heads_out, attn_low)
    heads_grad = (
        back_product(attn_low, full_out)
        .astype(jnp.bfloat16)
        .reshape(rows, kv_heads, group, head_dim)
    )

    def delta_step(index, accum):
        probs = probs_of(key_at(index), index)
        prob_grad = jnp.einsum(
            "tkgd,skd->kgts", heads_grad, value_at(index), preferred_element_type=jnp.float32
        )
        return accum + jnp.sum(probs * prob_grad, axis=-1)

    delta = lax.fori_loop(
        0, live_blocks, delta_step, jnp.zeros((kv_heads, group, rows), jnp.float32)
    )

    def grad_step(index, carry):
        accum, key_store, value_store = carry
        key_block = key_at(index)
        probs = probs_of(key_block, index)
        prob_grad = jnp.einsum(
            "tkgd,skd->kgts", heads_grad, value_at(index), preferred_element_type=jnp.float32
        )
        score_grad = (probs * (prob_grad - delta[..., None])).astype(jnp.bfloat16)
        accum = (
            accum
            + jnp.einsum(
                "kgts,skd->tkgd", score_grad, key_block, preferred_element_type=jnp.float32
            )
            * scale
        )
        key_grad = (
            jnp.einsum("kgts,tkgd->skd", score_grad, queries, preferred_element_type=jnp.float32)
            * scale
        )
        value_grad = jnp.einsum(
            "kgts,tkgd->skd",
            probs.astype(jnp.bfloat16),
            heads_grad,
            preferred_element_type=jnp.float32,
        )
        key_store = lax.dynamic_update_index_in_dim(key_store, key_grad, index, 0)
        value_store = lax.dynamic_update_index_in_dim(value_store, value_grad, index, 0)
        return (accum, key_store, value_store)

    store_zeros = jnp.zeros((pieces, rows, kv_heads, head_dim), jnp.float32)
    query_grad, key_grads, value_grads = lax.fori_loop(
        0, live_blocks, grad_step, (head_zeros, store_zeros, store_zeros)
    )
    key_grad_own, value_grad_own = (
        lax.psum_scatter(
            key_grads.reshape(pieces * rows, kv_heads, head_dim),
            "ctx",
            scatter_dimension=0,
            tiled=True,
        ),
        lax.psum_scatter(
            value_grads.reshape(pieces * rows, kv_heads, head_dim),
            "ctx",
            scatter_dimension=0,
            tiled=True,
        ),
    )

    def query_prep(proj, gain):
        return head_prep(proj, gain, positions)

    _, pull_query = jax.vjp(query_prep, query_proj, q_gain)
    query_proj_grad, q_gain_grad = pull_query(query_grad.reshape(rows, q_heads, head_dim))
    _, pull_key = jax.vjp(query_prep, key_proj, k_gain)
    key_proj_grad, k_gain_grad = pull_key(key_grad_own)
    query_low = query_proj_grad.astype(jnp.bfloat16)
    key_low = key_proj_grad.astype(jnp.bfloat16)
    value_low = value_grad_own.reshape(rows, -1).astype(jnp.bfloat16)
    query_wgrad = outer_product(normed_one, query_low)
    key_wgrad = outer_product(normed_one, key_low)
    value_wgrad = outer_product(normed_one, value_low)
    normed_one_part = (
        back_product(query_low, full_query)
        + back_product(key_low, full_key)
        + back_product(value_low, full_value)
    )
    normed_one_grad = lax.psum(normed_one_part, "tp")
    _, pull_one = jax.vjp(norm_rows, hidden, gain_one)
    hidden_part, gain_one_grad = pull_one(normed_one_grad)
    input_grad = resid_grad + hidden_part
    head_sums = lax.psum((q_gain_grad, k_gain_grad), ("shard", "ctx", "tp"))
    summed = (
        lax.psum_scatter(gain_one_grad, ("shard", "ctx"), scatter_dimension=0, tiled=True),
        lax.psum_scatter(gain_two_grad, ("shard", "ctx"), scatter_dimension=0, tiled=True),
        lax.psum_scatter(query_wgrad, ("shard", "ctx"), scatter_dimension=0, tiled=True),
        lax.psum_scatter(key_wgrad, ("shard", "ctx"), scatter_dimension=0, tiled=True),
        lax.psum_scatter(value_wgrad, ("shard", "ctx"), scatter_dimension=0, tiled=True),
        lax.psum_scatter(gate_wgrad, ("shard", "ctx"), scatter_dimension=0, tiled=True),
        lax.psum_scatter(up_wgrad, ("shard", "ctx"), scatter_dimension=0, tiled=True),
        lax.psum_scatter(out_wgrad, ("shard", "ctx"), scatter_dimension=1, tiled=True),
        lax.psum_scatter(down_wgrad, ("shard", "ctx"), scatter_dimension=1, tiled=True),
    )
    (
        gain_one_out,
        gain_two_out,
        query_out,
        key_out,
        value_out,
        gate_out,
        up_out,
        out_out,
        down_out,
    ) = summed
    return (
        block_out,
        input_grad,
        gain_one_out,
        gain_two_out,
        head_sums[0],
        head_sums[1],
        query_out,
        key_out,
        value_out,
        out_out,
        gate_out,
        up_out,
        down_out,
    )


def remote(src, dst, send, recv, dev):
    return pltpu.make_async_remote_copy(
        src_ref=src,
        dst_ref=dst,
        send_sem=send,
        recv_sem=recv,
        device_id=dev,
        device_id_type=MESH,
    )


def mm(a, b):
    return jnp.dot(a, b, preferred_element_type=F32)


def mm_nt(a, b):
    return lax.dot_general(a, b, (((1,), (1,)), ((), ())), preferred_element_type=F32)


def round_up(units):
    return -(-units // 256) * 256


class Place:
    def __init__(self, n_shard, n_tp):
        s = lax.axis_index("shard")
        c = lax.axis_index("ctx")
        t = lax.axis_index("tp")
        self.s, self.c, self.t = s, c, t
        self.core = lax.rem(s, 2)
        sib = s + 1 - 2 * self.core
        far = lax.rem(s + 2, n_shard)
        far_sib = far + 1 - 2 * self.core
        self.sib = (sib, c, t)
        self.x = (s, 1 - c, t)
        self.y = (far, c, t)
        first = 1 - self.core
        self.relay = (
            first * s + self.core * far,
            first * (1 - c) + self.core * c,
            t,
        )
        slot = lambda a, b: a * 2 + b
        self.own = slot(s, c)
        self.slots = {
            "S": slot(sib, c),
            "X": slot(s, 1 - c),
            "Y": slot(far, c),
            "D": slot(far, 1 - c),
            "SX": slot(sib, 1 - c),
            "SY": slot(far_sib, c),
            "SD": slot(far_sib, 1 - c),
        }
        self.relayed = first * self.slots["Y"] + self.core * self.slots["X"]
        self.n_tp = n_tp

    def z(self, t):
        return (self.s, self.c, t)

    def greet(self):
        peers = [self.sib, self.x, self.y]
        peers += [
            self.z(lax.rem(self.t + d, self.n_tp)) for d in range(1, self.n_tp)
        ]
        barrier = pltpu.get_barrier_semaphore()
        for peer in peers:
            pl.semaphore_signal(barrier, inc=1, device_id=peer, device_id_type=MESH)
        pl.semaphore_wait(barrier, len(peers))


ROLES = ("S", "X", "Y", "D", "SX", "SY", "SD")


class Gather:
    def __init__(self, at, own, full, send, recv, index, stride=0, first=0):
        self.at, self.own, self.full = at, own, full
        self.send, self.recv, self.index = send, recv, index
        self.rows, self.first = own.shape[0], first
        self.stride = stride or self.rows

    def block(self, slot):
        start = slot * self.stride + self.first
        return self.full.at[pl.ds(pl.multiple_of(start, self.rows), self.rows)]

    def copy(self, role, src, slot, dev):
        k = ROLES.index(role)
        return remote(
            src,
            self.block(slot),
            self.send.at[self.index, k],
            self.recv.at[self.index, k],
            dev,
        )

    def arrived(self, role):
        slot = self.at.slots[role]
        self.copy(role, self.block(slot), slot, self.at.sib).wait_recv()

    def start_x(self):
        self.copy("X", self.own, self.at.own, self.at.x).start()

    def start_y(self):
        self.copy("Y", self.own, self.at.own, self.at.y).start()

    def start_s(self):
        self.copy("S", self.own, self.at.own, self.at.sib).start()

    def start(self):
        self.start_x()
        self.start_y()
        self.start_s()

    def relay(self):
        at = self.at
        self.arrived("X")
        self.arrived("Y")
        self.copy("D", self.block(at.relayed), at.relayed, at.relay).start()
        for role in ("X", "Y"):
            slot = at.slots[role]
            self.copy("S" + role, self.block(slot), slot, at.sib).start()

    def relay_last(self):
        self.arrived("D")
        slot = self.at.slots["D"]
        self.copy("SD", self.block(slot), slot, self.at.sib).start()

    def finish(self):
        for role in ("S", "SX", "SY", "SD"):
            self.arrived(role)
        for role in ROLES:
            self.copy(role, self.own, self.at.own, self.at.sib).wait_send()


def column(row_ref, n):
    wide = jnp.broadcast_to(row_ref[...].astype(F32)[None, :], (8, n))
    return wide.T[:, 0:1]


def kernel_a(
    shape,
    length_ref,
    hid_ref,
    gain_one_ref,
    gain_two_ref,
    q_gain_ref,
    k_gain_ref,
    wq_ref,
    wk_ref,
    wv_ref,
    wo_ref,
    wg_ref,
    wu_ref,
    wd_ref,
    cos_ref,
    sin_ref,
    wqkv_out,
    wo_out,
    wg_full,
    wu_full,
    wd_full,
    heads_out,
    q_out,
    kv_out,
    inv_den,
    proj_out,
    resid_out,
    h2t_out,
    act_out,
    wqkv_full,
    wo_full,
    heads_all,
    q_t,
    kv_all,
    proj_t,
    resid,
    h2,
    h2t,
    s_qkv,
    s_woz,
    s_wg,
    s_wu,
    s_wd,
    wg,
    wu,
    act,
    h1,
    k_own,
    k_off,
    v_own,
    v_off,
    acc,
    g_send,
    g_recv,
    z_send,
    z_recv,
    h_send,
    h_recv,
    kv_sem,
    loc_sem,
    act_sem,
    out_sem,
):
    n_shard, n_tp, hd = shape
    at = Place(n_shard, n_tp)
    c, t = at.c, at.t
    rows, width = hid_ref.shape
    q_cols, kv_cols = wq_ref.shape[1], wk_ref.shape[1]
    q_heads, kv_heads = q_cols // hd, kv_cols // hd
    group = q_heads // kv_heads
    half = hd // 2
    at.greet()
    leaving = [
        pltpu.make_async_copy(src, dst, out_sem.at[i])
        for i, (src, dst) in enumerate(
            (
                (wqkv_full, wqkv_out),
                (proj_t, proj_out),
                (q_t, q_out),
                (kv_all, kv_out),
                (heads_all, heads_out),
                (wo_full, wo_out),
                (resid, resid_out),
                (h2t, h2t_out),
            )
        )
    ]

    col_one = column(gain_one_ref, gain_one_ref.shape[0])
    s_qkv[:, 0:q_cols] = (wq_ref[...].astype(F32) * col_one).astype(BF16)
    s_qkv[:, q_cols : q_cols + kv_cols] = (wk_ref[...].astype(F32) * col_one).astype(BF16)
    s_qkv[:, q_cols + kv_cols :] = (wv_ref[...].astype(F32) * col_one).astype(BF16)
    qkv = Gather(at, s_qkv, wqkv_full, g_send, g_recv, 0)
    out = Gather(at, s_woz, wo_full, g_send, g_recv, 1)
    gate = Gather(at, s_wg, wg_full, g_send, g_recv, 2)
    up = Gather(at, s_wu, wu_full, g_send, g_recv, 3)
    down = Gather(at, s_wd, wd_full, g_send, g_recv, 4)
    gathers = (qkv, out, gate, up, down)
    local = [
        pltpu.make_async_copy(g.own, g.block(at.own), loc_sem.at[i])
        for i, g in enumerate(gathers)
    ]
    loads = [
        pltpu.make_async_copy(wg_full, wg, loc_sem.at[5]),
        pltpu.make_async_copy(wu_full, wu, loc_sem.at[6]),
    ]
    qkv.start()
    local[0].start()

    wo_cols = pl.ds(pl.multiple_of(t * q_cols, q_cols), q_cols)
    s_woz[:, wo_cols] = wo_ref[...]

    def wo_part(d, owner):
        cols = pl.ds(pl.multiple_of(owner * q_cols, q_cols), q_cols)
        return remote(
            s_woz.at[:, cols],
            s_woz.at[:, cols],
            z_send.at[d],
            z_recv.at[d],
            at.z(lax.rem(t + d + 1, n_tp)),
        )

    for d in range(n_tp - 1):
        wo_part(d, t).start()

    def norm_one(i, _):
        r = pl.ds(pl.multiple_of(i * 64, 64), 64)
        x = hid_ref[r, :].astype(F32)
        scale = lax.rsqrt(jnp.mean(x * x, axis=-1, keepdims=True) + EPSILON)
        h1[r, :] = (x * scale).astype(BF16)
        return 0

    lax.fori_loop(0, rows // 64, norm_one, 0)
    qkv.relay()
    col_two = column(gain_two_ref, gain_two_ref.shape[0])
    units = wg_ref.shape[1]
    for src, dst in ((wg_ref, s_wg), (wu_ref, s_wu)):
        dst[:, 0:units] = (src[...].astype(F32) * col_two).astype(BF16)
        dst[:, units:] = jnp.zeros((dst.shape[0], dst.shape[1] - units), BF16)
    s_wd[:, 0:units] = wd_ref[...]
    s_wd[:, units:] = jnp.zeros((s_wd.shape[0], s_wd.shape[1] - units), BF16)
    qkv.relay_last()
    for d in range(n_tp - 1):
        wo_part(d, lax.rem(t + n_tp - d - 1, n_tp)).wait_recv()
    out.start()
    gate.start_y()
    local[0].wait()
    for cp in local[1:]:
        cp.start()
    qkv.finish()

    def project(i, _):
        r = pl.ds(pl.multiple_of(i * 256, 256), 256)
        proj_t[:, r] = mm(h1[r, :], wqkv_full[...]).T
        return 0

    lax.fori_loop(0, rows // 256, project, 0)
    leaving[0].start()
    leaving[1].start()
    here = pl.ds(pl.multiple_of(c * rows, rows), rows)
    k_gain = column(k_gain_ref, hd)
    q_gain = column(q_gain_ref, hd)

    def prepared(row, gain, factor):
        x = proj_t[pl.ds(pl.multiple_of(row, hd), hd), :]
        scale = lax.rsqrt(jnp.mean(x * x, axis=0, keepdims=True) + EPSILON)
        y = x * (scale * factor) * gain
        a, b = y[:half], y[half:]
        cosine, sine = cos_ref[:, here], sin_ref[:, here]
        return jnp.concatenate([a * cosine - b * sine, b * cosine + a * sine], axis=0)

    for g in range(kv_heads):
        key = prepared(q_cols + g * hd, k_gain, 1.0).astype(BF16)
        kv_all[c, g * hd : (g + 1) * hd, :] = key
    kv_all[c, kv_cols:, :] = proj_t[q_cols + kv_cols :, :].astype(BF16)
    kv_copy = remote(kv_all.at[c], kv_all.at[c], kv_sem.at[0], kv_sem.at[1], at.x)
    kv_back = remote(
        kv_all.at[1 - c], kv_all.at[1 - c], kv_sem.at[0], kv_sem.at[1], at.x
    )

    @pl.when(c == 0)
    def _():
        kv_copy.start()

    gate.start_x()
    gate.start_s()

    def prep_q(h, _):
        r = pl.multiple_of(h * hd, hd)
        q_t[pl.ds(r, hd), :] = prepared(r, q_gain, 1.0 / math.sqrt(hd)).astype(BF16)
        return 0

    lax.fori_loop(0, q_heads, prep_q, 0)
    leaving[2].start()
    length = length_ref[0]

    def load_block(index, k_nat, v_ext):
        pos = index * rows + lax.broadcasted_iota(jnp.int32, (1, rows), 1)
        live = (pos < length).astype(F32)
        first = (lax.broadcasted_iota(jnp.int32, (16, rows), 0) == 0).astype(F32)
        for g in range(kv_heads):
            k_nat[g] = kv_all[index, g * hd : (g + 1) * hd, :].astype(F32).T.astype(BF16)
            v = kv_all[index, kv_cols + g * hd : kv_cols + (g + 1) * hd, :].astype(F32)
            v_ext[g, 0:hd, :] = (v * live).astype(BF16)
            v_ext[g, hd:, :] = (first * live).astype(BF16)

    load_block(c, k_own, v_own)
    below = lax.broadcasted_iota(jnp.int32, (256, 256), 0) <= lax.broadcasted_iota(
        jnp.int32, (256, 256), 1
    )

    def own_block(h, _):
        g = h // group
        qh = q_t[pl.ds(pl.multiple_of(h * hd, hd), hd), :]
        for i in range(rows // 256):
            qi = qh[:, i * 256 : (i + 1) * 256]
            top = i * 256
            e = jnp.exp(mm(k_own[g, top : top + 256, :], qi))
            e = jnp.where(below, e, 0.0).astype(BF16)
            total = mm(v_own[g, :, top : top + 256], e)
            if i:
                e = jnp.exp(mm(k_own[g, 0:top, :], qi)).astype(BF16)
                total += mm(v_own[g, :, 0:top], e)
            acc[h, :, top : top + 256] = total
        return 0

    lax.fori_loop(0, q_heads, own_block, 0)
    out.relay()
    up.start()

    @pl.when(c == 1)
    def _():
        kv_back.wait_recv()
        load_block(1 - c, k_off, v_off)

        def other_block(h, _):
            g = h // group
            qh = q_t[pl.ds(pl.multiple_of(h * hd, hd), hd), :]
            for i in range(rows // 256):
                cols = slice(i * 256, (i + 1) * 256)
                e = jnp.exp(mm(k_off[g], qh[:, cols])).astype(BF16)
                acc[h, :, cols] += mm(v_off[g], e)
            return 0

        lax.fori_loop(0, q_heads, other_block, 0)

    @pl.when(c == 0)
    def _():
        kv_all[1 - c] = jnp.zeros(kv_all.shape[1:], BF16)

    leaving[3].start()

    def chunk_cols(owner, j):
        return pl.ds(pl.multiple_of(owner * q_cols + j * 128, 128), 128)

    def along(owner, j, way):
        ref = heads_all.at[:, chunk_cols(owner, j)]
        dev = at.z(jnp.minimum(t + 1, n_tp - 1) if way == 0 else jnp.maximum(t - 1, 0))
        return remote(ref, ref, h_send.at[way, owner, j], h_recv.at[way, owner, j], dev)

    chunks = q_cols // 128

    def pass_on(owner, j, way):
        @pl.when(t < n_tp - 1 if way == 0 else t > 0)
        def _():
            along(owner, j, way).start()

    for j in range(chunks):
        parts = []
        for h in range(2 * j, 2 * j + 2):
            inverse = 1.0 / acc[h, hd : hd + 1, :]
            inv_den[h : h + 1, :] = inverse
            parts.append(acc[h, 0:hd, :] * inverse)
        pair = jnp.concatenate(parts, axis=0)
        heads_all[:, chunk_cols(t, j)] = pair.T.astype(BF16)
        for way in (0, 1):
            pass_on(t, j, way)
    inv_den[q_heads:, :] = jnp.zeros((8 - q_heads, rows), F32)

    for d in range(1, n_tp):
        for j in range(chunks):

            @pl.when(t >= d)
            def _():
                along(t - d, j, 0).wait_recv()
                pass_on(t - d, j, 0)

            @pl.when(t + d < n_tp)
            def _():
                along(t + d, j, 1).wait_recv()
                pass_on(t + d, j, 1)

            step = (d - 1) * chunks + j
            if step == 2:
                gate.relay()
            if step == 4:
                out.relay_last()
            if step == 7:
                up.relay()
                down.start()

    out.finish()
    local[1].wait()
    leaving[4].start()
    leaving[5].start()

    def residual(i, _):
        r = pl.ds(pl.multiple_of(i * 128, 128), 128)
        x = hid_ref[r, :].astype(F32) + mm_nt(heads_all[r, :], wo_full[...])
        resid[r, :] = x
        scale = lax.rsqrt(jnp.mean(x * x, axis=-1, keepdims=True) + EPSILON)
        h = (x * scale).astype(BF16)
        h2[r, :] = h
        h2t[:, r] = h.T

        @pl.when(i == 1)
        def _():
            gate.relay_last()

        @pl.when(i == 3)
        def _():
            gate.finish()
            local[2].wait()
            loads[0].start()

        return 0

    lax.fori_loop(0, rows // 128, residual, 0)
    leaving[6].start()
    leaving[7].start()
    up.relay_last()
    up.finish()
    local[3].wait()
    loads[1].start()
    loads[0].wait()
    loads[1].wait()
    tiles = act.shape[2] // 256
    half = rows // 2

    def act_copy(f):
        cols = pl.ds(pl.multiple_of(f * 256, 256), 256)
        return pltpu.make_async_copy(
            act.at[:, :, cols], act_out.at[:, :, cols], act_sem.at[f]
        )

    def gate_up(f, _):
        cols = pl.ds(pl.multiple_of(f * 256, 256), 256)
        for i in (0, 1):
            r = slice(i * half, (i + 1) * half)
            g = mm(h2[r, :], wg[:, cols])
            u = mm(h2[r, :], wu[:, cols])
            s = 1.0 / (1.0 + jnp.exp(-g))
            silu = g * s
            act[0, r, cols] = (silu * u).astype(BF16)
            act[1, r, cols] = (u * (s * (1.0 + g * (1.0 - s)))).astype(BF16)
            act[2, r, cols] = silu.astype(BF16)

        act_copy(f).start()

        @pl.when(f == tiles - 2)
        def _():
            down.relay()

        return 0

    lax.fori_loop(0, tiles, gate_up, 0)
    down.relay_last()
    down.finish()
    local[4].wait()

    def act_done(f, _):
        act_copy(f).wait()
        return 0

    lax.fori_loop(0, tiles, act_done, 0)
    for owner in range(n_tp):
        for j in range(chunks):

            @pl.when(jnp.logical_and(t < n_tp - 1, owner <= t))
            def _():
                along(owner, j, 0).wait_send()

            @pl.when(jnp.logical_and(t > 0, owner >= t))
            def _():
                along(owner, j, 1).wait_send()

    for d in range(n_tp - 1):
        wo_part(d, t).wait_send()

    @pl.when(c == 0)
    def _():
        kv_copy.wait_send()

    for cp in leaving:
        cp.wait()


def rope_tables(positions, hd):
    freq = ROPE_BASE ** (-np.arange(hd // 2, dtype=np.float64) / (hd // 2))
    angle = freq[:, None] * np.arange(positions, dtype=np.float64)[None, :]
    return np.cos(angle).astype(np.float32), np.sin(angle).astype(np.float32)


def call_a(mesh, args):
    (hidden_in, seq_lengths, attn_gain, ffn_gain, query_gain, key_gain,
     w_query, w_key, w_value, w_out, w_gate, w_up, w_down) = args
    n_shard, n_ctx, n_tp = mesh.shape["shard"], mesh.shape["ctx"], mesh.shape["tp"]
    rows, width = hidden_in.shape
    hd = query_gain.shape[0]
    q_cols, kv_cols = w_query.shape[1], w_key.shape[1]
    q_heads, kv_heads = q_cols // hd, kv_cols // hd
    block = w_query.shape[0]
    padded = round_up(w_gate.shape[1])
    cosine, sine = rope_tables(n_ctx * rows, hd)
    vm = pl.BlockSpec(memory_space=pltpu.VMEM)
    hbm = pl.BlockSpec(memory_space=pltpu.HBM)
    sm = pl.BlockSpec(memory_space=pltpu.SMEM)
    qkv_cols = q_cols + 2 * kv_cols
    S = jax.ShapeDtypeStruct
    dma = pltpu.SemaphoreType.DMA
    chunks = q_cols // 128
    return pl.pallas_call(
        functools.partial(kernel_a, (n_shard, n_tp, hd)),
        out_shape=(
            S((width, qkv_cols), BF16),
            S((width, n_tp * q_cols), BF16),
            S((width, padded), BF16),
            S((width, padded), BF16),
            S((width, padded), BF16),
            S((rows, n_tp * q_cols), BF16),
            S((q_cols, rows), BF16),
            S((n_ctx, 2 * kv_cols, rows), BF16),
            S((8, rows), F32),
            S((qkv_cols, rows), F32),
            S((rows, width), F32),
            S((width, rows), BF16),
            S((3, rows, padded), BF16),
        ),
        in_specs=[sm] + [vm] * 14,
        out_specs=(hbm,) * 8 + (vm,) + (hbm,) * 4,
        scratch_shapes=[
            pltpu.VMEM((width, qkv_cols), BF16),
            pltpu.VMEM((width, n_tp * q_cols), BF16),
            pltpu.VMEM((rows, n_tp * q_cols), BF16),
            pltpu.VMEM((q_cols, rows), BF16),
            pltpu.VMEM((n_ctx, 2 * kv_cols, rows), BF16),
            pltpu.VMEM((qkv_cols, rows), F32),
            pltpu.VMEM((rows, width), F32),
            pltpu.VMEM((rows, width), BF16),
            pltpu.VMEM((width, rows), BF16),
            pltpu.VMEM((block, qkv_cols), BF16),
            pltpu.VMEM((block, n_tp * q_cols), BF16),
            pltpu.VMEM((block, padded), BF16),
            pltpu.VMEM((block, padded), BF16),
            pltpu.VMEM((block, padded), BF16),
            pltpu.VMEM((width, padded), BF16),
            pltpu.VMEM((width, padded), BF16),
            pltpu.VMEM((3, rows, padded), BF16),
            pltpu.VMEM((rows, width), BF16),
            pltpu.VMEM((kv_heads, rows, hd), BF16),
            pltpu.VMEM((kv_heads, rows, hd), BF16),
            pltpu.VMEM((kv_heads, hd + 16, rows), BF16),
            pltpu.VMEM((kv_heads, hd + 16, rows), BF16),
            pltpu.VMEM((q_heads, hd + 16, rows), F32),
            dma((5, 7)),
            dma((5, 7)),
            dma((n_tp - 1,)),
            dma((n_tp - 1,)),
            dma((2, n_tp, chunks)),
            dma((2, n_tp, chunks)),
            dma((2,)),
            dma((7,)),
            dma((padded // 256,)),
            dma((8,)),
        ],
        compiler_params=pltpu.CompilerParams(
            collective_id=0, has_side_effects=True, vmem_limit_bytes=VMEM_LIMIT
        ),
    )(
        seq_lengths, hidden_in, attn_gain, ffn_gain,
        query_gain, key_gain, w_query, w_key, w_value,
        w_out.T, w_gate, w_up, w_down.T, jnp.asarray(cosine), jnp.asarray(sine),
    )


LAG = 2


class Line:
    def __init__(self, at, part, landing, send, recv, chunks, folds=1):
        self.at, self.part, self.landing = at, part, landing
        self.send, self.recv, self.chunks, self.folds = send, recv, chunks, folds
        self.half = landing.shape[1]
        self.size = self.half // chunks
        self.last = at.n_tp - 1

    def pos(self, way):
        return self.at.t if way == 0 else self.last - self.at.t

    def dev(self, way, step):
        to = self.at.t + (step if way == 0 else -step)
        return self.at.z(jnp.clip(to, 0, self.last))

    def local(self, k):
        return pl.ds(pl.multiple_of(k * self.size, self.size), self.size)

    def rows(self, way, k):
        return pl.ds(self.start(way, k), self.size)

    def start(self, way, k):
        fold = self.half // self.folds
        if self.folds == 1:
            first = (1 - way) * fold + k * self.size
        else:
            per = self.chunks // self.folds
            group = lax.div(k, per)
            first = (2 * group + 1 - way) * fold + (k - group * per) * self.size
        return pl.multiple_of(first, self.size)

    def copy(self, way, k):
        return remote(
            self.part.at[self.rows(way, k)],
            self.landing.at[way, self.local(k)],
            self.send.at[way, k],
            self.recv.at[way, k],
            self.dev(way, 1),
        )

    def reduce(self, step, final):
        for way in (0, 1):
            pos = self.pos(way)
            k = step - pos * LAG
            live = jnp.logical_and(k >= 0, k < self.chunks)

            @pl.when(jnp.logical_and(live, pos > 0))
            def _():
                self.copy(way, k).wait_recv()
                value = self.part[self.rows(way, k), :].astype(F32)
                value += self.landing[way, self.local(k), :].astype(F32)

                @pl.when(pos < self.last)
                def _():
                    self.part[self.rows(way, k), :] = value.astype(BF16)

                @pl.when(pos == self.last)
                def _():
                    final(way, k, value)

            @pl.when(jnp.logical_and(live, pos < self.last))
            def _():
                self.copy(way, k).start()

    def drain(self):
        for way in (0, 1):

            @pl.when(self.pos(way) < self.last)
            def _():
                def one(k, _):
                    self.copy(way, k).wait_send()
                    return 0

                lax.fori_loop(0, self.chunks, one, 0)


class Back:
    def __init__(self, line, whole, send, recv, source=None):
        self.line, self.whole, self.send, self.recv = line, whole, send, recv
        self.source = source

    def copy(self, way, k, first=False):
        line = self.line
        dst = self.whole.at[line.rows(way, k)]
        src = self.source.at[way, line.local(k)] if first and self.source is not None else dst
        return remote(src, dst, self.send.at[way, k], self.recv.at[way, k], line.dev(way, -1))

    def step(self, step):
        line = self.line
        for way in (0, 1):
            pos = line.pos(way)
            k = step - (line.last - pos) * LAG
            live = jnp.logical_and(k >= 0, k < line.chunks)

            @pl.when(jnp.logical_and(live, pos < line.last))
            def _():
                self.copy(way, k).wait_recv()

                @pl.when(pos > 0)
                def _():
                    self.copy(way, k).start()

            @pl.when(jnp.logical_and(live, pos == line.last))
            def _():
                self.copy(way, k, True).start()

    def drain(self):
        line = self.line
        for way in (0, 1):

            @pl.when(line.pos(way) > 0)
            def _():
                def one(k, _):
                    self.copy(way, k).wait_send()
                    return 0

                lax.fori_loop(0, line.chunks, one, 0)


class Scatter:
    def __init__(self, at, source, room, tmp_sem, send, recv, index):
        self.at, self.source, self.room = at, source, room
        self.tmp_sem, self.send, self.recv, self.index = tmp_sem, send, recv, index
        self.rows = room.shape[0] // 8
        self.tmp, self.relayed = self.land(7), self.land(4)
        self.final = (self.land(5), self.land(6))
        self.direct, self.indirect = 1 + at.core, 2 - at.core
        self.other = (
            at.core * at.x[0] + (1 - at.core) * at.y[0],
            at.core * at.x[1] + (1 - at.core) * at.y[1],
            at.t,
        )
        self.mine = [at.own] + [at.slots[n] for n in ("X", "Y", "D")]
        self.theirs = [at.slots[n] for n in ("S", "SX", "SY", "SD")]

    def land(self, j):
        return self.room.at[pl.ds(pl.multiple_of(j * self.rows, self.rows), self.rows)]

    def block(self, slot):
        return self.source.at[pl.ds(pl.multiple_of(slot * self.rows, self.rows), self.rows)]

    def copy(self, k, src, dst, dev):
        return remote(src, dst, self.send.at[self.index, k], self.recv.at[self.index, k], dev)

    def share(self, j):
        return self.copy(j, self.block(self.theirs[j]), self.land(j), self.at.sib)

    def start(self):
        for j in (3, 1, 2, 0):
            self.share(j).start()
        self.fetch(3).start()

    def slot(self, j):
        if isinstance(j, int):
            return self.mine[j]
        return jnp.where(j == 1, self.mine[1], self.mine[2])

    def arrived(self, j):
        ref = self.land(j)
        self.copy(j, ref, ref, self.at.sib).wait_recv()

    def fetch(self, j):
        return pltpu.make_async_copy(self.block(self.slot(j)), self.tmp, self.tmp_sem)

    def add(self, j, extra=()):
        self.arrived(j)
        self.fetch(j).wait()
        land = self.land(j)

        def piece(i, _):
            r = pl.ds(pl.multiple_of(i * 64, 64), 64)
            value = land[r, :].astype(F32) + self.tmp[r, :].astype(F32)
            for ref in extra:
                value += ref[r, :].astype(F32)
            land[r, :] = value.astype(BF16)
            return 0

        lax.fori_loop(0, self.rows // 64, piece, 0)

    def hop(self, k):
        at = self.at
        if k == 4:
            return self.copy(4, self.land(3), self.relayed, at.relay)
        if k == 5:
            return self.copy(5, self.land(self.direct), self.final[0], at.relay)
        return self.copy(6, self.land(self.indirect), self.final[1], self.other)

    def first(self):
        self.add(3)
        self.fetch(self.direct).start()
        self.hop(4).start()
        self.add(self.direct)
        self.fetch(self.indirect).start()
        self.hop(5).start()

    def second(self):
        self.hop(4).wait_recv()
        self.add(self.indirect, (self.relayed,))
        self.fetch(0).start()
        self.hop(6).start()

    def finish(self, use):
        self.arrived(0)
        self.hop(5).wait_recv()
        self.hop(6).wait_recv()
        self.fetch(0).wait()
        land = self.land(0)

        def piece(i, _):
            r = pl.ds(pl.multiple_of(i * 64, 64), 64)
            value = land[r, :].astype(F32) + self.tmp[r, :].astype(F32)
            value += self.final[0][r, :].astype(F32) + self.final[1][r, :].astype(F32)
            use(r, value)
            return 0

        lax.fori_loop(0, self.rows // 64, piece, 0)

    def drain(self):
        for j in range(4):
            self.share(j).wait_send()
        for k in (4, 5, 6):
            self.hop(k).wait_send()


def kernel_b(
    shape,
    length_ref,
    og_ref,
    wd_hbm,
    act_hbm,
    wg_hbm,
    wu_hbm,
    h2t_hbm,
    resid_hbm,
    attn_low,
    rg_own,
    gate_sum,
    ffn_part,
    wgrads,
    f_part,
    d_part,
    wg,
    wu,
    wd,
    resid,
    left_t,
    gl,
    act,
    land_d,
    stage,
    d_send,
    d_recv,
    b_send,
    b_recv,
    s_send,
    s_recv,
    loc_sem,
    tile_sem,
    st_sem,
    free_sem,
):
    n_shard, n_tp, chunks = shape
    at = Place(n_shard, n_tp)
    rows, width = og_ref.shape
    padded = wd.shape[1]
    block = stage.shape[1]
    half = rows // 2
    tiles = padded // 256
    last = n_tp - 1
    def tile_load(f):
        cols = pl.ds(pl.multiple_of(f * 256, 256), 256)
        return (
            pltpu.make_async_copy(wd_hbm.at[:, cols], wd.at[:, cols], tile_sem.at[0, f]),
            pltpu.make_async_copy(
                act_hbm.at[1:3, :, cols], act.at[1:3, :, cols], tile_sem.at[1, f]
            ),
        )

    for f in range(tiles):
        for cp in tile_load(f):
            cp.start()
    pairs = (
        (wg_hbm, wg),
        (wu_hbm, wu),
        (resid_hbm, resid),
        (act_hbm.at[0], act.at[0]),
        (h2t_hbm, left_t.at[:, pl.ds(0, rows)]),
    )
    loads = [
        pltpu.make_async_copy(src, dst, loc_sem.at[i]) for i, (src, dst) in enumerate(pairs)
    ]
    for cp in loads:
        cp.start()
    at.greet()
    length = length_ref[0]

    def live_rows(start, n):
        pos = at.c * rows + start + lax.broadcasted_iota(jnp.int32, (n, 1), 0)
        return (pos < length).astype(F32)

    def mask_grad(i, _):
        start = pl.multiple_of(i * 128, 128)
        r = pl.ds(start, 128)
        low = (og_ref[r, :].astype(F32) * live_rows(start, 128)).astype(BF16)
        gl[r, :] = low
        left_t[:, pl.ds(pl.multiple_of(rows + start, 128), 128)] = low.T
        return 0

    lax.fori_loop(0, rows // 128, mask_grad, 0)

    quarter = half // 2
    lines, backs = [], []
    for n in (0, 1):
        r = pl.ds(n * half, half)
        line = Line(at, d_part.at[r], land_d.at[n], d_send.at[n], d_recv.at[n], chunks)
        lines.append(line)
        backs.append(Back(line, attn_low.at[r], b_send.at[n], b_recv.at[n]))

    def final_d2(n):
        def final(way, k, value):
            line = lines[n]
            start = n * half + (1 - way) * quarter + k * line.size
            r = pl.ds(pl.multiple_of(start, line.size), line.size)
            x = resid[r, :]
            scale = lax.rsqrt(jnp.mean(x * x, axis=-1, keepdims=True) + EPSILON)
            h = x * scale
            inner = jnp.mean(value * h, axis=-1, keepdims=True)
            grad = gl[r, :].astype(F32) + scale * (value - h * inner)
            rg_own[pl.ds(pl.multiple_of(n * quarter + k * line.size, line.size), line.size), :] = grad
            attn_low[r, :] = grad.astype(BF16)

        return final

    def move(n, step):
        lines[n].reduce(step, final_d2(n))
        backs[n].step(step - last * LAG)

    def moves(n, slot):
        for i in range(LAG):
            move(n, slot * LAG + i)

    def mid(n):
        r = slice(n * half, (n + 1) * half)

        def one(f, _):
            cols = pl.ds(pl.multiple_of(f * 256, 256), 256)
            if n == 0:
                for cp in tile_load(f):
                    cp.wait()
            g = mm(gl[r, :], wd[:, cols])
            act[1, r, cols] = (g * act[1, r, cols].astype(F32)).astype(BF16)
            act[2, r, cols] = (g * act[2, r, cols].astype(F32)).astype(BF16)
            if n == 1:

                @pl.when(lax.rem(f, 4) == 2)
                def _():
                    moves(0, 1 + lax.div(f, 4))

            return 0

        lax.fori_loop(0, tiles, one, 0)

    def back_part(q):
        r = slice(q * quarter, (q + 1) * quarter)
        total = mm_nt(act[1, r, :], wg[...]) + mm_nt(act[2, r, :], wu[...])
        d_part[r, :] = total.astype(BF16)

    mid(0)
    for cp in loads:
        cp.wait()
    back_part(0)
    back_part(1)
    moves(0, 0)
    mid(1)
    done = 1 + (tiles + 1) // 4
    back_part(2)
    moves(0, done)
    back_part(3)
    done = (done + 1) * LAG

    peers = (at.sib, at.x, at.y)
    for n, peer in enumerate(peers):
        pl.semaphore_signal(free_sem.at[n], inc=1, device_id=peer, device_id_type=MESH)
    gate = Scatter(at, wgrads.at[1], wg, loc_sem.at[0], s_send, s_recv, 0)

    def free(n):
        pl.semaphore_wait(free_sem.at[n], 1)

    blocks = width // block
    per_step = PER_STEP
    count = 3 * blocks
    def weight_of(n):
        return lax.rem(lax.div(n, blocks) + 1, 3)

    def stage_copy(n):
        w, slot = lax.rem(n, blocks), lax.rem(n, 2)
        return pltpu.make_async_copy(
            stage.at[slot],
            wgrads.at[weight_of(n), pl.ds(pl.multiple_of(w * block, block), block)],
            st_sem.at[slot],
        )

    def weight_grad(n):
        a, w, slot = weight_of(n), lax.rem(n, blocks), lax.rem(n, 2)

        @pl.when(n >= 2)
        def _():
            stage_copy(n - 2).wait()

        first = pl.multiple_of(jnp.where(a == 0, rows, 0), 128)
        left = left_t[pl.ds(pl.multiple_of(w * block, block), block), pl.ds(first, rows)]
        for f in range(tiles):
            cols = slice(f * 256, (f + 1) * 256)
            stage[slot, :, cols] = mm(left, act[a, :, cols]).astype(BF16)
        stage_copy(n).start()

    keeps = pltpu.make_async_copy(f_part, ffn_part, loc_sem.at[1])

    def forward_part(q):
        r = pl.ds(pl.multiple_of(q * quarter, quarter), quarter)
        total = mm_nt(act[0, r, :], wd[...])
        mine = (at.t == lax.rem(q, 2) * last).astype(F32)
        f_part[r, :] = (total + resid[r, :] * mine).astype(BF16)

    def use_gate(r, value):
        gate_sum[r, :] = value.astype(BF16)

    def start_gate():
        free(0)
        gate.start()

    def first_gate():
        free(1)
        free(2)
        gate.first()

    total = chunks + 2 * last * LAG
    begin = (blocks + 2 * per_step - 1) // per_step
    events = {
        begin: start_gate,
        begin + total // 12: first_gate,
        begin + total // 4: gate.second,
        total - 3: lambda: gate.finish(use_gate),
    }

    def tail(step, _):
        move(0, step + done)
        move(1, step)

        for n in range(per_step):

            @pl.when(step * per_step + n < count)
            def _():
                weight_grad(step * per_step + n)

        for when, todo in events.items():

            @pl.when(step == when)
            def _():
                todo()

        @pl.when(jnp.logical_and(step >= total - 10, step < total - 6))
        def _():
            forward_part(step - (total - 10))

        return 0

    steps = max(total, -(-count // per_step))
    lax.fori_loop(0, steps, tail, 0)
    keeps.start()
    stage_copy(count - 2).wait()
    stage_copy(count - 1).wait()
    gate.drain()
    for n in (0, 1):
        lines[n].drain()
        backs[n].drain()
    keeps.wait()


def call_b(mesh, chunks, seq_lengths, out_grad, wd_full, act, wg_full, wu_full, h2t, resid):
    n_shard, n_tp = mesh.shape["shard"], mesh.shape["tp"]
    rows, width = out_grad.shape
    block = width // (n_shard * mesh.shape["ctx"])
    padded = wg_full.shape[1]
    half = rows // 2
    vm = pl.BlockSpec(memory_space=pltpu.VMEM)
    hbm = pl.BlockSpec(memory_space=pltpu.HBM)
    sm = pl.BlockSpec(memory_space=pltpu.SMEM)
    S = jax.ShapeDtypeStruct
    dma = pltpu.SemaphoreType.DMA
    return pl.pallas_call(
        functools.partial(kernel_b, (n_shard, n_tp, chunks)),
        out_shape=(
            S((rows, width), BF16),
            S((half, width), F32),
            S((block, padded), BF16),
            S((rows, width), BF16),
            S((3, width, padded), BF16),
        ),
        in_specs=[sm, vm] + [hbm] * 6,
        out_specs=(vm, vm, vm, hbm, hbm),
        scratch_shapes=[
            pltpu.VMEM((rows, width), BF16),
            pltpu.VMEM((rows, width), BF16),
            pltpu.VMEM((width, padded), BF16),
            pltpu.VMEM((width, padded), BF16),
            pltpu.VMEM((width, padded), BF16),
            pltpu.VMEM((rows, width), F32),
            pltpu.VMEM((width, 2 * rows), BF16),
            pltpu.VMEM((rows, width), BF16),
            pltpu.VMEM((3, rows, padded), BF16),
            pltpu.VMEM((2, 2, half // 2, width), BF16),
            pltpu.VMEM((2, block, padded), BF16),
            dma((2, 2, chunks)),
            dma((2, 2, chunks)),
            dma((2, 2, chunks)),
            dma((2, 2, chunks)),
            dma((1, 7)),
            dma((1, 7)),
            dma((5,)),
            dma((2, padded // 256)),
            dma((2,)),
            pltpu.SemaphoreType.REGULAR((3,)),
        ],
        compiler_params=pltpu.CompilerParams(
            collective_id=1, has_side_effects=True, vmem_limit_bytes=VMEM_LIMIT
        ),
    )(seq_lengths, out_grad, wd_full, act, wg_full, wu_full, h2t, resid)


def kernel_c(
    shape,
    length_ref,
    attn_low,
    q_t,
    kv_all,
    inv_den,
    gain_one_ref,
    gain_two_ref,
    q_gain_ref,
    k_gain_ref,
    wq_ref,
    wk_ref,
    wv_ref,
    cos_ref,
    sin_ref,
    rg_hbm,
    hid_hbm,
    wqkv_hbm,
    proj_hbm,
    wg_hbm,
    wu_hbm,
    gate_hbm,
    ffn_hbm,
    wgrads,
    heads_hbm,
    wo_hbm,
    block_out,
    inp,
    g_query,
    g_key,
    g_value,
    g_out,
    g_up,
    g_down,
    small,
    rg_own,
    hid_ref,
    wqkv,
    proj_t,
    wg_ref,
    wu_ref,
    gate_sum,
    heads_own,
    wo_own,
    hg_t,
    delta,
    k_own,
    v_own,
    kt_own,
    dq_t,
    dkv,
    dkv_send,
    dkv_land,
    gain_acc,
    dqkv,
    f_part,
    d_part,
    land_f,
    land_d,
    left_t,
    part,
    room_w,
    room_p,
    cols_acc,
    qk,
    qk_land,
    tile,
    s_send,
    s_recv,
    f_send,
    f_recv,
    d_send,
    d_recv,
    b_send,
    b_recv,
    o_send,
    o_recv,
    e_send,
    e_recv,
    t_send,
    t_recv,
    loc_sem,
):
    n_shard, n_tp, chunks, hd = shape
    at = Place(n_shard, n_tp)
    c, t = at.c, at.t
    rows, width = hid_hbm.shape
    q_cols, kv_cols = wq_ref.shape[1], wk_ref.shape[1]
    q_heads, kv_heads = q_cols // hd, kv_cols // hd
    group = q_heads // kv_heads
    halfd = hd // 2
    half = rows // 2
    block = wq_ref.shape[0]
    units = wg_hbm.shape[1]
    last = n_tp - 1
    own_cols = pl.ds(pl.multiple_of(t * q_cols, q_cols), q_cols)
    quarter = half // 2
    loads = [
        pltpu.make_async_copy(heads_hbm.at[:, own_cols], heads_own, loc_sem.at[0]),
        pltpu.make_async_copy(wo_hbm.at[:, own_cols], wo_own, loc_sem.at[1]),
        pltpu.make_async_copy(ffn_hbm, f_part, loc_sem.at[2]),
    ]
    late = [
        pltpu.make_async_copy(src, dst, loc_sem.at[8 + i])
        for i, (src, dst) in enumerate(
            (
                (proj_hbm, proj_t),
                (wqkv_hbm, wqkv),
                (hid_hbm, hid_ref),
                (rg_hbm, rg_own),
                (wg_hbm, wg_ref),
                (wu_hbm, wu_ref),
                (gate_hbm, gate_sum),
            )
        )
    ]
    for cp in loads:
        cp.start()
    at.greet()
    down, up = (
        Scatter(at, wgrads.at[k], room_w.at[i], loc_sem.at[3 + i], s_send, s_recv, i)
        for i, k in enumerate((0, 2))
    )
    rest = Scatter(at, part, room_p, loc_sem.at[5], s_send, s_recv, 2)
    down.start()
    up.start()
    ffn = Line(at, f_part, land_f, f_send, f_recv, chunks, 2)
    ffn_back = Back(ffn, block_out, o_send, o_recv, land_f)
    d1 = Line(at, d_part, land_d, d_send, d_recv, chunks, 2)
    back = Back(d1, inp, b_send, b_recv)
    length = length_ref[0]

    def final_ffn(way, k, value):
        pos = c * rows + ffn.start(way, k)
        pos += lax.broadcasted_iota(jnp.int32, (ffn.size, 1), 0)
        value = value * (pos < length).astype(F32)
        land_f[way, ffn.local(k), :] = value.astype(BF16)

    def move_ffn(step):
        ffn.reduce(step, final_ffn)
        ffn_back.step(step - last * LAG)

    def moves_ffn(slot):
        for i in range(PER_SLOT):
            move_ffn(slot * PER_SLOT + i)

    def keep(n, way):
        return pltpu.make_async_copy(
            land_f.at[way, pl.ds(n * quarter, quarter)],
            block_out.at[pl.ds((2 * n + 1 - way) * quarter, quarter)],
            loc_sem.at[6 + n],
        )

    def keep_all(act):
        for way in (0, 1):

            @pl.when(t == (last if way == 0 else 0))
            def _():
                for n in (0, 1):
                    act(keep(n, way))

    for cp in loads:
        cp.wait()
    moves_ffn(0)
    for cp in late:
        cp.start()

    def heads_grad(i, _):
        r = pl.ds(pl.multiple_of(i * 256, 256), 256)
        hg_t[:, r] = mm(attn_low[r, :], wo_own[...]).T.astype(BF16)
        return 0

    lax.fori_loop(0, rows // 256, heads_grad, 0)
    for j in range(q_cols // 128):
        cols = slice(j * 128, (j + 1) * 128)
        both = heads_own[:, cols].astype(F32).T * hg_t[cols, :].astype(F32)
        for n in range(128 // hd):
            h = j * (128 // hd) + n
            delta[h : h + 1, :] = jnp.sum(both[n * hd : (n + 1) * hd], axis=0, keepdims=True)
    moves_ffn(1)
    down.first()

    def live_keys(index):
        pos = index * rows + lax.broadcasted_iota(jnp.int32, (1, rows), 1)
        return (pos < length).astype(F32)

    def load_block(index, k_nat, v_nat, kt):
        live = live_keys(index)
        for g in range(kv_heads):
            key = kv_all[index, g * hd : (g + 1) * hd, :].astype(F32)
            k_nat[g] = key.T.astype(BF16)
            kt[g] = (key * live).astype(BF16)
            value = kv_all[index, kv_cols + g * hd : kv_cols + (g + 1) * hd, :]
            v_nat[g] = value.astype(F32).T.astype(BF16)

    below = lax.broadcasted_iota(jnp.int32, (256, 256), 0) <= lax.broadcasted_iota(
        jnp.int32, (256, 256), 1
    )

    def segment(h, g, i, lo, hi, masked, k_nat, v_nat, kt):
        cols = slice(i * 256, (i + 1) * 256)
        hr = pl.ds(pl.multiple_of(h * hd, hd), hd)
        qi, oi = q_t[hr, cols], hg_t[hr, cols]
        p = jnp.exp(mm(k_nat[g, lo:hi, :], qi)) * inv_den[pl.ds(h, 1), cols]
        if masked:
            p = jnp.where(below, p, 0.0)
        dp = mm(v_nat[g, lo:hi, :], oi)
        ds = (p * (dp - delta[pl.ds(h, 1), cols])).astype(BF16)
        dq_t[hr, cols] += mm(kt[g, :, lo:hi], ds)
        dkv[g, :, lo:hi] += mm_nt(qi, ds)
        dkv[kv_heads + g, :, lo:hi] += mm_nt(oi, p.astype(BF16))

    dq_t[...] = jnp.zeros_like(dq_t)
    dkv[...] = jnp.zeros_like(dkv)
    give = remote(dkv_send, dkv_land, e_send.at[3], e_recv.at[3], at.x)

    @pl.when(c == 1)
    def _():
        load_block(0, k_own, v_own, kt_own)

        def one(h, _):
            for i in range(rows // 256):
                segment(h, h // group, i, 0, rows, False, k_own, v_own, kt_own)

            @pl.when(lax.rem(h, 2) == 1)
            def _():
                moves_ffn(2 + lax.div(h, 2))

            return 0

        lax.fori_loop(0, q_heads, one, 0)
        live = live_keys(0)
        for n in range(2 * kv_heads):
            dkv_send[n] = (dkv[n] * live).astype(BF16)
        give.start()
        dkv[...] = jnp.zeros_like(dkv)

    @pl.when(c == 0)
    def _():
        def one(h, _):
            moves_ffn(2 + h)
            return 0

        lax.fori_loop(0, q_heads // 2, one, 0)

    up.first()
    down.second()
    load_block(c, k_own, v_own, kt_own)

    def own_block(h, _):
        for i in range(rows // 256):
            segment(h, h // group, i, i * 256, (i + 1) * 256, True, k_own, v_own, kt_own)
            if i:
                segment(h, h // group, i, 0, i * 256, False, k_own, v_own, kt_own)


        @pl.when(lax.rem(h, 2) == 1)
        def _():
            moves_ffn(2 + lax.div(q_heads, 2) + lax.div(h, 2))

        return 0

    lax.fori_loop(0, q_heads, own_block, 0)
    moved = (2 + 2 * (q_heads // 2)) * PER_SLOT
    live = live_keys(c)
    for n in range(2 * kv_heads):
        dkv[n] = dkv[n] * live

    @pl.when(c == 0)
    def _():
        give.wait_recv()
        for n in range(2 * kv_heads):
            dkv[n] += dkv_land[n].astype(F32)

    here = pl.ds(pl.multiple_of(c * rows, rows), rows)
    gain_acc[...] = jnp.zeros_like(gain_acc)
    for cp in late:
        cp.wait()

    def through(which, row, grad, gain):
        x = proj_t[pl.ds(pl.multiple_of(row, hd), hd), :]
        scale = lax.rsqrt(jnp.mean(x * x, axis=0, keepdims=True) + EPSILON)
        xh = x * scale
        cosine, sine = cos_ref[:, here], sin_ref[:, here]
        a, b = grad[:halfd], grad[halfd:]
        grad = jnp.concatenate([a * cosine + b * sine, b * cosine - a * sine], axis=0)
        gain_acc[which] += grad * xh
        grad = grad * gain
        inner = jnp.mean(grad * xh, axis=0, keepdims=True)
        return scale * (grad - xh * inner)

    q_gain, k_gain = column(q_gain_ref, hd), column(k_gain_ref, hd)
    factor = 1.0 / math.sqrt(hd)

    def query_back(h, _):
        row = pl.multiple_of(h * hd, hd)
        r = pl.ds(row, hd)
        dq_t[r, :] = through(0, row, dq_t[r, :] * factor, q_gain)
        return 0

    lax.fori_loop(0, q_heads, query_back, 0)
    dqkv[:, 0:q_cols] = dq_t[...].T.astype(BF16)
    pair = jnp.concatenate(
        [through(1, q_cols + g * hd, dkv[g], k_gain) for g in range(kv_heads)], axis=0
    )
    dqkv[:, q_cols : q_cols + kv_cols] = pair.T.astype(BF16)
    pair = jnp.concatenate([dkv[kv_heads + g] for g in range(kv_heads)], axis=0)
    dqkv[:, q_cols + kv_cols :] = pair.T.astype(BF16)
    def as_row(v):
        return jnp.broadcast_to(v, (v.shape[0], 128)).T[0:1, :]

    qk[...] = jnp.zeros_like(qk)
    for n in (0, 1):
        qk[0, n : n + 1, 0:hd] = as_row(jnp.sum(gain_acc[n], axis=1, keepdims=True))

    def trade(n):
        dev = (at.sib, at.x, at.y)[n]
        return remote(qk.at[n], qk_land.at[n], e_send.at[n], e_recv.at[n], dev)

    def traded(n):
        trade(n).wait_recv()
        qk[n + 1] = qk[n] + qk_land[n]

    up.second()

    def final_d1(way, k, value):
        r = d1.rows(way, k)
        x = hid_ref[r, :].astype(F32)
        scale = lax.rsqrt(jnp.mean(x * x, axis=-1, keepdims=True) + EPSILON)
        h = x * scale
        inner = jnp.mean(value * h, axis=-1, keepdims=True)
        grad = rg_own[d1.local(k), :] + scale * (value - h * inner)
        inp[r, :] = grad.astype(BF16)

    ahead = LAG
    for q in range(4):
        r = slice(q * quarter, (q + 1) * quarter)
        d_part[r, :] = mm_nt(dqkv[r, :], wqkv[...]).astype(BF16)
        if q == 1:
            for step in range(ahead):
                d1.reduce(step, final_d1)

    def turn_hidden(i, _):
        r = pl.ds(pl.multiple_of(i * 128, 128), 128)
        x = hid_ref[r, :].astype(F32)
        scale = lax.rsqrt(jnp.mean(x * x, axis=-1, keepdims=True) + EPSILON)
        left_t[0, :, r] = (x * scale).astype(BF16).T
        left_t[1, :, r] = attn_low[r, :].T
        return 0

    def weight_part(w, _):
        r = pl.ds(pl.multiple_of(w * block, block), block)
        part[r, 0 : dqkv.shape[1]] = mm(left_t[0, r, :], dqkv[...]).astype(BF16)
        part[r, dqkv.shape[1] :] = mm(left_t[1, r, :], heads_own[...]).astype(BF16)
        return 0

    g_one = column(gain_one_ref, block)
    g_two = column(gain_two_ref, block)
    cols_acc[0] = jnp.broadcast_to(g_one, (block, 128))
    cols_acc[1] = jnp.broadcast_to(g_two, (block, 128))

    def use_down(r, value):
        g_down[r, :] = value[:, 0:units]

    def gate_gain():
        def piece(i, _):
            r = pl.ds(pl.multiple_of(i * 64, 64), 64)
            value = gate_sum[r, 0:units].astype(F32)
            total = jnp.sum(wg_ref[r, :].astype(F32) * value, axis=1, keepdims=True)
            cols_acc[3, r, :] = jnp.broadcast_to(total, (64, 128))
            return 0

        lax.fori_loop(0, block // 64, piece, 0)

    def use_up(r, value):
        value = value[:, 0:units]
        total = jnp.sum(wu_ref[r, :].astype(F32) * value, axis=1, keepdims=True)
        cols_acc[3, r, :] += jnp.broadcast_to(total, (64, 128))
        g_up[r, :] = value * cols_acc[1, r, 0:1]

    def use_rest(r, value):
        gain = cols_acc[0, r, 0:1]
        vq = value[:, 0:q_cols]
        vk = value[:, q_cols : q_cols + kv_cols]
        vv = value[:, q_cols + kv_cols : q_cols + 2 * kv_cols]
        total = jnp.sum(wq_ref[r, :].astype(F32) * vq, axis=1, keepdims=True)
        total += jnp.sum(wk_ref[r, :].astype(F32) * vk, axis=1, keepdims=True)
        total += jnp.sum(wv_ref[r, :].astype(F32) * vv, axis=1, keepdims=True)
        cols_acc[2, r, :] = jnp.broadcast_to(total, (64, 128))
        g_query[r, :] = vq * gain
        g_key[r, :] = vk * gain
        g_value[r, :] = vv * gain
        g_out[r, :] = value[:, q_cols + 2 * kv_cols :]

    def turn_all():
        lax.fori_loop(0, rows // 128, turn_hidden, 0)

    def parts():
        lax.fori_loop(0, width // block, weight_part, 0)
        rest.start()

    events = {
        0: (lambda: trade(0).start(), turn_all),
        1: (parts, lambda: traded(0), lambda: trade(1).start()),
        2: (lambda: traded(1), lambda: trade(2).start(), gate_gain),
        3: (rest.first, lambda: traded(2)),
        5: (lambda: down.finish(use_down),),
        6: (rest.second,),
        8: (lambda: up.finish(use_up),),
        10: (lambda: rest.finish(use_rest),),
    }

    def tail(step, _):
        d1.reduce(step + ahead, final_d1)
        back.step(step + ahead - last * LAG)
        move_ffn(step + moved)
        for when, todo in events.items():

            @pl.when(step == when * PER_SLOT)
            def _():
                for thing in todo:
                    thing()

        return 0

    lax.fori_loop(0, max(chunks + 2 * last * LAG, 10 * PER_SLOT + 1), tail, 0)
    keep_all(lambda cp: cp.start())

    def give_tile(d, owner):
        return remote(
            tile.at[owner], tile.at[owner], t_send.at[d], t_recv.at[d],
            at.z(lax.rem(t + d + 1, n_tp)),
        )

    tile[t] = jnp.zeros(tile.shape[1:], F32)
    tile[t, 0:1, 0:block] = cols_acc[2].T[0:1, :]
    tile[t, 1:2, 0:block] = cols_acc[3].T[0:1, :]
    tile[t, 2:4, 0:128] = qk[3, 0:2, :]
    for d in range(n_tp - 1):
        give_tile(d, t).start()
    for w in (down, up, rest):
        w.drain()
    for thing in (d1, back, ffn, ffn_back):
        thing.drain()
    keep_all(lambda cp: cp.wait())

    @pl.when(c == 1)
    def _():
        give.wait_send()

    for n in range(3):
        trade(n).wait_send()
    for d in range(n_tp - 1):
        give_tile(d, lax.rem(t + n_tp - d - 1, n_tp)).wait_recv()
    total = tile[0]
    for n in range(1, n_tp):
        total = total + tile[n]
    small[...] = total
    for d in range(n_tp - 1):
        give_tile(d, t).wait_send()


def call_c(mesh, chunks, args, kept):
    (hidden_in, seq_lengths, attn_gain, ffn_gain, query_gain, key_gain,
     w_query, w_key, w_value, w_gate, w_up) = args
    (attn_low, rg_own, gate_sum, ffn_part, wgrads, wqkv_full, wo_full, heads_all, q_t, kv_all, inv_den,
     proj_t) = kept
    n_shard, n_ctx, n_tp = mesh.shape["shard"], mesh.shape["ctx"], mesh.shape["tp"]
    rows, width = hidden_in.shape
    quarter = rows // 4
    hd = query_gain.shape[0]
    q_cols, kv_cols = w_query.shape[1], w_key.shape[1]
    qkv_cols = q_cols + 2 * kv_cols
    kv_heads = kv_cols // hd
    block, units = w_gate.shape
    padded = wgrads.shape[2]
    cosine, sine = rope_tables(n_ctx * rows, hd)
    vm = pl.BlockSpec(memory_space=pltpu.VMEM)
    hbm = pl.BlockSpec(memory_space=pltpu.HBM)
    sm = pl.BlockSpec(memory_space=pltpu.SMEM)
    S = jax.ShapeDtypeStruct
    V = pltpu.VMEM
    dma = pltpu.SemaphoreType.DMA
    return pl.pallas_call(
        functools.partial(kernel_c, (n_shard, n_tp, chunks, hd)),
        out_shape=(
            S((rows, width), BF16),
            S((rows, width), BF16),
            S((block, q_cols), F32),
            S((block, kv_cols), F32),
            S((block, kv_cols), F32),
            S((block, q_cols), F32),
            S((block, units), F32),
            S((block, units), F32),
            S((8, 256), F32),
        ),
        in_specs=[sm] + [vm] * 13 + [hbm] * 11,
        out_specs=(hbm,) + (vm,) * 8,
        scratch_shapes=[
            V((rows // 2, width), F32),
            V((rows, width), BF16),
            V((width, qkv_cols), BF16),
            V((qkv_cols, rows), F32),
            V((block, units), BF16),
            V((block, units), BF16),
            V((block, padded), BF16),
            V((rows, q_cols), BF16),
            V((width, q_cols), BF16),
            V((q_cols, rows), BF16),
            V((8, rows), F32),
            V((kv_heads, rows, hd), BF16),
            V((kv_heads, rows, hd), BF16),
            V((kv_heads, hd, rows), BF16),
            V((q_cols, rows), F32),
            V((2 * kv_heads, hd, rows), F32),
            V((2 * kv_heads, hd, rows), BF16),
            V((2 * kv_heads, hd, rows), BF16),
            V((2, hd, rows), F32),
            V((rows, qkv_cols), BF16),
            V((rows, width), BF16),
            V((rows, width), BF16),
            V((2, 2 * quarter, width), BF16),
            V((2, 2 * quarter, width), BF16),
            V((2, width, rows), BF16),
            V((width, qkv_cols + q_cols), BF16),
            V((2, 8 * block, padded), BF16),
            V((8 * block, qkv_cols + q_cols), BF16),
            V((4, block, 128), F32),
            V((4, 8, 128), F32),
            V((3, 8, 128), F32),
            V((n_tp, 8, 256), F32),
            dma((3, 7)),
            dma((3, 7)),
            dma((2, chunks)),
            dma((2, chunks)),
            dma((2, chunks)),
            dma((2, chunks)),
            dma((2, chunks)),
            dma((2, chunks)),
            dma((2, chunks)),
            dma((2, chunks)),
            dma((4,)),
            dma((4,)),
            dma((n_tp - 1,)),
            dma((n_tp - 1,)),
            dma((15,)),
        ],
        compiler_params=pltpu.CompilerParams(
            collective_id=2, has_side_effects=True, vmem_limit_bytes=VMEM_LIMIT
        ),
    )(
        seq_lengths, attn_low, q_t, kv_all, inv_den,
        attn_gain, ffn_gain, query_gain, key_gain, w_query, w_key, w_value,
        jnp.asarray(cosine), jnp.asarray(sine), rg_own, hidden_in, wqkv_full, proj_t,
        w_gate, w_up, gate_sum, ffn_part, wgrads, heads_all, wo_full,
    )


CHUNKS = 6
CHUNKS_C = 12
PER_STEP = 3
PER_SLOT = 2


def fast_body(mesh, *args):
    (hidden_in, seq_lengths, attn_gain, ffn_gain, query_gain, key_gain,
     w_query, w_key, w_value, w_out, w_gate, w_up, w_down, out_grad) = args
    (wqkv_full, wo_full, wg_full, wu_full, wd_full, heads_all, q_t, kv_all, inv_den, proj_t,
     resid, h2t, act) = call_a(mesh, args[:13])
    attn_low, rg_own, gate_sum, ffn_part, wgrads = call_b(
        mesh, CHUNKS, seq_lengths, out_grad, wd_full, act, wg_full, wu_full, h2t, resid
    )
    (block_out, inp, g_query, g_key, g_value, g_out, g_up, g_down, small) = call_c(
        mesh, CHUNKS_C,
        (hidden_in, seq_lengths, attn_gain, ffn_gain, query_gain, key_gain, w_query, w_key,
         w_value, w_gate, w_up),
        (attn_low, rg_own, gate_sum, ffn_part, wgrads, wqkv_full, wo_full, heads_all, q_t, kv_all, inv_den,
         proj_t),
    )
    block, hd = w_query.shape[0], query_gain.shape[0]
    g_gate = gate_sum[:, : w_gate.shape[1]].astype(F32) * ffn_gain.astype(F32)[:, None]
    return (
        block_out, inp.astype(F32), small[0, :block], small[1, :block], small[2, :hd],
        small[3, :hd], g_query, g_key, g_value, g_out.T, g_gate, g_up, g_down.T,
    )


def solution(mesh):
    sizes = mesh.shape
    plane_of_eight = sizes["shard"] == 4 and sizes["ctx"] == 2 and sizes["tp"] > 1
    run = functools.partial(fast_body, mesh) if plane_of_eight else body
    placed = (
        P(("shard", "ctx"), None),
        P("shard"),
        P(("shard", "ctx")),
        P(("shard", "ctx")),
        P(),
        P(),
        P(("shard", "ctx"), "tp"),
        P(("shard", "ctx"), "tp"),
        P(("shard", "ctx"), "tp"),
        P("tp", ("shard", "ctx")),
        P(("shard", "ctx"), "tp"),
        P(("shard", "ctx"), "tp"),
        P("tp", ("shard", "ctx")),
        P(("shard", "ctx"), None),
    )
    return jax.shard_map(
        run,
        mesh=mesh,
        in_specs=placed,
        out_specs=(
            P(("shard", "ctx"), None),
            P(("shard", "ctx"), None),
            P(("shard", "ctx")),
            P(("shard", "ctx")),
            P(),
            P(),
            P(("shard", "ctx"), "tp"),
            P(("shard", "ctx"), "tp"),
            P(("shard", "ctx"), "tp"),
            P("tp", ("shard", "ctx")),
            P(("shard", "ctx"), "tp"),
            P(("shard", "ctx"), "tp"),
            P("tp", ("shard", "ctx")),
        ),
        check_vma=False,
    )
```

```python
import functools
import math

import jax
import jax.numpy as jnp
import numpy as np
from jax import lax
from jax.experimental import pallas as pl
from jax.experimental.pallas import tpu as pltpu
from jax.sharding import PartitionSpec as P

EPSILON = 1e-05
ROPE_BASE = 1000000.0
MESH = pl.DeviceIdType.MESH
F32 = jnp.float32
BF16 = jnp.bfloat16
VMEM_LIMIT = 60 << 20


def norm_rows(value, gain):
    scale = lax.rsqrt(jnp.mean(value * value, axis=-1, keepdims=True) + EPSILON)
    return value * scale * gain


def rotate(values, positions):
    half = values.shape[-1] // 2
    freq = ROPE_BASE ** (-jnp.arange(half, dtype=jnp.float32) / half)
    angle = positions.astype(jnp.float32)[:, None] * freq[None, :]
    cosine = jnp.cos(angle)[:, None, :]
    sine = jnp.sin(angle)[:, None, :]
    first = values[..., :half]
    second = values[..., half:]
    return jnp.concatenate(
        [first * cosine - second * sine, second * cosine + first * sine], axis=-1
    )


def head_prep(proj, gain, positions):
    heads = proj.reshape(proj.shape[0], -1, gain.shape[0])
    return rotate(norm_rows(heads, gain), positions)


def activation(gate_in, up_in):
    return jax.nn.silu(gate_in) * up_in


def forward_product(left, right):
    return jnp.dot(left, right, preferred_element_type=jnp.float32)


def outer_product(left, right):
    return lax.dot_general(
        left, right, (((0,), (0,)), ((), ())), preferred_element_type=jnp.float32
    )


def back_product(grad, weight):
    return lax.dot_general(
        grad, weight, (((1,), (1,)), ((), ())), preferred_element_type=jnp.float32
    )


def body(
    hidden_in,
    seq_lengths,
    attn_gain,
    ffn_gain,
    query_gain,
    key_gain,
    w_query,
    w_key,
    w_value,
    w_out,
    w_gate,
    w_up,
    w_down,
    out_grad,
):
    rows = hidden_in.shape[0]
    head_dim = query_gain.shape[0]
    kv_heads = w_key.shape[1] // head_dim
    q_heads = w_query.shape[1] // head_dim
    group = q_heads // kv_heads
    pieces = lax.axis_size("ctx")
    scale = 1.0 / math.sqrt(head_dim)
    positions = lax.axis_index("ctx") * rows + jnp.arange(rows, dtype=jnp.int32)
    length = seq_lengths[0]
    valid = (positions < length).astype(jnp.float32)[:, None]
    live_blocks = jnp.minimum(lax.axis_index("ctx"), (length - 1) // rows) + 1
    gathered = (
        lax.all_gather(attn_gain, ("shard", "ctx"), axis=0, tiled=True),
        lax.all_gather(ffn_gain, ("shard", "ctx"), axis=0, tiled=True),
        lax.all_gather(w_query, ("shard", "ctx"), axis=0, tiled=True),
        lax.all_gather(w_key, ("shard", "ctx"), axis=0, tiled=True),
        lax.all_gather(w_value, ("shard", "ctx"), axis=0, tiled=True),
        lax.all_gather(w_gate, ("shard", "ctx"), axis=0, tiled=True),
        lax.all_gather(w_up, ("shard", "ctx"), axis=0, tiled=True),
        lax.all_gather(w_out, ("shard", "ctx"), axis=1, tiled=True),
        lax.all_gather(w_down, ("shard", "ctx"), axis=1, tiled=True),
    )
    gain_one = gathered[0].astype(jnp.float32)
    gain_two = gathered[1].astype(jnp.float32)
    full_query, full_key, full_value, full_gate, full_up, full_out, full_down = gathered[2:]
    q_gain = query_gain.astype(jnp.float32)
    k_gain = key_gain.astype(jnp.float32)
    hidden = hidden_in.astype(jnp.float32)
    normed_one = norm_rows(hidden, gain_one).astype(jnp.bfloat16)
    query_proj = forward_product(normed_one, full_query)
    key_proj = forward_product(normed_one, full_key)
    value_proj = forward_product(normed_one, full_value)
    queries = (
        head_prep(query_proj, q_gain, positions)
        .astype(jnp.bfloat16)
        .reshape(rows, kv_heads, group, head_dim)
    )
    keys_own = head_prep(key_proj, k_gain, positions).astype(jnp.bfloat16)
    values_own = value_proj.reshape(rows, kv_heads, head_dim).astype(jnp.bfloat16)
    keys_all, values_all = (
        lax.all_gather(keys_own, "ctx", axis=0, tiled=True),
        lax.all_gather(values_own, "ctx", axis=0, tiled=True),
    )
    key_blocks = keys_all.reshape(pieces, rows, kv_heads, head_dim)
    value_blocks = values_all.reshape(pieces, rows, kv_heads, head_dim)

    def key_at(index):
        return lax.dynamic_index_in_dim(key_blocks, index, 0, keepdims=False)

    def value_at(index):
        return lax.dynamic_index_in_dim(value_blocks, index, 0, keepdims=False)

    def block_scores(key_block, index):
        key_pos = index * rows + jnp.arange(rows, dtype=jnp.int32)
        mask = ((key_pos[None, :] <= positions[:, None]) & (key_pos[None, :] < length))[None, None]
        raw = (
            jnp.einsum("tkgd,skd->kgts", queries, key_block, preferred_element_type=jnp.float32)
            * scale
        )
        return (jnp.where(mask, raw, -1e30), mask)

    def stats_step(index, carry):
        top, total = carry
        masked, mask = block_scores(key_at(index), index)
        new_top = jnp.maximum(top, jnp.max(masked, axis=-1))
        weight = jnp.where(mask, jnp.exp(masked - new_top[..., None]), 0.0)
        total = total * jnp.exp(top - new_top) + jnp.sum(weight, axis=-1)
        return (new_top, total)

    start = (
        jnp.full((kv_heads, group, rows), -1e30, jnp.float32),
        jnp.zeros((kv_heads, group, rows), jnp.float32),
    )
    top, total = lax.fori_loop(0, live_blocks, stats_step, start)
    log_total = top + jnp.log(total)

    def probs_of(key_block, index):
        masked, mask = block_scores(key_block, index)
        return jnp.where(mask, jnp.exp(masked - log_total[..., None]), 0.0)

    def mix_step(index, accum):
        probs = probs_of(key_at(index), index).astype(jnp.bfloat16)
        return accum + jnp.einsum(
            "kgts,skd->tkgd", probs, value_at(index), preferred_element_type=jnp.float32
        )

    head_zeros = jnp.zeros((rows, kv_heads, group, head_dim), jnp.float32)
    mixed = lax.fori_loop(0, live_blocks, mix_step, head_zeros)
    heads_out = mixed.reshape(rows, -1).astype(jnp.bfloat16)
    attn_term = forward_product(heads_out, full_out)
    resid = hidden + lax.psum(attn_term, "tp")
    normed_two = norm_rows(resid, gain_two).astype(jnp.bfloat16)
    gate = forward_product(normed_two, full_gate)
    up = forward_product(normed_two, full_up)
    middle = activation(gate, up).astype(jnp.bfloat16)
    ffn_term = forward_product(middle, full_down)
    ffn = lax.psum(ffn_term.astype(jnp.bfloat16), "tp").astype(jnp.float32)
    block_out = (valid * (resid + ffn)).astype(jnp.bfloat16)
    grad_top = valid * out_grad.astype(jnp.float32)
    grad_low = grad_top.astype(jnp.bfloat16)
    down_wgrad = outer_product(middle, grad_low)
    mid_grad = back_product(grad_low, full_down)
    _, pull_act = jax.vjp(activation, gate, up)
    gate_float, up_float = pull_act(mid_grad)
    gate_low = gate_float.astype(jnp.bfloat16)
    up_low = up_float.astype(jnp.bfloat16)
    gate_wgrad = outer_product(normed_two, gate_low)
    up_wgrad = outer_product(normed_two, up_low)
    normed_two_part = back_product(gate_low, full_gate) + back_product(up_low, full_up)
    normed_two_grad = lax.psum(normed_two_part, "tp")
    _, pull_two = jax.vjp(norm_rows, resid, gain_two)
    resid_part, gain_two_grad = pull_two(normed_two_grad)
    resid_grad = grad_top + resid_part
    attn_low = resid_grad.astype(jnp.bfloat16)
    out_wgrad = outer_product(heads_out, attn_low)
    heads_grad = (
        back_product(attn_low, full_out)
        .astype(jnp.bfloat16)
        .reshape(rows, kv_heads, group, head_dim)
    )

    def delta_step(index, accum):
        probs = probs_of(key_at(index), index)
        prob_grad = jnp.einsum(
            "tkgd,skd->kgts", heads_grad, value_at(index), preferred_element_type=jnp.float32
        )
        return accum + jnp.sum(probs * prob_grad, axis=-1)

    delta = lax.fori_loop(
        0, live_blocks, delta_step, jnp.zeros((kv_heads, group, rows), jnp.float32)
    )

    def grad_step(index, carry):
        accum, key_store, value_store = carry
        key_block = key_at(index)
        probs = probs_of(key_block, index)
        prob_grad = jnp.einsum(
            "tkgd,skd->kgts", heads_grad, value_at(index), preferred_element_type=jnp.float32
        )
        score_grad = (probs * (prob_grad - delta[..., None])).astype(jnp.bfloat16)
        accum = (
            accum
            + jnp.einsum(
                "kgts,skd->tkgd", score_grad, key_block, preferred_element_type=jnp.float32
            )
            * scale
        )
        key_grad = (
            jnp.einsum("kgts,tkgd->skd", score_grad, queries, preferred_element_type=jnp.float32)
            * scale
        )
        value_grad = jnp.einsum(
            "kgts,tkgd->skd",
            probs.astype(jnp.bfloat16),
            heads_grad,
            preferred_element_type=jnp.float32,
        )
        key_store = lax.dynamic_update_index_in_dim(key_store, key_grad, index, 0)
        value_store = lax.dynamic_update_index_in_dim(value_store, value_grad, index, 0)
        return (accum, key_store, value_store)

    store_zeros = jnp.zeros((pieces, rows, kv_heads, head_dim), jnp.float32)
    query_grad, key_grads, value_grads = lax.fori_loop(
        0, live_blocks, grad_step, (head_zeros, store_zeros, store_zeros)
    )
    key_grad_own, value_grad_own = (
        lax.psum_scatter(
            key_grads.reshape(pieces * rows, kv_heads, head_dim),
            "ctx",
            scatter_dimension=0,
            tiled=True,
        ),
        lax.psum_scatter(
            value_grads.reshape(pieces * rows, kv_heads, head_dim),
            "ctx",
            scatter_dimension=0,
            tiled=True,
        ),
    )

    def query_prep(proj, gain):
        return head_prep(proj, gain, positions)

    _, pull_query = jax.vjp(query_prep, query_proj, q_gain)
    query_proj_grad, q_gain_grad = pull_query(query_grad.reshape(rows, q_heads, head_dim))
    _, pull_key = jax.vjp(query_prep, key_proj, k_gain)
    key_proj_grad, k_gain_grad = pull_key(key_grad_own)
    query_low = query_proj_grad.astype(jnp.bfloat16)
    key_low = key_proj_grad.astype(jnp.bfloat16)
    value_low = value_grad_own.reshape(rows, -1).astype(jnp.bfloat16)
    query_wgrad = outer_product(normed_one, query_low)
    key_wgrad = outer_product(normed_one, key_low)
    value_wgrad = outer_product(normed_one, value_low)
    normed_one_part = (
        back_product(query_low, full_query)
        + back_product(key_low, full_key)
        + back_product(value_low, full_value)
    )
    normed_one_grad = lax.psum(normed_one_part, "tp")
    _, pull_one = jax.vjp(norm_rows, hidden, gain_one)
    hidden_part, gain_one_grad = pull_one(normed_one_grad)
    input_grad = resid_grad + hidden_part
    head_sums = lax.psum((q_gain_grad, k_gain_grad), ("shard", "ctx", "tp"))
    summed = (
        lax.psum_scatter(gain_one_grad, ("shard", "ctx"), scatter_dimension=0, tiled=True),
        lax.psum_scatter(gain_two_grad, ("shard", "ctx"), scatter_dimension=0, tiled=True),
        lax.psum_scatter(query_wgrad, ("shard", "ctx"), scatter_dimension=0, tiled=True),
        lax.psum_scatter(key_wgrad, ("shard", "ctx"), scatter_dimension=0, tiled=True),
        lax.psum_scatter(value_wgrad, ("shard", "ctx"), scatter_dimension=0, tiled=True),
        lax.psum_scatter(gate_wgrad, ("shard", "ctx"), scatter_dimension=0, tiled=True),
        lax.psum_scatter(up_wgrad, ("shard", "ctx"), scatter_dimension=0, tiled=True),
        lax.psum_scatter(out_wgrad, ("shard", "ctx"), scatter_dimension=1, tiled=True),
        lax.psum_scatter(down_wgrad, ("shard", "ctx"), scatter_dimension=1, tiled=True),
    )
    (
        gain_one_out,
        gain_two_out,
        query_out,
        key_out,
        value_out,
        gate_out,
        up_out,
        out_out,
        down_out,
    ) = summed
    return (
        block_out,
        input_grad,
        gain_one_out,
        gain_two_out,
        head_sums[0],
        head_sums[1],
        query_out,
        key_out,
        value_out,
        out_out,
        gate_out,
        up_out,
        down_out,
    )


def remote(src, dst, send, recv, dev):
    return pltpu.make_async_remote_copy(
        src_ref=src,
        dst_ref=dst,
        send_sem=send,
        recv_sem=recv,
        device_id=dev,
        device_id_type=MESH,
    )


def mm(a, b):
    return jnp.dot(a, b, preferred_element_type=F32)


def mm_nt(a, b):
    return lax.dot_general(a, b, (((1,), (1,)), ((), ())), preferred_element_type=F32)


def round_up(units):
    return -(-units // 256) * 256


class Place:
    def __init__(self, n_shard, n_tp):
        s = lax.axis_index("shard")
        c = lax.axis_index("ctx")
        t = lax.axis_index("tp")
        self.s, self.c, self.t = s, c, t
        self.core = lax.rem(s, 2)
        sib = s + 1 - 2 * self.core
        far = lax.rem(s + 2, n_shard)
        far_sib = far + 1 - 2 * self.core
        self.sib = (sib, c, t)
        self.x = (s, 1 - c, t)
        self.y = (far, c, t)
        first = 1 - self.core
        self.relay = (
            first * s + self.core * far,
            first * (1 - c) + self.core * c,
            t,
        )
        slot = lambda a, b: a * 2 + b
        self.own = slot(s, c)
        self.slots = {
            "S": slot(sib, c),
            "X": slot(s, 1 - c),
            "Y": slot(far, c),
            "D": slot(far, 1 - c),
            "SX": slot(sib, 1 - c),
            "SY": slot(far_sib, c),
            "SD": slot(far_sib, 1 - c),
        }
        self.relayed = first * self.slots["Y"] + self.core * self.slots["X"]
        self.n_tp = n_tp

    def z(self, t):
        return (self.s, self.c, t)

    def greet(self):
        peers = [self.sib, self.x, self.y]
        peers += [
            self.z(lax.rem(self.t + d, self.n_tp)) for d in range(1, self.n_tp)
        ]
        barrier = pltpu.get_barrier_semaphore()
        for peer in peers:
            pl.semaphore_signal(barrier, inc=1, device_id=peer, device_id_type=MESH)
        pl.semaphore_wait(barrier, len(peers))


ROLES = ("S", "X", "Y", "D", "SX", "SY", "SD")


class Gather:
    def __init__(self, at, own, full, send, recv, index, stride=0, first=0):
        self.at, self.own, self.full = at, own, full
        self.send, self.recv, self.index = send, recv, index
        self.rows, self.first = own.shape[0], first
        self.stride = stride or self.rows

    def block(self, slot):
        start = slot * self.stride + self.first
        return self.full.at[pl.ds(pl.multiple_of(start, self.rows), self.rows)]

    def copy(self, role, src, slot, dev):
        k = ROLES.index(role)
        return remote(
            src,
            self.block(slot),
            self.send.at[self.index, k],
            self.recv.at[self.index, k],
            dev,
        )

    def arrived(self, role):
        slot = self.at.slots[role]
        self.copy(role, self.block(slot), slot, self.at.sib).wait_recv()

    def start_x(self):
        self.copy("X", self.own, self.at.own, self.at.x).start()

    def start_y(self):
        self.copy("Y", self.own, self.at.own, self.at.y).start()

    def start_s(self):
        self.copy("S", self.own, self.at.own, self.at.sib).start()

    def start(self):
        self.start_x()
        self.start_y()
        self.start_s()

    def relay(self):
        at = self.at
        self.arrived("X")
        self.arrived("Y")
        self.copy("D", self.block(at.relayed), at.relayed, at.relay).start()
        for role in ("X", "Y"):
            slot = at.slots[role]
            self.copy("S" + role, self.block(slot), slot, at.sib).start()

    def relay_last(self):
        self.arrived("D")
        slot = self.at.slots["D"]
        self.copy("SD", self.block(slot), slot, self.at.sib).start()

    def finish(self):
        for role in ("S", "SX", "SY", "SD"):
            self.arrived(role)
        for role in ROLES:
            self.copy(role, self.own, self.at.own, self.at.sib).wait_send()


def column(row_ref, n):
    wide = jnp.broadcast_to(row_ref[...].astype(F32)[None, :], (8, n))
    return wide.T[:, 0:1]


def kernel_a(
    shape,
    length_ref,
    hid_ref,
    gain_one_ref,
    gain_two_ref,
    q_gain_ref,
    k_gain_ref,
    wq_ref,
    wk_ref,
    wv_ref,
    wo_ref,
    wg_ref,
    wu_ref,
    wd_ref,
    cos_ref,
    sin_ref,
    wqkv_out,
    wo_out,
    wg_full,
    wu_full,
    wd_full,
    heads_out,
    q_out,
    kv_out,
    inv_den,
    proj_out,
    resid_out,
    h2t_out,
    act_out,
    wqkv_full,
    wo_full,
    heads_all,
    q_t,
    kv_all,
    proj_t,
    resid,
    h2,
    h2t,
    s_qkv,
    s_woz,
    s_wg,
    s_wu,
    s_wd,
    wg,
    wu,
    act,
    h1,
    k_own,
    k_off,
    v_own,
    v_off,
    acc,
    g_send,
    g_recv,
    z_send,
    z_recv,
    h_send,
    h_recv,
    kv_sem,
    loc_sem,
    act_sem,
    out_sem,
):
    n_shard, n_tp, hd = shape
    at = Place(n_shard, n_tp)
    c, t = at.c, at.t
    rows, width = hid_ref.shape
    q_cols, kv_cols = wq_ref.shape[1], wk_ref.shape[1]
    q_heads, kv_heads = q_cols // hd, kv_cols // hd
    group = q_heads // kv_heads
    half = hd // 2
    at.greet()
    leaving = [
        pltpu.make_async_copy(src, dst, out_sem.at[i])
        for i, (src, dst) in enumerate(
            (
                (wqkv_full, wqkv_out),
                (proj_t, proj_out),
                (q_t, q_out),
                (kv_all, kv_out),
                (heads_all, heads_out),
                (wo_full, wo_out),
                (resid, resid_out),
                (h2t, h2t_out),
            )
        )
    ]

    col_one = column(gain_one_ref, gain_one_ref.shape[0])
    s_qkv[:, 0:q_cols] = (wq_ref[...].astype(F32) * col_one).astype(BF16)
    s_qkv[:, q_cols : q_cols + kv_cols] = (wk_ref[...].astype(F32) * col_one).astype(BF16)
    s_qkv[:, q_cols + kv_cols :] = (wv_ref[...].astype(F32) * col_one).astype(BF16)
    qkv = Gather(at, s_qkv, wqkv_full, g_send, g_recv, 0)
    out = Gather(at, s_woz, wo_full, g_send, g_recv, 1)
    gate = Gather(at, s_wg, wg_full, g_send, g_recv, 2)
    up = Gather(at, s_wu, wu_full, g_send, g_recv, 3)
    down = Gather(at, s_wd, wd_full, g_send, g_recv, 4)
    gathers = (qkv, out, gate, up, down)
    local = [
        pltpu.make_async_copy(g.own, g.block(at.own), loc_sem.at[i])
        for i, g in enumerate(gathers)
    ]
    loads = [
        pltpu.make_async_copy(wg_full, wg, loc_sem.at[5]),
        pltpu.make_async_copy(wu_full, wu, loc_sem.at[6]),
    ]
    qkv.start()
    local[0].start()

    wo_cols = pl.ds(pl.multiple_of(t * q_cols, q_cols), q_cols)
    s_woz[:, wo_cols] = wo_ref[...]

    def wo_part(d, owner):
        cols = pl.ds(pl.multiple_of(owner * q_cols, q_cols), q_cols)
        return remote(
            s_woz.at[:, cols],
            s_woz.at[:, cols],
            z_send.at[d],
            z_recv.at[d],
            at.z(lax.rem(t + d + 1, n_tp)),
        )

    for d in range(n_tp - 1):
        wo_part(d, t).start()

    def norm_one(i, _):
        r = pl.ds(pl.multiple_of(i * 64, 64), 64)
        x = hid_ref[r, :].astype(F32)
        scale = lax.rsqrt(jnp.mean(x * x, axis=-1, keepdims=True) + EPSILON)
        h1[r, :] = (x * scale).astype(BF16)
        return 0

    lax.fori_loop(0, rows // 64, norm_one, 0)
    qkv.relay()
    col_two = column(gain_two_ref, gain_two_ref.shape[0])
    units = wg_ref.shape[1]
    for src, dst in ((wg_ref, s_wg), (wu_ref, s_wu)):
        dst[:, 0:units] = (src[...].astype(F32) * col_two).astype(BF16)
        dst[:, units:] = jnp.zeros((dst.shape[0], dst.shape[1] - units), BF16)
    s_wd[:, 0:units] = wd_ref[...]
    s_wd[:, units:] = jnp.zeros((s_wd.shape[0], s_wd.shape[1] - units), BF16)
    qkv.relay_last()
    for d in range(n_tp - 1):
        wo_part(d, lax.rem(t + n_tp - d - 1, n_tp)).wait_recv()
    out.start()
    gate.start_y()
    local[0].wait()
    for cp in local[1:]:
        cp.start()
    qkv.finish()

    def project(i, _):
        r = pl.ds(pl.multiple_of(i * 256, 256), 256)
        proj_t[:, r] = mm(h1[r, :], wqkv_full[...]).T
        return 0

    lax.fori_loop(0, rows // 256, project, 0)
    leaving[0].start()
    leaving[1].start()
    here = pl.ds(pl.multiple_of(c * rows, rows), rows)
    k_gain = column(k_gain_ref, hd)
    q_gain = column(q_gain_ref, hd)

    def prepared(row, gain, factor):
        x = proj_t[pl.ds(pl.multiple_of(row, hd), hd), :]
        scale = lax.rsqrt(jnp.mean(x * x, axis=0, keepdims=True) + EPSILON)
        y = x * (scale * factor) * gain
        a, b = y[:half], y[half:]
        cosine, sine = cos_ref[:, here], sin_ref[:, here]
        return jnp.concatenate([a * cosine - b * sine, b * cosine + a * sine], axis=0)

    for g in range(kv_heads):
        key = prepared(q_cols + g * hd, k_gain, 1.0).astype(BF16)
        kv_all[c, g * hd : (g + 1) * hd, :] = key
    kv_all[c, kv_cols:, :] = proj_t[q_cols + kv_cols :, :].astype(BF16)
    kv_copy = remote(kv_all.at[c], kv_all.at[c], kv_sem.at[0], kv_sem.at[1], at.x)
    kv_back = remote(
        kv_all.at[1 - c], kv_all.at[1 - c], kv_sem.at[0], kv_sem.at[1], at.x
    )

    @pl.when(c == 0)
    def _():
        kv_copy.start()

    gate.start_x()
    gate.start_s()

    def prep_q(h, _):
        r = pl.multiple_of(h * hd, hd)
        q_t[pl.ds(r, hd), :] = prepared(r, q_gain, 1.0 / math.sqrt(hd)).astype(BF16)
        return 0

    lax.fori_loop(0, q_heads, prep_q, 0)
    leaving[2].start()
    length = length_ref[0]

    def load_block(index, k_nat, v_ext):
        pos = index * rows + lax.broadcasted_iota(jnp.int32, (1, rows), 1)
        live = (pos < length).astype(F32)
        first = (lax.broadcasted_iota(jnp.int32, (16, rows), 0) == 0).astype(F32)
        for g in range(kv_heads):
            k_nat[g] = kv_all[index, g * hd : (g + 1) * hd, :].astype(F32).T.astype(BF16)
            v = kv_all[index, kv_cols + g * hd : kv_cols + (g + 1) * hd, :].astype(F32)
            v_ext[g, 0:hd, :] = (v * live).astype(BF16)
            v_ext[g, hd:, :] = (first * live).astype(BF16)

    load_block(c, k_own, v_own)
    below = lax.broadcasted_iota(jnp.int32, (256, 256), 0) <= lax.broadcasted_iota(
        jnp.int32, (256, 256), 1
    )

    def own_block(h, _):
        g = h // group
        qh = q_t[pl.ds(pl.multiple_of(h * hd, hd), hd), :]
        for i in range(rows // 256):
            qi = qh[:, i * 256 : (i + 1) * 256]
            top = i * 256
            e = jnp.exp(mm(k_own[g, top : top + 256, :], qi))
            e = jnp.where(below, e, 0.0).astype(BF16)
            total = mm(v_own[g, :, top : top + 256], e)
            if i:
                e = jnp.exp(mm(k_own[g, 0:top, :], qi)).astype(BF16)
                total += mm(v_own[g, :, 0:top], e)
            acc[h, :, top : top + 256] = total
        return 0

    lax.fori_loop(0, q_heads, own_block, 0)
    out.relay()
    up.start()

    @pl.when(c == 1)
    def _():
        kv_back.wait_recv()
        load_block(1 - c, k_off, v_off)

        def other_block(h, _):
            g = h // group
            qh = q_t[pl.ds(pl.multiple_of(h * hd, hd), hd), :]
            for i in range(rows // 256):
                cols = slice(i * 256, (i + 1) * 256)
                e = jnp.exp(mm(k_off[g], qh[:, cols])).astype(BF16)
                acc[h, :, cols] += mm(v_off[g], e)
            return 0

        lax.fori_loop(0, q_heads, other_block, 0)

    @pl.when(c == 0)
    def _():
        kv_all[1 - c] = jnp.zeros(kv_all.shape[1:], BF16)

    leaving[3].start()

    def chunk_cols(owner, j):
        return pl.ds(pl.multiple_of(owner * q_cols + j * 128, 128), 128)

    def along(owner, j, way):
        ref = heads_all.at[:, chunk_cols(owner, j)]
        dev = at.z(jnp.minimum(t + 1, n_tp - 1) if way == 0 else jnp.maximum(t - 1, 0))
        return remote(ref, ref, h_send.at[way, owner, j], h_recv.at[way, owner, j], dev)

    chunks = q_cols // 128

    def pass_on(owner, j, way):
        @pl.when(t < n_tp - 1 if way == 0 else t > 0)
        def _():
            along(owner, j, way).start()

    for j in range(chunks):
        parts = []
        for h in range(2 * j, 2 * j + 2):
            inverse = 1.0 / acc[h, hd : hd + 1, :]
            inv_den[h : h + 1, :] = inverse
            parts.append(acc[h, 0:hd, :] * inverse)
        pair = jnp.concatenate(parts, axis=0)
        heads_all[:, chunk_cols(t, j)] = pair.T.astype(BF16)
        for way in (0, 1):
            pass_on(t, j, way)
    inv_den[q_heads:, :] = jnp.zeros((8 - q_heads, rows), F32)

    for d in range(1, n_tp):
        for j in range(chunks):

            @pl.when(t >= d)
            def _():
                along(t - d, j, 0).wait_recv()
                pass_on(t - d, j, 0)

            @pl.when(t + d < n_tp)
            def _():
                along(t + d, j, 1).wait_recv()
                pass_on(t + d, j, 1)

            step = (d - 1) * chunks + j
            if step == 2:
                gate.relay()
            if step == 4:
                out.relay_last()
            if step == 7:
                up.relay()
                down.start()

    out.finish()
    local[1].wait()
    leaving[4].start()
    leaving[5].start()

    def residual(i, _):
        r = pl.ds(pl.multiple_of(i * 128, 128), 128)
        x = hid_ref[r, :].astype(F32) + mm_nt(heads_all[r, :], wo_full[...])
        resid[r, :] = x
        scale = lax.rsqrt(jnp.mean(x * x, axis=-1, keepdims=True) + EPSILON)
        h = (x * scale).astype(BF16)
        h2[r, :] = h
        h2t[:, r] = h.T

        @pl.when(i == 1)
        def _():
            gate.relay_last()

        @pl.when(i == 3)
        def _():
            gate.finish()
            local[2].wait()
            loads[0].start()

        return 0

    lax.fori_loop(0, rows // 128, residual, 0)
    leaving[6].start()
    leaving[7].start()
    up.relay_last()
    up.finish()
    local[3].wait()
    loads[1].start()
    loads[0].wait()
    loads[1].wait()
    tiles = act.shape[2] // 256
    half = rows // 2

    def act_copy(f):
        cols = pl.ds(pl.multiple_of(f * 256, 256), 256)
        return pltpu.make_async_copy(
            act.at[:, :, cols], act_out.at[:, :, cols], act_sem.at[f]
        )

    def gate_up(f, _):
        cols = pl.ds(pl.multiple_of(f * 256, 256), 256)
        for i in (0, 1):
            r = slice(i * half, (i + 1) * half)
            g = mm(h2[r, :], wg[:, cols])
            u = mm(h2[r, :], wu[:, cols])
            s = 1.0 / (1.0 + jnp.exp(-g))
            silu = g * s
            act[0, r, cols] = (silu * u).astype(BF16)
            act[1, r, cols] = (u * (s * (1.0 + g * (1.0 - s)))).astype(BF16)
            act[2, r, cols] = silu.astype(BF16)

        act_copy(f).start()

        @pl.when(f == tiles - 2)
        def _():
            down.relay()

        return 0

    lax.fori_loop(0, tiles, gate_up, 0)
    down.relay_last()
    down.finish()
    local[4].wait()

    def act_done(f, _):
        act_copy(f).wait()
        return 0

    lax.fori_loop(0, tiles, act_done, 0)
    for owner in range(n_tp):
        for j in range(chunks):

            @pl.when(jnp.logical_and(t < n_tp - 1, owner <= t))
            def _():
                along(owner, j, 0).wait_send()

            @pl.when(jnp.logical_and(t > 0, owner >= t))
            def _():
                along(owner, j, 1).wait_send()

    for d in range(n_tp - 1):
        wo_part(d, t).wait_send()

    @pl.when(c == 0)
    def _():
        kv_copy.wait_send()

    for cp in leaving:
        cp.wait()


def rope_tables(positions, hd):
    freq = ROPE_BASE ** (-np.arange(hd // 2, dtype=np.float64) / (hd // 2))
    angle = freq[:, None] * np.arange(positions, dtype=np.float64)[None, :]
    return np.cos(angle).astype(np.float32), np.sin(angle).astype(np.float32)


def call_a(mesh, args):
    (hidden_in, seq_lengths, attn_gain, ffn_gain, query_gain, key_gain,
     w_query, w_key, w_value, w_out, w_gate, w_up, w_down) = args
    n_shard, n_ctx, n_tp = mesh.shape["shard"], mesh.shape["ctx"], mesh.shape["tp"]
    rows, width = hidden_in.shape
    hd = query_gain.shape[0]
    q_cols, kv_cols = w_query.shape[1], w_key.shape[1]
    q_heads, kv_heads = q_cols // hd, kv_cols // hd
    block = w_query.shape[0]
    padded = round_up(w_gate.shape[1])
    cosine, sine = rope_tables(n_ctx * rows, hd)
    vm = pl.BlockSpec(memory_space=pltpu.VMEM)
    hbm = pl.BlockSpec(memory_space=pltpu.HBM)
    sm = pl.BlockSpec(memory_space=pltpu.SMEM)
    qkv_cols = q_cols + 2 * kv_cols
    S = jax.ShapeDtypeStruct
    dma = pltpu.SemaphoreType.DMA
    chunks = q_cols // 128
    return pl.pallas_call(
        functools.partial(kernel_a, (n_shard, n_tp, hd)),
        out_shape=(
            S((width, qkv_cols), BF16),
            S((width, n_tp * q_cols), BF16),
            S((width, padded), BF16),
            S((width, padded), BF16),
            S((width, padded), BF16),
            S((rows, n_tp * q_cols), BF16),
            S((q_cols, rows), BF16),
            S((n_ctx, 2 * kv_cols, rows), BF16),
            S((8, rows), F32),
            S((qkv_cols, rows), F32),
            S((rows, width), F32),
            S((width, rows), BF16),
            S((3, rows, padded), BF16),
        ),
        in_specs=[sm] + [vm] * 14,
        out_specs=(hbm,) * 8 + (vm,) + (hbm,) * 4,
        scratch_shapes=[
            pltpu.VMEM((width, qkv_cols), BF16),
            pltpu.VMEM((width, n_tp * q_cols), BF16),
            pltpu.VMEM((rows, n_tp * q_cols), BF16),
            pltpu.VMEM((q_cols, rows), BF16),
            pltpu.VMEM((n_ctx, 2 * kv_cols, rows), BF16),
            pltpu.VMEM((qkv_cols, rows), F32),
            pltpu.VMEM((rows, width), F32),
            pltpu.VMEM((rows, width), BF16),
            pltpu.VMEM((width, rows), BF16),
            pltpu.VMEM((block, qkv_cols), BF16),
            pltpu.VMEM((block, n_tp * q_cols), BF16),
            pltpu.VMEM((block, padded), BF16),
            pltpu.VMEM((block, padded), BF16),
            pltpu.VMEM((block, padded), BF16),
            pltpu.VMEM((width, padded), BF16),
            pltpu.VMEM((width, padded), BF16),
            pltpu.VMEM((3, rows, padded), BF16),
            pltpu.VMEM((rows, width), BF16),
            pltpu.VMEM((kv_heads, rows, hd), BF16),
            pltpu.VMEM((kv_heads, rows, hd), BF16),
            pltpu.VMEM((kv_heads, hd + 16, rows), BF16),
            pltpu.VMEM((kv_heads, hd + 16, rows), BF16),
            pltpu.VMEM((q_heads, hd + 16, rows), F32),
            dma((5, 7)),
            dma((5, 7)),
            dma((n_tp - 1,)),
            dma((n_tp - 1,)),
            dma((2, n_tp, chunks)),
            dma((2, n_tp, chunks)),
            dma((2,)),
            dma((7,)),
            dma((padded // 256,)),
            dma((8,)),
        ],
        compiler_params=pltpu.CompilerParams(
            collective_id=0, has_side_effects=True, vmem_limit_bytes=VMEM_LIMIT
        ),
    )(
        seq_lengths, hidden_in, attn_gain, ffn_gain,
        query_gain, key_gain, w_query, w_key, w_value,
        w_out.T, w_gate, w_up, w_down.T, jnp.asarray(cosine), jnp.asarray(sine),
    )


LAG = 2


class Line:
    def __init__(self, at, part, landing, send, recv, chunks, folds=1):
        self.at, self.part, self.landing = at, part, landing
        self.send, self.recv, self.chunks, self.folds = send, recv, chunks, folds
        self.half = landing.shape[1]
        self.size = self.half // chunks
        self.last = at.n_tp - 1

    def pos(self, way):
        return self.at.t if way == 0 else self.last - self.at.t

    def dev(self, way, step):
        to = self.at.t + (step if way == 0 else -step)
        return self.at.z(jnp.clip(to, 0, self.last))

    def local(self, k):
        return pl.ds(pl.multiple_of(k * self.size, self.size), self.size)

    def rows(self, way, k):
        return pl.ds(self.start(way, k), self.size)

    def start(self, way, k):
        fold = self.half // self.folds
        if self.folds == 1:
            first = (1 - way) * fold + k * self.size
        else:
            per = self.chunks // self.folds
            group = lax.div(k, per)
            first = (2 * group + 1 - way) * fold + (k - group * per) * self.size
        return pl.multiple_of(first, self.size)

    def copy(self, way, k):
        return remote(
            self.part.at[self.rows(way, k)],
            self.landing.at[way, self.local(k)],
            self.send.at[way, k],
            self.recv.at[way, k],
            self.dev(way, 1),
        )

    def reduce(self, step, final):
        for way in (0, 1):
            pos = self.pos(way)
            k = step - pos * LAG
            live = jnp.logical_and(k >= 0, k < self.chunks)

            @pl.when(jnp.logical_and(live, pos > 0))
            def _():
                self.copy(way, k).wait_recv()
                value = self.part[self.rows(way, k), :].astype(F32)
                value += self.landing[way, self.local(k), :].astype(F32)

                @pl.when(pos < self.last)
                def _():
                    self.part[self.rows(way, k), :] = value.astype(BF16)

                @pl.when(pos == self.last)
                def _():
                    final(way, k, value)

            @pl.when(jnp.logical_and(live, pos < self.last))
            def _():
                self.copy(way, k).start()

    def drain(self):
        for way in (0, 1):

            @pl.when(self.pos(way) < self.last)
            def _():
                def one(k, _):
                    self.copy(way, k).wait_send()
                    return 0

                lax.fori_loop(0, self.chunks, one, 0)


class Back:
    def __init__(self, line, whole, send, recv, source=None):
        self.line, self.whole, self.send, self.recv = line, whole, send, recv
        self.source = source

    def copy(self, way, k, first=False):
        line = self.line
        dst = self.whole.at[line.rows(way, k)]
        src = self.source.at[way, line.local(k)] if first and self.source is not None else dst
        return remote(src, dst, self.send.at[way, k], self.recv.at[way, k], line.dev(way, -1))

    def step(self, step):
        line = self.line
        for way in (0, 1):
            pos = line.pos(way)
            k = step - (line.last - pos) * LAG
            live = jnp.logical_and(k >= 0, k < line.chunks)

            @pl.when(jnp.logical_and(live, pos < line.last))
            def _():
                self.copy(way, k).wait_recv()

                @pl.when(pos > 0)
                def _():
                    self.copy(way, k).start()

            @pl.when(jnp.logical_and(live, pos == line.last))
            def _():
                self.copy(way, k, True).start()

    def drain(self):
        line = self.line
        for way in (0, 1):

            @pl.when(line.pos(way) > 0)
            def _():
                def one(k, _):
                    self.copy(way, k).wait_send()
                    return 0

                lax.fori_loop(0, line.chunks, one, 0)


class Scatter:
    def __init__(self, at, source, room, tmp_sem, send, recv, index):
        self.at, self.source, self.room = at, source, room
        self.tmp_sem, self.send, self.recv, self.index = tmp_sem, send, recv, index
        self.rows = room.shape[0] // 8
        self.tmp, self.relayed = self.land(7), self.land(4)
        self.final = (self.land(5), self.land(6))
        self.direct, self.indirect = 1 + at.core, 2 - at.core
        self.other = (
            at.core * at.x[0] + (1 - at.core) * at.y[0],
            at.core * at.x[1] + (1 - at.core) * at.y[1],
            at.t,
        )
        self.mine = [at.own] + [at.slots[n] for n in ("X", "Y", "D")]
        self.theirs = [at.slots[n] for n in ("S", "SX", "SY", "SD")]

    def land(self, j):
        return self.room.at[pl.ds(pl.multiple_of(j * self.rows, self.rows), self.rows)]

    def block(self, slot):
        return self.source.at[pl.ds(pl.multiple_of(slot * self.rows, self.rows), self.rows)]

    def copy(self, k, src, dst, dev):
        return remote(src, dst, self.send.at[self.index, k], self.recv.at[self.index, k], dev)

    def share(self, j):
        return self.copy(j, self.block(self.theirs[j]), self.land(j), self.at.sib)

    def start(self):
        for j in (3, 1, 2, 0):
            self.share(j).start()
        self.fetch(3).start()

    def slot(self, j):
        if isinstance(j, int):
            return self.mine[j]
        return jnp.where(j == 1, self.mine[1], self.mine[2])

    def arrived(self, j):
        ref = self.land(j)
        self.copy(j, ref, ref, self.at.sib).wait_recv()

    def fetch(self, j):
        return pltpu.make_async_copy(self.block(self.slot(j)), self.tmp, self.tmp_sem)

    def add(self, j, extra=()):
        self.arrived(j)
        self.fetch(j).wait()
        land = self.land(j)

        def piece(i, _):
            r = pl.ds(pl.multiple_of(i * 64, 64), 64)
            value = land[r, :].astype(F32) + self.tmp[r, :].astype(F32)
            for ref in extra:
                value += ref[r, :].astype(F32)
            land[r, :] = value.astype(BF16)
            return 0

        lax.fori_loop(0, self.rows // 64, piece, 0)

    def hop(self, k):
        at = self.at
        if k == 4:
            return self.copy(4, self.land(3), self.relayed, at.relay)
        if k == 5:
            return self.copy(5, self.land(self.direct), self.final[0], at.relay)
        return self.copy(6, self.land(self.indirect), self.final[1], self.other)

    def first(self):
        self.add(3)
        self.fetch(self.direct).start()
        self.hop(4).start()
        self.add(self.direct)
        self.fetch(self.indirect).start()
        self.hop(5).start()

    def second(self):
        self.hop(4).wait_recv()
        self.add(self.indirect, (self.relayed,))
        self.fetch(0).start()
        self.hop(6).start()

    def finish(self, use):
        self.arrived(0)
        self.hop(5).wait_recv()
        self.hop(6).wait_recv()
        self.fetch(0).wait()
        land = self.land(0)

        def piece(i, _):
            r = pl.ds(pl.multiple_of(i * 64, 64), 64)
            value = land[r, :].astype(F32) + self.tmp[r, :].astype(F32)
            value += self.final[0][r, :].astype(F32) + self.final[1][r, :].astype(F32)
            use(r, value)
            return 0

        lax.fori_loop(0, self.rows // 64, piece, 0)

    def drain(self):
        for j in range(4):
            self.share(j).wait_send()
        for k in (4, 5, 6):
            self.hop(k).wait_send()


def kernel_b(
    shape,
    length_ref,
    og_ref,
    wd_hbm,
    act_hbm,
    wg_hbm,
    wu_hbm,
    h2t_hbm,
    resid_hbm,
    attn_low,
    rg_out,
    gate_out,
    ffn_part,
    wgrads,
    rg_own,
    gate_sum,
    f_part,
    d_part,
    wg,
    wu,
    wd,
    resid,
    left_t,
    gl,
    act,
    land_d,
    stage,
    d_send,
    d_recv,
    b_send,
    b_recv,
    s_send,
    s_recv,
    loc_sem,
    tile_sem,
    st_sem,
    free_sem,
):
    n_shard, n_tp, chunks = shape
    at = Place(n_shard, n_tp)
    rows, width = og_ref.shape
    padded = wd.shape[1]
    block = stage.shape[1]
    half = rows // 2
    tiles = padded // 256
    last = n_tp - 1
    def tile_load(f):
        cols = pl.ds(pl.multiple_of(f * 256, 256), 256)
        return (
            pltpu.make_async_copy(wd_hbm.at[:, cols], wd.at[:, cols], tile_sem.at[0, f]),
            pltpu.make_async_copy(
                act_hbm.at[1:3, :, cols], act.at[1:3, :, cols], tile_sem.at[1, f]
            ),
        )

    for f in range(tiles):
        for cp in tile_load(f):
            cp.start()
    pairs = (
        (wg_hbm, wg),
        (wu_hbm, wu),
        (resid_hbm, resid),
        (act_hbm.at[0], act.at[0]),
        (h2t_hbm, left_t.at[:, pl.ds(0, rows)]),
    )
    loads = [
        pltpu.make_async_copy(src, dst, loc_sem.at[i]) for i, (src, dst) in enumerate(pairs)
    ]
    for cp in loads:
        cp.start()
    at.greet()
    length = length_ref[0]

    def live_rows(start, n):
        pos = at.c * rows + start + lax.broadcasted_iota(jnp.int32, (n, 1), 0)
        return (pos < length).astype(F32)

    def mask_grad(i, _):
        start = pl.multiple_of(i * 128, 128)
        r = pl.ds(start, 128)
        low = (og_ref[r, :].astype(F32) * live_rows(start, 128)).astype(BF16)
        gl[r, :] = low
        left_t[:, pl.ds(pl.multiple_of(rows + start, 128), 128)] = low.T
        return 0

    lax.fori_loop(0, rows // 128, mask_grad, 0)

    quarter = half // 2
    lines, backs = [], []
    for n in (0, 1):
        r = pl.ds(n * half, half)
        line = Line(at, d_part.at[r], land_d.at[n], d_send.at[n], d_recv.at[n], chunks)
        lines.append(line)
        backs.append(Back(line, attn_low.at[r], b_send.at[n], b_recv.at[n]))

    def final_d2(n):
        def final(way, k, value):
            line = lines[n]
            start = n * half + (1 - way) * quarter + k * line.size
            r = pl.ds(pl.multiple_of(start, line.size), line.size)
            x = resid[r, :]
            scale = lax.rsqrt(jnp.mean(x * x, axis=-1, keepdims=True) + EPSILON)
            h = x * scale
            inner = jnp.mean(value * h, axis=-1, keepdims=True)
            grad = gl[r, :].astype(F32) + scale * (value - h * inner)
            rg_own[pl.ds(pl.multiple_of(n * quarter + k * line.size, line.size), line.size), :] = grad
            attn_low[r, :] = grad.astype(BF16)

        return final

    def move(n, step):
        lines[n].reduce(step, final_d2(n))
        backs[n].step(step - last * LAG)

    def moves(n, slot):
        for i in range(LAG):
            move(n, slot * LAG + i)

    def mid(n):
        r = slice(n * half, (n + 1) * half)

        def one(f, _):
            cols = pl.ds(pl.multiple_of(f * 256, 256), 256)
            if n == 0:
                for cp in tile_load(f):
                    cp.wait()
            g = mm(gl[r, :], wd[:, cols])
            act[1, r, cols] = (g * act[1, r, cols].astype(F32)).astype(BF16)
            act[2, r, cols] = (g * act[2, r, cols].astype(F32)).astype(BF16)
            if n == 1:

                @pl.when(lax.rem(f, 4) == 2)
                def _():
                    moves(0, 1 + lax.div(f, 4))

            return 0

        lax.fori_loop(0, tiles, one, 0)

    def back_part(q):
        r = slice(q * quarter, (q + 1) * quarter)
        total = mm_nt(act[1, r, :], wg[...]) + mm_nt(act[2, r, :], wu[...])
        d_part[r, :] = total.astype(BF16)

    mid(0)
    for cp in loads:
        cp.wait()
    back_part(0)
    back_part(1)
    moves(0, 0)
    mid(1)
    done = 1 + (tiles + 1) // 4
    back_part(2)
    moves(0, done)
    back_part(3)
    done = (done + 1) * LAG

    peers = (at.sib, at.x, at.y)
    for n, peer in enumerate(peers):
        pl.semaphore_signal(free_sem.at[n], inc=1, device_id=peer, device_id_type=MESH)
    gate = Scatter(at, wgrads.at[1], wg, loc_sem.at[0], s_send, s_recv, 0)

    def free(n):
        pl.semaphore_wait(free_sem.at[n], 1)

    blocks = width // block
    per_step = PER_STEP
    count = 3 * blocks
    def weight_of(n):
        return lax.rem(lax.div(n, blocks) + 1, 3)

    def stage_copy(n):
        w, slot = lax.rem(n, blocks), lax.rem(n, 2)
        return pltpu.make_async_copy(
            stage.at[slot],
            wgrads.at[weight_of(n), pl.ds(pl.multiple_of(w * block, block), block)],
            st_sem.at[slot],
        )

    def weight_grad(n):
        a, w, slot = weight_of(n), lax.rem(n, blocks), lax.rem(n, 2)

        @pl.when(n >= 2)
        def _():
            stage_copy(n - 2).wait()

        first = pl.multiple_of(jnp.where(a == 0, rows, 0), 128)
        left = left_t[pl.ds(pl.multiple_of(w * block, block), block), pl.ds(first, rows)]
        for f in range(tiles):
            cols = slice(f * 256, (f + 1) * 256)
            stage[slot, :, cols] = mm(left, act[a, :, cols]).astype(BF16)
        stage_copy(n).start()

    keeps = pltpu.make_async_copy(f_part, ffn_part, loc_sem.at[1])

    def forward_part(q):
        r = pl.ds(pl.multiple_of(q * quarter, quarter), quarter)
        total = mm_nt(act[0, r, :], wd[...])
        mine = (at.t == lax.rem(q, 2) * last).astype(F32)
        f_part[r, :] = (total + resid[r, :] * mine).astype(BF16)

    def use_gate(r, value):
        gate_sum[r, :] = value.astype(BF16)

    def start_gate():
        free(0)
        gate.start()

    def first_gate():
        free(1)
        free(2)
        gate.first()

    leaving = [
        pltpu.make_async_copy(rg_own, rg_out, loc_sem.at[2]),
        pltpu.make_async_copy(gate_sum, gate_out, loc_sem.at[3]),
    ]

    def finish_gate():
        gate.finish(use_gate)
        leaving[1].start()

    total = chunks + 2 * last * LAG
    begin = (blocks + 2 * per_step - 1) // per_step
    events = {
        begin: start_gate,
        begin + total // 12: first_gate,
        begin + total // 4: gate.second,
        total - 4: leaving[0].start,
        total - 3: finish_gate,
    }

    def tail(step, _):
        move(0, step + done)
        move(1, step)

        for n in range(per_step):

            @pl.when(step * per_step + n < count)
            def _():
                weight_grad(step * per_step + n)

        for when, todo in events.items():

            @pl.when(step == when)
            def _():
                todo()

        @pl.when(jnp.logical_and(step >= total - 10, step < total - 6))
        def _():
            forward_part(step - (total - 10))

        return 0

    steps = max(total, -(-count // per_step))
    lax.fori_loop(0, steps, tail, 0)
    keeps.start()
    stage_copy(count - 2).wait()
    stage_copy(count - 1).wait()
    gate.drain()
    for n in (0, 1):
        lines[n].drain()
        backs[n].drain()
    keeps.wait()
    for cp in leaving:
        cp.wait()


def call_b(mesh, chunks, seq_lengths, out_grad, wd_full, act, wg_full, wu_full, h2t, resid):
    n_shard, n_tp = mesh.shape["shard"], mesh.shape["tp"]
    rows, width = out_grad.shape
    block = width // (n_shard * mesh.shape["ctx"])
    padded = wg_full.shape[1]
    half = rows // 2
    vm = pl.BlockSpec(memory_space=pltpu.VMEM)
    hbm = pl.BlockSpec(memory_space=pltpu.HBM)
    sm = pl.BlockSpec(memory_space=pltpu.SMEM)
    S = jax.ShapeDtypeStruct
    dma = pltpu.SemaphoreType.DMA
    return pl.pallas_call(
        functools.partial(kernel_b, (n_shard, n_tp, chunks)),
        out_shape=(
            S((rows, width), BF16),
            S((half, width), F32),
            S((block, padded), BF16),
            S((rows, width), BF16),
            S((3, width, padded), BF16),
        ),
        in_specs=[sm, vm] + [hbm] * 6,
        out_specs=(vm, hbm, hbm, hbm, hbm),
        scratch_shapes=[
            pltpu.VMEM((half, width), F32),
            pltpu.VMEM((block, padded), BF16),
            pltpu.VMEM((rows, width), BF16),
            pltpu.VMEM((rows, width), BF16),
            pltpu.VMEM((width, padded), BF16),
            pltpu.VMEM((width, padded), BF16),
            pltpu.VMEM((width, padded), BF16),
            pltpu.VMEM((rows, width), F32),
            pltpu.VMEM((width, 2 * rows), BF16),
            pltpu.VMEM((rows, width), BF16),
            pltpu.VMEM((3, rows, padded), BF16),
            pltpu.VMEM((2, 2, half // 2, width), BF16),
            pltpu.VMEM((2, block, padded), BF16),
            dma((2, 2, chunks)),
            dma((2, 2, chunks)),
            dma((2, 2, chunks)),
            dma((2, 2, chunks)),
            dma((1, 7)),
            dma((1, 7)),
            dma((5,)),
            dma((2, padded // 256)),
            dma((2,)),
            pltpu.SemaphoreType.REGULAR((3,)),
        ],
        compiler_params=pltpu.CompilerParams(
            collective_id=1, has_side_effects=True, vmem_limit_bytes=VMEM_LIMIT
        ),
    )(seq_lengths, out_grad, wd_full, act, wg_full, wu_full, h2t, resid)


def kernel_c(
    shape,
    length_ref,
    attn_low,
    q_t,
    kv_all,
    inv_den,
    gain_one_ref,
    gain_two_ref,
    q_gain_ref,
    k_gain_ref,
    wq_ref,
    wk_ref,
    wv_ref,
    cos_ref,
    sin_ref,
    rg_hbm,
    hid_hbm,
    wqkv_hbm,
    proj_hbm,
    wg_hbm,
    wu_hbm,
    gate_hbm,
    ffn_hbm,
    wgrads,
    heads_hbm,
    wo_hbm,
    block_out,
    inp,
    query_out,
    key_out,
    value_out,
    out_out,
    up_out,
    down_out,
    small,
    g_query,
    g_key,
    g_value,
    g_out,
    g_up,
    g_down,
    rg_own,
    hid_ref,
    wqkv,
    proj_t,
    wg_ref,
    wu_ref,
    gate_sum,
    heads_own,
    wo_own,
    hg_t,
    delta,
    k_own,
    v_own,
    kt_own,
    dq_t,
    dkv,
    dkv_send,
    dkv_land,
    gain_acc,
    dqkv,
    f_part,
    d_part,
    land_f,
    land_d,
    left_t,
    part,
    room_w,
    room_p,
    cols_acc,
    qk,
    qk_land,
    tile,
    s_send,
    s_recv,
    f_send,
    f_recv,
    d_send,
    d_recv,
    b_send,
    b_recv,
    o_send,
    o_recv,
    e_send,
    e_recv,
    t_send,
    t_recv,
    loc_sem,
    out_sem,
):
    n_shard, n_tp, chunks, hd = shape
    at = Place(n_shard, n_tp)
    c, t = at.c, at.t
    rows, width = hid_hbm.shape
    q_cols, kv_cols = wq_ref.shape[1], wk_ref.shape[1]
    q_heads, kv_heads = q_cols // hd, kv_cols // hd
    group = q_heads // kv_heads
    halfd = hd // 2
    half = rows // 2
    block = wq_ref.shape[0]
    units = wg_hbm.shape[1]
    last = n_tp - 1
    own_cols = pl.ds(pl.multiple_of(t * q_cols, q_cols), q_cols)
    quarter = half // 2
    loads = [
        pltpu.make_async_copy(heads_hbm.at[:, own_cols], heads_own, loc_sem.at[0]),
        pltpu.make_async_copy(wo_hbm.at[:, own_cols], wo_own, loc_sem.at[1]),
        pltpu.make_async_copy(ffn_hbm, f_part, loc_sem.at[2]),
    ]
    late = [
        pltpu.make_async_copy(src, dst, loc_sem.at[8 + i])
        for i, (src, dst) in enumerate(
            (
                (proj_hbm, proj_t),
                (wqkv_hbm, wqkv),
                (hid_hbm, hid_ref),
                (rg_hbm, rg_own),
                (wg_hbm, wg_ref),
                (wu_hbm, wu_ref),
                (gate_hbm, gate_sum),
            )
        )
    ]
    for cp in loads:
        cp.start()
    at.greet()
    down, up = (
        Scatter(at, wgrads.at[k], room_w.at[i], loc_sem.at[3 + i], s_send, s_recv, i)
        for i, k in enumerate((0, 2))
    )
    rest = Scatter(at, part, room_p, loc_sem.at[5], s_send, s_recv, 2)
    down.start()
    up.start()
    ffn = Line(at, f_part, land_f, f_send, f_recv, chunks, 2)
    ffn_back = Back(ffn, block_out, o_send, o_recv, land_f)
    d1 = Line(at, d_part, land_d, d_send, d_recv, chunks, 2)
    back = Back(d1, inp, b_send, b_recv)
    length = length_ref[0]

    def final_ffn(way, k, value):
        pos = c * rows + ffn.start(way, k)
        pos += lax.broadcasted_iota(jnp.int32, (ffn.size, 1), 0)
        value = value * (pos < length).astype(F32)
        land_f[way, ffn.local(k), :] = value.astype(BF16)

    def move_ffn(step):
        ffn.reduce(step, final_ffn)
        ffn_back.step(step - last * LAG)

    def moves_ffn(slot):
        for i in range(PER_SLOT):
            move_ffn(slot * PER_SLOT + i)

    def keep(n, way):
        return pltpu.make_async_copy(
            land_f.at[way, pl.ds(n * quarter, quarter)],
            block_out.at[pl.ds((2 * n + 1 - way) * quarter, quarter)],
            loc_sem.at[6 + n],
        )

    def keep_all(act):
        for way in (0, 1):

            @pl.when(t == (last if way == 0 else 0))
            def _():
                for n in (0, 1):
                    act(keep(n, way))

    for cp in loads:
        cp.wait()
    moves_ffn(0)
    for cp in late:
        cp.start()

    def heads_grad(i, _):
        r = pl.ds(pl.multiple_of(i * 256, 256), 256)
        hg_t[:, r] = mm(attn_low[r, :], wo_own[...]).T.astype(BF16)
        return 0

    lax.fori_loop(0, rows // 256, heads_grad, 0)
    for j in range(q_cols // 128):
        cols = slice(j * 128, (j + 1) * 128)
        both = heads_own[:, cols].astype(F32).T * hg_t[cols, :].astype(F32)
        for n in range(128 // hd):
            h = j * (128 // hd) + n
            delta[h : h + 1, :] = jnp.sum(both[n * hd : (n + 1) * hd], axis=0, keepdims=True)
    moves_ffn(1)
    down.first()

    def live_keys(index):
        pos = index * rows + lax.broadcasted_iota(jnp.int32, (1, rows), 1)
        return (pos < length).astype(F32)

    def load_block(index, k_nat, v_nat, kt):
        live = live_keys(index)
        for g in range(kv_heads):
            key = kv_all[index, g * hd : (g + 1) * hd, :].astype(F32)
            k_nat[g] = key.T.astype(BF16)
            kt[g] = (key * live).astype(BF16)
            value = kv_all[index, kv_cols + g * hd : kv_cols + (g + 1) * hd, :]
            v_nat[g] = value.astype(F32).T.astype(BF16)

    below = lax.broadcasted_iota(jnp.int32, (256, 256), 0) <= lax.broadcasted_iota(
        jnp.int32, (256, 256), 1
    )

    def segment(h, g, i, lo, hi, masked, k_nat, v_nat, kt):
        cols = slice(i * 256, (i + 1) * 256)
        hr = pl.ds(pl.multiple_of(h * hd, hd), hd)
        qi, oi = q_t[hr, cols], hg_t[hr, cols]
        p = jnp.exp(mm(k_nat[g, lo:hi, :], qi)) * inv_den[pl.ds(h, 1), cols]
        if masked:
            p = jnp.where(below, p, 0.0)
        dp = mm(v_nat[g, lo:hi, :], oi)
        ds = (p * (dp - delta[pl.ds(h, 1), cols])).astype(BF16)
        dq_t[hr, cols] += mm(kt[g, :, lo:hi], ds)
        dkv[g, :, lo:hi] += mm_nt(qi, ds)
        dkv[kv_heads + g, :, lo:hi] += mm_nt(oi, p.astype(BF16))

    dq_t[...] = jnp.zeros_like(dq_t)
    dkv[...] = jnp.zeros_like(dkv)
    give = remote(dkv_send, dkv_land, e_send.at[3], e_recv.at[3], at.x)

    @pl.when(c == 1)
    def _():
        load_block(0, k_own, v_own, kt_own)

        def one(h, _):
            for i in range(rows // 256):
                segment(h, h // group, i, 0, rows, False, k_own, v_own, kt_own)

            @pl.when(lax.rem(h, 2) == 1)
            def _():
                moves_ffn(2 + lax.div(h, 2))

            return 0

        lax.fori_loop(0, q_heads, one, 0)
        live = live_keys(0)
        for n in range(2 * kv_heads):
            dkv_send[n] = (dkv[n] * live).astype(BF16)
        give.start()
        dkv[...] = jnp.zeros_like(dkv)

    @pl.when(c == 0)
    def _():
        def one(h, _):
            moves_ffn(2 + h)
            return 0

        lax.fori_loop(0, q_heads // 2, one, 0)

    up.first()
    down.second()
    load_block(c, k_own, v_own, kt_own)

    def own_block(h, _):
        for i in range(rows // 256):
            segment(h, h // group, i, i * 256, (i + 1) * 256, True, k_own, v_own, kt_own)
            if i:
                segment(h, h // group, i, 0, i * 256, False, k_own, v_own, kt_own)


        @pl.when(lax.rem(h, 2) == 1)
        def _():
            moves_ffn(2 + lax.div(q_heads, 2) + lax.div(h, 2))

        return 0

    lax.fori_loop(0, q_heads, own_block, 0)
    moved = (2 + 2 * (q_heads // 2)) * PER_SLOT
    live = live_keys(c)
    for n in range(2 * kv_heads):
        dkv[n] = dkv[n] * live

    @pl.when(c == 0)
    def _():
        give.wait_recv()
        for n in range(2 * kv_heads):
            dkv[n] += dkv_land[n].astype(F32)

    here = pl.ds(pl.multiple_of(c * rows, rows), rows)
    gain_acc[...] = jnp.zeros_like(gain_acc)
    for cp in late:
        cp.wait()

    def through(which, row, grad, gain):
        x = proj_t[pl.ds(pl.multiple_of(row, hd), hd), :]
        scale = lax.rsqrt(jnp.mean(x * x, axis=0, keepdims=True) + EPSILON)
        xh = x * scale
        cosine, sine = cos_ref[:, here], sin_ref[:, here]
        a, b = grad[:halfd], grad[halfd:]
        grad = jnp.concatenate([a * cosine + b * sine, b * cosine - a * sine], axis=0)
        gain_acc[which] += grad * xh
        grad = grad * gain
        inner = jnp.mean(grad * xh, axis=0, keepdims=True)
        return scale * (grad - xh * inner)

    q_gain, k_gain = column(q_gain_ref, hd), column(k_gain_ref, hd)
    factor = 1.0 / math.sqrt(hd)

    def query_back(h, _):
        row = pl.multiple_of(h * hd, hd)
        r = pl.ds(row, hd)
        dq_t[r, :] = through(0, row, dq_t[r, :] * factor, q_gain)
        return 0

    lax.fori_loop(0, q_heads, query_back, 0)
    dqkv[:, 0:q_cols] = dq_t[...].T.astype(BF16)
    pair = jnp.concatenate(
        [through(1, q_cols + g * hd, dkv[g], k_gain) for g in range(kv_heads)], axis=0
    )
    dqkv[:, q_cols : q_cols + kv_cols] = pair.T.astype(BF16)
    pair = jnp.concatenate([dkv[kv_heads + g] for g in range(kv_heads)], axis=0)
    dqkv[:, q_cols + kv_cols :] = pair.T.astype(BF16)
    def as_row(v):
        return jnp.broadcast_to(v, (v.shape[0], 128)).T[0:1, :]

    qk[...] = jnp.zeros_like(qk)
    for n in (0, 1):
        qk[0, n : n + 1, 0:hd] = as_row(jnp.sum(gain_acc[n], axis=1, keepdims=True))

    def trade(n):
        dev = (at.sib, at.x, at.y)[n]
        return remote(qk.at[n], qk_land.at[n], e_send.at[n], e_recv.at[n], dev)

    def traded(n):
        trade(n).wait_recv()
        qk[n + 1] = qk[n] + qk_land[n]

    up.second()

    def final_d1(way, k, value):
        r = d1.rows(way, k)
        x = hid_ref[r, :].astype(F32)
        scale = lax.rsqrt(jnp.mean(x * x, axis=-1, keepdims=True) + EPSILON)
        h = x * scale
        inner = jnp.mean(value * h, axis=-1, keepdims=True)
        grad = rg_own[d1.local(k), :] + scale * (value - h * inner)
        inp[r, :] = grad.astype(BF16)

    ahead = LAG
    for q in range(4):
        r = slice(q * quarter, (q + 1) * quarter)
        d_part[r, :] = mm_nt(dqkv[r, :], wqkv[...]).astype(BF16)
        if q == 1:
            for step in range(ahead):
                d1.reduce(step, final_d1)

    def turn_hidden(i, _):
        r = pl.ds(pl.multiple_of(i * 128, 128), 128)
        x = hid_ref[r, :].astype(F32)
        scale = lax.rsqrt(jnp.mean(x * x, axis=-1, keepdims=True) + EPSILON)
        left_t[0, :, r] = (x * scale).astype(BF16).T
        left_t[1, :, r] = attn_low[r, :].T
        return 0

    def weight_part(w, _):
        r = pl.ds(pl.multiple_of(w * block, block), block)
        part[r, 0 : dqkv.shape[1]] = mm(left_t[0, r, :], dqkv[...]).astype(BF16)
        part[r, dqkv.shape[1] :] = mm(left_t[1, r, :], heads_own[...]).astype(BF16)
        return 0

    g_one = column(gain_one_ref, block)
    g_two = column(gain_two_ref, block)
    cols_acc[0] = jnp.broadcast_to(g_one, (block, 128))
    cols_acc[1] = jnp.broadcast_to(g_two, (block, 128))

    def use_down(r, value):
        g_down[r, :] = value[:, 0:units]

    def gate_gain():
        def piece(i, _):
            r = pl.ds(pl.multiple_of(i * 64, 64), 64)
            value = gate_sum[r, 0:units].astype(F32)
            total = jnp.sum(wg_ref[r, :].astype(F32) * value, axis=1, keepdims=True)
            cols_acc[3, r, :] = jnp.broadcast_to(total, (64, 128))
            return 0

        lax.fori_loop(0, block // 64, piece, 0)

    def use_up(r, value):
        value = value[:, 0:units]
        total = jnp.sum(wu_ref[r, :].astype(F32) * value, axis=1, keepdims=True)
        cols_acc[3, r, :] += jnp.broadcast_to(total, (64, 128))
        g_up[r, :] = value * cols_acc[1, r, 0:1]

    def use_rest(r, value):
        gain = cols_acc[0, r, 0:1]
        vq = value[:, 0:q_cols]
        vk = value[:, q_cols : q_cols + kv_cols]
        vv = value[:, q_cols + kv_cols : q_cols + 2 * kv_cols]
        total = jnp.sum(wq_ref[r, :].astype(F32) * vq, axis=1, keepdims=True)
        total += jnp.sum(wk_ref[r, :].astype(F32) * vk, axis=1, keepdims=True)
        total += jnp.sum(wv_ref[r, :].astype(F32) * vv, axis=1, keepdims=True)
        cols_acc[2, r, :] = jnp.broadcast_to(total, (64, 128))
        g_query[r, :] = vq * gain
        g_key[r, :] = vk * gain
        g_value[r, :] = vv * gain
        g_out[r, :] = value[:, q_cols + 2 * kv_cols :]

    def turn_all():
        lax.fori_loop(0, rows // 128, turn_hidden, 0)

    def parts():
        lax.fori_loop(0, width // block, weight_part, 0)
        rest.start()

    leaving = [
        pltpu.make_async_copy(src, dst, out_sem.at[i])
        for i, (src, dst) in enumerate(
            (
                (g_down, down_out),
                (g_up, up_out),
                (g_query, query_out),
                (g_key, key_out),
                (g_value, value_out),
                (g_out, out_out),
            )
        )
    ]

    def finish_rest():
        rest.finish(use_rest)
        for cp in leaving[2:]:
            cp.start()

    events = {
        0: (lambda: trade(0).start(), turn_all),
        1: (parts, lambda: traded(0), lambda: trade(1).start()),
        2: (lambda: traded(1), lambda: trade(2).start(), gate_gain),
        4: (rest.first, lambda: traded(2)),
        8: (lambda: down.finish(use_down), leaving[0].start),
        10: (rest.second,),
        14: (lambda: up.finish(use_up), leaving[1].start),
        18: (finish_rest,),
        19: (lambda: give_tiles(),),
    }

    def give_tile(d, owner):
        return remote(
            tile.at[owner], tile.at[owner], t_send.at[d], t_recv.at[d],
            at.z(lax.rem(t + d + 1, n_tp)),
        )

    def give_tiles():
        tile[t] = jnp.zeros(tile.shape[1:], F32)
        tile[t, 0:1, 0:block] = cols_acc[2].T[0:1, :]
        tile[t, 1:2, 0:block] = cols_acc[3].T[0:1, :]
        tile[t, 2:4, 0:128] = qk[3, 0:2, :]
        for d in range(n_tp - 1):
            give_tile(d, t).start()

    def tail(step, _):
        d1.reduce(step + ahead, final_d1)
        back.step(step + ahead - last * LAG)
        move_ffn(step + moved)
        for when, todo in events.items():

            @pl.when(step == when)
            def _():
                for thing in todo:
                    thing()

        return 0

    lax.fori_loop(0, max(chunks + 2 * last * LAG, 20), tail, 0)
    keep_all(lambda cp: cp.start())

    for w in (down, up, rest):
        w.drain()
    for thing in (d1, back, ffn, ffn_back):
        thing.drain()
    keep_all(lambda cp: cp.wait())
    for cp in leaving:
        cp.wait()

    @pl.when(c == 1)
    def _():
        give.wait_send()

    for n in range(3):
        trade(n).wait_send()
    for d in range(n_tp - 1):
        give_tile(d, lax.rem(t + n_tp - d - 1, n_tp)).wait_recv()
    total = tile[0]
    for n in range(1, n_tp):
        total = total + tile[n]
    small[...] = total
    for d in range(n_tp - 1):
        give_tile(d, t).wait_send()


def call_c(mesh, chunks, args, kept):
    (hidden_in, seq_lengths, attn_gain, ffn_gain, query_gain, key_gain,
     w_query, w_key, w_value, w_gate, w_up) = args
    (attn_low, rg_own, gate_sum, ffn_part, wgrads, wqkv_full, wo_full, heads_all, q_t, kv_all, inv_den,
     proj_t) = kept
    n_shard, n_ctx, n_tp = mesh.shape["shard"], mesh.shape["ctx"], mesh.shape["tp"]
    rows, width = hidden_in.shape
    quarter = rows // 4
    hd = query_gain.shape[0]
    q_cols, kv_cols = w_query.shape[1], w_key.shape[1]
    qkv_cols = q_cols + 2 * kv_cols
    kv_heads = kv_cols // hd
    block, units = w_gate.shape
    padded = wgrads.shape[2]
    cosine, sine = rope_tables(n_ctx * rows, hd)
    vm = pl.BlockSpec(memory_space=pltpu.VMEM)
    hbm = pl.BlockSpec(memory_space=pltpu.HBM)
    sm = pl.BlockSpec(memory_space=pltpu.SMEM)
    S = jax.ShapeDtypeStruct
    V = pltpu.VMEM
    dma = pltpu.SemaphoreType.DMA
    return pl.pallas_call(
        functools.partial(kernel_c, (n_shard, n_tp, chunks, hd)),
        out_shape=(
            S((rows, width), BF16),
            S((rows, width), BF16),
            S((block, q_cols), F32),
            S((block, kv_cols), F32),
            S((block, kv_cols), F32),
            S((block, q_cols), F32),
            S((block, units), F32),
            S((block, units), F32),
            S((8, 256), F32),
        ),
        in_specs=[sm] + [vm] * 13 + [hbm] * 11,
        out_specs=(hbm, vm) + (hbm,) * 6 + (vm,),
        scratch_shapes=[
            V((block, q_cols), F32),
            V((block, kv_cols), F32),
            V((block, kv_cols), F32),
            V((block, q_cols), F32),
            V((block, units), F32),
            V((block, units), F32),
            V((rows // 2, width), F32),
            V((rows, width), BF16),
            V((width, qkv_cols), BF16),
            V((qkv_cols, rows), F32),
            V((block, units), BF16),
            V((block, units), BF16),
            V((block, padded), BF16),
            V((rows, q_cols), BF16),
            V((width, q_cols), BF16),
            V((q_cols, rows), BF16),
            V((8, rows), F32),
            V((kv_heads, rows, hd), BF16),
            V((kv_heads, rows, hd), BF16),
            V((kv_heads, hd, rows), BF16),
            V((q_cols, rows), F32),
            V((2 * kv_heads, hd, rows), F32),
            V((2 * kv_heads, hd, rows), BF16),
            V((2 * kv_heads, hd, rows), BF16),
            V((2, hd, rows), F32),
            V((rows, qkv_cols), BF16),
            V((rows, width), BF16),
            V((rows, width), BF16),
            V((2, 2 * quarter, width), BF16),
            V((2, 2 * quarter, width), BF16),
            V((2, width, rows), BF16),
            V((width, qkv_cols + q_cols), BF16),
            V((2, 8 * block, padded), BF16),
            V((8 * block, qkv_cols + q_cols), BF16),
            V((4, block, 128), F32),
            V((4, 8, 128), F32),
            V((3, 8, 128), F32),
            V((n_tp, 8, 256), F32),
            dma((3, 7)),
            dma((3, 7)),
            dma((2, chunks)),
            dma((2, chunks)),
            dma((2, chunks)),
            dma((2, chunks)),
            dma((2, chunks)),
            dma((2, chunks)),
            dma((2, chunks)),
            dma((2, chunks)),
            dma((4,)),
            dma((4,)),
            dma((n_tp - 1,)),
            dma((n_tp - 1,)),
            dma((15,)),
            dma((6,)),
        ],
        compiler_params=pltpu.CompilerParams(
            collective_id=2, has_side_effects=True, vmem_limit_bytes=VMEM_LIMIT
        ),
    )(
        seq_lengths, attn_low, q_t, kv_all, inv_den,
        attn_gain, ffn_gain, query_gain, key_gain, w_query, w_key, w_value,
        jnp.asarray(cosine), jnp.asarray(sine), rg_own, hidden_in, wqkv_full, proj_t,
        w_gate, w_up, gate_sum, ffn_part, wgrads, heads_all, wo_full,
    )


CHUNKS = 6
CHUNKS_C = 12
PER_STEP = 4
PER_SLOT = 2


def fast_body(mesh, *args):
    (hidden_in, seq_lengths, attn_gain, ffn_gain, query_gain, key_gain,
     w_query, w_key, w_value, w_out, w_gate, w_up, w_down, out_grad) = args
    (wqkv_full, wo_full, wg_full, wu_full, wd_full, heads_all, q_t, kv_all, inv_den, proj_t,
     resid, h2t, act) = call_a(mesh, args[:13])
    attn_low, rg_own, gate_sum, ffn_part, wgrads = call_b(
        mesh, CHUNKS, seq_lengths, out_grad, wd_full, act, wg_full, wu_full, h2t, resid
    )
    (block_out, inp, g_query, g_key, g_value, g_out, g_up, g_down, small) = call_c(
        mesh, CHUNKS_C,
        (hidden_in, seq_lengths, attn_gain, ffn_gain, query_gain, key_gain, w_query, w_key,
         w_value, w_gate, w_up),
        (attn_low, rg_own, gate_sum, ffn_part, wgrads, wqkv_full, wo_full, heads_all, q_t, kv_all, inv_den,
         proj_t),
    )
    block, hd = w_query.shape[0], query_gain.shape[0]
    g_gate = gate_sum[:, : w_gate.shape[1]].astype(F32) * ffn_gain.astype(F32)[:, None]
    return (
        block_out, inp.astype(F32), small[0, :block], small[1, :block], small[2, :hd],
        small[3, :hd], g_query, g_key, g_value, g_out.T, g_gate, g_up, g_down.T,
    )


def solution(mesh):
    sizes = mesh.shape
    plane_of_eight = sizes["shard"] == 4 and sizes["ctx"] == 2 and sizes["tp"] > 1
    run = functools.partial(fast_body, mesh) if plane_of_eight else body
    placed = (
        P(("shard", "ctx"), None),
        P("shard"),
        P(("shard", "ctx")),
        P(("shard", "ctx")),
        P(),
        P(),
        P(("shard", "ctx"), "tp"),
        P(("shard", "ctx"), "tp"),
        P(("shard", "ctx"), "tp"),
        P("tp", ("shard", "ctx")),
        P(("shard", "ctx"), "tp"),
        P(("shard", "ctx"), "tp"),
        P("tp", ("shard", "ctx")),
        P(("shard", "ctx"), None),
    )
    return jax.shard_map(
        run,
        mesh=mesh,
        in_specs=placed,
        out_specs=(
            P(("shard", "ctx"), None),
            P(("shard", "ctx"), None),
            P(("shard", "ctx")),
            P(("shard", "ctx")),
            P(),
            P(),
            P(("shard", "ctx"), "tp"),
            P(("shard", "ctx"), "tp"),
            P(("shard", "ctx"), "tp"),
            P("tp", ("shard", "ctx")),
            P(("shard", "ctx"), "tp"),
            P(("shard", "ctx"), "tp"),
            P("tp", ("shard", "ctx")),
        ),
        check_vma=False,
    )
```

```python
import functools
import math

import jax
import jax.numpy as jnp
import numpy as np
from jax import lax
from jax.experimental import pallas as pl
from jax.experimental.pallas import tpu as pltpu
from jax.sharding import PartitionSpec as P

EPSILON = 1e-05
ROPE_BASE = 1000000.0
MESH = pl.DeviceIdType.MESH
F32 = jnp.float32
BF16 = jnp.bfloat16
VMEM_LIMIT = 60 << 20


def norm_rows(value, gain):
    scale = lax.rsqrt(jnp.mean(value * value, axis=-1, keepdims=True) + EPSILON)
    return value * scale * gain


def rotate(values, positions):
    half = values.shape[-1] // 2
    freq = ROPE_BASE ** (-jnp.arange(half, dtype=jnp.float32) / half)
    angle = positions.astype(jnp.float32)[:, None] * freq[None, :]
    cosine = jnp.cos(angle)[:, None, :]
    sine = jnp.sin(angle)[:, None, :]
    first = values[..., :half]
    second = values[..., half:]
    return jnp.concatenate(
        [first * cosine - second * sine, second * cosine + first * sine], axis=-1
    )


def head_prep(proj, gain, positions):
    heads = proj.reshape(proj.shape[0], -1, gain.shape[0])
    return rotate(norm_rows(heads, gain), positions)


def activation(gate_in, up_in):
    return jax.nn.silu(gate_in) * up_in


def forward_product(left, right):
    return jnp.dot(left, right, preferred_element_type=jnp.float32)


def outer_product(left, right):
    return lax.dot_general(
        left, right, (((0,), (0,)), ((), ())), preferred_element_type=jnp.float32
    )


def back_product(grad, weight):
    return lax.dot_general(
        grad, weight, (((1,), (1,)), ((), ())), preferred_element_type=jnp.float32
    )


def body(
    hidden_in,
    seq_lengths,
    attn_gain,
    ffn_gain,
    query_gain,
    key_gain,
    w_query,
    w_key,
    w_value,
    w_out,
    w_gate,
    w_up,
    w_down,
    out_grad,
):
    rows = hidden_in.shape[0]
    head_dim = query_gain.shape[0]
    kv_heads = w_key.shape[1] // head_dim
    q_heads = w_query.shape[1] // head_dim
    group = q_heads // kv_heads
    pieces = lax.axis_size("ctx")
    scale = 1.0 / math.sqrt(head_dim)
    positions = lax.axis_index("ctx") * rows + jnp.arange(rows, dtype=jnp.int32)
    length = seq_lengths[0]
    valid = (positions < length).astype(jnp.float32)[:, None]
    live_blocks = jnp.minimum(lax.axis_index("ctx"), (length - 1) // rows) + 1
    gathered = (
        lax.all_gather(attn_gain, ("shard", "ctx"), axis=0, tiled=True),
        lax.all_gather(ffn_gain, ("shard", "ctx"), axis=0, tiled=True),
        lax.all_gather(w_query, ("shard", "ctx"), axis=0, tiled=True),
        lax.all_gather(w_key, ("shard", "ctx"), axis=0, tiled=True),
        lax.all_gather(w_value, ("shard", "ctx"), axis=0, tiled=True),
        lax.all_gather(w_gate, ("shard", "ctx"), axis=0, tiled=True),
        lax.all_gather(w_up, ("shard", "ctx"), axis=0, tiled=True),
        lax.all_gather(w_out, ("shard", "ctx"), axis=1, tiled=True),
        lax.all_gather(w_down, ("shard", "ctx"), axis=1, tiled=True),
    )
    gain_one = gathered[0].astype(jnp.float32)
    gain_two = gathered[1].astype(jnp.float32)
    full_query, full_key, full_value, full_gate, full_up, full_out, full_down = gathered[2:]
    q_gain = query_gain.astype(jnp.float32)
    k_gain = key_gain.astype(jnp.float32)
    hidden = hidden_in.astype(jnp.float32)
    normed_one = norm_rows(hidden, gain_one).astype(jnp.bfloat16)
    query_proj = forward_product(normed_one, full_query)
    key_proj = forward_product(normed_one, full_key)
    value_proj = forward_product(normed_one, full_value)
    queries = (
        head_prep(query_proj, q_gain, positions)
        .astype(jnp.bfloat16)
        .reshape(rows, kv_heads, group, head_dim)
    )
    keys_own = head_prep(key_proj, k_gain, positions).astype(jnp.bfloat16)
    values_own = value_proj.reshape(rows, kv_heads, head_dim).astype(jnp.bfloat16)
    keys_all, values_all = (
        lax.all_gather(keys_own, "ctx", axis=0, tiled=True),
        lax.all_gather(values_own, "ctx", axis=0, tiled=True),
    )
    key_blocks = keys_all.reshape(pieces, rows, kv_heads, head_dim)
    value_blocks = values_all.reshape(pieces, rows, kv_heads, head_dim)

    def key_at(index):
        return lax.dynamic_index_in_dim(key_blocks, index, 0, keepdims=False)

    def value_at(index):
        return lax.dynamic_index_in_dim(value_blocks, index, 0, keepdims=False)

    def block_scores(key_block, index):
        key_pos = index * rows + jnp.arange(rows, dtype=jnp.int32)
        mask = ((key_pos[None, :] <= positions[:, None]) & (key_pos[None, :] < length))[None, None]
        raw = (
            jnp.einsum("tkgd,skd->kgts", queries, key_block, preferred_element_type=jnp.float32)
            * scale
        )
        return (jnp.where(mask, raw, -1e30), mask)

    def stats_step(index, carry):
        top, total = carry
        masked, mask = block_scores(key_at(index), index)
        new_top = jnp.maximum(top, jnp.max(masked, axis=-1))
        weight = jnp.where(mask, jnp.exp(masked - new_top[..., None]), 0.0)
        total = total * jnp.exp(top - new_top) + jnp.sum(weight, axis=-1)
        return (new_top, total)

    start = (
        jnp.full((kv_heads, group, rows), -1e30, jnp.float32),
        jnp.zeros((kv_heads, group, rows), jnp.float32),
    )
    top, total = lax.fori_loop(0, live_blocks, stats_step, start)
    log_total = top + jnp.log(total)

    def probs_of(key_block, index):
        masked, mask = block_scores(key_block, index)
        return jnp.where(mask, jnp.exp(masked - log_total[..., None]), 0.0)

    def mix_step(index, accum):
        probs = probs_of(key_at(index), index).astype(jnp.bfloat16)
        return accum + jnp.einsum(
            "kgts,skd->tkgd", probs, value_at(index), preferred_element_type=jnp.float32
        )

    head_zeros = jnp.zeros((rows, kv_heads, group, head_dim), jnp.float32)
    mixed = lax.fori_loop(0, live_blocks, mix_step, head_zeros)
    heads_out = mixed.reshape(rows, -1).astype(jnp.bfloat16)
    attn_term = forward_product(heads_out, full_out)
    resid = hidden + lax.psum(attn_term, "tp")
    normed_two = norm_rows(resid, gain_two).astype(jnp.bfloat16)
    gate = forward_product(normed_two, full_gate)
    up = forward_product(normed_two, full_up)
    middle = activation(gate, up).astype(jnp.bfloat16)
    ffn_term = forward_product(middle, full_down)
    ffn = lax.psum(ffn_term.astype(jnp.bfloat16), "tp").astype(jnp.float32)
    block_out = (valid * (resid + ffn)).astype(jnp.bfloat16)
    grad_top = valid * out_grad.astype(jnp.float32)
    grad_low = grad_top.astype(jnp.bfloat16)
    down_wgrad = outer_product(middle, grad_low)
    mid_grad = back_product(grad_low, full_down)
    _, pull_act = jax.vjp(activation, gate, up)
    gate_float, up_float = pull_act(mid_grad)
    gate_low = gate_float.astype(jnp.bfloat16)
    up_low = up_float.astype(jnp.bfloat16)
    gate_wgrad = outer_product(normed_two, gate_low)
    up_wgrad = outer_product(normed_two, up_low)
    normed_two_part = back_product(gate_low, full_gate) + back_product(up_low, full_up)
    normed_two_grad = lax.psum(normed_two_part, "tp")
    _, pull_two = jax.vjp(norm_rows, resid, gain_two)
    resid_part, gain_two_grad = pull_two(normed_two_grad)
    resid_grad = grad_top + resid_part
    attn_low = resid_grad.astype(jnp.bfloat16)
    out_wgrad = outer_product(heads_out, attn_low)
    heads_grad = (
        back_product(attn_low, full_out)
        .astype(jnp.bfloat16)
        .reshape(rows, kv_heads, group, head_dim)
    )

    def delta_step(index, accum):
        probs = probs_of(key_at(index), index)
        prob_grad = jnp.einsum(
            "tkgd,skd->kgts", heads_grad, value_at(index), preferred_element_type=jnp.float32
        )
        return accum + jnp.sum(probs * prob_grad, axis=-1)

    delta = lax.fori_loop(
        0, live_blocks, delta_step, jnp.zeros((kv_heads, group, rows), jnp.float32)
    )

    def grad_step(index, carry):
        accum, key_store, value_store = carry
        key_block = key_at(index)
        probs = probs_of(key_block, index)
        prob_grad = jnp.einsum(
            "tkgd,skd->kgts", heads_grad, value_at(index), preferred_element_type=jnp.float32
        )
        score_grad = (probs * (prob_grad - delta[..., None])).astype(jnp.bfloat16)
        accum = (
            accum
            + jnp.einsum(
                "kgts,skd->tkgd", score_grad, key_block, preferred_element_type=jnp.float32
            )
            * scale
        )
        key_grad = (
            jnp.einsum("kgts,tkgd->skd", score_grad, queries, preferred_element_type=jnp.float32)
            * scale
        )
        value_grad = jnp.einsum(
            "kgts,tkgd->skd",
            probs.astype(jnp.bfloat16),
            heads_grad,
            preferred_element_type=jnp.float32,
        )
        key_store = lax.dynamic_update_index_in_dim(key_store, key_grad, index, 0)
        value_store = lax.dynamic_update_index_in_dim(value_store, value_grad, index, 0)
        return (accum, key_store, value_store)

    store_zeros = jnp.zeros((pieces, rows, kv_heads, head_dim), jnp.float32)
    query_grad, key_grads, value_grads = lax.fori_loop(
        0, live_blocks, grad_step, (head_zeros, store_zeros, store_zeros)
    )
    key_grad_own, value_grad_own = (
        lax.psum_scatter(
            key_grads.reshape(pieces * rows, kv_heads, head_dim),
            "ctx",
            scatter_dimension=0,
            tiled=True,
        ),
        lax.psum_scatter(
            value_grads.reshape(pieces * rows, kv_heads, head_dim),
            "ctx",
            scatter_dimension=0,
            tiled=True,
        ),
    )

    def query_prep(proj, gain):
        return head_prep(proj, gain, positions)

    _, pull_query = jax.vjp(query_prep, query_proj, q_gain)
    query_proj_grad, q_gain_grad = pull_query(query_grad.reshape(rows, q_heads, head_dim))
    _, pull_key = jax.vjp(query_prep, key_proj, k_gain)
    key_proj_grad, k_gain_grad = pull_key(key_grad_own)
    query_low = query_proj_grad.astype(jnp.bfloat16)
    key_low = key_proj_grad.astype(jnp.bfloat16)
    value_low = value_grad_own.reshape(rows, -1).astype(jnp.bfloat16)
    query_wgrad = outer_product(normed_one, query_low)
    key_wgrad = outer_product(normed_one, key_low)
    value_wgrad = outer_product(normed_one, value_low)
    normed_one_part = (
        back_product(query_low, full_query)
        + back_product(key_low, full_key)
        + back_product(value_low, full_value)
    )
    normed_one_grad = lax.psum(normed_one_part, "tp")
    _, pull_one = jax.vjp(norm_rows, hidden, gain_one)
    hidden_part, gain_one_grad = pull_one(normed_one_grad)
    input_grad = resid_grad + hidden_part
    head_sums = lax.psum((q_gain_grad, k_gain_grad), ("shard", "ctx", "tp"))
    summed = (
        lax.psum_scatter(gain_one_grad, ("shard", "ctx"), scatter_dimension=0, tiled=True),
        lax.psum_scatter(gain_two_grad, ("shard", "ctx"), scatter_dimension=0, tiled=True),
        lax.psum_scatter(query_wgrad, ("shard", "ctx"), scatter_dimension=0, tiled=True),
        lax.psum_scatter(key_wgrad, ("shard", "ctx"), scatter_dimension=0, tiled=True),
        lax.psum_scatter(value_wgrad, ("shard", "ctx"), scatter_dimension=0, tiled=True),
        lax.psum_scatter(gate_wgrad, ("shard", "ctx"), scatter_dimension=0, tiled=True),
        lax.psum_scatter(up_wgrad, ("shard", "ctx"), scatter_dimension=0, tiled=True),
        lax.psum_scatter(out_wgrad, ("shard", "ctx"), scatter_dimension=1, tiled=True),
        lax.psum_scatter(down_wgrad, ("shard", "ctx"), scatter_dimension=1, tiled=True),
    )
    (
        gain_one_out,
        gain_two_out,
        query_out,
        key_out,
        value_out,
        gate_out,
        up_out,
        out_out,
        down_out,
    ) = summed
    return (
        block_out,
        input_grad,
        gain_one_out,
        gain_two_out,
        head_sums[0],
        head_sums[1],
        query_out,
        key_out,
        value_out,
        out_out,
        gate_out,
        up_out,
        down_out,
    )


def remote(src, dst, send, recv, dev):
    return pltpu.make_async_remote_copy(
        src_ref=src,
        dst_ref=dst,
        send_sem=send,
        recv_sem=recv,
        device_id=dev,
        device_id_type=MESH,
    )


def mm(a, b):
    return jnp.dot(a, b, preferred_element_type=F32)


def mm_nt(a, b):
    return lax.dot_general(a, b, (((1,), (1,)), ((), ())), preferred_element_type=F32)


def round_up(units):
    return -(-units // 256) * 256


class Place:
    def __init__(self, n_shard, n_tp):
        s = lax.axis_index("shard")
        c = lax.axis_index("ctx")
        t = lax.axis_index("tp")
        self.s, self.c, self.t = s, c, t
        self.core = lax.rem(s, 2)
        sib = s + 1 - 2 * self.core
        far = lax.rem(s + 2, n_shard)
        far_sib = far + 1 - 2 * self.core
        self.sib = (sib, c, t)
        self.x = (s, 1 - c, t)
        self.y = (far, c, t)
        first = 1 - self.core
        self.relay = (
            first * s + self.core * far,
            first * (1 - c) + self.core * c,
            t,
        )
        slot = lambda a, b: a * 2 + b
        self.own = slot(s, c)
        self.slots = {
            "S": slot(sib, c),
            "X": slot(s, 1 - c),
            "Y": slot(far, c),
            "D": slot(far, 1 - c),
            "SX": slot(sib, 1 - c),
            "SY": slot(far_sib, c),
            "SD": slot(far_sib, 1 - c),
        }
        self.relayed = first * self.slots["Y"] + self.core * self.slots["X"]
        self.n_tp = n_tp

    def z(self, t):
        return (self.s, self.c, t)

    def greet(self):
        peers = [self.sib, self.x, self.y]
        peers += [
            self.z(lax.rem(self.t + d, self.n_tp)) for d in range(1, self.n_tp)
        ]
        barrier = pltpu.get_barrier_semaphore()
        for peer in peers:
            pl.semaphore_signal(barrier, inc=1, device_id=peer, device_id_type=MESH)
        pl.semaphore_wait(barrier, len(peers))


ROLES = ("S", "X", "Y", "D", "SX", "SY", "SD")


class Gather:
    def __init__(self, at, own, full, send, recv, index, stride=0, first=0):
        self.at, self.own, self.full = at, own, full
        self.send, self.recv, self.index = send, recv, index
        self.rows, self.first = own.shape[0], first
        self.stride = stride or self.rows

    def block(self, slot):
        start = slot * self.stride + self.first
        return self.full.at[pl.ds(pl.multiple_of(start, self.rows), self.rows)]

    def copy(self, role, src, slot, dev):
        k = ROLES.index(role)
        return remote(
            src,
            self.block(slot),
            self.send.at[self.index, k],
            self.recv.at[self.index, k],
            dev,
        )

    def arrived(self, role):
        slot = self.at.slots[role]
        self.copy(role, self.block(slot), slot, self.at.sib).wait_recv()

    def start_x(self):
        self.copy("X", self.own, self.at.own, self.at.x).start()

    def start_y(self):
        self.copy("Y", self.own, self.at.own, self.at.y).start()

    def start_s(self):
        self.copy("S", self.own, self.at.own, self.at.sib).start()

    def start(self):
        self.start_x()
        self.start_y()
        self.start_s()

    def relay(self):
        at = self.at
        self.arrived("X")
        self.arrived("Y")
        self.copy("D", self.block(at.relayed), at.relayed, at.relay).start()
        for role in ("X", "Y"):
            slot = at.slots[role]
            self.copy("S" + role, self.block(slot), slot, at.sib).start()

    def relay_last(self):
        self.arrived("D")
        slot = self.at.slots["D"]
        self.copy("SD", self.block(slot), slot, self.at.sib).start()

    def finish(self):
        for role in ("S", "SX", "SY", "SD"):
            self.arrived(role)
        for role in ROLES:
            self.copy(role, self.own, self.at.own, self.at.sib).wait_send()


def column(row_ref, n):
    wide = jnp.broadcast_to(row_ref[...].astype(F32)[None, :], (8, n))
    return wide.T[:, 0:1]


def kernel_a(
    shape,
    length_ref,
    hid_ref,
    gain_one_ref,
    gain_two_ref,
    q_gain_ref,
    k_gain_ref,
    wq_ref,
    wk_ref,
    wv_ref,
    wo_ref,
    wg_ref,
    wu_ref,
    wd_ref,
    cos_ref,
    sin_ref,
    wqkv_out,
    wo_out,
    wg_full,
    wu_full,
    wd_full,
    heads_out,
    q_out,
    kv_out,
    inv_den,
    proj_out,
    resid_out,
    h2t_out,
    act_out,
    wqkv_full,
    wo_full,
    heads_all,
    q_t,
    kv_all,
    proj_t,
    resid,
    h2,
    h2t,
    s_qkv,
    s_woz,
    s_wg,
    s_wu,
    s_wd,
    wg,
    wu,
    act,
    h1,
    k_own,
    k_off,
    v_own,
    v_off,
    acc,
    g_send,
    g_recv,
    z_send,
    z_recv,
    h_send,
    h_recv,
    kv_sem,
    loc_sem,
    act_sem,
    out_sem,
):
    n_shard, n_tp, hd = shape
    at = Place(n_shard, n_tp)
    c, t = at.c, at.t
    rows, width = hid_ref.shape
    q_cols, kv_cols = wq_ref.shape[1], wk_ref.shape[1]
    q_heads, kv_heads = q_cols // hd, kv_cols // hd
    group = q_heads // kv_heads
    half = hd // 2
    at.greet()
    leaving = [
        pltpu.make_async_copy(src, dst, out_sem.at[i])
        for i, (src, dst) in enumerate(
            (
                (wqkv_full, wqkv_out),
                (proj_t, proj_out),
                (q_t, q_out),
                (kv_all, kv_out),
                (heads_all, heads_out),
                (wo_full, wo_out),
                (resid, resid_out),
                (h2t, h2t_out),
            )
        )
    ]

    col_one = column(gain_one_ref, gain_one_ref.shape[0])
    s_qkv[:, 0:q_cols] = (wq_ref[...].astype(F32) * col_one).astype(BF16)
    s_qkv[:, q_cols : q_cols + kv_cols] = (wk_ref[...].astype(F32) * col_one).astype(BF16)
    s_qkv[:, q_cols + kv_cols :] = (wv_ref[...].astype(F32) * col_one).astype(BF16)
    qkv = Gather(at, s_qkv, wqkv_full, g_send, g_recv, 0)
    out = Gather(at, s_woz, wo_full, g_send, g_recv, 1)
    gate = Gather(at, s_wg, wg_full, g_send, g_recv, 2)
    up = Gather(at, s_wu, wu_full, g_send, g_recv, 3)
    down = Gather(at, s_wd, wd_full, g_send, g_recv, 4)
    gathers = (qkv, out, gate, up, down)
    local = [
        pltpu.make_async_copy(g.own, g.block(at.own), loc_sem.at[i])
        for i, g in enumerate(gathers)
    ]
    loads = [
        pltpu.make_async_copy(wg_full, wg, loc_sem.at[5]),
        pltpu.make_async_copy(wu_full, wu, loc_sem.at[6]),
    ]
    qkv.start()
    local[0].start()

    wo_cols = pl.ds(pl.multiple_of(t * q_cols, q_cols), q_cols)
    s_woz[:, wo_cols] = wo_ref[...]

    def wo_part(d, owner):
        cols = pl.ds(pl.multiple_of(owner * q_cols, q_cols), q_cols)
        return remote(
            s_woz.at[:, cols],
            s_woz.at[:, cols],
            z_send.at[d],
            z_recv.at[d],
            at.z(lax.rem(t + d + 1, n_tp)),
        )

    for d in range(n_tp - 1):
        wo_part(d, t).start()

    def norm_one(i, _):
        r = pl.ds(pl.multiple_of(i * 64, 64), 64)
        x = hid_ref[r, :].astype(F32)
        scale = lax.rsqrt(jnp.mean(x * x, axis=-1, keepdims=True) + EPSILON)
        h1[r, :] = (x * scale).astype(BF16)
        return 0

    lax.fori_loop(0, rows // 64, norm_one, 0)
    qkv.relay()
    col_two = column(gain_two_ref, gain_two_ref.shape[0])
    units = wg_ref.shape[1]
    for src, dst in ((wg_ref, s_wg), (wu_ref, s_wu)):
        dst[:, 0:units] = (src[...].astype(F32) * col_two).astype(BF16)
        dst[:, units:] = jnp.zeros((dst.shape[0], dst.shape[1] - units), BF16)
    s_wd[:, 0:units] = wd_ref[...]
    s_wd[:, units:] = jnp.zeros((s_wd.shape[0], s_wd.shape[1] - units), BF16)
    qkv.relay_last()
    for d in range(n_tp - 1):
        wo_part(d, lax.rem(t + n_tp - d - 1, n_tp)).wait_recv()
    out.start()
    gate.start_y()
    local[0].wait()
    for cp in local[1:]:
        cp.start()
    qkv.finish()

    def project(i, _):
        r = pl.ds(pl.multiple_of(i * 256, 256), 256)
        proj_t[:, r] = mm(h1[r, :], wqkv_full[...]).T
        return 0

    lax.fori_loop(0, rows // 256, project, 0)
    leaving[0].start()
    leaving[1].start()
    here = pl.ds(pl.multiple_of(c * rows, rows), rows)
    k_gain = column(k_gain_ref, hd)
    q_gain = column(q_gain_ref, hd)

    def prepared(row, gain, factor):
        x = proj_t[pl.ds(pl.multiple_of(row, hd), hd), :]
        scale = lax.rsqrt(jnp.mean(x * x, axis=0, keepdims=True) + EPSILON)
        y = x * (scale * factor) * gain
        a, b = y[:half], y[half:]
        cosine, sine = cos_ref[:, here], sin_ref[:, here]
        return jnp.concatenate([a * cosine - b * sine, b * cosine + a * sine], axis=0)

    for g in range(kv_heads):
        key = prepared(q_cols + g * hd, k_gain, 1.0).astype(BF16)
        kv_all[c, g * hd : (g + 1) * hd, :] = key
    kv_all[c, kv_cols:, :] = proj_t[q_cols + kv_cols :, :].astype(BF16)
    kv_copy = remote(kv_all.at[c], kv_all.at[c], kv_sem.at[0], kv_sem.at[1], at.x)
    kv_back = remote(
        kv_all.at[1 - c], kv_all.at[1 - c], kv_sem.at[0], kv_sem.at[1], at.x
    )

    @pl.when(c == 0)
    def _():
        kv_copy.start()

    gate.start_x()
    gate.start_s()

    def prep_q(h, _):
        r = pl.multiple_of(h * hd, hd)
        q_t[pl.ds(r, hd), :] = prepared(r, q_gain, 1.0 / math.sqrt(hd)).astype(BF16)
        return 0

    lax.fori_loop(0, q_heads, prep_q, 0)
    leaving[2].start()
    length = length_ref[0]

    def load_block(index, k_nat, v_ext):
        pos = index * rows + lax.broadcasted_iota(jnp.int32, (1, rows), 1)
        live = (pos < length).astype(F32)
        first = (lax.broadcasted_iota(jnp.int32, (16, rows), 0) == 0).astype(F32)
        for g in range(kv_heads):
            k_nat[g] = kv_all[index, g * hd : (g + 1) * hd, :].astype(F32).T.astype(BF16)
            v = kv_all[index, kv_cols + g * hd : kv_cols + (g + 1) * hd, :].astype(F32)
            v_ext[g, 0:hd, :] = (v * live).astype(BF16)
            v_ext[g, hd:, :] = (first * live).astype(BF16)

    load_block(c, k_own, v_own)
    below = lax.broadcasted_iota(jnp.int32, (256, 256), 0) <= lax.broadcasted_iota(
        jnp.int32, (256, 256), 1
    )

    def own_block(h, _):
        g = h // group
        qh = q_t[pl.ds(pl.multiple_of(h * hd, hd), hd), :]
        for i in range(rows // 256):
            qi = qh[:, i * 256 : (i + 1) * 256]
            top = i * 256
            e = jnp.exp(mm(k_own[g, top : top + 256, :], qi))
            e = jnp.where(below, e, 0.0).astype(BF16)
            total = mm(v_own[g, :, top : top + 256], e)
            if i:
                e = jnp.exp(mm(k_own[g, 0:top, :], qi)).astype(BF16)
                total += mm(v_own[g, :, 0:top], e)
            acc[h, :, top : top + 256] = total
        return 0

    lax.fori_loop(0, q_heads, own_block, 0)
    out.relay()
    up.start()

    @pl.when(c == 1)
    def _():
        kv_back.wait_recv()
        load_block(1 - c, k_off, v_off)

        def other_block(h, _):
            g = h // group
            qh = q_t[pl.ds(pl.multiple_of(h * hd, hd), hd), :]
            for i in range(rows // 256):
                cols = slice(i * 256, (i + 1) * 256)
                e = jnp.exp(mm(k_off[g], qh[:, cols])).astype(BF16)
                acc[h, :, cols] += mm(v_off[g], e)
            return 0

        lax.fori_loop(0, q_heads, other_block, 0)

    @pl.when(c == 0)
    def _():
        kv_all[1 - c] = jnp.zeros(kv_all.shape[1:], BF16)

    leaving[3].start()

    def chunk_cols(owner, j):
        return pl.ds(pl.multiple_of(owner * q_cols + j * 128, 128), 128)

    def along(owner, j, way):
        ref = heads_all.at[:, chunk_cols(owner, j)]
        dev = at.z(jnp.minimum(t + 1, n_tp - 1) if way == 0 else jnp.maximum(t - 1, 0))
        return remote(ref, ref, h_send.at[way, owner, j], h_recv.at[way, owner, j], dev)

    chunks = q_cols // 128

    def pass_on(owner, j, way):
        @pl.when(t < n_tp - 1 if way == 0 else t > 0)
        def _():
            along(owner, j, way).start()

    for j in range(chunks):
        parts = []
        for h in range(2 * j, 2 * j + 2):
            inverse = 1.0 / acc[h, hd : hd + 1, :]
            inv_den[h : h + 1, :] = inverse
            parts.append(acc[h, 0:hd, :] * inverse)
        pair = jnp.concatenate(parts, axis=0)
        heads_all[:, chunk_cols(t, j)] = pair.T.astype(BF16)
        for way in (0, 1):
            pass_on(t, j, way)
    inv_den[q_heads:, :] = jnp.zeros((8 - q_heads, rows), F32)

    for d in range(1, n_tp):
        for j in range(chunks):

            @pl.when(t >= d)
            def _():
                along(t - d, j, 0).wait_recv()
                pass_on(t - d, j, 0)

            @pl.when(t + d < n_tp)
            def _():
                along(t + d, j, 1).wait_recv()
                pass_on(t + d, j, 1)

            step = (d - 1) * chunks + j
            if step == 2:
                gate.relay()
            if step == 4:
                out.relay_last()
            if step == 7:
                up.relay()
                down.start()

    out.finish()
    local[1].wait()
    leaving[4].start()
    leaving[5].start()

    def residual(i, _):
        r = pl.ds(pl.multiple_of(i * 128, 128), 128)
        x = hid_ref[r, :].astype(F32) + mm_nt(heads_all[r, :], wo_full[...])
        resid[r, :] = x
        scale = lax.rsqrt(jnp.mean(x * x, axis=-1, keepdims=True) + EPSILON)
        h = (x * scale).astype(BF16)
        h2[r, :] = h
        h2t[:, r] = h.T

        @pl.when(i == 1)
        def _():
            gate.relay_last()

        @pl.when(i == 3)
        def _():
            gate.finish()
            local[2].wait()
            loads[0].start()

        return 0

    lax.fori_loop(0, rows // 128, residual, 0)
    leaving[6].start()
    leaving[7].start()
    up.relay_last()
    up.finish()
    local[3].wait()
    loads[1].start()
    loads[0].wait()
    loads[1].wait()
    tiles = act.shape[2] // 256
    half = rows // 2

    def act_copy(f):
        cols = pl.ds(pl.multiple_of(f * 256, 256), 256)
        return pltpu.make_async_copy(
            act.at[:, :, cols], act_out.at[:, :, cols], act_sem.at[f]
        )

    def gate_up(f, _):
        cols = pl.ds(pl.multiple_of(f * 256, 256), 256)
        for i in (0, 1):
            r = slice(i * half, (i + 1) * half)
            g = mm(h2[r, :], wg[:, cols])
            u = mm(h2[r, :], wu[:, cols])
            s = 1.0 / (1.0 + jnp.exp(-g))
            silu = g * s
            act[0, r, cols] = (silu * u).astype(BF16)
            act[1, r, cols] = (u * (s * (1.0 + g * (1.0 - s)))).astype(BF16)
            act[2, r, cols] = silu.astype(BF16)

        act_copy(f).start()

        @pl.when(f == tiles // 2 - 1)
        def _():
            down.relay()

        return 0

    lax.fori_loop(0, tiles, gate_up, 0)
    down.relay_last()
    down.finish()
    local[4].wait()

    def act_done(f, _):
        act_copy(f).wait()
        return 0

    lax.fori_loop(0, tiles, act_done, 0)
    for owner in range(n_tp):
        for j in range(chunks):

            @pl.when(jnp.logical_and(t < n_tp - 1, owner <= t))
            def _():
                along(owner, j, 0).wait_send()

            @pl.when(jnp.logical_and(t > 0, owner >= t))
            def _():
                along(owner, j, 1).wait_send()

    for d in range(n_tp - 1):
        wo_part(d, t).wait_send()

    @pl.when(c == 0)
    def _():
        kv_copy.wait_send()

    for cp in leaving:
        cp.wait()


def rope_tables(positions, hd):
    freq = ROPE_BASE ** (-np.arange(hd // 2, dtype=np.float64) / (hd // 2))
    angle = freq[:, None] * np.arange(positions, dtype=np.float64)[None, :]
    return np.cos(angle).astype(np.float32), np.sin(angle).astype(np.float32)


def call_a(mesh, args):
    (hidden_in, seq_lengths, attn_gain, ffn_gain, query_gain, key_gain,
     w_query, w_key, w_value, w_out, w_gate, w_up, w_down) = args
    n_shard, n_ctx, n_tp = mesh.shape["shard"], mesh.shape["ctx"], mesh.shape["tp"]
    rows, width = hidden_in.shape
    hd = query_gain.shape[0]
    q_cols, kv_cols = w_query.shape[1], w_key.shape[1]
    q_heads, kv_heads = q_cols // hd, kv_cols // hd
    block = w_query.shape[0]
    padded = round_up(w_gate.shape[1])
    cosine, sine = rope_tables(n_ctx * rows, hd)
    vm = pl.BlockSpec(memory_space=pltpu.VMEM)
    hbm = pl.BlockSpec(memory_space=pltpu.HBM)
    sm = pl.BlockSpec(memory_space=pltpu.SMEM)
    qkv_cols = q_cols + 2 * kv_cols
    S = jax.ShapeDtypeStruct
    dma = pltpu.SemaphoreType.DMA
    chunks = q_cols // 128
    return pl.pallas_call(
        functools.partial(kernel_a, (n_shard, n_tp, hd)),
        out_shape=(
            S((width, qkv_cols), BF16),
            S((width, n_tp * q_cols), BF16),
            S((width, padded), BF16),
            S((width, padded), BF16),
            S((width, padded), BF16),
            S((rows, n_tp * q_cols), BF16),
            S((q_cols, rows), BF16),
            S((n_ctx, 2 * kv_cols, rows), BF16),
            S((8, rows), F32),
            S((qkv_cols, rows), F32),
            S((rows, width), F32),
            S((width, rows), BF16),
            S((3, rows, padded), BF16),
        ),
        in_specs=[sm] + [vm] * 14,
        out_specs=(hbm,) * 8 + (vm,) + (hbm,) * 4,
        scratch_shapes=[
            pltpu.VMEM((width, qkv_cols), BF16),
            pltpu.VMEM((width, n_tp * q_cols), BF16),
            pltpu.VMEM((rows, n_tp * q_cols), BF16),
            pltpu.VMEM((q_cols, rows), BF16),
            pltpu.VMEM((n_ctx, 2 * kv_cols, rows), BF16),
            pltpu.VMEM((qkv_cols, rows), F32),
            pltpu.VMEM((rows, width), F32),
            pltpu.VMEM((rows, width), BF16),
            pltpu.VMEM((width, rows), BF16),
            pltpu.VMEM((block, qkv_cols), BF16),
            pltpu.VMEM((block, n_tp * q_cols), BF16),
            pltpu.VMEM((block, padded), BF16),
            pltpu.VMEM((block, padded), BF16),
            pltpu.VMEM((block, padded), BF16),
            pltpu.VMEM((width, padded), BF16),
            pltpu.VMEM((width, padded), BF16),
            pltpu.VMEM((3, rows, padded), BF16),
            pltpu.VMEM((rows, width), BF16),
            pltpu.VMEM((kv_heads, rows, hd), BF16),
            pltpu.VMEM((kv_heads, rows, hd), BF16),
            pltpu.VMEM((kv_heads, hd + 16, rows), BF16),
            pltpu.VMEM((kv_heads, hd + 16, rows), BF16),
            pltpu.VMEM((q_heads, hd + 16, rows), F32),
            dma((5, 7)),
            dma((5, 7)),
            dma((n_tp - 1,)),
            dma((n_tp - 1,)),
            dma((2, n_tp, chunks)),
            dma((2, n_tp, chunks)),
            dma((2,)),
            dma((7,)),
            dma((padded // 256,)),
            dma((8,)),
        ],
        compiler_params=pltpu.CompilerParams(
            collective_id=0, has_side_effects=True, vmem_limit_bytes=VMEM_LIMIT
        ),
    )(
        seq_lengths, hidden_in, attn_gain, ffn_gain,
        query_gain, key_gain, w_query, w_key, w_value,
        w_out.T, w_gate, w_up, w_down.T, jnp.asarray(cosine), jnp.asarray(sine),
    )


LAG = 2


class Line:
    def __init__(self, at, part, landing, send, recv, chunks, folds=1):
        self.at, self.part, self.landing = at, part, landing
        self.send, self.recv, self.chunks, self.folds = send, recv, chunks, folds
        self.half = landing.shape[1]
        self.size = self.half // chunks
        self.last = at.n_tp - 1

    def pos(self, way):
        return self.at.t if way == 0 else self.last - self.at.t

    def dev(self, way, step):
        to = self.at.t + (step if way == 0 else -step)
        return self.at.z(jnp.clip(to, 0, self.last))

    def local(self, k):
        return pl.ds(pl.multiple_of(k * self.size, self.size), self.size)

    def rows(self, way, k):
        return pl.ds(self.start(way, k), self.size)

    def start(self, way, k):
        fold = self.half // self.folds
        if self.folds == 1:
            first = (1 - way) * fold + k * self.size
        else:
            per = self.chunks // self.folds
            group = lax.div(k, per)
            first = (2 * group + 1 - way) * fold + (k - group * per) * self.size
        return pl.multiple_of(first, self.size)

    def copy(self, way, k):
        return remote(
            self.part.at[self.rows(way, k)],
            self.landing.at[way, self.local(k)],
            self.send.at[way, k],
            self.recv.at[way, k],
            self.dev(way, 1),
        )

    def reduce(self, step, final):
        for way in (0, 1):
            pos = self.pos(way)
            k = step - pos * LAG
            live = jnp.logical_and(k >= 0, k < self.chunks)

            @pl.when(jnp.logical_and(live, pos > 0))
            def _():
                self.copy(way, k).wait_recv()
                value = self.part[self.rows(way, k), :].astype(F32)
                value += self.landing[way, self.local(k), :].astype(F32)

                @pl.when(pos < self.last)
                def _():
                    self.part[self.rows(way, k), :] = value.astype(BF16)

                @pl.when(pos == self.last)
                def _():
                    final(way, k, value)

            @pl.when(jnp.logical_and(live, pos < self.last))
            def _():
                self.copy(way, k).start()

    def drain(self):
        for way in (0, 1):

            @pl.when(self.pos(way) < self.last)
            def _():
                def one(k, _):
                    self.copy(way, k).wait_send()
                    return 0

                lax.fori_loop(0, self.chunks, one, 0)


class Back:
    def __init__(self, line, whole, send, recv, source=None):
        self.line, self.whole, self.send, self.recv = line, whole, send, recv
        self.source = source

    def copy(self, way, k, first=False):
        line = self.line
        dst = self.whole.at[line.rows(way, k)]
        src = self.source.at[way, line.local(k)] if first and self.source is not None else dst
        return remote(src, dst, self.send.at[way, k], self.recv.at[way, k], line.dev(way, -1))

    def step(self, step):
        line = self.line
        for way in (0, 1):
            pos = line.pos(way)
            k = step - (line.last - pos) * LAG
            live = jnp.logical_and(k >= 0, k < line.chunks)

            @pl.when(jnp.logical_and(live, pos < line.last))
            def _():
                self.copy(way, k).wait_recv()

                @pl.when(pos > 0)
                def _():
                    self.copy(way, k).start()

            @pl.when(jnp.logical_and(live, pos == line.last))
            def _():
                self.copy(way, k, True).start()

    def drain(self):
        line = self.line
        for way in (0, 1):

            @pl.when(line.pos(way) > 0)
            def _():
                def one(k, _):
                    self.copy(way, k).wait_send()
                    return 0

                lax.fori_loop(0, line.chunks, one, 0)


class Scatter:
    def __init__(self, at, source, room, tmp_sem, send, recv, index):
        self.at, self.source, self.room = at, source, room
        self.tmp_sem, self.send, self.recv, self.index = tmp_sem, send, recv, index
        self.rows = room.shape[0] // 8
        self.tmp, self.relayed = self.land(7), self.land(4)
        self.final = (self.land(5), self.land(6))
        self.direct, self.indirect = 1 + at.core, 2 - at.core
        self.other = (
            at.core * at.x[0] + (1 - at.core) * at.y[0],
            at.core * at.x[1] + (1 - at.core) * at.y[1],
            at.t,
        )
        self.mine = [at.own] + [at.slots[n] for n in ("X", "Y", "D")]
        self.theirs = [at.slots[n] for n in ("S", "SX", "SY", "SD")]

    def land(self, j):
        return self.room.at[pl.ds(pl.multiple_of(j * self.rows, self.rows), self.rows)]

    def block(self, slot):
        return self.source.at[pl.ds(pl.multiple_of(slot * self.rows, self.rows), self.rows)]

    def copy(self, k, src, dst, dev):
        return remote(src, dst, self.send.at[self.index, k], self.recv.at[self.index, k], dev)

    def share(self, j):
        return self.copy(j, self.block(self.theirs[j]), self.land(j), self.at.sib)

    def start(self):
        for j in (3, 1, 2, 0):
            self.share(j).start()
        self.fetch(3).start()

    def slot(self, j):
        if isinstance(j, int):
            return self.mine[j]
        return jnp.where(j == 1, self.mine[1], self.mine[2])

    def arrived(self, j):
        ref = self.land(j)
        self.copy(j, ref, ref, self.at.sib).wait_recv()

    def fetch(self, j):
        return pltpu.make_async_copy(self.block(self.slot(j)), self.tmp, self.tmp_sem)

    def add(self, j, extra=()):
        self.arrived(j)
        self.fetch(j).wait()
        land = self.land(j)

        def piece(i, _):
            r = pl.ds(pl.multiple_of(i * 64, 64), 64)
            value = land[r, :].astype(F32) + self.tmp[r, :].astype(F32)
            for ref in extra:
                value += ref[r, :].astype(F32)
            land[r, :] = value.astype(BF16)
            return 0

        lax.fori_loop(0, self.rows // 64, piece, 0)

    def hop(self, k):
        at = self.at
        if k == 4:
            return self.copy(4, self.land(3), self.relayed, at.relay)
        if k == 5:
            return self.copy(5, self.land(self.direct), self.final[0], at.relay)
        return self.copy(6, self.land(self.indirect), self.final[1], self.other)

    def first(self):
        self.add(3)
        self.fetch(self.direct).start()
        self.hop(4).start()
        self.add(self.direct)
        self.fetch(self.indirect).start()
        self.hop(5).start()

    def second(self):
        self.hop(4).wait_recv()
        self.add(self.indirect, (self.relayed,))
        self.fetch(0).start()
        self.hop(6).start()

    def finish(self, use):
        self.arrived(0)
        self.hop(5).wait_recv()
        self.hop(6).wait_recv()
        self.fetch(0).wait()
        land = self.land(0)

        def piece(i, _):
            r = pl.ds(pl.multiple_of(i * 64, 64), 64)
            value = land[r, :].astype(F32) + self.tmp[r, :].astype(F32)
            value += self.final[0][r, :].astype(F32) + self.final[1][r, :].astype(F32)
            use(r, value)
            return 0

        lax.fori_loop(0, self.rows // 64, piece, 0)

    def drain(self):
        for j in range(4):
            self.share(j).wait_send()
        for k in (4, 5, 6):
            self.hop(k).wait_send()


def kernel_b(
    shape,
    length_ref,
    og_ref,
    wd_hbm,
    act_hbm,
    wg_hbm,
    wu_hbm,
    h2t_hbm,
    resid_hbm,
    attn_low,
    rg_out,
    gate_out,
    ffn_part,
    wgrads,
    rg_own,
    gate_sum,
    f_part,
    d_part,
    wg,
    wu,
    wd,
    resid,
    left_t,
    gl,
    act,
    land_d,
    stage,
    d_send,
    d_recv,
    b_send,
    b_recv,
    s_send,
    s_recv,
    loc_sem,
    tile_sem,
    st_sem,
    free_sem,
):
    n_shard, n_tp, chunks = shape
    at = Place(n_shard, n_tp)
    rows, width = og_ref.shape
    padded = wd.shape[1]
    block = stage.shape[1]
    half = rows // 2
    tiles = padded // 256
    last = n_tp - 1
    def tile_load(f):
        cols = pl.ds(pl.multiple_of(f * 256, 256), 256)
        return (
            pltpu.make_async_copy(wd_hbm.at[:, cols], wd.at[:, cols], tile_sem.at[0, f]),
            pltpu.make_async_copy(
                act_hbm.at[1:3, :, cols], act.at[1:3, :, cols], tile_sem.at[1, f]
            ),
        )

    for f in range(tiles):
        for cp in tile_load(f):
            cp.start()
    pairs = (
        (wg_hbm, wg),
        (wu_hbm, wu),
        (resid_hbm, resid),
        (act_hbm.at[0], act.at[0]),
        (h2t_hbm, left_t.at[:, pl.ds(0, rows)]),
    )
    loads = [
        pltpu.make_async_copy(src, dst, loc_sem.at[i]) for i, (src, dst) in enumerate(pairs)
    ]
    for cp in loads:
        cp.start()
    at.greet()
    length = length_ref[0]

    def live_rows(start, n):
        pos = at.c * rows + start + lax.broadcasted_iota(jnp.int32, (n, 1), 0)
        return (pos < length).astype(F32)

    def mask_grad(i, _):
        start = pl.multiple_of(i * 128, 128)
        r = pl.ds(start, 128)
        low = (og_ref[r, :].astype(F32) * live_rows(start, 128)).astype(BF16)
        gl[r, :] = low
        left_t[:, pl.ds(pl.multiple_of(rows + start, 128), 128)] = low.T
        return 0

    lax.fori_loop(0, rows // 128, mask_grad, 0)

    quarter = half // 2
    lines, backs = [], []
    for n in (0, 1):
        r = pl.ds(n * half, half)
        line = Line(at, d_part.at[r], land_d.at[n], d_send.at[n], d_recv.at[n], chunks)
        lines.append(line)
        backs.append(Back(line, attn_low.at[r], b_send.at[n], b_recv.at[n]))

    def final_d2(n):
        def final(way, k, value):
            line = lines[n]
            start = n * half + (1 - way) * quarter + k * line.size
            r = pl.ds(pl.multiple_of(start, line.size), line.size)
            x = resid[r, :]
            scale = lax.rsqrt(jnp.mean(x * x, axis=-1, keepdims=True) + EPSILON)
            h = x * scale
            inner = jnp.mean(value * h, axis=-1, keepdims=True)
            grad = gl[r, :].astype(F32) + scale * (value - h * inner)
            rg_own[pl.ds(pl.multiple_of(n * quarter + k * line.size, line.size), line.size), :] = grad
            attn_low[r, :] = grad.astype(BF16)

        return final

    def move(n, step):
        lines[n].reduce(step, final_d2(n))
        backs[n].step(step - last * LAG)

    def moves(n, slot):
        for i in range(LAG):
            move(n, slot * LAG + i)

    def mid(n):
        r = slice(n * half, (n + 1) * half)

        def one(f, _):
            cols = pl.ds(pl.multiple_of(f * 256, 256), 256)
            if n == 0:
                for cp in tile_load(f):
                    cp.wait()
            g = mm(gl[r, :], wd[:, cols])
            act[1, r, cols] = (g * act[1, r, cols].astype(F32)).astype(BF16)
            act[2, r, cols] = (g * act[2, r, cols].astype(F32)).astype(BF16)
            if n == 1:

                @pl.when(lax.rem(f, 4) == 2)
                def _():
                    moves(0, 1 + lax.div(f, 4))

            return 0

        lax.fori_loop(0, tiles, one, 0)

    def back_part(q):
        r = slice(q * quarter, (q + 1) * quarter)
        total = mm_nt(act[1, r, :], wg[...]) + mm_nt(act[2, r, :], wu[...])
        d_part[r, :] = total.astype(BF16)

    mid(0)
    for cp in loads:
        cp.wait()
    back_part(0)
    back_part(1)
    moves(0, 0)
    mid(1)
    done = 1 + (tiles + 1) // 4
    back_part(2)
    moves(0, done)
    back_part(3)
    done = (done + 1) * LAG

    peers = (at.sib, at.x, at.y)
    for n, peer in enumerate(peers):
        pl.semaphore_signal(free_sem.at[n], inc=1, device_id=peer, device_id_type=MESH)
    gate = Scatter(at, wgrads.at[1], wg, loc_sem.at[0], s_send, s_recv, 0)

    def free(n):
        pl.semaphore_wait(free_sem.at[n], 1)

    blocks = width // block
    per_step = PER_STEP
    count = 3 * blocks
    def weight_of(n):
        return lax.rem(lax.div(n, blocks) + 1, 3)

    def stage_copy(n):
        w, slot = lax.rem(n, blocks), lax.rem(n, 2)
        return pltpu.make_async_copy(
            stage.at[slot],
            wgrads.at[weight_of(n), pl.ds(pl.multiple_of(w * block, block), block)],
            st_sem.at[slot],
        )

    def weight_grad(n):
        a, w, slot = weight_of(n), lax.rem(n, blocks), lax.rem(n, 2)

        @pl.when(n >= 2)
        def _():
            stage_copy(n - 2).wait()

        first = pl.multiple_of(jnp.where(a == 0, rows, 0), 128)
        left = left_t[pl.ds(pl.multiple_of(w * block, block), block), pl.ds(first, rows)]
        for f in range(tiles):
            cols = slice(f * 256, (f + 1) * 256)
            stage[slot, :, cols] = mm(left, act[a, :, cols]).astype(BF16)
        stage_copy(n).start()

    keeps = pltpu.make_async_copy(f_part, ffn_part, loc_sem.at[1])

    def forward_part(q):
        r = pl.ds(pl.multiple_of(q * quarter, quarter), quarter)
        total = mm_nt(act[0, r, :], wd[...])
        mine = (at.t == lax.rem(q, 2) * last).astype(F32)
        f_part[r, :] = (total + resid[r, :] * mine).astype(BF16)

    def use_gate(r, value):
        gate_sum[r, :] = value.astype(BF16)

    def start_gate():
        free(0)
        gate.start()

    def first_gate():
        free(1)
        free(2)
        gate.first()

    leaving = [
        pltpu.make_async_copy(rg_own, rg_out, loc_sem.at[2]),
        pltpu.make_async_copy(gate_sum, gate_out, loc_sem.at[3]),
    ]

    def finish_gate():
        gate.finish(use_gate)
        leaving[1].start()

    total = chunks + 2 * last * LAG
    begin = (blocks + 2 * per_step - 1) // per_step
    events = {
        begin: start_gate,
        begin + total // 12: first_gate,
        begin + total // 4: gate.second,
        total - 4: leaving[0].start,
        total - 3: finish_gate,
    }

    def tail(step, _):
        move(0, step + done)
        move(1, step)

        for n in range(per_step):

            @pl.when(step * per_step + n < count)
            def _():
                weight_grad(step * per_step + n)

        for when, todo in events.items():

            @pl.when(step == when)
            def _():
                todo()

        @pl.when(jnp.logical_and(step >= total - 10, step < total - 6))
        def _():
            forward_part(step - (total - 10))

        return 0

    steps = max(total, -(-count // per_step))
    lax.fori_loop(0, steps, tail, 0)
    keeps.start()
    stage_copy(count - 2).wait()
    stage_copy(count - 1).wait()
    gate.drain()
    for n in (0, 1):
        lines[n].drain()
        backs[n].drain()
    keeps.wait()
    for cp in leaving:
        cp.wait()


def call_b(mesh, chunks, seq_lengths, out_grad, wd_full, act, wg_full, wu_full, h2t, resid):
    n_shard, n_tp = mesh.shape["shard"], mesh.shape["tp"]
    rows, width = out_grad.shape
    block = width // (n_shard * mesh.shape["ctx"])
    padded = wg_full.shape[1]
    half = rows // 2
    vm = pl.BlockSpec(memory_space=pltpu.VMEM)
    hbm = pl.BlockSpec(memory_space=pltpu.HBM)
    sm = pl.BlockSpec(memory_space=pltpu.SMEM)
    S = jax.ShapeDtypeStruct
    dma = pltpu.SemaphoreType.DMA
    return pl.pallas_call(
        functools.partial(kernel_b, (n_shard, n_tp, chunks)),
        out_shape=(
            S((rows, width), BF16),
            S((half, width), F32),
            S((block, padded), BF16),
            S((rows, width), BF16),
            S((3, width, padded), BF16),
        ),
        in_specs=[sm, vm] + [hbm] * 6,
        out_specs=(vm, hbm, hbm, hbm, hbm),
        scratch_shapes=[
            pltpu.VMEM((half, width), F32),
            pltpu.VMEM((block, padded), BF16),
            pltpu.VMEM((rows, width), BF16),
            pltpu.VMEM((rows, width), BF16),
            pltpu.VMEM((width, padded), BF16),
            pltpu.VMEM((width, padded), BF16),
            pltpu.VMEM((width, padded), BF16),
            pltpu.VMEM((rows, width), F32),
            pltpu.VMEM((width, 2 * rows), BF16),
            pltpu.VMEM((rows, width), BF16),
            pltpu.VMEM((3, rows, padded), BF16),
            pltpu.VMEM((2, 2, half // 2, width), BF16),
            pltpu.VMEM((2, block, padded), BF16),
            dma((2, 2, chunks)),
            dma((2, 2, chunks)),
            dma((2, 2, chunks)),
            dma((2, 2, chunks)),
            dma((1, 7)),
            dma((1, 7)),
            dma((5,)),
            dma((2, padded // 256)),
            dma((2,)),
            pltpu.SemaphoreType.REGULAR((3,)),
        ],
        compiler_params=pltpu.CompilerParams(
            collective_id=1, has_side_effects=True, vmem_limit_bytes=VMEM_LIMIT
        ),
    )(seq_lengths, out_grad, wd_full, act, wg_full, wu_full, h2t, resid)


def kernel_c(
    shape,
    length_ref,
    attn_low,
    q_t,
    kv_all,
    inv_den,
    gain_one_ref,
    gain_two_ref,
    q_gain_ref,
    k_gain_ref,
    wq_ref,
    wk_ref,
    wv_ref,
    cos_ref,
    sin_ref,
    rg_hbm,
    hid_hbm,
    wqkv_hbm,
    proj_hbm,
    wg_hbm,
    wu_hbm,
    gate_hbm,
    ffn_hbm,
    wgrads,
    heads_hbm,
    wo_hbm,
    block_out,
    inp,
    query_out,
    key_out,
    value_out,
    out_out,
    up_out,
    down_out,
    small,
    g_query,
    g_key,
    g_value,
    g_out,
    g_up,
    g_down,
    rg_own,
    hid_ref,
    wqkv,
    proj_t,
    wg_ref,
    wu_ref,
    gate_sum,
    heads_own,
    wo_own,
    hg_t,
    delta,
    k_own,
    v_own,
    kt_own,
    dq_t,
    dkv,
    dkv_send,
    dkv_land,
    gain_acc,
    dqkv,
    f_part,
    d_part,
    land_f,
    land_d,
    left_t,
    part,
    room_w,
    room_p,
    cols_acc,
    qk,
    qk_land,
    tile,
    s_send,
    s_recv,
    f_send,
    f_recv,
    d_send,
    d_recv,
    b_send,
    b_recv,
    o_send,
    o_recv,
    e_send,
    e_recv,
    t_send,
    t_recv,
    loc_sem,
    out_sem,
):
    n_shard, n_tp, chunks, hd = shape
    at = Place(n_shard, n_tp)
    c, t = at.c, at.t
    rows, width = hid_hbm.shape
    q_cols, kv_cols = wq_ref.shape[1], wk_ref.shape[1]
    q_heads, kv_heads = q_cols // hd, kv_cols // hd
    group = q_heads // kv_heads
    halfd = hd // 2
    half = rows // 2
    block = wq_ref.shape[0]
    units = wg_hbm.shape[1]
    last = n_tp - 1
    own_cols = pl.ds(pl.multiple_of(t * q_cols, q_cols), q_cols)
    quarter = half // 2
    loads = [
        pltpu.make_async_copy(heads_hbm.at[:, own_cols], heads_own, loc_sem.at[0]),
        pltpu.make_async_copy(wo_hbm.at[:, own_cols], wo_own, loc_sem.at[1]),
        pltpu.make_async_copy(ffn_hbm, f_part, loc_sem.at[2]),
    ]
    late = [
        pltpu.make_async_copy(src, dst, loc_sem.at[8 + i])
        for i, (src, dst) in enumerate(
            (
                (proj_hbm, proj_t),
                (wqkv_hbm, wqkv),
                (hid_hbm, hid_ref),
                (rg_hbm, rg_own),
                (wg_hbm, wg_ref),
                (wu_hbm, wu_ref),
                (gate_hbm, gate_sum),
            )
        )
    ]
    for cp in loads:
        cp.start()
    at.greet()
    down, up = (
        Scatter(at, wgrads.at[k], room_w.at[i], loc_sem.at[3 + i], s_send, s_recv, i)
        for i, k in enumerate((0, 2))
    )
    rest = Scatter(at, part, room_p, loc_sem.at[5], s_send, s_recv, 2)
    down.start()
    up.start()
    ffn = Line(at, f_part, land_f, f_send, f_recv, chunks, 2)
    ffn_back = Back(ffn, block_out, o_send, o_recv, land_f)
    d1 = Line(at, d_part, land_d, d_send, d_recv, chunks, 2)
    back = Back(d1, inp, b_send, b_recv)
    length = length_ref[0]

    def final_ffn(way, k, value):
        pos = c * rows + ffn.start(way, k)
        pos += lax.broadcasted_iota(jnp.int32, (ffn.size, 1), 0)
        value = value * (pos < length).astype(F32)
        land_f[way, ffn.local(k), :] = value.astype(BF16)

    def move_ffn(step):
        ffn.reduce(step, final_ffn)
        ffn_back.step(step - last * LAG)

    def moves_ffn(slot):
        for i in range(PER_SLOT):
            move_ffn(slot * PER_SLOT + i)

    def keep(n, way):
        return pltpu.make_async_copy(
            land_f.at[way, pl.ds(n * quarter, quarter)],
            block_out.at[pl.ds((2 * n + 1 - way) * quarter, quarter)],
            loc_sem.at[6 + n],
        )

    def keep_all(act):
        for way in (0, 1):

            @pl.when(t == (last if way == 0 else 0))
            def _():
                for n in (0, 1):
                    act(keep(n, way))

    for cp in loads:
        cp.wait()
    moves_ffn(0)
    for cp in late:
        cp.start()

    def heads_grad(i, _):
        r = pl.ds(pl.multiple_of(i * 256, 256), 256)
        hg_t[:, r] = mm(attn_low[r, :], wo_own[...]).T.astype(BF16)
        return 0

    lax.fori_loop(0, rows // 256, heads_grad, 0)
    for j in range(q_cols // 128):
        cols = slice(j * 128, (j + 1) * 128)
        both = heads_own[:, cols].astype(F32).T * hg_t[cols, :].astype(F32)
        for n in range(128 // hd):
            h = j * (128 // hd) + n
            delta[h : h + 1, :] = jnp.sum(both[n * hd : (n + 1) * hd], axis=0, keepdims=True)
    moves_ffn(1)
    down.first()

    def live_keys(index):
        pos = index * rows + lax.broadcasted_iota(jnp.int32, (1, rows), 1)
        return (pos < length).astype(F32)

    def load_block(index, k_nat, v_nat, kt):
        live = live_keys(index)
        for g in range(kv_heads):
            key = kv_all[index, g * hd : (g + 1) * hd, :].astype(F32)
            k_nat[g] = key.T.astype(BF16)
            kt[g] = (key * live).astype(BF16)
            value = kv_all[index, kv_cols + g * hd : kv_cols + (g + 1) * hd, :]
            v_nat[g] = value.astype(F32).T.astype(BF16)

    below = lax.broadcasted_iota(jnp.int32, (256, 256), 0) <= lax.broadcasted_iota(
        jnp.int32, (256, 256), 1
    )

    def segment(h, g, i, lo, hi, masked, k_nat, v_nat, kt):
        cols = slice(i * 256, (i + 1) * 256)
        hr = pl.ds(pl.multiple_of(h * hd, hd), hd)
        qi, oi = q_t[hr, cols], hg_t[hr, cols]
        p = jnp.exp(mm(k_nat[g, lo:hi, :], qi)) * inv_den[pl.ds(h, 1), cols]
        if masked:
            p = jnp.where(below, p, 0.0)
        dp = mm(v_nat[g, lo:hi, :], oi)
        ds = (p * (dp - delta[pl.ds(h, 1), cols])).astype(BF16)
        dq_t[hr, cols] += mm(kt[g, :, lo:hi], ds)
        dkv[g, :, lo:hi] += mm_nt(qi, ds)
        dkv[kv_heads + g, :, lo:hi] += mm_nt(oi, p.astype(BF16))

    dq_t[...] = jnp.zeros_like(dq_t)
    dkv[...] = jnp.zeros_like(dkv)
    give = remote(dkv_send, dkv_land, e_send.at[3], e_recv.at[3], at.x)

    @pl.when(c == 1)
    def _():
        load_block(0, k_own, v_own, kt_own)

        def one(h, _):
            for i in range(rows // 256):
                segment(h, h // group, i, 0, rows, False, k_own, v_own, kt_own)

            @pl.when(lax.rem(h, 2) == 1)
            def _():
                moves_ffn(2 + lax.div(h, 2))

            return 0

        lax.fori_loop(0, q_heads, one, 0)
        live = live_keys(0)
        for n in range(2 * kv_heads):
            dkv_send[n] = (dkv[n] * live).astype(BF16)
        give.start()
        dkv[...] = jnp.zeros_like(dkv)

    @pl.when(c == 0)
    def _():
        def one(h, _):
            moves_ffn(2 + h)
            return 0

        lax.fori_loop(0, q_heads // 2, one, 0)

    up.first()
    down.second()
    load_block(c, k_own, v_own, kt_own)

    def own_block(h, _):
        for i in range(rows // 256):
            segment(h, h // group, i, i * 256, (i + 1) * 256, True, k_own, v_own, kt_own)
            if i:
                segment(h, h // group, i, 0, i * 256, False, k_own, v_own, kt_own)


        @pl.when(lax.rem(h, 2) == 1)
        def _():
            moves_ffn(2 + lax.div(q_heads, 2) + lax.div(h, 2))

        return 0

    lax.fori_loop(0, q_heads, own_block, 0)
    moved = (2 + 2 * (q_heads // 2)) * PER_SLOT
    live = live_keys(c)
    for n in range(2 * kv_heads):
        dkv[n] = dkv[n] * live

    @pl.when(c == 0)
    def _():
        give.wait_recv()
        for n in range(2 * kv_heads):
            dkv[n] += dkv_land[n].astype(F32)

    here = pl.ds(pl.multiple_of(c * rows, rows), rows)
    gain_acc[...] = jnp.zeros_like(gain_acc)
    for cp in late:
        cp.wait()

    def through(which, row, grad, gain):
        x = proj_t[pl.ds(pl.multiple_of(row, hd), hd), :]
        scale = lax.rsqrt(jnp.mean(x * x, axis=0, keepdims=True) + EPSILON)
        xh = x * scale
        cosine, sine = cos_ref[:, here], sin_ref[:, here]
        a, b = grad[:halfd], grad[halfd:]
        grad = jnp.concatenate([a * cosine + b * sine, b * cosine - a * sine], axis=0)
        gain_acc[which] += grad * xh
        grad = grad * gain
        inner = jnp.mean(grad * xh, axis=0, keepdims=True)
        return scale * (grad - xh * inner)

    q_gain, k_gain = column(q_gain_ref, hd), column(k_gain_ref, hd)
    factor = 1.0 / math.sqrt(hd)

    def query_back(h, _):
        row = pl.multiple_of(h * hd, hd)
        r = pl.ds(row, hd)
        dq_t[r, :] = through(0, row, dq_t[r, :] * factor, q_gain)
        return 0

    lax.fori_loop(0, q_heads, query_back, 0)
    dqkv[:, 0:q_cols] = dq_t[...].T.astype(BF16)
    pair = jnp.concatenate(
        [through(1, q_cols + g * hd, dkv[g], k_gain) for g in range(kv_heads)], axis=0
    )
    dqkv[:, q_cols : q_cols + kv_cols] = pair.T.astype(BF16)
    pair = jnp.concatenate([dkv[kv_heads + g] for g in range(kv_heads)], axis=0)
    dqkv[:, q_cols + kv_cols :] = pair.T.astype(BF16)
    def as_row(v):
        return jnp.broadcast_to(v, (v.shape[0], 128)).T[0:1, :]

    qk[...] = jnp.zeros_like(qk)
    for n in (0, 1):
        qk[0, n : n + 1, 0:hd] = as_row(jnp.sum(gain_acc[n], axis=1, keepdims=True))

    def trade(n):
        dev = (at.sib, at.x, at.y)[n]
        return remote(qk.at[n], qk_land.at[n], e_send.at[n], e_recv.at[n], dev)

    def traded(n):
        trade(n).wait_recv()
        qk[n + 1] = qk[n] + qk_land[n]

    up.second()

    def final_d1(way, k, value):
        r = d1.rows(way, k)
        x = hid_ref[r, :].astype(F32)
        scale = lax.rsqrt(jnp.mean(x * x, axis=-1, keepdims=True) + EPSILON)
        h = x * scale
        inner = jnp.mean(value * h, axis=-1, keepdims=True)
        grad = rg_own[d1.local(k), :] + scale * (value - h * inner)
        inp[r, :] = grad.astype(BF16)

    ahead = LAG
    for q in range(4):
        r = slice(q * quarter, (q + 1) * quarter)
        d_part[r, :] = mm_nt(dqkv[r, :], wqkv[...]).astype(BF16)
        if q == 1:
            for step in range(ahead):
                d1.reduce(step, final_d1)

    def turn_hidden(i, _):
        r = pl.ds(pl.multiple_of(i * 128, 128), 128)
        x = hid_ref[r, :].astype(F32)
        scale = lax.rsqrt(jnp.mean(x * x, axis=-1, keepdims=True) + EPSILON)
        left_t[0, :, r] = (x * scale).astype(BF16).T
        left_t[1, :, r] = attn_low[r, :].T
        return 0

    def weight_part(w, _):
        r = pl.ds(pl.multiple_of(w * block, block), block)
        part[r, 0 : dqkv.shape[1]] = mm(left_t[0, r, :], dqkv[...]).astype(BF16)
        part[r, dqkv.shape[1] :] = mm(left_t[1, r, :], heads_own[...]).astype(BF16)
        return 0

    g_one = column(gain_one_ref, block)
    g_two = column(gain_two_ref, block)
    cols_acc[0] = jnp.broadcast_to(g_one, (block, 128))
    cols_acc[1] = jnp.broadcast_to(g_two, (block, 128))

    def use_down(r, value):
        g_down[r, :] = value[:, 0:units]

    def gate_gain():
        def piece(i, _):
            r = pl.ds(pl.multiple_of(i * 64, 64), 64)
            value = gate_sum[r, 0:units].astype(F32)
            total = jnp.sum(wg_ref[r, :].astype(F32) * value, axis=1, keepdims=True)
            cols_acc[3, r, :] = jnp.broadcast_to(total, (64, 128))
            return 0

        lax.fori_loop(0, block // 64, piece, 0)

    def use_up(r, value):
        value = value[:, 0:units]
        total = jnp.sum(wu_ref[r, :].astype(F32) * value, axis=1, keepdims=True)
        cols_acc[3, r, :] += jnp.broadcast_to(total, (64, 128))
        g_up[r, :] = value * cols_acc[1, r, 0:1]

    def use_rest(r, value):
        gain = cols_acc[0, r, 0:1]
        vq = value[:, 0:q_cols]
        vk = value[:, q_cols : q_cols + kv_cols]
        vv = value[:, q_cols + kv_cols : q_cols + 2 * kv_cols]
        total = jnp.sum(wq_ref[r, :].astype(F32) * vq, axis=1, keepdims=True)
        total += jnp.sum(wk_ref[r, :].astype(F32) * vk, axis=1, keepdims=True)
        total += jnp.sum(wv_ref[r, :].astype(F32) * vv, axis=1, keepdims=True)
        cols_acc[2, r, :] = jnp.broadcast_to(total, (64, 128))
        g_query[r, :] = vq * gain
        g_key[r, :] = vk * gain
        g_value[r, :] = vv * gain
        g_out[r, :] = value[:, q_cols + 2 * kv_cols :]

    def turn_all():
        lax.fori_loop(0, rows // 128, turn_hidden, 0)

    def parts():
        lax.fori_loop(0, width // block, weight_part, 0)
        rest.start()

    leaving = [
        pltpu.make_async_copy(src, dst, out_sem.at[i])
        for i, (src, dst) in enumerate(
            (
                (g_down, down_out),
                (g_up, up_out),
                (g_query, query_out),
                (g_key, key_out),
                (g_value, value_out),
                (g_out, out_out),
            )
        )
    ]

    def finish_rest():
        rest.finish(use_rest)
        for cp in leaving[2:]:
            cp.start()

    events = {
        0: (lambda: trade(0).start(), turn_all),
        1: (parts, lambda: traded(0), lambda: trade(1).start()),
        2: (lambda: traded(1), lambda: trade(2).start(), gate_gain),
        4: (rest.first, lambda: traded(2)),
        8: (lambda: down.finish(use_down), leaving[0].start),
        10: (rest.second,),
        14: (lambda: up.finish(use_up), leaving[1].start),
        18: (finish_rest,),
        19: (lambda: give_tiles(),),
    }

    def give_tile(d, owner):
        return remote(
            tile.at[owner], tile.at[owner], t_send.at[d], t_recv.at[d],
            at.z(lax.rem(t + d + 1, n_tp)),
        )

    def give_tiles():
        tile[t] = jnp.zeros(tile.shape[1:], F32)
        tile[t, 0:1, 0:block] = cols_acc[2].T[0:1, :]
        tile[t, 1:2, 0:block] = cols_acc[3].T[0:1, :]
        tile[t, 2:4, 0:128] = qk[3, 0:2, :]
        for d in range(n_tp - 1):
            give_tile(d, t).start()

    def tail(step, _):
        d1.reduce(step + ahead, final_d1)
        back.step(step + ahead - last * LAG)
        move_ffn(step + moved)
        for when, todo in events.items():

            @pl.when(step == when)
            def _():
                for thing in todo:
                    thing()

        return 0

    lax.fori_loop(0, max(chunks + 2 * last * LAG, 20), tail, 0)
    keep_all(lambda cp: cp.start())

    for w in (down, up, rest):
        w.drain()
    for thing in (d1, back, ffn, ffn_back):
        thing.drain()
    keep_all(lambda cp: cp.wait())
    for cp in leaving:
        cp.wait()

    @pl.when(c == 1)
    def _():
        give.wait_send()

    for n in range(3):
        trade(n).wait_send()
    for d in range(n_tp - 1):
        give_tile(d, lax.rem(t + n_tp - d - 1, n_tp)).wait_recv()
    total = tile[0]
    for n in range(1, n_tp):
        total = total + tile[n]
    small[...] = total
    for d in range(n_tp - 1):
        give_tile(d, t).wait_send()


def call_c(mesh, chunks, args, kept):
    (hidden_in, seq_lengths, attn_gain, ffn_gain, query_gain, key_gain,
     w_query, w_key, w_value, w_gate, w_up) = args
    (attn_low, rg_own, gate_sum, ffn_part, wgrads, wqkv_full, wo_full, heads_all, q_t, kv_all, inv_den,
     proj_t) = kept
    n_shard, n_ctx, n_tp = mesh.shape["shard"], mesh.shape["ctx"], mesh.shape["tp"]
    rows, width = hidden_in.shape
    quarter = rows // 4
    hd = query_gain.shape[0]
    q_cols, kv_cols = w_query.shape[1], w_key.shape[1]
    qkv_cols = q_cols + 2 * kv_cols
    kv_heads = kv_cols // hd
    block, units = w_gate.shape
    padded = wgrads.shape[2]
    cosine, sine = rope_tables(n_ctx * rows, hd)
    vm = pl.BlockSpec(memory_space=pltpu.VMEM)
    hbm = pl.BlockSpec(memory_space=pltpu.HBM)
    sm = pl.BlockSpec(memory_space=pltpu.SMEM)
    S = jax.ShapeDtypeStruct
    V = pltpu.VMEM
    dma = pltpu.SemaphoreType.DMA
    return pl.pallas_call(
        functools.partial(kernel_c, (n_shard, n_tp, chunks, hd)),
        out_shape=(
            S((rows, width), BF16),
            S((rows, width), BF16),
            S((block, q_cols), F32),
            S((block, kv_cols), F32),
            S((block, kv_cols), F32),
            S((block, q_cols), F32),
            S((block, units), F32),
            S((block, units), F32),
            S((8, 256), F32),
        ),
        in_specs=[sm] + [vm] * 13 + [hbm] * 11,
        out_specs=(hbm, vm) + (hbm,) * 6 + (vm,),
        scratch_shapes=[
            V((block, q_cols), F32),
            V((block, kv_cols), F32),
            V((block, kv_cols), F32),
            V((block, q_cols), F32),
            V((block, units), F32),
            V((block, units), F32),
            V((rows // 2, width), F32),
            V((rows, width), BF16),
            V((width, qkv_cols), BF16),
            V((qkv_cols, rows), F32),
            V((block, units), BF16),
            V((block, units), BF16),
            V((block, padded), BF16),
            V((rows, q_cols), BF16),
            V((width, q_cols), BF16),
            V((q_cols, rows), BF16),
            V((8, rows), F32),
            V((kv_heads, rows, hd), BF16),
            V((kv_heads, rows, hd), BF16),
            V((kv_heads, hd, rows), BF16),
            V((q_cols, rows), F32),
            V((2 * kv_heads, hd, rows), F32),
            V((2 * kv_heads, hd, rows), BF16),
            V((2 * kv_heads, hd, rows), BF16),
            V((2, hd, rows), F32),
            V((rows, qkv_cols), BF16),
            V((rows, width), BF16),
            V((rows, width), BF16),
            V((2, 2 * quarter, width), BF16),
            V((2, 2 * quarter, width), BF16),
            V((2, width, rows), BF16),
            V((width, qkv_cols + q_cols), BF16),
            V((2, 8 * block, padded), BF16),
            V((8 * block, qkv_cols + q_cols), BF16),
            V((4, block, 128), F32),
            V((4, 8, 128), F32),
            V((3, 8, 128), F32),
            V((n_tp, 8, 256), F32),
            dma((3, 7)),
            dma((3, 7)),
            dma((2, chunks)),
            dma((2, chunks)),
            dma((2, chunks)),
            dma((2, chunks)),
            dma((2, chunks)),
            dma((2, chunks)),
            dma((2, chunks)),
            dma((2, chunks)),
            dma((4,)),
            dma((4,)),
            dma((n_tp - 1,)),
            dma((n_tp - 1,)),
            dma((15,)),
            dma((6,)),
        ],
        compiler_params=pltpu.CompilerParams(
            collective_id=2, has_side_effects=True, vmem_limit_bytes=VMEM_LIMIT
        ),
    )(
        seq_lengths, attn_low, q_t, kv_all, inv_den,
        attn_gain, ffn_gain, query_gain, key_gain, w_query, w_key, w_value,
        jnp.asarray(cosine), jnp.asarray(sine), rg_own, hidden_in, wqkv_full, proj_t,
        w_gate, w_up, gate_sum, ffn_part, wgrads, heads_all, wo_full,
    )


CHUNKS = 6
CHUNKS_C = 12
PER_STEP = 4
PER_SLOT = 2


def fast_body(mesh, *args):
    (hidden_in, seq_lengths, attn_gain, ffn_gain, query_gain, key_gain,
     w_query, w_key, w_value, w_out, w_gate, w_up, w_down, out_grad) = args
    (wqkv_full, wo_full, wg_full, wu_full, wd_full, heads_all, q_t, kv_all, inv_den, proj_t,
     resid, h2t, act) = call_a(mesh, args[:13])
    attn_low, rg_own, gate_sum, ffn_part, wgrads = call_b(
        mesh, CHUNKS, seq_lengths, out_grad, wd_full, act, wg_full, wu_full, h2t, resid
    )
    (block_out, inp, g_query, g_key, g_value, g_out, g_up, g_down, small) = call_c(
        mesh, CHUNKS_C,
        (hidden_in, seq_lengths, attn_gain, ffn_gain, query_gain, key_gain, w_query, w_key,
         w_value, w_gate, w_up),
        (attn_low, rg_own, gate_sum, ffn_part, wgrads, wqkv_full, wo_full, heads_all, q_t, kv_all, inv_den,
         proj_t),
    )
    block, hd = w_query.shape[0], query_gain.shape[0]
    g_gate = gate_sum[:, : w_gate.shape[1]].astype(F32) * ffn_gain.astype(F32)[:, None]
    return (
        block_out, inp.astype(F32), small[0, :block], small[1, :block], small[2, :hd],
        small[3, :hd], g_query, g_key, g_value, g_out.T, g_gate, g_up, g_down.T,
    )


def solution(mesh):
    sizes = mesh.shape
    plane_of_eight = sizes["shard"] == 4 and sizes["ctx"] == 2 and sizes["tp"] > 1
    run = functools.partial(fast_body, mesh) if plane_of_eight else body
    placed = (
        P(("shard", "ctx"), None),
        P("shard"),
        P(("shard", "ctx")),
        P(("shard", "ctx")),
        P(),
        P(),
        P(("shard", "ctx"), "tp"),
        P(("shard", "ctx"), "tp"),
        P(("shard", "ctx"), "tp"),
        P("tp", ("shard", "ctx")),
        P(("shard", "ctx"), "tp"),
        P(("shard", "ctx"), "tp"),
        P("tp", ("shard", "ctx")),
        P(("shard", "ctx"), None),
    )
    return jax.shard_map(
        run,
        mesh=mesh,
        in_specs=placed,
        out_specs=(
            P(("shard", "ctx"), None),
            P(("shard", "ctx"), None),
            P(("shard", "ctx")),
            P(("shard", "ctx")),
            P(),
            P(),
            P(("shard", "ctx"), "tp"),
            P(("shard", "ctx"), "tp"),
            P(("shard", "ctx"), "tp"),
            P("tp", ("shard", "ctx")),
            P(("shard", "ctx"), "tp"),
            P(("shard", "ctx"), "tp"),
            P("tp", ("shard", "ctx")),
        ),
        check_vma=False,
    )
```
